32 devices in a mesh: dp: 8 (over z, y), fsdp: 4 (over x, core).
Axes of the slice: x: 2, y: 2, z: 4, core: 2. Of those that a mesh axis runs over, the one named last changes fastest.
Arguments:
- clean_latent: float32 [32, 320, 20], P(('dp', 'fsdp')), may hold values from -6 to 6
- noise: float32 [32, 320, 20], P(('dp', 'fsdp')), may hold values from -6 to 6
- text_feats: bfloat16 [32, 256, 1024], P(('dp', 'fsdp')), may hold values from -6 to 6
- text_lengths: int32 [32], P(('dp', 'fsdp')), may hold values from 5 to 256, as said below
- timesteps: int32 [32], P(('dp', 'fsdp')), may hold values from 0 to 999
- valid_frames: int32 [32], P(('dp', 'fsdp')), may hold values from 1 to 320, as said below
- w_in: float32 [2, 768, 10752], P(None, ('dp', 'fsdp')), may hold values from -0.21875 to 0.21875
- w_text: float32 [2, 1024, 1536], P(None, ('dp', 'fsdp')), may hold values from -0.1875 to 0.1875
- w_out: float32 [2, 4608, 768], P(None, ('dp', 'fsdp')), may hold values from -0.4375 to 0.4375
- gains: float32 [2, 768], P(None, ('dp', 'fsdp')), may hold values from 0.5 to 1.5
- w_lead: float32 [276, 768], P(None, ('dp', 'fsdp')), may hold values from -0.5 to 0.5
- w_head: float32 [768, 2324], P(('dp', 'fsdp')), may hold values from -0.21875 to 0.21875
- first_in: float32 [2, 768, 10752], P(None, ('dp', 'fsdp')), as said below
- second_in: float32 [2, 768, 10752], P(None, ('dp', 'fsdp')), as said below
- first_text: float32 [2, 1024, 1536], P(None, ('dp', 'fsdp')), as said below
- second_text: float32 [2, 1024, 1536], P(None, ('dp', 'fsdp')), as said below
- first_out: float32 [2, 4608, 768], P(None, ('dp', 'fsdp')), as said below
- second_out: float32 [2, 4608, 768], P(None, ('dp', 'fsdp')), as said below
- first_gains: float32 [2, 768], P(None, ('dp', 'fsdp')), as said below
- second_gains: float32 [2, 768], P(None, ('dp', 'fsdp')), as said below
- first_lead: float32 [276, 768], P(None, ('dp', 'fsdp')), as said below
- second_lead: float32 [276, 768], P(None, ('dp', 'fsdp')), as said below
- first_head: float32 [768, 2324], P(('dp', 'fsdp')), as said below
- second_head: float32 [768, 2324], P(('dp', 'fsdp')), as said below
Outputs:
- loss_sum: float32 [], replicated
- frame_count: float32 [], replicated
- grad_norm: float32 [], replicated
- moment_in: float32 [2, 768, 10752], P(None, ('dp', 'fsdp'))
- square_in: float32 [2, 768, 10752], P(None, ('dp', 'fsdp'))
- weight_in: float32 [2, 768, 10752], P(None, ('dp', 'fsdp'))
- moment_text: float32 [2, 1024, 1536], P(None, ('dp', 'fsdp'))
- square_text: float32 [2, 1024, 1536], P(None, ('dp', 'fsdp'))
- weight_text: float32 [2, 1024, 1536], P(None, ('dp', 'fsdp'))
- moment_out: float32 [2, 4608, 768], P(None, ('dp', 'fsdp'))
- square_out: float32 [2, 4608, 768], P(None, ('dp', 'fsdp'))
- weight_out: float32 [2, 4608, 768], P(None, ('dp', 'fsdp'))
- moment_gains: float32 [2, 768], P(None, ('dp', 'fsdp'))
- square_gains: float32 [2, 768], P(None, ('dp', 'fsdp'))
- weight_gains: float32 [2, 768], P(None, ('dp', 'fsdp'))
- moment_lead: float32 [276, 768], P(None, ('dp', 'fsdp'))
- square_lead: float32 [276, 768], P(None, ('dp', 'fsdp'))
- weight_lead: float32 [276, 768], P(None, ('dp', 'fsdp'))
- moment_head: float32 [768, 2324], P(('dp', 'fsdp'))
- square_head: float32 [768, 2324], P(('dp', 'fsdp'))
- weight_head: float32 [768, 2324], P(('dp', 'fsdp'))
The draws below stay inside these ranges and needn't reach their ends.
Inputs may be any that keep to these rules, and one draw needn't show every extreme that they name: `text_lengths`: the first clip's caption has 5 tokens and the second's 256. `valid_frames`: the last clip has all 320 frames. `first_in`: entries of both signs. `second_in`: Positive. `first_text`: entries of both signs. `second_text`: Positive. `first_out`: entries of both signs. `second_out`: Positive. `first_gains`: entries of both signs. `second_gains`: Positive. `first_lead`: entries of both signs. `second_lead`: Positive. `first_head`: entries of both signs. `second_head`: Positive.
All inputs are finite; a program needn't handle non-finite values.
Results may differ from the reference program's by a relative error of at most 0.013.
The reference program's roundings to bfloat16 on the way count: a program that leaves them out, or rounds other values in their place, can miss the bound.
Values may be sent and summed in bfloat16 or wider, within the bound.
A program may use at most 448 MiB of HBM per device.

```python
import math
import jax
import jax.numpy as jnp
from jax import lax

D = 768
HEADS = 12
HEAD_DIM = 64
FF = 3072
TEXT_DIM = 1024
CH = 20
FREQS = 256
FRAMES = 320
CAPTION = 256
LAYERS = 2
STEP = 10
CLIPS_DEV = 1
CLIPS = 32
DP_WAYS = 8
FSDP_WAYS = 4
PARAMS = 28737024


def moment_draw(key, shape, size, second):
    grad_size = size * PARAMS ** (-0.5)
    key_mag, key_sign = jax.random.split(jax.random.fold_in(key, 7))
    factor = jnp.exp(jax.random.uniform(key_mag, shape, jnp.float32, math.log(0.5), math.log(2.0)))
    if second:
        return grad_size * grad_size * factor
    signs = jnp.where(jax.random.bernoulli(key_sign, 0.5, shape), 1.0, -1.0)
    return grad_size * factor * signs


def draw_first_in(key, part):
    return moment_draw(key, (LAYERS, D, 10 * D + FF), 1.0, False)


def draw_second_in(key, part):
    return moment_draw(key, (LAYERS, D, 10 * D + FF), 1.0, True)


def draw_first_text(key, part):
    return moment_draw(key, (LAYERS, TEXT_DIM, 2 * D), 1.0, False)


def draw_second_text(key, part):
    return moment_draw(key, (LAYERS, TEXT_DIM, 2 * D), 1.0, True)


def draw_first_out(key, part):
    return moment_draw(key, (LAYERS, 2 * D + FF, D), 1.0, False)


def draw_second_out(key, part):
    return moment_draw(key, (LAYERS, 2 * D + FF, D), 1.0, True)


def draw_first_gains(key, part):
    return moment_draw(key, (LAYERS, D), 1.5, False)


def draw_second_gains(key, part):
    return moment_draw(key, (LAYERS, D), 1.5, True)


def draw_first_lead(key, part):
    return moment_draw(key, (FREQS + CH, D), 1.0, False)


def draw_second_lead(key, part):
    return moment_draw(key, (FREQS + CH, D), 1.0, True)


def draw_first_head(key, part):
    return moment_draw(key, (D, 3 * D + CH), 1.0, False)


def draw_second_head(key, part):
    return moment_draw(key, (D, 3 * D + CH), 1.0, True)


def draw_text_lengths(key, part):
    clip_index = jnp.arange(CLIPS, dtype=jnp.int32)
    lengths = jax.random.randint(jax.random.fold_in(key, 11), (CLIPS,), 5, CAPTION + 1)
    lengths = jnp.where(clip_index == 0, 5, lengths)
    return jnp.where(clip_index == 1, CAPTION, lengths).astype(jnp.int32)


def draw_valid_frames(key, part):
    clip_index = jnp.arange(CLIPS, dtype=jnp.int32)
    device = clip_index // CLIPS_DEV
    row_index = device // FSDP_WAYS
    col_index = device % FSDP_WAYS
    row_span = max(DP_WAYS - 1, 1)
    col_span = max(FSDP_WAYS - 1, 1)
    tenths = 3 + 7 * (row_index * col_span + col_index * row_span) // (2 * row_span * col_span)
    base_count = FRAMES * tenths // 10
    cut_count = jax.random.randint(jax.random.fold_in(key, 13), (CLIPS,), 0, FRAMES // 10 + 1)
    valid = jnp.maximum(base_count - cut_count, 1)
    return jnp.where(clip_index == CLIPS - 1, FRAMES, valid).astype(jnp.int32)


def plant(array, stream_key, smallest, largest):
    index_at = [jax.random.randint(jax.random.fold_in(stream_key, axis), (), 0, length) for axis, length in enumerate(array.shape)]
    widest = array.shape.index(max(array.shape))
    next_to = index_at[:widest] + [(index_at[widest] + 1) % array.shape[widest]] + index_at[widest + 1:]
    return array.at[tuple(index_at)].set(smallest).at[tuple(next_to)].set(largest)


def block_scale(key, shape, cuts, least, top_value):
    level = 1.0
    for axis_at, shards_of in cuts:
        heights = jax.random.uniform(jax.random.fold_in(jax.random.fold_in(key, 6), axis_at), (shards_of,), jnp.float32, least / len(cuts), top_value / len(cuts))
        level = level * jnp.repeat(jnp.exp(heights), shape[axis_at] // shards_of).reshape((-1,) + (1,) * (len(shape) - 1 - axis_at))
    return level


def scatter_about(stream_key, shape, scale, bound, cuts=(), held_as=jnp.bfloat16):
    level = block_scale(stream_key, shape, cuts, -0.22, 0.18) if cuts else 1.0
    array = jax.random.normal(stream_key, shape, jnp.float32) * scale * level
    return jnp.minimum(jnp.maximum(array, -bound), bound).astype(held_as)


def setup_inputs(seed: int = 0) -> dict:
    seeds = jax.random.split(jax.random.key(seed), 25)
    return {
        "clean_latent": scatter_about(seeds[0], (CLIPS, FRAMES, CH), 1.0, 6.0, ((0, 32),), jnp.float32),
        "noise": scatter_about(seeds[1], (CLIPS, FRAMES, CH), 1.0, 6.0, ((0, 32),), jnp.float32),
        "text_feats": scatter_about(seeds[2], (CLIPS, CAPTION, TEXT_DIM), 1.0, 6.0, ((0, 32),)),
        "text_lengths": draw_text_lengths(jax.random.fold_in(seeds[24], 71), 0),
        "timesteps": plant(jax.random.randint(seeds[4], (CLIPS,), 0, 1000), jax.random.fold_in(seeds[4], 1), 0, 999).astype(jnp.int32),
        "valid_frames": draw_valid_frames(jax.random.fold_in(seeds[24], 71), 0),
        "w_in": scatter_about(seeds[6], (LAYERS, D, 10 * D + FF), D ** -0.5, 0.21875, ((1, 32),), jnp.float32),
        "w_text": scatter_about(seeds[7], (LAYERS, TEXT_DIM, 2 * D), TEXT_DIM ** -0.5, 0.1875, ((1, 32),), jnp.float32),
        "w_out": scatter_about(seeds[8], (LAYERS, 2 * D + FF, D), (D // 4) ** -0.5, 0.4375, ((1, 32),), jnp.float32),
        "gains": jnp.clip(1.0 + 0.1 * jax.random.normal(seeds[9], (LAYERS, D), jnp.float32), 0.5, 1.5),
        "w_lead": scatter_about(seeds[10], (FREQS + CH, D), 128 ** -0.5, 0.5, ((1, 32),), jnp.float32),
        "w_head": scatter_about(seeds[11], (D, 3 * D + CH), D ** -0.5, 0.21875, ((0, 32),), jnp.float32),
        "first_in": draw_first_in(jax.random.fold_in(seeds[24], 71), 0),
        "second_in": draw_second_in(jax.random.fold_in(seeds[24], 71), 0),
        "first_text": draw_first_text(jax.random.fold_in(seeds[24], 71), 0),
        "second_text": draw_second_text(jax.random.fold_in(seeds[24], 71), 0),
        "first_out": draw_first_out(jax.random.fold_in(seeds[24], 71), 0),
        "second_out": draw_second_out(jax.random.fold_in(seeds[24], 71), 0),
        "first_gains": draw_first_gains(jax.random.fold_in(seeds[24], 71), 0),
        "second_gains": draw_second_gains(jax.random.fold_in(seeds[24], 71), 0),
        "first_lead": draw_first_lead(jax.random.fold_in(seeds[24], 71), 0),
        "second_lead": draw_second_lead(jax.random.fold_in(seeds[24], 71), 0),
        "first_head": draw_first_head(jax.random.fold_in(seeds[24], 71), 0),
        "second_head": draw_second_head(jax.random.fold_in(seeds[24], 71), 0),
    }


@jax.custom_vjp
def low(v):
    return lax.optimization_barrier(v.astype(jnp.bfloat16)).astype(jnp.float32)

@jax.custom_vjp
def low_back(v):
    return v

def low_keep(v):
    return (low(v), None)

def low_pass(kept, grad):
    return (grad,)

def back_keep(v):
    return (v, None)

def back_low(kept, grad):
    return (low(grad),)
low.defvjp(low_keep, low_pass)
low_back.defvjp(back_keep, back_low)
EPSILON = 1e-06
NEGATIVE = -1e+30
BETA_ONE = 0.5
BETA_TWO = 0.5
LEARN_RATE = 0.02
GAIN_RATE = 0.3
WEIGHT_DECAY = 0.01
ADAM_EPSILON = 1e-08
CLIP_NORM = 1.0

def dense(left, right):
    return low_back(jnp.matmul(low(left), low(right), precision=lax.Precision.HIGHEST))

def norm_rows(values):
    centred = values - lax.optimization_barrier(jnp.mean(values, -1, keepdims=True))
    return centred * lax.rsqrt(lax.optimization_barrier(jnp.mean(centred * centred, -1, keepdims=True)) + EPSILON)

def split_heads(values):
    return values.reshape(values.shape[0], values.shape[1], HEADS, HEAD_DIM)

def attend(queries, keys, values, keep):
    scores = jnp.einsum('bqhd,bkhd->bhqk', split_heads(low(queries)), split_heads(low(keys)), precision=lax.Precision.HIGHEST) * HEAD_DIM ** (-0.5)
    scores = jnp.where(keep[:, None, None, :], low_back(scores), NEGATIVE)
    shifted = jnp.exp(scores - lax.optimization_barrier(jnp.max(scores, -1, keepdims=True)))
    probs = shifted / lax.optimization_barrier(jnp.sum(shifted, -1, keepdims=True))
    mixed = jnp.einsum('bhqk,bkhd->bqhd', low(probs), split_heads(low(values)), precision=lax.Precision.HIGHEST)
    return low_back(mixed).reshape(queries.shape)

def noise_level(steps):
    phase = (steps.astype(jnp.float32) / 1000.0 + 0.008) / 1.008 * (math.pi / 2)
    return jnp.cos(phase) ** 2

def time_features(steps):
    half_width = FREQS // 2
    frequency = jnp.exp(-math.log(10000.0) * jnp.arange(half_width, dtype=jnp.float32) / half_width)
    angles = steps.astype(jnp.float32)[:, None] * frequency[None, :]
    return jnp.concatenate([jnp.cos(angles), jnp.sin(angles)], -1)

def block(stream, cond, text, frame_keep, text_keep, w_joint, w_textkv, w_back, gain):
    modulation = dense(cond, w_joint[:, 4 * D + FF:])[:, None, :]
    normed = norm_rows(stream) * (1.0 + modulation[..., D:2 * D]) + modulation[..., :D]
    self_proj = dense(normed, w_joint[:, :3 * D])
    mixed = attend(self_proj[..., :D], self_proj[..., D:2 * D], self_proj[..., 2 * D:], frame_keep)
    stream = stream + modulation[..., 2 * D:3 * D] * dense(mixed, w_back[:D])
    normed = norm_rows(stream) * low(gain)
    cross_query = dense(normed, w_joint[:, 3 * D:4 * D])
    cross_kv = dense(text, w_textkv)
    mixed = attend(cross_query, cross_kv[..., :D], cross_kv[..., D:], text_keep)
    stream = stream + dense(mixed, w_back[D:2 * D])
    normed = norm_rows(stream) * (1.0 + modulation[..., 4 * D:5 * D]) + modulation[..., 3 * D:4 * D]
    hidden = jax.nn.gelu(dense(normed, w_joint[:, 4 * D:4 * D + FF]))
    return stream + modulation[..., 5 * D:] * dense(hidden, w_back[2 * D:])

def group_sum(params, clean, noise, text, text_len, steps, valid):
    w_in, w_text, w_out, gains, w_lead, w_head = params
    level = noise_level(steps)[:, None, None]
    noisy = jnp.sqrt(level) * clean + jnp.sqrt(1.0 - level) * noise
    temb = dense(jax.nn.silu(dense(time_features(steps), w_lead[:FREQS])), w_head[:, :D])
    cond = jax.nn.silu(temb)
    stream = dense(noisy, w_lead[FREQS:])
    frame_keep = jnp.arange(FRAMES, dtype=jnp.int32)[None, :] < valid[:, None]
    text_keep = jnp.arange(CAPTION, dtype=jnp.int32)[None, :] < text_len[:, None]
    for index in range(LAYERS):
        stream = block(stream, cond, text, frame_keep, text_keep, w_in[index], w_text[index], w_out[index], gains[index])
    final_mod = dense(cond, w_head[:, D:3 * D])[:, None, :]
    normed = norm_rows(stream) * (1.0 + final_mod[..., D:]) + final_mod[..., :D]
    error = dense(normed, w_head[:, 3 * D:]) - noise
    return jnp.sum(jnp.where(frame_keep[..., None], error * error, 0.0))

def adam_update(weight, grad, first, second, rate):
    first_new = BETA_ONE * first + (1.0 - BETA_ONE) * grad
    second_new = BETA_TWO * second + (1.0 - BETA_TWO) * grad * grad
    first_hat = first_new / (1.0 - BETA_ONE ** STEP)
    second_hat = second_new / (1.0 - BETA_TWO ** STEP)
    weight_new = weight - rate * (first_hat / (jnp.sqrt(second_hat) + ADAM_EPSILON) + WEIGHT_DECAY * weight)
    return (first_new, second_new, weight_new)

def reference(clean_latent, noise, text_feats, text_lengths, timesteps, valid_frames, w_in, w_text, w_out, gains, w_lead, w_head, first_in, second_in, first_text, second_text, first_out, second_out, first_gains, second_gains, first_lead, second_lead, first_head, second_head):
    params = (w_in, w_text, w_out, gains, w_lead, w_head)
    group = min(8, CLIPS)
    frame_count = jnp.sum(valid_frames).astype(jnp.float32)
    back_scale = 1.0 / frame_count

    def split(values):
        return values.reshape((CLIPS // group, group) + values.shape[1:])
    data = (split(clean_latent), split(noise), split(text_feats.astype(jnp.float32)), split(text_lengths), split(timesteps), split(valid_frames))

    def one_group(carry, batch_data):
        grads, total = carry
        value, pull = jax.vjp(lambda weights: group_sum(weights, *batch_data), params)
        grad_new, = pull(back_scale)
        return ((jax.tree.map(jnp.add, grads, grad_new), total + value), None)
    start = (jax.tree.map(jnp.zeros_like, params), jnp.zeros((), jnp.float32))
    (grads, loss_sum), _ = lax.scan(one_group, start, data)
    grad_norm = jnp.sqrt(sum((jnp.sum(item * item) for item in grads)))
    factor = CLIP_NORM / jnp.maximum(grad_norm, CLIP_NORM)
    firsts = (first_in, first_text, first_out, first_gains, first_lead, first_head)
    seconds = (second_in, second_text, second_out, second_gains, second_lead, second_head)
    rates = (LEARN_RATE, LEARN_RATE, LEARN_RATE, GAIN_RATE, LEARN_RATE, LEARN_RATE)
    results = []
    for weight, grad, first, second, rate in zip(params, grads, firsts, seconds, rates):
        results.extend(adam_update(weight, grad * factor, first, second, rate))
    return (loss_sum, frame_count, grad_norm, results[0], results[1], results[2], results[3], results[4], results[5], results[6], results[7], results[8], results[9], results[10], results[11], results[12], results[13], results[14], results[15], results[16], results[17])
```

```python
import functools
import math

import jax
import jax.numpy as jnp
from jax import lax
from jax.experimental import pallas as pl
from jax.experimental.pallas import tpu as pltpu
from jax.sharding import PartitionSpec as P

D = 768
HEADS = 12
HEAD_DIM = 64
FF = 3072
FREQS = 256
LAYERS = 2
STEP = 10
MOD = 6 * D
JOINT = 4 * D + FF

EPSILON = 1e-06
NEGATIVE = -1e30
BETA_ONE = 0.5
BETA_TWO = 0.5
LEARN_RATE = 0.02
GAIN_RATE = 0.3
WEIGHT_DECAY = 0.01
ADAM_EPSILON = 1e-08
CLIP_NORM = 1.0

ALL = ("dp", "fsdp")
MESH = pl.DeviceIdType.MESH
VMEM_LIMIT = 60 * 1024 * 1024


def place(ways):
    dp_ways, fsdp_ways = ways
    row, col = lax.axis_index("dp"), lax.axis_index("fsdp")
    sizes = (dp_ways // 2, 2, fsdp_ways // 2)
    spot = (row // 2, lax.rem(row, 2), col // 2)
    return sizes, spot, lax.rem(col, 2)


def device_at(spot, core):
    z, y, x = spot
    return (z * 2 + y, x * 2 + core)


def moved(spot, axis, size, steps):
    spot = list(spot)
    spot[axis] = lax.rem(spot[axis] + steps, size)
    return tuple(spot)


def greet_peers(sizes, spot, core):
    barrier = pltpu.get_barrier_semaphore()
    count = 1
    pl.semaphore_signal(barrier, inc=1, device_id=device_at(spot, 1 - core), device_id_type=MESH)
    for axis in range(3):
        for steps in range(1, sizes[axis]):
            count += 1
            pl.semaphore_signal(
                barrier,
                inc=1,
                device_id=device_at(moved(spot, axis, sizes[axis], steps), core),
                device_id_type=MESH,
            )
    pl.semaphore_wait(barrier, count)


def remote(source, target, send, recv, device):
    return pltpu.make_async_remote_copy(
        src_ref=source, dst_ref=target, send_sem=send, recv_sem=recv, device_id=device, device_id_type=MESH
    )


def exchange_kernel(ways, shared, x_ref, out_ref, send_sem, recv_sem):
    dp_ways, fsdp_ways = ways
    count = dp_ways * fsdp_ways
    me = lax.axis_index("dp") * fsdp_ways + lax.axis_index("fsdp")

    def device(index):
        return (index // fsdp_ways, lax.rem(index, fsdp_ways))

    barrier = pltpu.get_barrier_semaphore()
    for step in range(1, count):
        pl.semaphore_signal(
            barrier, inc=1, device_id=device(lax.rem(me + step, count)), device_id_type=MESH
        )
    pl.semaphore_wait(barrier, count - 1)

    def copy(step):
        other = lax.rem(me + step, count)
        return remote(
            x_ref if shared else x_ref.at[other],
            out_ref.at[me],
            send_sem.at[step],
            recv_sem.at[step],
            device(other),
        )

    for step in range(1, count):
        copy(step).start()
    out_ref[me] = x_ref[...] if shared else x_ref[me]
    for step in range(1, count):
        origin = lax.rem(me + count - step, count)
        remote(
            x_ref if shared else x_ref.at[0],
            out_ref.at[origin],
            send_sem.at[step],
            recv_sem.at[step],
            device(origin),
        ).wait_recv()
    for step in range(1, count):
        copy(step).wait_send()


def exchange(values, ways, shared, number):
    count = ways[0] * ways[1]
    tile = values.shape if shared else values.shape[1:]
    return pl.pallas_call(
        functools.partial(exchange_kernel, ways, shared),
        out_shape=jax.ShapeDtypeStruct((count,) + tile, values.dtype),
        in_specs=[pl.BlockSpec(memory_space=pltpu.VMEM)],
        out_specs=pl.BlockSpec(memory_space=pltpu.VMEM),
        scratch_shapes=[pltpu.SemaphoreType.DMA((count,)), pltpu.SemaphoreType.DMA((count,))],
        compiler_params=pltpu.CompilerParams(
            collective_id=number, has_side_effects=True, vmem_limit_bytes=VMEM_LIMIT
        ),
    )(values)


def gather_kernel(ways, rows, halves, items, layers, *refs):
    members = len(rows)
    shards = refs[:members]
    fulls = refs[members : members + members * layers]
    rest = refs[members + members * layers :]
    stages = rest[:members]
    blocks = rest[members : 2 * members]
    pre_send, pre_recv, own_sem, put_sem, z_send, z_recv, a_send, a_recv, b_send, b_recv, c_send, c_recv = rest[2 * members :]
    sizes, spot, core = place(ways)
    z, y, x = spot
    partner = device_at(spot, 1 - core)
    greet_peers(sizes, spot, core)

    def full(layer, member):
        return fulls[layer * members + member]

    pre = []
    for layer in range(layers):
        for member in range(members):
            height, half = rows[member], halves[member]
            place_in = stages[member].at[layer, pl.ds(pl.multiple_of(core * height, 8), height)]
            mine = shards[member].at[layer, :, pl.ds(pl.multiple_of(core * half, 128), half)]
            other = shards[member].at[layer, :, pl.ds(pl.multiple_of((1 - core) * half, 128), half)]
            index = layer * members + member
            sent = remote(other, place_in, pre_send.at[index], pre_recv.at[index], partner)
            sent.start()
            kept = pltpu.make_async_copy(mine, place_in, own_sem.at[index])
            kept.start()
            pre.append((sent, kept))
    arrived = set()
    puts = []

    def ready(layer, member):
        if (layer, member) in arrived:
            return
        arrived.add((layer, member))
        index = layer * members + member
        height = rows[member]
        sent, kept = pre[index]
        kept.wait()
        theirs = stages[member].at[layer, pl.ds(pl.multiple_of((1 - core) * height, 8), height)]
        remote(theirs, theirs, pre_send.at[index], pre_recv.at[index], partner).wait_recv()
        blocks[member][layer] = stages[member][layer].astype(jnp.bfloat16)
        half = halves[member]
        put = pltpu.make_async_copy(
            blocks[member].at[layer],
            full(layer, member).at[z, y, x, :, pl.ds(pl.multiple_of(core * half, 128), half)],
            put_sem.at[index],
        )
        put.start()
        puts.append((index, put))

    def columns(member, start, size, side):
        return pl.ds(pl.multiple_of(side * halves[member] + start, 128), size)

    sent_all = []

    def z_start(i):
        layer, member, start, size, order = items[i]
        ready(layer, member)
        for steps in range(1, sizes[0]):
            copy = remote(
                blocks[member].at[layer, :, pl.ds(start, size)],
                full(layer, member).at[z, y, x, :, columns(member, start, size, core)],
                z_send.at[i, steps - 1],
                z_recv.at[i, steps - 1],
                device_at(moved(spot, 0, sizes[0], steps), core),
            )
            copy.start()
            sent_all.append(copy)

    def z_wait(i):
        layer, member, start, size, order = items[i]
        for steps in range(1, sizes[0]):
            origin = lax.rem(z + sizes[0] - steps, sizes[0])
            land = full(layer, member).at[origin, y, x, :, columns(member, start, size, core)]
            remote(land, land, z_send.at[i, steps - 1], z_recv.at[i, steps - 1], partner).wait_recv()

    put_done = set()

    def own_put(layer, member):
        index = layer * members + member
        if index not in put_done:
            put_done.add(index)
            dict(puts)[index].wait()

    def region(i, first_index, second_index, side):
        layer, member, start, size, order = items[i]
        cols = columns(member, start, size, side)
        if order == 0:
            return full(layer, member).at[:, second_index, first_index, :, cols]
        return full(layer, member).at[:, first_index, second_index, :, cols]

    def line(i, second_index, side):
        layer, member, start, size, order = items[i]
        cols = columns(member, start, size, side)
        if order == 0:
            return full(layer, member).at[:, second_index, :, :, cols]
        return full(layer, member).at[:, :, second_index, :, cols]

    def axes(i):
        return (2, 1) if items[i][4] == 0 else (1, 2)

    def a_start(i):
        layer, member = items[i][:2]
        own_put(layer, member)
        first, second = axes(i)
        for steps in range(1, sizes[first]):
            mine = region(i, spot[first], spot[second], core)
            copy = remote(
                mine, mine, a_send.at[i, steps - 1], a_recv.at[i, steps - 1],
                device_at(moved(spot, first, sizes[first], steps), core),
            )
            copy.start()
            sent_all.append(copy)

    def a_wait(i):
        first, second = axes(i)
        for steps in range(1, sizes[first]):
            origin = lax.rem(spot[first] + sizes[first] - steps, sizes[first])
            land = region(i, origin, spot[second], core)
            remote(land, land, a_send.at[i, steps - 1], a_recv.at[i, steps - 1], partner).wait_recv()

    def b_start(i):
        first, second = axes(i)
        mine = line(i, spot[second], core)
        for steps in range(1, sizes[second]):
            copy = remote(
                mine, mine, b_send.at[i, steps - 1], b_recv.at[i, steps - 1],
                device_at(moved(spot, second, sizes[second], steps), core),
            )
            copy.start()
            sent_all.append(copy)
        copy = remote(mine, mine, c_send.at[i, 0], c_recv.at[i, 0], partner)
        copy.start()
        sent_all.append(copy)

    def b_wait(i):
        first, second = axes(i)
        for steps in range(1, sizes[second]):
            origin = lax.rem(spot[second] + sizes[second] - steps, sizes[second])
            land = line(i, origin, core)
            remote(land, land, b_send.at[i, steps - 1], b_recv.at[i, steps - 1], partner).wait_recv()
            copy = remote(land, land, c_send.at[i, steps], c_recv.at[i, steps], partner)
            copy.start()
            sent_all.append(copy)

    def c_wait(i):
        first, second = axes(i)
        for steps in range(sizes[second]):
            origin = lax.rem(spot[second] + sizes[second] - steps, sizes[second])
            land = line(i, origin, 1 - core)
            remote(land, land, c_send.at[i, steps], c_recv.at[i, steps], partner).wait_recv()

    total = len(items)
    ahead, lag_b, lag_c = 4, 2, 4
    for i in range(min(ahead, total)):
        z_start(i)
    for i in range(total + lag_c):
        if i < total:
            z_wait(i)
            if i + ahead < total:
                z_start(i + ahead)
            a_start(i)
        if 0 <= i - lag_b < total:
            a_wait(i - lag_b)
            b_start(i - lag_b)
        if 0 <= i - lag_c < total:
            b_wait(i - lag_c)
    for i in range(total):
        c_wait(i)
    for sent, _ in pre:
        sent.wait_send()
    for copy in sent_all:
        copy.wait_send()


def gather_weights(shards, halves, ways, number, items):
    layers = shards[0].shape[0]
    rows = [s.shape[1] for s in shards]
    members = len(shards)
    sizes = (ways[0] // 2, 2, ways[1] // 2)
    count = layers * members
    n = len(items)
    sem = pltpu.SemaphoreType.DMA
    out = pl.pallas_call(
        functools.partial(gather_kernel, ways, rows, halves, items, layers),
        out_shape=[
            jax.ShapeDtypeStruct(sizes + (2 * rows[m], 2 * halves[m]), jnp.bfloat16)
            for _ in range(layers)
            for m in range(members)
        ],
        in_specs=[pl.BlockSpec(memory_space=pl.ANY)] * members,
        out_specs=[pl.BlockSpec(memory_space=pl.ANY)] * count,
        scratch_shapes=[pltpu.VMEM((layers, 2 * rows[m], halves[m]), jnp.float32) for m in range(members)]
        + [pltpu.VMEM((layers, 2 * rows[m], halves[m]), jnp.bfloat16) for m in range(members)]
        + [sem((count,))] * 4
        + [sem((n, sizes[0]))] * 2
        + [sem((n, max(sizes)))] * 6,
        compiler_params=pltpu.CompilerParams(
            collective_id=number, has_side_effects=True, vmem_limit_bytes=VMEM_LIMIT
        ),
    )(*shards)
    return [
        [out[l * members + m].reshape(-1, 2 * halves[m]) for m in range(members)] for l in range(layers)
    ]


def plan(halves, layers):
    items = []
    for layer in range(layers):
        flip = layer % 2
        for member, width in enumerate(halves):
            size = width // 4 if width % 512 == 0 else (width // 2 if width % 256 == 0 else 128)
            for start in range(0, width, size):
                items.append((layer, member, start, size, (len(items) + 0) % 2))
    return items


def scatter_kernel(ways, rows, halves, items, layers, *refs):
    members = len(rows)
    n = len(items)
    grads = refs[: members * layers]
    outs = refs[members * layers : members * layers + members]
    rest = list(refs[members * layers + members :])

    def take(count):
        taken = rest[:count]
        del rest[:count]
        return taken

    locals_ = take(members)
    whole, part_a, part_b, part_z, sums = (take(n) for _ in range(5))
    l_sem, c_send, c_recv, a_send, a_recv, b_send, b_recv, z_send, z_recv, e_send, e_recv, o_sem = rest
    sizes, spot, core = place(ways)
    z, y, x = spot
    partner = device_at(spot, 1 - core)
    greet_peers(sizes, spot, core)
    sent_all = []
    seen = {}
    slots = []
    for layer, member, *_ in items:
        slots.append(seen.get(member, 0) % 2)
        seen[member] = seen.get(member, 0) + 1

    def columns(i, side):
        _, member, start, size, _ = items[i]
        return pl.ds(pl.multiple_of(side * halves[member] + start, 128), size)

    def grad(i):
        return grads[items[i][0] * members + items[i][1]]

    def local(i):
        return locals_[items[i][1]].at[slots[i]]

    def axes(i):
        return (2, 1) if items[i][4] == 0 else (1, 2)

    def l_copy(i):
        return pltpu.make_async_copy(grad(i).at[:, :, :, :, columns(i, core)], local(i), l_sem.at[i])

    def c_copy(i):
        return remote(
            grad(i).at[:, :, :, :, columns(i, 1 - core)], whole[i], c_send.at[i], c_recv.at[i], partner
        )

    def line(i, second_index):
        if items[i][4] == 0:
            return whole[i].at[:, second_index]
        return whole[i].at[:, :, second_index]

    def send(copy):
        copy.start()
        sent_all.append(copy)

    def add_local(i):
        kept = local(i)

        @pl.loop(0, sizes[0])
        def _(index):
            whole[i][index] = (
                whole[i][index].astype(jnp.float32) + kept[index].astype(jnp.float32)
            ).astype(jnp.bfloat16)

    def a_start(i):
        first, second = axes(i)
        for steps in range(1, sizes[second]):
            target = moved(spot, second, sizes[second], steps)
            send(
                remote(
                    line(i, target[second]), part_a[i].at[steps - 1],
                    a_send.at[i, steps - 1], a_recv.at[i, steps - 1], device_at(target, core),
                )
            )

    def a_finish(i):
        first, second = axes(i)
        for steps in range(1, sizes[second]):
            land = part_a[i].at[steps - 1]
            remote(land, land, a_send.at[i, steps - 1], a_recv.at[i, steps - 1], partner).wait_recv()
        mine = line(i, spot[second])

        @pl.loop(0, sizes[0])
        def _(index):
            total = mine[index].astype(jnp.float32)
            for steps in range(1, sizes[second]):
                total = total + part_a[i][steps - 1, index].astype(jnp.float32)
            mine[index] = total.astype(jnp.bfloat16)

    def b_start(i):
        first, second = axes(i)
        for steps in range(1, sizes[first]):
            target = moved(spot, first, sizes[first], steps)
            send(
                remote(
                    whole[i].at[:, target[1], target[2]], part_b[i].at[steps - 1],
                    b_send.at[i, steps - 1], b_recv.at[i, steps - 1], device_at(target, core),
                )
            )

    def b_finish(i):
        first, second = axes(i)
        for steps in range(1, sizes[first]):
            land = part_b[i].at[steps - 1]
            remote(land, land, b_send.at[i, steps - 1], b_recv.at[i, steps - 1], partner).wait_recv()
        mine = whole[i].at[:, y, x]

        @pl.loop(0, sizes[0])
        def _(index):
            total = mine[index].astype(jnp.float32)
            for steps in range(1, sizes[first]):
                total = total + part_b[i][steps - 1, index].astype(jnp.float32)
            mine[index] = total.astype(jnp.bfloat16)

    def z_start(i):
        for steps in range(1, sizes[0]):
            target = moved(spot, 0, sizes[0], steps)
            send(
                remote(
                    whole[i].at[target[0], y, x], part_z[i].at[steps - 1],
                    z_send.at[i, steps - 1], z_recv.at[i, steps - 1], device_at(target, core),
                )
            )

    def owned(i, side):
        layer, member = items[i][:2]
        height = rows[member]
        return sums[i].at[pl.ds(pl.multiple_of(side * height, 8), height)]

    def e_copy(i):
        layer, member = items[i][:2]
        return remote(
            owned(i, 1 - core), outs[member].at[layer, :, columns(i, core)],
            e_send.at[i], e_recv.at[i], partner,
        )

    def o_copy(i):
        layer, member = items[i][:2]
        return pltpu.make_async_copy(
            owned(i, core), outs[member].at[layer, :, columns(i, core)], o_sem.at[i]
        )

    def z_finish(i):
        for steps in range(1, sizes[0]):
            land = part_z[i].at[steps - 1]
            remote(land, land, z_send.at[i, steps - 1], z_recv.at[i, steps - 1], partner).wait_recv()
        total = whole[i][z, y, x].astype(jnp.float32)
        for steps in range(1, sizes[0]):
            total = total + part_z[i][steps - 1].astype(jnp.float32)
        sums[i][...] = total
        e_copy(i).start()
        o_copy(i).start()

    ahead = 3
    lag_a, lag_b, lag_z = 2, 4, 6
    for i in range(min(2, n)):
        l_copy(i).start()
    for i in range(min(ahead, n)):
        send(c_copy(i))
    for i in range(n + lag_z):
        if i < n:
            c_copy(i).wait_recv()
            l_copy(i).wait()
            add_local(i)
            a_start(i)
            if i + 2 < n:
                l_copy(i + 2).start()
            if i + ahead < n:
                send(c_copy(i + ahead))
        if 0 <= i - lag_a < n:
            a_finish(i - lag_a)
            b_start(i - lag_a)
        if 0 <= i - lag_b < n:
            b_finish(i - lag_b)
            z_start(i - lag_b)
        if 0 <= i - lag_z < n:
            z_finish(i - lag_z)
    for i in range(n):
        e_copy(i).wait()
        o_copy(i).wait()
    for copy in sent_all:
        copy.wait_send()


def scatter_grads(grads, rows, halves, ways, number, items):
    layers, members = len(grads), len(rows)
    sizes = (ways[0] // 2, 2, ways[1] // 2)
    n = len(items)
    sem = pltpu.SemaphoreType.DMA
    low = jnp.bfloat16

    def axis_sizes(order):
        return (sizes[2], sizes[1]) if order == 0 else (sizes[1], sizes[2])

    most = [max(s for _, m, _, s, _ in items if m == member) for member in range(members)]
    scratch = [pltpu.VMEM((2,) + sizes + (2 * rows[m], most[m]), low) for m in range(members)]
    scratch += [pltpu.VMEM(sizes + (2 * rows[m], s), low) for _, m, _, s, _ in items]
    scratch += [
        pltpu.VMEM((axis_sizes(o)[1] - 1, sizes[0], axis_sizes(o)[0], 2 * rows[m], s), low)
        for _, m, _, s, o in items
    ]
    scratch += [
        pltpu.VMEM((axis_sizes(o)[0] - 1, sizes[0], 2 * rows[m], s), low) for _, m, _, s, o in items
    ]
    scratch += [pltpu.VMEM((sizes[0] - 1, 2 * rows[m], s), low) for _, m, _, s, _ in items]
    scratch += [pltpu.VMEM((2 * rows[m], s), jnp.float32) for _, m, _, s, _ in items]
    scratch += [sem((n,))] * 3 + [sem((n, max(sizes)))] * 6 + [sem((n,))] * 3
    flat = [
        grads[l][m].reshape(sizes + (2 * rows[m], 2 * halves[m]))
        for l in range(layers)
        for m in range(members)
    ]
    return pl.pallas_call(
        functools.partial(scatter_kernel, ways, rows, halves, items, layers),
        out_shape=[
            jax.ShapeDtypeStruct((layers, rows[m], 2 * halves[m]), jnp.float32) for m in range(members)
        ],
        in_specs=[pl.BlockSpec(memory_space=pl.ANY)] * len(flat),
        out_specs=[pl.BlockSpec(memory_space=pl.ANY)] * members,
        scratch_shapes=scratch,
        compiler_params=pltpu.CompilerParams(
            collective_id=number, has_side_effects=True, vmem_limit_bytes=VMEM_LIMIT
        ),
    )(*flat)


def to_low(values):
    return values.astype(jnp.bfloat16)


def norm_rows(values):
    centred = values - jnp.mean(values, -1, keepdims=True)
    return centred * lax.rsqrt(jnp.mean(centred * centred, -1, keepdims=True) + EPSILON)


def modulate(stream, shift, scale_part):
    return norm_rows(stream) * (1.0 + scale_part) + shift


def gained_norm(stream, gain):
    return norm_rows(stream) * gain


def dense(left, right):
    return jnp.dot(left, right, preferred_element_type=jnp.float32)


def dense_back(left, right):
    return lax.dot_general(left, right, (((1,), (1,)), ((), ())), preferred_element_type=jnp.float32)


def weight_grad(left, right):
    return lax.dot_general(left, right, (((0,), (0,)), ((), ())), preferred_element_type=jnp.float32)


def split_heads(values):
    return values.reshape(values.shape[0], HEADS, HEAD_DIM)


def attention(queries, keys, values, keep):
    scores = jnp.einsum(
        "qhd,khd->hqk", split_heads(queries), split_heads(keys), preferred_element_type=jnp.float32
    ) * HEAD_DIM ** (-0.5)
    scores = jnp.where(keep[None, None, :], scores, NEGATIVE)
    shifted = jnp.exp(scores - jnp.max(scores, -1, keepdims=True))
    probs = shifted / jnp.sum(shifted, -1, keepdims=True)
    mixed = jnp.einsum(
        "hqk,khd->qhd", to_low(probs), split_heads(values), preferred_element_type=jnp.float32
    )
    return (to_low(mixed.reshape(queries.shape)), probs)


def attention_back(queries, keys, values, probs, grad_mixed):
    grad_heads = split_heads(to_low(grad_mixed))
    grad_values = jnp.einsum(
        "hqk,qhd->khd", to_low(probs), grad_heads, preferred_element_type=jnp.float32
    )
    grad_probs = jnp.einsum(
        "qhd,khd->hqk", grad_heads, split_heads(values), preferred_element_type=jnp.float32
    )
    grad_scores = to_low(probs * (grad_probs - jnp.sum(probs * grad_probs, -1, keepdims=True)))
    grad_queries = jnp.einsum(
        "hqk,khd->qhd", grad_scores, split_heads(keys), preferred_element_type=jnp.float32
    ) * HEAD_DIM ** (-0.5)
    grad_keys = jnp.einsum(
        "hqk,qhd->khd", grad_scores, split_heads(queries), preferred_element_type=jnp.float32
    ) * HEAD_DIM ** (-0.5)
    return (
        grad_queries.reshape(queries.shape),
        grad_keys.reshape(keys.shape),
        grad_values.reshape(values.shape),
    )


def noise_level(steps):
    phase = (steps.astype(jnp.float32) / 1000.0 + 0.008) / 1.008 * (math.pi / 2)
    return jnp.cos(phase) ** 2


def time_features(steps):
    half_width = FREQS // 2
    frequency = jnp.exp(-math.log(10000.0) * jnp.arange(half_width, dtype=jnp.float32) / half_width)
    angles = steps.astype(jnp.float32)[:, None] * frequency[None, :]
    return jnp.concatenate([jnp.cos(angles), jnp.sin(angles)], -1)


def layer_forward(stream, modulation, text_low, frame_keep, text_keep, weights):
    w_joint, w_textkv, w_back, gain = weights
    normed_one, pull_one = jax.vjp(modulate, stream, modulation[:D], modulation[D : 2 * D])
    input_one = to_low(normed_one)
    self_proj = to_low(dense(input_one, w_joint[:, : 3 * D]))
    mixed_one, probs_one = attention(
        self_proj[:, :D], self_proj[:, D : 2 * D], self_proj[:, 2 * D :], frame_keep
    )
    branch_one = dense(mixed_one, w_back[:D])
    stream_two = stream + modulation[2 * D : 3 * D] * branch_one
    normed_two, pull_two = jax.vjp(gained_norm, stream_two, gain)
    input_two = to_low(normed_two)
    cross_query = to_low(dense(input_two, w_joint[:, 3 * D : 4 * D]))
    cross_kv = to_low(dense(text_low, w_textkv))
    mixed_two, probs_two = attention(cross_query, cross_kv[:, :D], cross_kv[:, D:], text_keep)
    stream_three = stream_two + dense(mixed_two, w_back[D : 2 * D])
    normed_three, pull_three = jax.vjp(
        modulate, stream_three, modulation[3 * D : 4 * D], modulation[4 * D : 5 * D]
    )
    input_three = to_low(normed_three)
    hidden_act, pull_act = jax.vjp(jax.nn.gelu, dense(input_three, w_joint[:, 4 * D :]))
    hidden_low = to_low(hidden_act)
    branch_three = dense(hidden_low, w_back[2 * D :])
    result = stream_three + modulation[5 * D :] * branch_three
    saved = (
        pull_one,
        input_one,
        self_proj,
        mixed_one,
        probs_one,
        branch_one,
        pull_two,
        input_two,
        cross_query,
        cross_kv,
        mixed_two,
        probs_two,
        pull_three,
        input_three,
        pull_act,
        hidden_low,
        branch_three,
    )
    return (result, saved)


def layer_backward(saved, grad_out, modulation, text_low, weights):
    w_joint, w_textkv, w_back, gain = weights
    (
        pull_one,
        input_one,
        self_proj,
        mixed_one,
        probs_one,
        branch_one,
        pull_two,
        input_two,
        cross_query,
        cross_kv,
        mixed_two,
        probs_two,
        pull_three,
        input_three,
        pull_act,
        hidden_low,
        branch_three,
    ) = saved
    grad_three = to_low(grad_out * modulation[5 * D :])
    grad_gate_two = jnp.sum(grad_out * branch_three, 0)
    grad_down = weight_grad(hidden_low, grad_three)
    (grad_pre,) = pull_act(dense_back(grad_three, w_back[2 * D :]))
    grad_pre = to_low(grad_pre)
    grad_up = weight_grad(input_three, grad_pre)
    grad_inner, grad_shift_two, grad_scale_two = pull_three(dense_back(grad_pre, w_joint[:, 4 * D :]))
    grad_stream = grad_out + grad_inner
    grad_cross_out = to_low(grad_stream)
    grad_co = weight_grad(mixed_two, grad_cross_out)
    grad_cq, grad_ck, grad_cv = attention_back(
        cross_query,
        cross_kv[:, :D],
        cross_kv[:, D:],
        probs_two,
        dense_back(grad_cross_out, w_back[D : 2 * D]),
    )
    grad_cq = to_low(grad_cq)
    grad_text_w = weight_grad(text_low, to_low(jnp.concatenate([grad_ck, grad_cv], -1)))
    grad_query_w = weight_grad(input_two, grad_cq)
    grad_inner, grad_gain = pull_two(dense_back(grad_cq, w_joint[:, 3 * D : 4 * D]))
    grad_stream = grad_stream + grad_inner
    grad_one = to_low(grad_stream * modulation[2 * D : 3 * D])
    grad_gate_one = jnp.sum(grad_stream * branch_one, 0)
    grad_ao = weight_grad(mixed_one, grad_one)
    grad_q, grad_k, grad_v = attention_back(
        self_proj[:, :D],
        self_proj[:, D : 2 * D],
        self_proj[:, 2 * D :],
        probs_one,
        dense_back(grad_one, w_back[:D]),
    )
    grad_self = to_low(jnp.concatenate([grad_q, grad_k, grad_v], -1))
    grad_self_w = weight_grad(input_one, grad_self)
    grad_inner, grad_shift_one, grad_scale_one = pull_one(dense_back(grad_self, w_joint[:, : 3 * D]))
    grad_stream = grad_stream + grad_inner
    grad_mod = jnp.concatenate(
        [grad_shift_one, grad_scale_one, grad_gate_one, grad_shift_two, grad_scale_two, grad_gate_two]
    )
    grads = (
        to_low(jnp.concatenate([grad_self_w, grad_query_w, grad_up], 1)),
        to_low(grad_text_w),
        to_low(jnp.concatenate([grad_ao, grad_co, grad_down], 0)),
    )
    return (grad_stream, grad_mod, grads, grad_gain)


def adam_update(weight, grad, first, second, rate):
    first_new = BETA_ONE * first + (1.0 - BETA_ONE) * grad
    second_new = BETA_TWO * second + (1.0 - BETA_TWO) * grad * grad
    first_hat = first_new / (1.0 - BETA_ONE**STEP)
    second_hat = second_new / (1.0 - BETA_TWO**STEP)
    weight_new = weight - rate * (
        first_hat / (jnp.sqrt(second_hat) + ADAM_EPSILON) + WEIGHT_DECAY * weight
    )
    return (first_new, second_new, weight_new)


def tiles(values, lead=()):
    flat = values.reshape(lead + (-1,))
    short = -flat.shape[-1] % 1024
    flat = jnp.pad(flat, [(0, 0)] * len(lead) + [(0, short)])
    return flat.reshape(lead + (-1, 128))


def body(
    ways,
    clean_latent,
    noise,
    text_feats,
    text_lengths,
    timesteps,
    valid_frames,
    w_in,
    w_text,
    w_out,
    gains,
    w_lead,
    w_head,
    first_in,
    second_in,
    first_text,
    second_text,
    first_out,
    second_out,
    first_gains,
    second_gains,
    first_lead,
    second_lead,
    first_head,
    second_head,
):
    count = ways[0] * ways[1]
    own = w_head.shape[0]
    channels = noise.shape[-1]
    clean_latent, noise, text_low = clean_latent[0], noise[0], text_feats[0]
    frames, caption = clean_latent.shape[0], text_low.shape[0]
    frame_keep = lax.iota(jnp.int32, frames) < valid_frames[0]
    text_keep = lax.iota(jnp.int32, caption) < text_lengths[0]
    rows = [w_in.shape[1], w_text.shape[1], w_out.shape[1]]
    halves = [JOINT // 2, D, D // 2]
    aligned = all(height % 8 == 0 for height in rows) and ways[0] % 2 == 0 and ways[1] % 2 == 0
    items = plan(halves, LAYERS)

    def to_all(values, number):
        if aligned:
            return exchange(values, ways, True, number)
        return lax.all_gather(values, ALL, axis=0, tiled=False)

    def to_each(values, number):
        if aligned:
            return exchange(values, ways, False, number)
        return lax.all_to_all(values, ALL, 0, 0, tiled=True)

    sinus = time_features(timesteps)
    lead_low, head_low = to_low(w_lead), to_low(w_head)
    small = jnp.concatenate(
        [
            lead_low[FREQS:].astype(jnp.float32).reshape(-1),
            head_low[:, 3 * D :].astype(jnp.float32).reshape(-1),
            to_low(gains).astype(jnp.float32).reshape(-1),
        ]
    )
    facts = jnp.concatenate([to_low(sinus).astype(jnp.float32)[0], valid_frames.astype(jnp.float32)])
    packed = to_all(jnp.concatenate([tiles(facts), tiles(small)], 0), 3).reshape(count, -1)
    facts_size = 1024
    sinus_all = to_low(packed[:, :FREQS])
    frame_count = jnp.sum(packed[:, FREQS])
    small_all = packed[:, facts_size:]
    at = channels * own
    lead_in = to_low(small_all[:, :at].reshape(count, channels, own).transpose(1, 0, 2).reshape(channels, D))
    head_pred = to_low(small_all[:, at : 2 * at].reshape(D, channels))
    gains_all = small_all[:, 2 * at : 2 * at + LAYERS * own].reshape(count, LAYERS, own)
    gains_all = gains_all.transpose(1, 0, 2).reshape(LAYERS, D)

    act_time, pull_time = jax.vjp(jax.nn.silu, dense(sinus_all, lead_low[:FREQS]))
    act_low = to_low(act_time)
    temb_part = dense(act_low, head_low[:, :D]).reshape(count, count, own).transpose(1, 0, 2)
    temb = jnp.sum(to_each(tiles(temb_part, (count,)), 4), 0).reshape(-1)[:D].reshape(count, own)
    cond, pull_cond = jax.vjp(jax.nn.silu, temb)
    cond_low = to_low(cond)
    mod_low = jnp.concatenate(
        [to_low(w_in[layer, :, JOINT:]) for layer in range(LAYERS)] + [head_low[:, D : 3 * D]], 1
    )
    mod_part = dense(cond_low, mod_low)
    mods = jnp.sum(to_each(tiles(mod_part, (count,)), 5), 0).reshape(-1)[: mod_low.shape[1]]

    if aligned:
        weights = gather_weights([w_in, w_text, w_out], halves, ways, 1, items)
    else:
        weights = [
            [
                lax.all_gather(to_low(shard[layer]), ALL, axis=0, tiled=True)
                for shard in (w_in[:, :, :JOINT], w_text, w_out)
            ]
            for layer in range(LAYERS)
        ]

    level = noise_level(timesteps)
    noisy_low = to_low(jnp.sqrt(level) * clean_latent + jnp.sqrt(1.0 - level) * noise)
    stream = dense(noisy_low, lead_in)
    saved = []
    for layer in range(LAYERS):
        stream, kept = layer_forward(
            stream,
            mods[layer * MOD : (layer + 1) * MOD],
            text_low,
            frame_keep,
            text_keep,
            (*weights[layer], gains_all[layer]),
        )
        saved.append(kept)
    final_mod = mods[LAYERS * MOD :]
    normed_final, pull_final = jax.vjp(modulate, stream, final_mod[:D], final_mod[D:])
    final_low = to_low(normed_final)
    error = dense(final_low, head_pred) - noise
    loss_part = jnp.sum(jnp.where(frame_keep[:, None], error * error, 0.0))
    grad_pred = to_low(jnp.where(frame_keep[:, None], error * (2.0 / frame_count), 0.0))
    grad_pred_w = weight_grad(final_low, grad_pred)
    grad_stream, grad_shift_f, grad_scale_f = pull_final(dense_back(grad_pred, head_pred))
    grad_mods = [None] * LAYERS + [jnp.concatenate([grad_shift_f, grad_scale_f])]
    big = [None] * LAYERS
    grad_gains = [None] * LAYERS
    for layer in reversed(range(LAYERS)):
        grad_stream, grad_mods[layer], big[layer], grad_gains[layer] = layer_backward(
            saved[layer],
            grad_stream,
            mods[layer * MOD : (layer + 1) * MOD],
            text_low,
            (*weights[layer], gains_all[layer]),
        )
    grad_in_w = weight_grad(noisy_low, to_low(grad_stream))

    mods_all = to_all(tiles(to_low(jnp.concatenate(grad_mods)).astype(jnp.float32)), 6)
    mods_all = to_low(mods_all.reshape(count, -1)[:, : mod_low.shape[1]])
    grad_mod_w = weight_grad(cond_low, mods_all)
    (grad_temb,) = pull_cond(dense_back(mods_all, mod_low))
    small_grads = jnp.concatenate(
        [
            grad_in_w.reshape(channels, count, own).transpose(1, 0, 2).reshape(count, -1),
            grad_pred_w.reshape(count, -1),
            jnp.stack(grad_gains).reshape(LAYERS, count, own).transpose(1, 0, 2).reshape(count, -1),
        ],
        1,
    )
    temb_tile = tiles(to_low(grad_temb).astype(jnp.float32))
    sent = jnp.concatenate(
        [jnp.broadcast_to(temb_tile[None], (count,) + temb_tile.shape), tiles(small_grads, (count,))], 1
    )
    got = to_each(sent, 7).reshape(count, -1)
    temb_all = to_low(got[:, :D].reshape(count, count, own).transpose(1, 0, 2).reshape(count, D))
    small_sum = jnp.sum(got[:, temb_tile.size :], 0)
    grad_time_two = weight_grad(act_low, temb_all)
    (grad_pre_time,) = pull_time(dense_back(temb_all, head_low[:, :D]))
    grad_time_one = weight_grad(sinus_all, to_low(grad_pre_time))

    if aligned:
        sums = scatter_grads(big, rows, halves, ways, 2, items)
    else:
        sums = [
            jnp.stack(
                [
                    lax.psum_scatter(big[layer][member], ALL, scatter_dimension=0, tiled=True)
                    for layer in range(LAYERS)
                ]
            ).astype(jnp.float32)
            for member in range(3)
        ]
    mod_grads = grad_mod_w[:, : LAYERS * MOD].reshape(own, LAYERS, MOD).transpose(1, 0, 2)
    grad_list = [
        jnp.concatenate([sums[0], mod_grads], 2),
        sums[1],
        sums[2],
        small_sum[2 * at : 2 * at + LAYERS * own].reshape(LAYERS, own),
        jnp.concatenate([grad_time_one, small_sum[:at].reshape(channels, own)], 0),
        jnp.concatenate(
            [grad_time_two, grad_mod_w[:, LAYERS * MOD :], small_sum[at : 2 * at].reshape(own, channels)], 1
        ),
    ]
    local_squares = sum((jnp.sum(item * item) for item in grad_list))
    totals = jnp.sum(to_all(tiles(jnp.stack([loss_part, local_squares])), 8), 0).reshape(-1)
    loss_sum = totals[0]
    grad_norm = jnp.sqrt(totals[1])
    factor = CLIP_NORM / jnp.maximum(grad_norm, CLIP_NORM)
    params = (w_in, w_text, w_out, gains, w_lead, w_head)
    firsts = (first_in, first_text, first_out, first_gains, first_lead, first_head)
    seconds = (second_in, second_text, second_out, second_gains, second_lead, second_head)
    rates = (LEARN_RATE, LEARN_RATE, LEARN_RATE, GAIN_RATE, LEARN_RATE, LEARN_RATE)
    results = []
    for weight, grad, first, second, rate in zip(params, grad_list, firsts, seconds, rates):
        results.extend(adam_update(weight, grad * factor, first, second, rate))
    return (loss_sum, frame_count, grad_norm, *results)


def solution(mesh):
    ways = (mesh.shape["dp"], mesh.shape["fsdp"])
    clips = [P(ALL, None, None)] * 3 + [P(ALL)] * 3
    weights = [P(None, ALL, None)] * 3 + [P(None, ALL)] * 2 + [P(ALL, None)]
    moments = [spec for spec in weights for _ in range(2)]
    results = [spec for spec in weights for _ in range(3)]
    return jax.shard_map(
        functools.partial(body, ways),
        mesh=mesh,
        in_specs=tuple(clips + weights + moments),
        out_specs=tuple([P()] * 3 + results),
        check_vma=False,
    )
```

```python
import functools
import math

import jax
import jax.numpy as jnp
from jax import lax
from jax.experimental import pallas as pl
from jax.experimental.pallas import tpu as pltpu
from jax.sharding import PartitionSpec as P

D = 768
HEADS = 12
HEAD_DIM = 64
FF = 3072
FREQS = 256
LAYERS = 2
STEP = 10
MOD = 6 * D
JOINT = 4 * D + FF

EPSILON = 1e-06
NEGATIVE = -1e30
BETA_ONE = 0.5
BETA_TWO = 0.5
LEARN_RATE = 0.02
GAIN_RATE = 0.3
WEIGHT_DECAY = 0.01
ADAM_EPSILON = 1e-08
CLIP_NORM = 1.0

ALL = ("dp", "fsdp")
MESH = pl.DeviceIdType.MESH
VMEM_LIMIT = 60 * 1024 * 1024


def place(ways):
    dp_ways, fsdp_ways = ways
    row, col = lax.axis_index("dp"), lax.axis_index("fsdp")
    sizes = (dp_ways // 2, 2, fsdp_ways // 2)
    spot = (row // 2, lax.rem(row, 2), col // 2)
    return sizes, spot, lax.rem(col, 2)


def device_at(spot, core):
    z, y, x = spot
    return (z * 2 + y, x * 2 + core)


def moved(spot, axis, size, steps):
    spot = list(spot)
    spot[axis] = lax.rem(spot[axis] + steps, size)
    return tuple(spot)


def greet_peers(sizes, spot, core):
    barrier = pltpu.get_barrier_semaphore()
    count = 1
    pl.semaphore_signal(barrier, inc=1, device_id=device_at(spot, 1 - core), device_id_type=MESH)
    for axis in range(3):
        for steps in range(1, sizes[axis]):
            count += 1
            pl.semaphore_signal(
                barrier,
                inc=1,
                device_id=device_at(moved(spot, axis, sizes[axis], steps), core),
                device_id_type=MESH,
            )
    pl.semaphore_wait(barrier, count)


def remote(source, target, send, recv, device):
    return pltpu.make_async_remote_copy(
        src_ref=source, dst_ref=target, send_sem=send, recv_sem=recv, device_id=device, device_id_type=MESH
    )


def exchange_kernel(ways, shared, x_ref, out_ref, send_sem, recv_sem):
    dp_ways, fsdp_ways = ways
    count = dp_ways * fsdp_ways
    me = lax.axis_index("dp") * fsdp_ways + lax.axis_index("fsdp")

    def device(index):
        return (index // fsdp_ways, lax.rem(index, fsdp_ways))

    barrier = pltpu.get_barrier_semaphore()
    for step in range(1, count):
        pl.semaphore_signal(
            barrier, inc=1, device_id=device(lax.rem(me + step, count)), device_id_type=MESH
        )
    pl.semaphore_wait(barrier, count - 1)

    def copy(step):
        other = lax.rem(me + step, count)
        return remote(
            x_ref if shared else x_ref.at[other],
            out_ref.at[me],
            send_sem.at[step],
            recv_sem.at[step],
            device(other),
        )

    for step in range(1, count):
        copy(step).start()
    out_ref[me] = x_ref[...] if shared else x_ref[me]
    for step in range(1, count):
        origin = lax.rem(me + count - step, count)
        remote(
            x_ref if shared else x_ref.at[0],
            out_ref.at[origin],
            send_sem.at[step],
            recv_sem.at[step],
            device(origin),
        ).wait_recv()
    for step in range(1, count):
        copy(step).wait_send()


def exchange(values, ways, shared, number):
    count = ways[0] * ways[1]
    tile = values.shape if shared else values.shape[1:]
    return pl.pallas_call(
        functools.partial(exchange_kernel, ways, shared),
        out_shape=jax.ShapeDtypeStruct((count,) + tile, values.dtype),
        in_specs=[pl.BlockSpec(memory_space=pltpu.VMEM)],
        out_specs=pl.BlockSpec(memory_space=pltpu.VMEM),
        scratch_shapes=[pltpu.SemaphoreType.DMA((count,)), pltpu.SemaphoreType.DMA((count,))],
        compiler_params=pltpu.CompilerParams(
            collective_id=number, has_side_effects=True, vmem_limit_bytes=VMEM_LIMIT
        ),
    )(values)


def gather_kernel(ways, rows, halves, items, layers, *refs):
    members = len(rows)
    shards = refs[:members]
    fulls = refs[members : members + members * layers]
    rest = refs[members + members * layers :]
    stages = rest[:members]
    blocks = rest[members : 2 * members]
    pre_send, pre_recv, own_sem, put_sem, *sends, c_send, c_recv = rest[2 * members :]
    sends, recvs = sends[0::2], sends[1::2]
    sizes, spot, core = place(ways)
    z, y, x = spot
    partner = device_at(spot, 1 - core)
    greet_peers(sizes, spot, core)

    def full(layer, member):
        return fulls[layer * members + member]

    pre = []
    for layer in range(layers):
        for member in range(members):
            height, half = rows[member], halves[member]
            place_in = stages[member].at[layer, pl.ds(pl.multiple_of(core * height, 8), height)]
            mine = shards[member].at[layer, :, pl.ds(pl.multiple_of(core * half, 128), half)]
            other = shards[member].at[layer, :, pl.ds(pl.multiple_of((1 - core) * half, 128), half)]
            index = layer * members + member
            sent = remote(other, place_in, pre_send.at[index], pre_recv.at[index], partner)
            sent.start()
            kept = pltpu.make_async_copy(mine, place_in, own_sem.at[index])
            kept.start()
            pre.append((sent, kept))
    arrived = set()
    put_done = set()
    sent_all = []

    def columns(i, side):
        _, member, start, size, _ = items[i]
        return pl.ds(pl.multiple_of(side * halves[member] + start, 128), size)

    def put(layer, member):
        half = halves[member]
        return pltpu.make_async_copy(
            blocks[member].at[layer],
            full(layer, member).at[z, y, x, :, pl.ds(pl.multiple_of(core * half, 128), half)],
            put_sem.at[layer * members + member],
        )

    def ready(layer, member):
        if (layer, member) in arrived:
            return
        arrived.add((layer, member))
        index = layer * members + member
        height = rows[member]
        sent, kept = pre[index]
        kept.wait()
        theirs = stages[member].at[layer, pl.ds(pl.multiple_of((1 - core) * height, 8), height)]
        remote(theirs, theirs, pre_send.at[index], pre_recv.at[index], partner).wait_recv()
        blocks[member][layer] = stages[member][layer].astype(jnp.bfloat16)
        put(layer, member).start()

    def own_put(layer, member):
        if (layer, member) not in put_done:
            put_done.add((layer, member))
            put(layer, member).wait()

    def region(i, phase, origin, side):
        layer, member, start, size, order = items[i]
        index = [slice(None) if order.index(axis) < phase else spot[axis] for axis in range(3)]
        if phase < 3 and origin is not None:
            index[order[phase]] = origin
        return full(layer, member).at[(*index, slice(None), columns(i, side))]

    def send(copy):
        copy.start()
        sent_all.append(copy)

    def start(i, phase):
        layer, member, first, size, order = items[i]
        axis = order[phase]
        if phase == 0:
            ready(layer, member)
            source = blocks[member].at[layer, :, pl.ds(first, size)]
        else:
            own_put(layer, member)
            source = region(i, phase, None, core)
        for steps in range(1, sizes[axis]):
            send(
                remote(
                    source, region(i, phase, spot[axis], core),
                    sends[phase].at[i, steps - 1], recvs[phase].at[i, steps - 1],
                    device_at(moved(spot, axis, sizes[axis], steps), core),
                )
            )
        if phase == 2:
            send(remote(source, source, c_send.at[i, 0], c_recv.at[i, 0], partner))

    def finish(i, phase):
        axis = items[i][4][phase]
        for steps in range(1, sizes[axis]):
            land = region(i, phase, lax.rem(spot[axis] + sizes[axis] - steps, sizes[axis]), core)
            remote(land, land, sends[phase].at[i, steps - 1], recvs[phase].at[i, steps - 1], partner).wait_recv()
            if phase == 2:
                send(remote(land, land, c_send.at[i, steps], c_recv.at[i, steps], partner))

    def c_wait(i):
        axis = items[i][4][2]
        for steps in range(sizes[axis]):
            land = region(i, 2, lax.rem(spot[axis] + sizes[axis] - steps, sizes[axis]), 1 - core)
            remote(land, land, c_send.at[i, steps], c_recv.at[i, steps], partner).wait_recv()

    for i, phase in schedule(items, GATHER_LAGS):
        if phase > 0:
            finish(i, phase - 1)
        if phase < 3:
            start(i, phase)
    for i in range(len(items)):
        c_wait(i)
    for layer in range(layers):
        for member in range(members):
            own_put(layer, member)
    for sent, _ in pre:
        sent.wait_send()
    for copy in sent_all:
        copy.wait_send()


def gather_weights(shards, halves, ways, number, items):
    layers = shards[0].shape[0]
    rows = [s.shape[1] for s in shards]
    members = len(shards)
    sizes = (ways[0] // 2, 2, ways[1] // 2)
    count = layers * members
    n = len(items)
    sem = pltpu.SemaphoreType.DMA
    out = pl.pallas_call(
        functools.partial(gather_kernel, ways, rows, halves, items, layers),
        out_shape=[
            jax.ShapeDtypeStruct(sizes + (2 * rows[m], 2 * halves[m]), jnp.bfloat16)
            for _ in range(layers)
            for m in range(members)
        ],
        in_specs=[pl.BlockSpec(memory_space=pl.ANY)] * members,
        out_specs=[pl.BlockSpec(memory_space=pl.ANY)] * count,
        scratch_shapes=[pltpu.VMEM((layers, 2 * rows[m], halves[m]), jnp.float32) for m in range(members)]
        + [pltpu.VMEM((layers, 2 * rows[m], halves[m]), jnp.bfloat16) for m in range(members)]
        + [sem((count,))] * 4
        + [sem((n, max(sizes)))] * 8,
        compiler_params=pltpu.CompilerParams(
            collective_id=number, has_side_effects=True, vmem_limit_bytes=VMEM_LIMIT
        ),
    )(*shards)
    return [
        [out[l * members + m].reshape(-1, 2 * halves[m]) for m in range(members)] for l in range(layers)
    ]


ORDERS = ((0, 2, 1), (0, 1, 2), (2, 0, 1), (1, 0, 2))
GATHER_LAGS = ((-3.0, 0.0, 2.0, 4.0), (-3.0, 0.0, 2.0, 4.0))
SCATTER_LAGS = ((-2.0, 0.0, 2.0, 4.0, 6.0), (-2.0, 0.0, 2.0, 4.0, 6.0))
GATHER_PATTERN = (0, 1)
SCATTER_PATTERN = (0, 1)


def schedule(items, lags):
    steps = []
    for i, item in enumerate(items):
        own = lags[0 if item[4][0] == 0 else 1]
        steps.extend((i + lag, -phase, i) for phase, lag in enumerate(own))
    return [(i, -phase) for _, phase, i in sorted(steps)]


def plan(halves, layers, pattern):
    items = []
    for layer in layers:
        for member, width in enumerate(halves):
            size = width // 4 if width % 512 == 0 else (width // 2 if width % 256 == 0 else 128)
            for start in range(0, width, size):
                items.append((layer, member, start, size, ORDERS[pattern[len(items) % len(pattern)]]))
    return items


ACTS = ("n1", "n2", "n3", "mixed1", "mixed2", "hidden", "g_self", "g_cq", "g_pre", "g_ckv", "g_one", "g_cross", "g_three")


def scatter_kernel(ways, rows, halves, items, layers, *refs):
    members = len(rows)
    n = len(items)
    rest = list(refs)

    def take(count):
        taken = rest[:count]
        del rest[:count]
        return taken

    (text_in,) = take(1)
    acts = [dict(zip(ACTS, take(len(ACTS)))) for _ in range(layers)]
    outs = take(members)
    lefts, rights, text, right_text, hidden, mixes, right_out = take(7)
    ring = take(members)
    whole = take(n)
    parts = [take(n) for _ in range(3)]
    sums = take(n)
    load_sem, c_send, c_recv, *sems, e_send, e_recv, o_sem = rest
    sends, recvs = sems[0::2], sems[1::2]
    sizes, spot, core = place(ways)
    partner = device_at(spot, 1 - core)
    greet_peers(sizes, spot, core)
    frames = hidden.shape[0]
    sent_all = []

    def send(copy):
        copy.start()
        sent_all.append(copy)

    def loads(layer, member):
        a = acts[layer]
        if member == 0:
            pairs = [(a["n1"], lefts.at[0]), (a["n2"], lefts.at[1]), (a["n3"], lefts.at[2])]
            pairs += [(a["g_self"].at[:, j * D : (j + 1) * D], rights.at[j]) for j in range(3)]
            pairs += [(a["g_cq"], rights.at[3])]
            pairs += [(a["g_pre"].at[:, j * D : (j + 1) * D], rights.at[4 + j]) for j in range(4)]
        elif member == 1:
            pairs = [(a["g_ckv"].at[:, j * D : (j + 1) * D], right_text.at[j]) for j in range(2)]
            if layer == items[0][0]:
                pairs.append((text_in, text))
        else:
            pairs = [(a["mixed1"], mixes.at[0]), (a["mixed2"], mixes.at[1]), (a["hidden"], hidden)]
            for j, name in enumerate(("g_one", "g_cross", "g_three")):
                pairs += [(a[name].at[:, side * (D // 2) : (side + 1) * (D // 2)], right_out.at[side, j]) for side in range(2)]
        return [
            pltpu.make_async_copy(source, target, load_sem.at[layer, member, j])
            for j, (source, target) in enumerate(pairs)
        ]

    def load(layer, member):
        for copy in loads(layer, member):
            copy.start()

    loaded = set()

    def need(layer, member):
        if (layer, member) not in loaded:
            loaded.add((layer, member))
            for copy in loads(layer, member):
                copy.wait()

    def product(i, side, store):
        layer, member, start, size, _ = items[i]
        need(layer, member)
        if member == 0:
            j = start // D
            at = pl.ds(start % D, size)
            left = jnp.where(side == 1, 2, 0 if j < 3 else 1)
            right = rights[side * 4 + j, :, at]
            for row in range(0, D, 384):
                store(pl.ds(row, 384), dot_tn(lefts[left, :, row : row + 384], right))
        elif member == 1:
            right = right_text[side, :, pl.ds(start, size)]
            for row in range(0, text.shape[1], 512):
                store(pl.ds(row, 512), dot_tn(text[:, row : row + 512], right))
        else:
            cols = pl.ds(start, size)
            for j in range(2):
                store(pl.ds(j * D, D), dot_tn(mixes[j], right_out[side, j, :, cols]))

            @pl.loop(0, 4)
            def _(j):
                at = pl.multiple_of(j * D, D)
                store(pl.ds(pl.multiple_of(2 * D + j * D, D), D), dot_tn(hidden[:, pl.ds(at, D)], right_out[side, 2, :, cols]))

    def columns(i, side):
        _, member, start, size, _ = items[i]
        return pl.ds(pl.multiple_of(side * halves[member] + start, 128), size)

    def blocks(ref, i):
        return ref.reshape(sizes + (2 * rows[items[i][1]], items[i][3]))

    ring_at, used = [], {}
    for i, (_, member, *_) in enumerate(items):
        ring_at.append(used.setdefault(member, []))
        ring_at[-1] = len(used[member])
        used[member].append(i)

    def c_copy(i):
        member, size = items[i][1], items[i][3]
        slot = ring_at[i] % 2
        return remote(ring[member].at[slot, :, pl.ds(0, size)], whole[i], c_send.at[i], c_recv.at[i], partner)

    def give(i):
        member, size = items[i][1], items[i][3]
        slot = ring_at[i] % 2
        if ring_at[i] >= 2:
            c_copy(used[member][ring_at[i] - 2]).wait_send()
        target = ring[member].at[slot]

        def store(at, value):
            target[at, pl.ds(0, size)] = value.astype(jnp.bfloat16)

        product(i, 1 - core, store)
        c_copy(i).start()

    def combine(i):
        c_copy(i).wait_recv()
        target = whole[i]

        def store(at, value):
            target[at, :] = (target[at, :].astype(jnp.float32) + value).astype(jnp.bfloat16)

        product(i, core, store)
        layer, member = items[i][:2]
        if i == used_last[layer, member] and (layer, member) in after:
            load(*after[layer, member])

    used_last, after, seen_layers = {}, {}, []
    for i, item in enumerate(items):
        used_last[item[:2]] = i
        if item[0] not in seen_layers:
            seen_layers.append(item[0])
    for early, late in zip(seen_layers, seen_layers[1:]):
        for member in range(members):
            after[early, member] = (late, member)

    def way(i):
        return items[i][4][::-1]

    def region(i, phase, place_on):
        order = way(i)
        index = [spot[axis] if axis in order[:phase] else slice(None) for axis in range(3)]
        index[order[phase]] = place_on
        return blocks(whole[i], i).at[tuple(index)]

    def start(i, phase):
        axis = way(i)[phase]
        for steps in range(1, sizes[axis]):
            target = moved(spot, axis, sizes[axis], steps)
            send(
                remote(
                    region(i, phase, target[axis]), parts[phase][i].at[steps - 1],
                    sends[phase].at[i, steps - 1], recvs[phase].at[i, steps - 1], device_at(target, core),
                )
            )

    def owned(i, side):
        height = rows[items[i][1]]
        return sums[i].at[pl.ds(pl.multiple_of(side * height, 8), height)]

    def e_copy(i):
        layer, member = items[i][:2]
        return remote(
            owned(i, 1 - core), outs[member].at[layer, :, columns(i, core)], e_send.at[i], e_recv.at[i], partner
        )

    def o_copy(i):
        layer, member = items[i][:2]
        return pltpu.make_async_copy(owned(i, core), outs[member].at[layer, :, columns(i, core)], o_sem.at[i])

    def finish(i, phase):
        axis = way(i)[phase]
        for steps in range(1, sizes[axis]):
            land = parts[phase][i].at[steps - 1]
            remote(land, land, sends[phase].at[i, steps - 1], recvs[phase].at[i, steps - 1], partner).wait_recv()
        mine = region(i, phase, spot[axis])
        landed = parts[phase][i]

        def total(index):
            value = mine[index].astype(jnp.float32)
            for steps in range(1, sizes[axis]):
                value = value + landed[(steps - 1, *index)].astype(jnp.float32)
            return value

        if phase == 2:
            sums[i][...] = total((Ellipsis,))
            e_copy(i).start()
            o_copy(i).start()
        else:
            left = [sizes[other] for other in range(3) if other not in way(i)[: phase + 1]]

            @pl.loop(0, left[0])
            def _(index):
                mine[index] = total((index,)).astype(jnp.bfloat16)

    for member in range(members):
        load(items[0][0], member)
    for i, step in schedule(items, SCATTER_LAGS):
        if step == 0:
            give(i)
            continue
        if step == 1:
            combine(i)
        else:
            finish(i, step - 2)
        if step < 4:
            start(i, step - 1)
    for i in range(n):
        e_copy(i).wait()
        o_copy(i).wait()
    for member in range(members):
        for i in used[member][-2:]:
            c_copy(i).wait_send()
    for copy in sent_all:
        copy.wait_send()


def scatter_grads(kept, text, rows, halves, ways, number, items):
    layers, members = len(kept), len(rows)
    sizes = (ways[0] // 2, 2, ways[1] // 2)
    n = len(items)
    sem = pltpu.SemaphoreType.DMA
    low = jnp.bfloat16
    chips = sizes[0] * sizes[1] * sizes[2]
    frames, tokens = kept[0]["n1"].shape[0], text.shape[0]
    most = [max(s for _, m, _, s, _ in items if m == member) for member in range(members)]
    vmem = pltpu.VMEM

    def part(item, phase):
        _, member, _, size, order = item
        order = order[::-1]
        left = tuple(sizes[axis] for axis in range(3) if axis not in order[: phase + 1])
        return vmem((sizes[order[phase]] - 1, *left, 2 * rows[member], size), low)

    scratch = [
        vmem((3, frames, D), low),
        vmem((8, frames, D), low),
        vmem(text.shape, low),
        vmem((2, tokens, D), low),
        vmem((frames, FF), low),
        vmem((2, frames, D), low),
        vmem((2, 3, frames, D // 2), low),
    ]
    scratch += [vmem((2, chips * 2 * rows[m], most[m]), low) for m in range(members)]
    scratch += [vmem((chips * 2 * rows[m], s), low) for _, m, _, s, _ in items]
    scratch += [part(item, phase) for phase in range(3) for item in items]
    scratch += [vmem((2 * rows[m], s), jnp.float32) for _, m, _, s, _ in items]
    scratch += [sem((layers, members, 11))] + [sem((n,))] * 2 + [sem((n, max(sizes)))] * 6 + [sem((n,))] * 3
    flat = [text] + [k[name] for k in kept for name in ACTS]
    return pl.pallas_call(
        functools.partial(scatter_kernel, ways, rows, halves, items, layers),
        out_shape=[
            jax.ShapeDtypeStruct((layers, rows[m], 2 * halves[m]), jnp.float32) for m in range(members)
        ],
        in_specs=[pl.BlockSpec(memory_space=pl.ANY)] * len(flat),
        out_specs=[pl.BlockSpec(memory_space=pl.ANY)] * members,
        scratch_shapes=scratch,
        compiler_params=pltpu.CompilerParams(
            collective_id=number, has_side_effects=True, vmem_limit_bytes=VMEM_LIMIT
        ),
    )(*flat)


def to_low(values):
    return values.astype(jnp.bfloat16)


def dense(left, right):
    return jnp.dot(left, right, preferred_element_type=jnp.float32)


def dense_back(left, right):
    return lax.dot_general(left, right, (((1,), (1,)), ((), ())), preferred_element_type=jnp.float32)


def weight_grad(left, right):
    return lax.dot_general(left, right, (((0,), (0,)), ((), ())), preferred_element_type=jnp.float32)


def noise_level(steps):
    phase = (steps.astype(jnp.float32) / 1000.0 + 0.008) / 1.008 * (math.pi / 2)
    return jnp.cos(phase) ** 2


def time_features(steps):
    half_width = FREQS // 2
    frequency = jnp.exp(-math.log(10000.0) * jnp.arange(half_width, dtype=jnp.float32) / half_width)
    angles = steps.astype(jnp.float32)[:, None] * frequency[None, :]
    return jnp.concatenate([jnp.cos(angles), jnp.sin(angles)], -1)


ROOT = math.sqrt(2.0 / math.pi)
CUBE = 0.044715
CHUNK = 64
WIDE = 512


def dot_nn(left, right):
    return lax.dot_general(left, right, (((1,), (0,)), ((), ())), preferred_element_type=jnp.float32)


def dot_nt(left, right):
    return lax.dot_general(left, right, (((1,), (1,)), ((), ())), preferred_element_type=jnp.float32)


def dot_tn(left, right):
    return lax.dot_general(left, right, (((0,), (0,)), ((), ())), preferred_element_type=jnp.float32)


def over_rows(count, step):
    @pl.loop(0, count // CHUNK)
    def _(index):
        step(pl.ds(pl.multiple_of(index * CHUNK, CHUNK), CHUNK))


def over_columns(count, width, step):
    @pl.loop(0, count // width)
    def _(index):
        step(pl.multiple_of(index * width, width))


def scaled(values):
    centred = values - jnp.mean(values, -1, keepdims=True)
    factor = lax.rsqrt(jnp.mean(centred * centred, -1, keepdims=True) + EPSILON)
    return centred * factor, factor


def norm_pull(normed, factor, grad):
    middle = jnp.mean(grad, -1, keepdims=True)
    along = jnp.mean(grad * normed, -1, keepdims=True)
    return factor * (grad - middle - normed * along)


def row_sum(values):
    return jnp.sum(values, 0, keepdims=True)


def probabilities(query, key, keep):
    scores = dot_nt(query, key) * HEAD_DIM ** (-0.5)
    scores = jnp.where(keep, scores, NEGATIVE)
    shifted = jnp.exp(scores - jnp.max(scores, -1, keepdims=True))
    return shifted * (1.0 / jnp.sum(shifted, -1, keepdims=True))


def attend(q_at, k_at, v_at, keep, store):
    first = lax.broadcasted_iota(jnp.int32, (1, 2 * HEAD_DIM), 1) < HEAD_DIM

    def pair(index):
        query, key, value = q_at(index), k_at(index), v_at(index)
        zero = jnp.zeros_like(query)
        out_a = dot_nn(to_low(probabilities(jnp.where(first, query, zero), key, keep)), value)
        out_b = dot_nn(to_low(probabilities(jnp.where(first, zero, query), key, keep)), value)
        store(index, to_low(jnp.where(first, out_a, out_b)))

    for index in range(HEADS // 2):
        pair(index)


def attend_back(q_at, k_at, v_at, grad_at, keep, store):
    first = lax.broadcasted_iota(jnp.int32, (1, 2 * HEAD_DIM), 1) < HEAD_DIM

    def pair(index):
        query, key, value, grad = q_at(index), k_at(index), v_at(index), grad_at(index)
        zero = jnp.zeros_like(query)
        parts = []
        for mine in (first, jnp.logical_not(first)):
            probs = probabilities(jnp.where(mine, query, zero), key, keep)
            grad_value = dot_tn(to_low(probs), grad)
            grad_probs = dot_nt(jnp.where(mine, grad, zero), value)
            inner = jnp.sum(probs * grad_probs, -1, keepdims=True)
            grad_scores = to_low(probs * (grad_probs - inner))
            grad_query = dot_nn(grad_scores, key) * HEAD_DIM ** (-0.5)
            grad_key = dot_tn(grad_scores, query) * HEAD_DIM ** (-0.5)
            parts.append((grad_query, grad_key, grad_value))
        store(index, *(to_low(jnp.where(first, a, b)) for a, b in zip(*parts)))

    for index in range(HEADS // 2):
        pair(index)


def tile_of(ref, base):
    return lambda index: ref[:, base + index * 2 * HEAD_DIM : base + (index + 1) * 2 * HEAD_DIM]


SAVED = (
    ("stream", D, jnp.float32),
    ("n1", D, jnp.bfloat16),
    ("qkv", 3 * D, jnp.bfloat16),
    ("mixed1", D, jnp.bfloat16),
    ("branch1", D, jnp.float32),
    ("stream2", D, jnp.float32),
    ("n2", D, jnp.bfloat16),
    ("cq", D, jnp.bfloat16),
    ("ckv", 2 * D, jnp.bfloat16),
    ("mixed2", D, jnp.bfloat16),
    ("stream3", D, jnp.float32),
    ("n3", D, jnp.bfloat16),
    ("branch3", D, jnp.float32),
)
GRADS = (
    ("g_self", 3 * D),
    ("g_cq", D),
    ("g_pre", FF),
    ("g_ckv", 2 * D),
    ("g_one", D),
    ("g_cross", D),
    ("g_three", D),
)
PARTS = ("qkv", "cq", "up", "text", "ao", "co", "down")
KEPT = ("n1", "n2", "n3", "mixed1", "mixed2", "hidden") + tuple(name for name, _ in GRADS)


class Names:
    def __init__(self, **refs):
        self.__dict__.update(refs)


def block_forward(s, hidden, result, mods, text, frame_keep, text_keep, w, need, done, emit):
    frames = s.stream.shape[0]

    def norm_one(rows):
        normed, _ = scaled(s.stream[rows, :])
        s.n1[rows, :] = to_low(normed * (1.0 + mods[1:2, :]) + mods[0:1, :])

    over_rows(frames, norm_one)
    emit("n1", s.n1)
    need("qkv")

    def project(column):
        cols = pl.ds(column, 256)
        s.qkv[:, cols] = to_low(dot_nn(s.n1[...], w.win[:, cols]))

    over_columns(3 * D, 256, project)
    done("qkv")

    def mix_one(index, value):
        s.mixed1[:, index * 128 : (index + 1) * 128] = value

    attend(tile_of(s.qkv, 0), tile_of(s.qkv, D), tile_of(s.qkv, 2 * D), frame_keep, mix_one)
    emit("mixed1", s.mixed1)
    need("ao")

    def branch_one(column):
        cols = pl.ds(column, 256)
        branch = dot_nn(s.mixed1[...], w.wout[0:D, cols])
        s.branch1[:, cols] = branch
        s.stream2[:, cols] = s.stream[:, cols] + mods[2:3, cols] * branch

    over_columns(D, 256, branch_one)
    done("ao")

    def norm_two(rows):
        normed, _ = scaled(s.stream2[rows, :])
        s.n2[rows, :] = to_low(normed * mods[6:7, :])

    over_rows(frames, norm_two)
    emit("n2", s.n2)
    need("cq")

    def project_cross(column):
        cols = pl.ds(column, 256)
        s.cq[:, cols] = to_low(dot_nn(s.n2[...], w.win[:, pl.ds(3 * D + column, 256)]))

    over_columns(D, 256, project_cross)
    done("cq")
    need("text")

    def project_text(column):
        cols = pl.ds(column, 256)
        s.ckv[:, cols] = to_low(dot_nn(text[...], w.wtext[:, cols]))

    over_columns(2 * D, 256, project_text)
    done("text")

    def mix_two(index, value):
        s.mixed2[:, index * 128 : (index + 1) * 128] = value

    attend(tile_of(s.cq, 0), tile_of(s.ckv, 0), tile_of(s.ckv, D), text_keep, mix_two)
    emit("mixed2", s.mixed2)
    need("co")

    def branch_two(column):
        cols = pl.ds(column, 256)
        s.stream3[:, cols] = s.stream2[:, cols] + dot_nn(s.mixed2[...], w.wout[D : 2 * D, cols])

    over_columns(D, 256, branch_two)
    done("co")

    def norm_three(rows):
        normed, _ = scaled(s.stream3[rows, :])
        s.n3[rows, :] = to_low(normed * (1.0 + mods[4:5, :]) + mods[3:4, :])

    over_rows(frames, norm_three)
    emit("n3", s.n3)
    need("up")

    def expand(column):
        upper = dot_nn(s.n3[...], w.win[:, pl.ds(4 * D + column, WIDE)])
        tanh = jnp.tanh(ROOT * (upper + CUBE * (upper * upper * upper)))
        hidden[:, pl.ds(column, WIDE)] = to_low(0.5 * upper * (1.0 + tanh))

    over_columns(FF, WIDE, expand)
    done("up")
    emit("hidden", hidden)
    need("down")

    def branch_three(column):
        cols = pl.ds(column, 256)
        branch = dot_nn(hidden[...], w.wout[2 * D :, cols])
        s.branch3[:, cols] = branch
        result[:, cols] = s.stream3[:, cols] + mods[5:6, cols] * branch

    over_columns(D, 256, branch_three)
    done("down")


def block_backward(s, g, grad, mods, grad_mods, inner, mixed, frame_keep, text_keep, w, need, done, emit):
    frames = s.stream.shape[0]
    grad_mods[...] = jnp.zeros_like(grad_mods)

    def gate_three(rows):
        grad_out = grad[rows, :]
        g.g_three[rows, :] = to_low(grad_out * mods[5:6, :])
        grad_mods[5:6, :] += row_sum(grad_out * s.branch3[rows, :])

    over_rows(frames, gate_three)
    emit("g_three", g.g_three)
    need("down")
    need("up")

    def shrink(column):
        wide = pl.ds(column, WIDE)
        back = dot_nt(g.g_three[...], w.wout[pl.ds(2 * D + column, WIDE), :])
        upper = dot_nn(s.n3[...], w.win[:, pl.ds(4 * D + column, WIDE)])
        square = upper * upper
        tanh = jnp.tanh(ROOT * (upper + CUBE * (square * upper)))
        slope = 0.5 * (1.0 + tanh) + (0.5 * ROOT) * upper * (1.0 - tanh * tanh) * (1.0 + (3.0 * CUBE) * square)
        g.g_pre[:, wide] = to_low(back * slope)

    over_columns(FF, WIDE, shrink)
    done("down")
    emit("g_pre", g.g_pre)

    def inner_three(column):
        inner[:, pl.ds(column, 256)] = dot_nt(g.g_pre[...], w.win[pl.ds(column, 256), 4 * D :])

    over_columns(D, 256, inner_three)
    done("up")

    def pull_three(rows):
        normed, factor = scaled(s.stream3[rows, :])
        back = inner[rows, :]
        grad_mods[3:4, :] += row_sum(back)
        grad_mods[4:5, :] += row_sum(back * normed)
        total = grad[rows, :] + norm_pull(normed, factor, back * (1.0 + mods[4:5, :]))
        grad[rows, :] = total
        g.g_cross[rows, :] = to_low(total)

    over_rows(frames, pull_three)
    emit("g_cross", g.g_cross)
    need("co")

    def back_cross(column):
        mixed[:, pl.ds(column, 256)] = to_low(dot_nt(g.g_cross[...], w.wout[pl.ds(D + column, 256), :]))

    over_columns(D, 256, back_cross)
    done("co")

    def store_cross(index, grad_query, grad_key, grad_value):
        cols = slice(index * 128, (index + 1) * 128)
        g.g_cq[:, cols] = grad_query
        g.g_ckv[:, cols] = grad_key
        g.g_ckv[:, D + index * 128 : D + (index + 1) * 128] = grad_value

    attend_back(
        tile_of(s.cq, 0), tile_of(s.ckv, 0), tile_of(s.ckv, D), tile_of(mixed, 0), text_keep, store_cross
    )
    emit("g_cq", g.g_cq)
    emit("g_ckv", g.g_ckv)
    need("cq")

    def inner_two(column):
        inner[:, pl.ds(column, 256)] = dot_nt(g.g_cq[...], w.win[pl.ds(column, 256), 3 * D : 4 * D])

    over_columns(D, 256, inner_two)
    done("cq")

    def pull_two(rows):
        normed, factor = scaled(s.stream2[rows, :])
        back = inner[rows, :]
        grad_mods[6:7, :] += row_sum(back * normed)
        total = grad[rows, :] + norm_pull(normed, factor, back * mods[6:7, :])
        grad[rows, :] = total
        g.g_one[rows, :] = to_low(total * mods[2:3, :])
        grad_mods[2:3, :] += row_sum(total * s.branch1[rows, :])

    over_rows(frames, pull_two)
    emit("g_one", g.g_one)
    need("ao")

    def back_self(column):
        mixed[:, pl.ds(column, 256)] = to_low(dot_nt(g.g_one[...], w.wout[pl.ds(column, 256), :]))

    over_columns(D, 256, back_self)
    done("ao")

    def store_self(index, grad_query, grad_key, grad_value):
        cols = slice(index * 128, (index + 1) * 128)
        g.g_self[:, cols] = grad_query
        g.g_self[:, D + index * 128 : D + (index + 1) * 128] = grad_key
        g.g_self[:, 2 * D + index * 128 : 2 * D + (index + 1) * 128] = grad_value

    attend_back(
        tile_of(s.qkv, 0), tile_of(s.qkv, D), tile_of(s.qkv, 2 * D), tile_of(mixed, 0), frame_keep, store_self
    )
    emit("g_self", g.g_self)
    need("qkv")

    def inner_one(column):
        inner[:, pl.ds(column, 256)] = dot_nt(g.g_self[...], w.win[pl.ds(column, 256), : 3 * D])

    over_columns(D, 256, inner_one)
    done("qkv")

    def pull_one(rows):
        normed, factor = scaled(s.stream[rows, :])
        back = inner[rows, :]
        grad_mods[0:1, :] += row_sum(back)
        grad_mods[1:2, :] += row_sum(back * normed)
        grad[rows, :] = grad[rows, :] + norm_pull(normed, factor, back * (1.0 + mods[1:2, :]))

    over_rows(frames, pull_one)


def model_kernel(*refs):
    refs = list(refs)

    def take(count):
        taken = refs[:count]
        del refs[:count]
        return taken

    lengths, factor_ref, stream_ref, mods_ref, final_mods, text, noise, head = take(8)
    weights = [take(3) for _ in range(LAYERS)]
    loss_ref, grad_ref, grad_mods_ref, grad_final, grad_head = take(5)
    kept_out = [dict(zip(KEPT, take(len(KEPT)))) for _ in range(LAYERS)]
    win, wtext, wout = take(3)
    saved = [Names(**dict(zip((name for name, *_ in SAVED), take(len(SAVED))))) for _ in range(LAYERS)]
    g = Names(**dict(zip((name for name, _ in GRADS), take(len(GRADS)))))
    hidden, inner, mixed, final_low = take(4)
    load_sem, keep_sem = refs
    w = Names(win=win, wtext=wtext, wout=wout)
    frames, tokens = stream_ref.shape[0], text.shape[0]
    frame_keep = lax.broadcasted_iota(jnp.int32, (1, frames), 1) < lengths[0]
    text_keep = lax.broadcasted_iota(jnp.int32, (1, tokens), 1) < lengths[1]

    def load(layer, part):
        w_in, w_text, w_out = weights[layer]
        source, target = {
            "qkv": (w_in.at[:, : 3 * D], win.at[:, : 3 * D]),
            "cq": (w_in.at[:, 3 * D : 4 * D], win.at[:, 3 * D : 4 * D]),
            "up": (w_in.at[:, 4 * D :], win.at[:, 4 * D :]),
            "text": (w_text, wtext),
            "ao": (w_out.at[:D], wout.at[:D]),
            "co": (w_out.at[D : 2 * D], wout.at[D : 2 * D]),
            "down": (w_out.at[2 * D :], wout.at[2 * D :]),
        }[part]
        return pltpu.make_async_copy(source, target, load_sem.at[PARTS.index(part)])

    flying = {}

    def keep(layer):
        def emit(name, ref):
            copy = pltpu.make_async_copy(
                ref, kept_out[layer][name], keep_sem.at[layer, KEPT.index(name)]
            )
            copy.start()
            flying[name, layer] = copy

        return emit

    def settle(layer, names):
        for name in names:
            copy = flying.pop((name, layer), None)
            if copy is not None:
                copy.wait()

    nothing = lambda part: None
    for part in ("qkv", "ao", "cq", "text", "co", "up", "down"):
        load(0, part).start()
    over_rows(frames, lambda rows: saved[0].stream.__setitem__((rows, slice(None)), stream_ref[rows, :]))
    for layer in range(LAYERS):
        last = layer == LAYERS - 1
        if layer > 0:
            settle(layer - 1, ("hidden",))
        block_forward(
            saved[layer], hidden, grad_ref if last else saved[layer + 1].stream,
            mods_ref.at[layer], text, frame_keep, text_keep, w,
            lambda part: load(layer, part).wait(),
            nothing if last else (lambda part: load(layer + 1, part).start()),
            keep(layer),
        )

    def norm_final(rows):
        normed, _ = scaled(grad_ref[rows, :])
        final_low[rows, :] = to_low(normed * (1.0 + final_mods[1:2, :]) + final_mods[0:1, :])

    over_rows(frames, norm_final)
    error = dot_nn(final_low[...], head[...]) - noise[...]
    counted = lax.broadcasted_iota(jnp.int32, (frames, 1), 0) < lengths[0]
    error = jnp.where(counted, error, 0.0)
    loss_ref[...] = jnp.broadcast_to(row_sum(error * error), loss_ref.shape)
    grad_pred = to_low(error * factor_ref[0])
    grad_head[...] = dot_tn(final_low[...], grad_pred)
    inner[...] = dot_nt(grad_pred, head[...])
    grad_final[...] = jnp.zeros_like(grad_final)

    def pull_final(rows):
        normed, factor = scaled(grad_ref[rows, :])
        back = inner[rows, :]
        grad_final[0:1, :] += row_sum(back)
        grad_final[1:2, :] += row_sum(back * normed)
        grad_ref[rows, :] = norm_pull(normed, factor, back * (1.0 + final_mods[1:2, :]))

    over_rows(frames, pull_final)
    for layer in reversed(range(LAYERS)):
        last = layer == LAYERS - 1
        if not last:
            settle(layer + 1, [name for name, _ in GRADS])
        block_backward(
            saved[layer], g, grad_ref, mods_ref.at[layer], grad_mods_ref.at[layer], inner, mixed,
            frame_keep, text_keep, w,
            nothing if last else (lambda part: load(layer, part).wait()),
            nothing if layer == 0 else (lambda part: load(layer - 1, part).start()),
            keep(layer),
        )
    for layer in range(LAYERS):
        settle(layer, KEPT)


def run_model(stream, mods, final_mods, text, noise, head, lengths, factor, weights):
    frames, tokens = stream.shape[0], text.shape[0]
    low, full = jnp.bfloat16, jnp.float32
    widths = {**{name: width for name, width, _ in SAVED}, **dict(GRADS), "hidden": FF}

    def height(name):
        return tokens if name in ("ckv", "g_ckv") else frames

    kept = [jax.ShapeDtypeStruct((height(name), widths[name]), low) for name in KEPT]
    shape = jax.ShapeDtypeStruct
    here, there = pl.BlockSpec(memory_space=pltpu.VMEM), pl.BlockSpec(memory_space=pl.ANY)
    scalar = pl.BlockSpec(memory_space=pltpu.SMEM)
    out = pl.pallas_call(
        model_kernel,
        out_shape=[
            shape((8, noise.shape[1]), full),
            shape((frames, D), full),
            shape((LAYERS, 8, D), full),
            shape((8, D), full),
            shape((D, noise.shape[1]), full),
        ]
        + kept * LAYERS,
        in_specs=[scalar, scalar] + [here] * 6 + [there] * (3 * LAYERS),
        out_specs=[here] * 5 + [there] * (len(KEPT) * LAYERS),
        scratch_shapes=[pltpu.VMEM((D, JOINT), low), pltpu.VMEM((text.shape[1], 2 * D), low), pltpu.VMEM((2 * D + FF, D), low)]
        + [pltpu.VMEM((height(name), width), kind) for name, width, kind in SAVED] * LAYERS
        + [pltpu.VMEM((height(name), width), low) for name, width in GRADS]
        + [
            pltpu.VMEM((frames, FF), low),
            pltpu.VMEM((frames, D), full),
            pltpu.VMEM((frames, D), low),
            pltpu.VMEM((frames, D), low),
            pltpu.SemaphoreType.DMA((len(PARTS),)),
            pltpu.SemaphoreType.DMA((LAYERS, len(KEPT))),
        ],
        compiler_params=pltpu.CompilerParams(vmem_limit_bytes=VMEM_LIMIT),
    )(lengths, factor, stream, mods, final_mods, text, noise, head, *[w for layer in weights for w in layer])
    head_part, rest = out[:5], out[5:]
    count = len(KEPT)
    return head_part, [dict(zip(KEPT, rest[l * count : (l + 1) * count])) for l in range(LAYERS)]


def adam_update(weight, grad, first, second, rate):
    first_new = BETA_ONE * first + (1.0 - BETA_ONE) * grad
    second_new = BETA_TWO * second + (1.0 - BETA_TWO) * grad * grad
    first_hat = first_new / (1.0 - BETA_ONE**STEP)
    second_hat = second_new / (1.0 - BETA_TWO**STEP)
    weight_new = weight - rate * (
        first_hat / (jnp.sqrt(second_hat) + ADAM_EPSILON) + WEIGHT_DECAY * weight
    )
    return (first_new, second_new, weight_new)


def tiles(values, lead=()):
    flat = values.reshape(lead + (-1,))
    short = -flat.shape[-1] % 1024
    flat = jnp.pad(flat, [(0, 0)] * len(lead) + [(0, short)])
    return flat.reshape(lead + (-1, 128))


def body(
    ways,
    clean_latent,
    noise,
    text_feats,
    text_lengths,
    timesteps,
    valid_frames,
    w_in,
    w_text,
    w_out,
    gains,
    w_lead,
    w_head,
    first_in,
    second_in,
    first_text,
    second_text,
    first_out,
    second_out,
    first_gains,
    second_gains,
    first_lead,
    second_lead,
    first_head,
    second_head,
):
    count = ways[0] * ways[1]
    own = w_head.shape[0]
    channels = noise.shape[-1]
    clean_latent, noise, text_low = clean_latent[0], noise[0], text_feats[0]
    frames, caption = clean_latent.shape[0], text_low.shape[0]
    frame_keep = lax.iota(jnp.int32, frames) < valid_frames[0]
    text_keep = lax.iota(jnp.int32, caption) < text_lengths[0]
    rows = [w_in.shape[1], w_text.shape[1], w_out.shape[1]]
    halves = [JOINT // 2, D, D // 2]
    aligned = all(height % 8 == 0 for height in rows) and ways[0] % 2 == 0 and ways[1] % 2 == 0

    def to_all(values, number):
        if aligned:
            return exchange(values, ways, True, number)
        return lax.all_gather(values, ALL, axis=0, tiled=False)

    def to_each(values, number):
        if aligned:
            return exchange(values, ways, False, number)
        return lax.all_to_all(values, ALL, 0, 0, tiled=True)

    sinus = time_features(timesteps)
    lead_low, head_low = to_low(w_lead), to_low(w_head)
    small = jnp.concatenate(
        [
            lead_low[FREQS:].astype(jnp.float32).reshape(-1),
            head_low[:, 3 * D :].astype(jnp.float32).reshape(-1),
            to_low(gains).astype(jnp.float32).reshape(-1),
        ]
    )
    facts = jnp.concatenate([to_low(sinus).astype(jnp.float32)[0], valid_frames.astype(jnp.float32)])
    packed = to_all(jnp.concatenate([tiles(facts), tiles(small)], 0), 3).reshape(count, -1)
    facts_size = 1024
    sinus_all = to_low(packed[:, :FREQS])
    frame_count = jnp.sum(packed[:, FREQS])
    small_all = packed[:, facts_size:]
    at = channels * own
    lead_in = to_low(small_all[:, :at].reshape(count, channels, own).transpose(1, 0, 2).reshape(channels, D))
    head_pred = to_low(small_all[:, at : 2 * at].reshape(D, channels))
    gains_all = small_all[:, 2 * at : 2 * at + LAYERS * own].reshape(count, LAYERS, own)
    gains_all = gains_all.transpose(1, 0, 2).reshape(LAYERS, D)

    act_time, pull_time = jax.vjp(jax.nn.silu, dense(sinus_all, lead_low[:FREQS]))
    act_low = to_low(act_time)
    temb_part = dense(act_low, head_low[:, :D]).reshape(count, count, own).transpose(1, 0, 2)
    temb = jnp.sum(to_each(tiles(temb_part, (count,)), 4), 0).reshape(-1)[:D].reshape(count, own)
    cond, pull_cond = jax.vjp(jax.nn.silu, temb)
    cond_low = to_low(cond)
    mod_low = jnp.concatenate(
        [to_low(w_in[layer, :, JOINT:]) for layer in range(LAYERS)] + [head_low[:, D : 3 * D]], 1
    )
    mod_part = dense(cond_low, mod_low)
    mods = jnp.sum(to_each(tiles(mod_part, (count,)), 5), 0).reshape(-1)[: mod_low.shape[1]]

    if aligned:
        items = plan(halves, range(LAYERS), GATHER_PATTERN)
        weights = gather_weights([w_in, w_text, w_out], halves, ways, 1, items)
    else:
        weights = [
            [
                lax.all_gather(to_low(shard[layer]), ALL, axis=0, tiled=True)
                for shard in (w_in[:, :, :JOINT], w_text, w_out)
            ]
            for layer in range(LAYERS)
        ]

    level = noise_level(timesteps)
    noisy_low = to_low(jnp.sqrt(level) * clean_latent + jnp.sqrt(1.0 - level) * noise)
    stream = dense(noisy_low, lead_in)
    block_mods = jnp.concatenate(
        [mods[: LAYERS * MOD].reshape(LAYERS, 6, D), gains_all[:, None], jnp.zeros((LAYERS, 1, D))], 1
    )
    final_mods = jnp.pad(mods[LAYERS * MOD :].reshape(2, D), [(0, 6), (0, 0)])
    short = [(0, 0), (0, 128 - channels)]
    (loss_lanes, grad_stream, grad_blocks, grad_final, grad_pred_w), kept = run_model(
        stream,
        block_mods,
        final_mods,
        text_low,
        jnp.pad(noise, short),
        jnp.pad(head_pred, short),
        jnp.concatenate([valid_frames, text_lengths]),
        (2.0 / frame_count).reshape(1),
        weights,
    )
    loss_part = jnp.sum(loss_lanes[0])
    grad_pred_w = grad_pred_w[:, :channels]
    grad_mods = [grad_blocks[:, :6].reshape(-1), grad_final[:2].reshape(-1)]
    grad_gains = grad_blocks[:, 6]
    grad_in_w = weight_grad(noisy_low, to_low(grad_stream))

    mods_all = to_all(tiles(to_low(jnp.concatenate(grad_mods)).astype(jnp.float32)), 6)
    mods_all = to_low(mods_all.reshape(count, -1)[:, : mod_low.shape[1]])
    grad_mod_w = weight_grad(cond_low, mods_all)
    (grad_temb,) = pull_cond(dense_back(mods_all, mod_low))
    small_grads = jnp.concatenate(
        [
            grad_in_w.reshape(channels, count, own).transpose(1, 0, 2).reshape(count, -1),
            grad_pred_w.reshape(count, -1),
            grad_gains.reshape(LAYERS, count, own).transpose(1, 0, 2).reshape(count, -1),
        ],
        1,
    )
    temb_tile = tiles(to_low(grad_temb).astype(jnp.float32))
    sent = jnp.concatenate(
        [jnp.broadcast_to(temb_tile[None], (count,) + temb_tile.shape), tiles(small_grads, (count,))], 1
    )
    got = to_each(sent, 7).reshape(count, -1)
    temb_all = to_low(got[:, :D].reshape(count, count, own).transpose(1, 0, 2).reshape(count, D))
    small_sum = jnp.sum(got[:, temb_tile.size :], 0)
    grad_time_two = weight_grad(act_low, temb_all)
    (grad_pre_time,) = pull_time(dense_back(temb_all, head_low[:, :D]))
    grad_time_one = weight_grad(sinus_all, to_low(grad_pre_time))

    if aligned:
        items = plan(halves, list(reversed(range(LAYERS))), SCATTER_PATTERN)
        sums = scatter_grads(kept, text_low, rows, halves, ways, 2, items)
    else:
        sums = [[], [], []]
        for k in kept:
            joint = [weight_grad(k[a], k[b]) for a, b in (("n1", "g_self"), ("n2", "g_cq"), ("n3", "g_pre"))]
            back = [weight_grad(k[a], k[b]) for a, b in (("mixed1", "g_one"), ("mixed2", "g_cross"), ("hidden", "g_three"))]
            grads = (jnp.concatenate(joint, 1), weight_grad(text_low, k["g_ckv"]), jnp.concatenate(back, 0))
            for member, grad in enumerate(grads):
                sums[member].append(lax.psum_scatter(grad, ALL, scatter_dimension=0, tiled=True))
        sums = [jnp.stack(part) for part in sums]
    mod_grads = grad_mod_w[:, : LAYERS * MOD].reshape(own, LAYERS, MOD).transpose(1, 0, 2)
    grad_list = [
        jnp.concatenate([sums[0], mod_grads], 2),
        sums[1],
        sums[2],
        small_sum[2 * at : 2 * at + LAYERS * own].reshape(LAYERS, own),
        jnp.concatenate([grad_time_one, small_sum[:at].reshape(channels, own)], 0),
        jnp.concatenate(
            [grad_time_two, grad_mod_w[:, LAYERS * MOD :], small_sum[at : 2 * at].reshape(own, channels)], 1
        ),
    ]
    local_squares = sum((jnp.sum(item * item) for item in grad_list))
    totals = jnp.sum(to_all(tiles(jnp.stack([loss_part, local_squares])), 8), 0).reshape(-1)
    loss_sum = totals[0]
    grad_norm = jnp.sqrt(totals[1])
    factor = CLIP_NORM / jnp.maximum(grad_norm, CLIP_NORM)
    params = (w_in, w_text, w_out, gains, w_lead, w_head)
    firsts = (first_in, first_text, first_out, first_gains, first_lead, first_head)
    seconds = (second_in, second_text, second_out, second_gains, second_lead, second_head)
    rates = (LEARN_RATE, LEARN_RATE, LEARN_RATE, GAIN_RATE, LEARN_RATE, LEARN_RATE)
    results = []
    for weight, grad, first, second, rate in zip(params, grad_list, firsts, seconds, rates):
        results.extend(adam_update(weight, grad * factor, first, second, rate))
    return (loss_sum, frame_count, grad_norm, *results)


def solution(mesh):
    ways = (mesh.shape["dp"], mesh.shape["fsdp"])
    clips = [P(ALL, None, None)] * 3 + [P(ALL)] * 3
    weights = [P(None, ALL, None)] * 3 + [P(None, ALL)] * 2 + [P(ALL, None)]
    moments = [spec for spec in weights for _ in range(2)]
    results = [spec for spec in weights for _ in range(3)]
    return jax.shard_map(
        functools.partial(body, ways),
        mesh=mesh,
        in_specs=tuple(clips + weights + moments),
        out_specs=tuple([P()] * 3 + results),
        check_vma=False,
    )
```

```python
import functools
import math

import jax
import jax.numpy as jnp
from jax import lax
from jax.experimental import pallas as pl
from jax.experimental.pallas import tpu as pltpu
from jax.sharding import PartitionSpec as P

D = 768
HEADS = 12
HEAD_DIM = 64
FF = 3072
FREQS = 256
LAYERS = 2
STEP = 10
MOD = 6 * D
JOINT = 4 * D + FF

EPSILON = 1e-06
NEGATIVE = -1e30
BETA_ONE = 0.5
BETA_TWO = 0.5
LEARN_RATE = 0.02
GAIN_RATE = 0.3
WEIGHT_DECAY = 0.01
ADAM_EPSILON = 1e-08
CLIP_NORM = 1.0

ALL = ("dp", "fsdp")
MESH = pl.DeviceIdType.MESH
VMEM_LIMIT = 60 * 1024 * 1024


def place(ways):
    dp_ways, fsdp_ways = ways
    row, col = lax.axis_index("dp"), lax.axis_index("fsdp")
    sizes = (dp_ways // 2, 2, fsdp_ways // 2)
    spot = (row // 2, lax.rem(row, 2), col // 2)
    return sizes, spot, lax.rem(col, 2)


def device_at(spot, core):
    z, y, x = spot
    return (z * 2 + y, x * 2 + core)


def moved(spot, axis, size, steps):
    spot = list(spot)
    spot[axis] = lax.rem(spot[axis] + steps, size)
    return tuple(spot)


def greet_peers(sizes, spot, core):
    barrier = pltpu.get_barrier_semaphore()
    count = 1
    pl.semaphore_signal(barrier, inc=1, device_id=device_at(spot, 1 - core), device_id_type=MESH)
    for axis in range(3):
        for steps in range(1, sizes[axis]):
            count += 1
            pl.semaphore_signal(
                barrier,
                inc=1,
                device_id=device_at(moved(spot, axis, sizes[axis], steps), core),
                device_id_type=MESH,
            )
    pl.semaphore_wait(barrier, count)


def remote(source, target, send, recv, device):
    return pltpu.make_async_remote_copy(
        src_ref=source, dst_ref=target, send_sem=send, recv_sem=recv, device_id=device, device_id_type=MESH
    )


def greet_all(ways, me):
    count = ways[0] * ways[1]
    barrier = pltpu.get_barrier_semaphore()
    for step in range(1, count):
        pl.semaphore_signal(
            barrier, inc=1, device_id=numbered(ways, lax.rem(me + step, count)), device_id_type=MESH
        )
    pl.semaphore_wait(barrier, count - 1)


def numbered(ways, index):
    return (index // ways[1], lax.rem(index, ways[1]))


ROUNDS = ("core", 2, 1, 0)


class Hops:
    def __init__(self, sizes, spot, core):
        self.sizes, self.spot, self.core = sizes, spot, core

    def count(self, axis):
        return 2 if axis == "core" else self.sizes[axis]

    def place(self, axis):
        return self.core if axis == "core" else self.spot[axis]

    def other(self, axis, steps):
        if axis == "core":
            return 1 - self.core, device_at(self.spot, 1 - self.core)
        spot = moved(self.spot, axis, self.sizes[axis], steps)
        return spot[axis], device_at(spot, self.core)


def sum_steps(hops, totals, landed, send_sem, recv_sem, sent):
    first = [sum(hops.count(axis) - 1 for axis in ROUNDS[:turn]) for turn in range(len(ROUNDS))]

    def copies(turn):
        axis = ROUNDS[turn]
        return [
            remote(
                totals.at[turn], landed.at[first[turn] + steps - 1],
                send_sem.at[turn, steps - 1], recv_sem.at[turn, steps - 1], hops.other(axis, steps)[1],
            )
            for steps in range(1, hops.count(axis))
        ]

    def begin(turn):
        for copy in copies(turn):
            copy.start()
            sent.append(copy)

    def go_on(turn):
        for copy in copies(turn):
            copy.wait_recv()
        total = totals[turn]
        for steps in range(1, hops.count(ROUNDS[turn])):
            total = total + landed[first[turn] + steps - 1]
        totals[turn + 1] = total
        if turn + 1 < len(ROUNDS):
            begin(turn + 1)

    return [lambda: begin(0)] + [functools.partial(go_on, turn) for turn in range(len(ROUNDS))]


def split_steps(hops, rows, landed, out, send_sem, recv_sem, sent):
    places = {"core": 3, 2: 2, 1: 1, 0: 0}

    def index(turn, place_on):
        at = [slice(None)] * 4
        for early in ROUNDS[:turn]:
            at[places[early]] = hops.place(early)
        at[places[ROUNDS[turn]]] = place_on
        return tuple(at)

    def copies(turn):
        axis = ROUNDS[turn]
        made = []
        for steps in range(1, hops.count(axis)):
            place_on, device = hops.other(axis, steps)
            made.append(
                remote(
                    rows.at[index(turn, place_on)], landed[turn].at[steps - 1],
                    send_sem.at[turn, steps - 1], recv_sem.at[turn, steps - 1], device,
                )
            )
        return made

    def begin(turn):
        for copy in copies(turn):
            copy.start()
            sent.append(copy)

    def go_on(turn):
        for copy in copies(turn):
            copy.wait_recv()
        axis = ROUNDS[turn]
        mine = rows.at[index(turn, hops.place(axis))]
        others = range(hops.count(axis) - 1)
        if turn == 3:
            out[...] = sum((landed[turn][k] for k in others), mine[...])
        else:

            @pl.loop(0, hops.sizes[0])
            def _(z):
                mine[z] = sum((landed[turn][k, z] for k in others), mine[z])

            begin(turn + 1)

    return [lambda: begin(0)] + [functools.partial(go_on, turn) for turn in range(len(ROUNDS))]


def split_shapes(sizes, tile):
    z, y, x = sizes
    return [
        pltpu.VMEM((1, z, y, x) + tile, jnp.float32),
        pltpu.VMEM((x - 1, z, y) + tile, jnp.float32),
        pltpu.VMEM((y - 1, z) + tile, jnp.float32),
        pltpu.VMEM((z - 1,) + tile, jnp.float32),
    ]


def spread_steps(hops, rows, send_sem, recv_sem, sent):
    turns = (0, 2, 1, "core")
    places = {"core": 3, 2: 2, 1: 1, 0: 0}

    def index(turn, place_on):
        at = [hops.spot[0], hops.spot[1], hops.spot[2], hops.core]
        for early in turns[:turn]:
            at[places[early]] = slice(None)
        at[places[turns[turn]]] = place_on
        return tuple(at)

    def copies(turn, origin):
        axis = turns[turn]
        made = []
        for steps in range(1, hops.count(axis)):
            device = hops.other(axis, steps)[1]
            place_on = hops.other(axis, hops.count(axis) - steps)[0] if origin else hops.place(axis)
            part = rows.at[index(turn, place_on)]
            made.append(remote(part, part, send_sem.at[turn, steps - 1], recv_sem.at[turn, steps - 1], device))
        return made

    def begin(turn):
        for copy in copies(turn, False):
            copy.start()
            sent.append(copy)

    def go_on(turn):
        for copy in copies(turn, True):
            copy.wait_recv()
        if turn + 1 < len(turns):
            begin(turn + 1)

    return [lambda: begin(0)] + [functools.partial(go_on, turn) for turn in range(len(turns))]


def sigmoid(values):
    return 1.0 / (1.0 + jnp.exp(-values))


def chosen(me, own, width):
    shape = (D, width)
    row, column = (lax.broadcasted_iota(jnp.int32, shape, axis) for axis in range(2))
    return jnp.logical_and(row == me * own + column, column < own).astype(jnp.float32)


SHARE = 32
MOD_ROWS = (LAYERS * MOD + 2 * D) // 128
MOD_TILE = (-(-MOD_ROWS // 8) * 8, 128)


def gather_kernel(ways, rows, halves, items, layers, own, *refs):
    members = len(rows)
    refs = list(refs)

    def take(count):
        taken = refs[:count]
        del refs[:count]
        return taken

    shards = take(members)
    facts_in, lead_own, head_own, mod_own = take(4)
    fulls = take(members * layers)
    facts, pre_time, temb_own, mods = take(4)
    totals, landed, mod_parts = take(3)
    mod_landed = take(4)
    facts_send, facts_recv, sum_send, sum_recv, split_send, split_recv = take(6)
    rest = refs
    stages = rest[:members]
    blocks = rest[members : 2 * members]
    pre_send, pre_recv, own_sem, put_sem, *sends, c_send, c_recv = rest[2 * members :]
    sends, recvs = sends[0::2], sends[1::2]
    sizes, spot, core = place(ways)
    z, y, x = spot
    partner = device_at(spot, 1 - core)
    count = ways[0] * ways[1]
    me = lax.axis_index("dp") * ways[1] + lax.axis_index("fsdp")
    greet_all(ways, me)

    def facts_copy(step):
        return remote(
            facts_in, facts.at[me], facts_send.at[step], facts_recv.at[step],
            numbered(ways, lax.rem(me + step, count)),
        )

    for step in range(1, count):
        facts_copy(step).start()
    facts[me] = facts_in[...]

    def full(layer, member):
        return fulls[layer * members + member]

    pre = []
    for layer in range(layers):
        for member in range(members):
            height, half = rows[member], halves[member]
            place_in = stages[member].at[layer, pl.ds(pl.multiple_of(core * height, 8), height)]
            mine = shards[member].at[layer, :, pl.ds(pl.multiple_of(core * half, 128), half)]
            other = shards[member].at[layer, :, pl.ds(pl.multiple_of((1 - core) * half, 128), half)]
            index = layer * members + member
            sent = remote(other, place_in, pre_send.at[index], pre_recv.at[index], partner)
            sent.start()
            kept = pltpu.make_async_copy(mine, place_in, own_sem.at[index])
            kept.start()
            pre.append((sent, kept))
    arrived = set()
    put_done = set()
    sent_all = []

    def columns(i, side):
        _, member, start, size, _ = items[i]
        return pl.ds(pl.multiple_of(side * halves[member] + start, 128), size)

    def put(layer, member):
        half = halves[member]
        return pltpu.make_async_copy(
            blocks[member].at[layer],
            full(layer, member).at[z, y, x, :, pl.ds(pl.multiple_of(core * half, 128), half)],
            put_sem.at[layer * members + member],
        )

    def ready(layer, member):
        if (layer, member) in arrived:
            return
        arrived.add((layer, member))
        index = layer * members + member
        height = rows[member]
        sent, kept = pre[index]
        kept.wait()
        theirs = stages[member].at[layer, pl.ds(pl.multiple_of((1 - core) * height, 8), height)]
        remote(theirs, theirs, pre_send.at[index], pre_recv.at[index], partner).wait_recv()
        blocks[member][layer] = stages[member][layer].astype(jnp.bfloat16)
        put(layer, member).start()

    def own_put(layer, member):
        if (layer, member) not in put_done:
            put_done.add((layer, member))
            put(layer, member).wait()

    def region(i, phase, origin, side):
        layer, member, start, size, order = items[i]
        index = [slice(None) if order.index(axis) < phase else spot[axis] for axis in range(3)]
        if phase < 3 and origin is not None:
            index[order[phase]] = origin
        return full(layer, member).at[(*index, slice(None), columns(i, side))]

    def send(copy):
        copy.start()
        sent_all.append(copy)

    def start(i, phase):
        layer, member, first, size, order = items[i]
        axis = order[phase]
        if phase == 0:
            ready(layer, member)
            source = blocks[member].at[layer, :, pl.ds(first, size)]
        else:
            own_put(layer, member)
            source = region(i, phase, None, core)
        for steps in range(1, sizes[axis]):
            send(
                remote(
                    source, region(i, phase, spot[axis], core),
                    sends[phase].at[i, steps - 1], recvs[phase].at[i, steps - 1],
                    device_at(moved(spot, axis, sizes[axis], steps), core),
                )
            )
        if phase == 2:
            send(remote(source, source, c_send.at[i, 0], c_recv.at[i, 0], partner))

    def finish(i, phase):
        axis = items[i][4][phase]
        for steps in range(1, sizes[axis]):
            land = region(i, phase, lax.rem(spot[axis] + sizes[axis] - steps, sizes[axis]), core)
            remote(land, land, sends[phase].at[i, steps - 1], recvs[phase].at[i, steps - 1], partner).wait_recv()
            if phase == 2:
                send(remote(land, land, c_send.at[i, steps], c_recv.at[i, steps], partner))

    def c_wait(i):
        axis = items[i][4][2]
        for steps in range(sizes[axis]):
            land = region(i, 2, lax.rem(spot[axis] + sizes[axis] - steps, sizes[axis]), 1 - core)
            remote(land, land, c_send.at[i, steps], c_recv.at[i, steps], partner).wait_recv()

    hops = Hops(sizes, spot, core)

    def time_layers():
        for step in range(1, count):
            origin = lax.rem(me + count - step, count)
            remote(
                facts_in, facts.at[origin], facts_send.at[step], facts_recv.at[step], numbered(ways, origin)
            ).wait_recv()
        value = dot_nn(to_low(facts[:, 0, :]), lead_own[:128, :]) + dot_nn(to_low(facts[:, 1, :]), lead_own[128:, :])
        pre_time[...] = value
        totals[0] = dot_nn(to_low(value * sigmoid(value))[:, :SHARE], head_own[...])
        sums[0]()

    def modulation():
        temb = lax.dot_general(
            totals[4], chosen(me, own, 128), (((1,), (0,)), ((), ())),
            precision=lax.Precision.HIGHEST, preferred_element_type=jnp.float32,
        )
        temb_own[...] = temb
        cond = to_low(temb * sigmoid(temb))[:, :SHARE]
        mod_parts[:, MOD_ROWS:, :] = jnp.zeros((count, MOD_TILE[0] - MOD_ROWS, 128), jnp.float32)
        for j in range(0, MOD_ROWS, 4):
            part = dot_nn(cond, mod_own[:, j * 128 : (j + 4) * 128])
            for k in range(4):
                mod_parts[:, j + k, :] = part[:, k * 128 : (k + 1) * 128]
        splits[0]()

    sums = sum_steps(hops, totals, landed, sum_send, sum_recv, sent_all)
    splits = split_steps(
        hops, mod_parts.reshape(sizes + (2,) + MOD_TILE), mod_landed, mods, split_send, split_recv, sent_all
    )
    side = [time_layers] + sums[1:] + [modulation] + splits[1:]
    for i, phase in schedule(items, GATHER_LAGS):
        if phase == 1 and side:
            side.pop(0)()
        if phase > 0:
            finish(i, phase - 1)
        if phase < 3:
            start(i, phase)
    for i in range(len(items)):
        c_wait(i)
    for step in side:
        step()
    for layer in range(layers):
        for member in range(members):
            own_put(layer, member)
    for step in range(1, count):
        facts_copy(step).wait_send()
    for sent, _ in pre:
        sent.wait_send()
    for copy in sent_all:
        copy.wait_send()


def gather_weights(shards, facts, lead_own, head_own, mod_own, own, halves, ways, number, items):
    layers = shards[0].shape[0]
    rows = [s.shape[1] for s in shards]
    members = len(shards)
    sizes = (ways[0] // 2, 2, ways[1] // 2)
    devices = ways[0] * ways[1]
    count = layers * members
    n = len(items)
    sem, vmem, full = pltpu.SemaphoreType.DMA, pltpu.VMEM, jnp.float32
    here, there = pl.BlockSpec(memory_space=pltpu.VMEM), pl.BlockSpec(memory_space=pl.ANY)
    out = pl.pallas_call(
        functools.partial(gather_kernel, ways, rows, halves, items, layers, own),
        out_shape=[
            jax.ShapeDtypeStruct(sizes + (2 * rows[m], 2 * halves[m]), jnp.bfloat16)
            for _ in range(layers)
            for m in range(members)
        ]
        + [
            jax.ShapeDtypeStruct((devices,) + facts.shape, full),
            jax.ShapeDtypeStruct((devices, 128), full),
            jax.ShapeDtypeStruct((devices, 128), full),
            jax.ShapeDtypeStruct(MOD_TILE, full),
        ],
        in_specs=[there] * members + [here] * 4,
        out_specs=[there] * count + [here] * 4,
        scratch_shapes=[
            vmem((len(ROUNDS) + 1, devices, D), full),
            vmem((sizes[0] + sizes[1] + sizes[2] - 2, devices, D), full),
            vmem((devices,) + MOD_TILE, full),
        ]
        + split_shapes(sizes, MOD_TILE)
        + [sem((devices,))] * 2
        + [sem((len(ROUNDS), max(sizes)))] * 4
        + [vmem((layers, 2 * rows[m], halves[m]), full) for m in range(members)]
        + [vmem((layers, 2 * rows[m], halves[m]), jnp.bfloat16) for m in range(members)]
        + [sem((count,))] * 4
        + [sem((n, max(sizes)))] * 8,
        compiler_params=pltpu.CompilerParams(
            collective_id=number, has_side_effects=True, vmem_limit_bytes=VMEM_LIMIT
        ),
    )(*shards, facts, lead_own, head_own, mod_own)
    weights = [
        [out[l * members + m].reshape(-1, 2 * halves[m]) for m in range(members)] for l in range(layers)
    ]
    return weights, *out[count:]


ORDERS = ((0, 2, 1), (0, 1, 2), (2, 0, 1), (1, 0, 2))
GATHER_LAGS = ((-1.5, 0.0, 3.0, 7.5), (-3.0, 0.0, 2.0, 6.5))
SCATTER_LAGS = ((-2.0, 0.0, 4.5, 7.5, 9.0), (-2.0, 0.0, 4.5, 6.5, 9.5))
GATHER_PATTERN = (1, 0, 1, 2, 1, 1, 0, 1, 0, 1, 2, 1, 2, 1, 3, 1, 2, 1)
SCATTER_PATTERN = GATHER_PATTERN[::-1]


def schedule(items, lags):
    steps = []
    for i, item in enumerate(items):
        own = lags[0 if item[4][0] == 0 else 1]
        steps.extend((i + lag, -phase, i) for phase, lag in enumerate(own))
    return [(i, -phase) for _, phase, i in sorted(steps)]


def plan(halves, layers, pattern):
    items = []
    for layer in layers:
        for member, width in enumerate(halves):
            size = width // 4 if width % 512 == 0 else (width // 2 if width % 256 == 0 else 128)
            for start in range(0, width, size):
                items.append((layer, member, start, size, ORDERS[pattern[len(items) % len(pattern)]]))
    return items


RINGS = (2, 1, 1)
ACTS = ("n1", "n2", "n3", "mixed1", "mixed2", "hidden", "g_self", "g_cq", "g_pre", "g_ckv", "g_one", "g_cross", "g_three")


def scatter_kernel(ways, rows, halves, items, layers, own, *refs):
    members = len(rows)
    n = len(items)
    rest = list(refs)

    def take(count):
        taken = rest[:count]
        del rest[:count]
        return taken

    (text_in,) = take(1)
    acts = [dict(zip(ACTS, take(len(ACTS)))) for _ in range(layers)]
    mods_in, small_in, loss_in, facts, pre_time, temb_own, head_own, mod_own = take(8)
    outs = take(members)
    grad_mod, grad_time_one, grad_time_two, small_out, final = take(5)
    all_mods, small_rows, totals, landed, squares = take(5)
    small_landed = take(4)
    spread_send, spread_recv, sum_send, sum_recv, split_send, split_recv, end_send, end_recv = take(8)
    ends, end_landed = take(2)
    lefts, rights, text, right_text, hidden, mixes, right_out = take(7)
    ring = take(members)
    whole = take(n)
    parts = [take(n) for _ in range(3)]
    partial = take(n)
    load_sem, c_send, c_recv, *sems, e_send, e_recv, o_sem = rest
    sends, recvs = sems[0::2], sems[1::2]
    sizes, spot, core = place(ways)
    partner = device_at(spot, 1 - core)
    greet_peers(sizes, spot, core)
    frames = hidden.shape[0]
    sent_all = []
    me = lax.axis_index("dp") * ways[1] + lax.axis_index("fsdp")
    hops = Hops(sizes, spot, core)
    squares[...] = jnp.zeros_like(squares)

    def count_squares(value):
        squares[...] += jnp.broadcast_to(jnp.sum(value * value, (0, 1), keepdims=True), squares.shape)

    temb = temb_own[...]
    share = sigmoid(temb)
    cond = to_low(temb * share)[:, :SHARE]
    gate = sigmoid(pre_time[...])
    act = to_low(pre_time[...] * gate)[:, :SHARE]
    slope_temb = (share * (1.0 + temb * (1.0 - share)))[:, :SHARE]
    slope_time = (gate * (1.0 + pre_time[...] * (1.0 - gate)))[:, :SHARE]
    all_mods[me] = mods_in[...]
    sums = sum_steps(hops, totals, landed, sum_send, sum_recv, sent_all)
    spreads = spread_steps(
        hops, all_mods.reshape(sizes + (2,) + MOD_TILE), spread_send, spread_recv, sent_all
    )
    tile = tuple(small_in.shape[1:])
    splits = split_steps(
        hops, small_rows.reshape(sizes + (2,) + tile), small_landed, small_out, split_send, split_recv, sent_all
    )

    def begin_small():
        small_rows[...] = small_in[...]
        splits[0]()

    def modulation_back():
        back = jnp.zeros((all_mods.shape[0], SHARE), jnp.float32)
        for j in range(MOD_ROWS):
            cols = slice(j * 128, (j + 1) * 128)
            grad = to_low(all_mods[:, j, :])
            back = back + dot_nt(grad, mod_own[:, cols])
            grad_mod[:, cols] = dot_tn(cond, grad)
        grad_temb = to_low(back * slope_temb)
        pick = to_low(chosen(me, own, SHARE))
        totals[0] = dot_nt(grad_temb, pick)
        for column in range(0, MOD_ROWS * 128, MOD):
            count_squares(grad_mod[:, column : min(column + MOD, MOD_ROWS * 128)])
        sums[0]()

    def time_back():
        grad_temb = to_low(totals[4])
        grad_time_two[...] = dot_tn(act, grad_temb)
        grad_time = to_low(dot_nt(grad_temb, head_own[...]) * slope_time)
        for j in range(2):
            grad_time_one[j * 128 : (j + 1) * 128, :] = dot_tn(to_low(facts[:, j, :]), grad_time)
        count_squares(grad_time_two[...])
        count_squares(grad_time_one[...])
        count_squares(small_out[...])

    side = [spreads[0], begin_small]
    side += [step for pair in zip(spreads[1:], splits[1:]) for step in pair]
    side += [modulation_back] + sums[1:] + [time_back]

    def send(copy):
        copy.start()
        sent_all.append(copy)

    def loads(layer, member):
        a = acts[layer]
        if member == 0:
            pairs = [(a["n1"], lefts.at[0]), (a["n2"], lefts.at[1]), (a["n3"], lefts.at[2])]
            pairs += [(a["g_self"].at[:, j * D : (j + 1) * D], rights.at[j]) for j in range(3)]
            pairs += [(a["g_cq"], rights.at[3])]
            pairs += [(a["g_pre"].at[:, j * D : (j + 1) * D], rights.at[4 + j]) for j in range(4)]
        elif member == 1:
            pairs = [(a["g_ckv"].at[:, j * D : (j + 1) * D], right_text.at[j]) for j in range(2)]
            if layer == items[0][0]:
                pairs.append((text_in, text))
        else:
            pairs = [(a["mixed1"], mixes.at[0]), (a["mixed2"], mixes.at[1]), (a["hidden"], hidden)]
            for j, name in enumerate(("g_one", "g_cross", "g_three")):
                pairs += [(a[name].at[:, side * (D // 2) : (side + 1) * (D // 2)], right_out.at[side, j]) for side in range(2)]
        return [
            pltpu.make_async_copy(source, target, load_sem.at[layer, member, j])
            for j, (source, target) in enumerate(pairs)
        ]

    def load(layer, member):
        for copy in loads(layer, member):
            copy.start()

    loaded = set()

    def need(layer, member):
        if (layer, member) not in loaded:
            loaded.add((layer, member))
            for copy in loads(layer, member):
                copy.wait()

    def product(i, side, store):
        layer, member, start, size, _ = items[i]
        need(layer, member)
        if member == 0:
            j = start // D
            at = pl.ds(start % D, size)
            left = jnp.where(side == 1, 2, 0 if j < 3 else 1)
            right = rights[side * 4 + j, :, at]
            for row in range(0, D, 384):
                store(pl.ds(row, 384), dot_tn(lefts[left, :, row : row + 384], right))
        elif member == 1:
            right = right_text[side, :, pl.ds(start, size)]
            for row in range(0, text.shape[1], 512):
                store(pl.ds(row, 512), dot_tn(text[:, row : row + 512], right))
        else:
            cols = pl.ds(start, size)
            for j in range(2):
                store(pl.ds(j * D, D), dot_tn(mixes[j], right_out[side, j, :, cols]))

            @pl.loop(0, 4)
            def _(j):
                at = pl.multiple_of(j * D, D)
                store(pl.ds(pl.multiple_of(2 * D + j * D, D), D), dot_tn(hidden[:, pl.ds(at, D)], right_out[side, 2, :, cols]))

    def columns(i, side):
        _, member, start, size, _ = items[i]
        return pl.ds(pl.multiple_of(side * halves[member] + start, 128), size)

    def blocks(ref, i):
        return ref.reshape(sizes + (2 * rows[items[i][1]], items[i][3]))

    ring_at, used = [], {}
    for i, (_, member, *_) in enumerate(items):
        ring_at.append(used.setdefault(member, []))
        ring_at[-1] = len(used[member])
        used[member].append(i)

    def c_copy(i):
        member, size = items[i][1], items[i][3]
        slot = ring_at[i] % RINGS[member]
        return remote(ring[member].at[slot, :, pl.ds(0, size)], whole[i], c_send.at[i], c_recv.at[i], partner)

    def give(i):
        member, size = items[i][1], items[i][3]
        slot = ring_at[i] % RINGS[member]
        if ring_at[i] >= RINGS[member]:
            c_copy(used[member][ring_at[i] - RINGS[member]]).wait_send()
        target = ring[member].at[slot]

        def store(at, value):
            target[at, pl.ds(0, size)] = value.astype(jnp.bfloat16)

        product(i, 1 - core, store)
        c_copy(i).start()

    def combine(i):
        c_copy(i).wait_recv()
        target = whole[i]

        def store(at, value):
            target[at, :] = (target[at, :].astype(jnp.float32) + value).astype(jnp.bfloat16)

        product(i, core, store)
        layer, member = items[i][:2]
        if i == used_last[layer, member] and (layer, member) in after:
            load(*after[layer, member])

    used_last, after, seen_layers = {}, {}, []
    for i, item in enumerate(items):
        used_last[item[:2]] = i
        if item[0] not in seen_layers:
            seen_layers.append(item[0])
    for early, late in zip(seen_layers, seen_layers[1:]):
        for member in range(members):
            after[early, member] = (late, member)

    def way(i):
        return items[i][4][::-1]

    def region(i, phase, place_on):
        order = way(i)
        index = [spot[axis] if axis in order[:phase] else slice(None) for axis in range(3)]
        index[order[phase]] = place_on
        return blocks(whole[i], i).at[tuple(index)]

    def start(i, phase):
        axis = way(i)[phase]
        for steps in range(1, sizes[axis]):
            target = moved(spot, axis, sizes[axis], steps)
            send(
                remote(
                    region(i, phase, target[axis]), parts[phase][i].at[steps - 1],
                    sends[phase].at[i, steps - 1], recvs[phase].at[i, steps - 1], device_at(target, core),
                )
            )

    def owned(i, side):
        height = rows[items[i][1]]
        return partial[i].at[pl.ds(pl.multiple_of(side * height, 8), height)]

    def e_copy(i):
        layer, member = items[i][:2]
        return remote(
            owned(i, 1 - core), outs[member].at[layer, :, columns(i, core)], e_send.at[i], e_recv.at[i], partner
        )

    def o_copy(i):
        layer, member = items[i][:2]
        return pltpu.make_async_copy(owned(i, core), outs[member].at[layer, :, columns(i, core)], o_sem.at[i])

    def finish(i, phase):
        axis = way(i)[phase]
        for steps in range(1, sizes[axis]):
            land = parts[phase][i].at[steps - 1]
            remote(land, land, sends[phase].at[i, steps - 1], recvs[phase].at[i, steps - 1], partner).wait_recv()
        mine = region(i, phase, spot[axis])
        landed = parts[phase][i]

        def total(index):
            value = mine[index].astype(jnp.float32)
            for steps in range(1, sizes[axis]):
                value = value + landed[(steps - 1, *index)].astype(jnp.float32)
            return value

        if phase == 2:
            pieces_sum = total((Ellipsis,))
            partial[i][...] = pieces_sum
            count_squares(pieces_sum)
            e_copy(i).start()
            o_copy(i).start()
        else:
            left = [sizes[other] for other in range(3) if other not in way(i)[: phase + 1]]

            @pl.loop(0, left[0])
            def _(index):
                mine[index] = total((index,)).astype(jnp.bfloat16)

    for member in range(members):
        load(items[0][0], member)
    for i, step in schedule(items, SCATTER_LAGS):
        if step == 0:
            give(i)
            continue
        if step in (1, 2) and side:
            side.pop(0)()
        if step == 1:
            combine(i)
        else:
            finish(i, step - 2)
        if step < 4:
            start(i, step - 1)
    for step in side:
        step()
    lane = lax.broadcasted_iota(jnp.int32, squares.shape, 0)
    ends[0] = jnp.where(lane == 0, squares[...], loss_in[...])
    for step in sum_steps(hops, ends, end_landed, end_send, end_recv, sent_all):
        step()
    final[...] = ends[len(ROUNDS)]
    for i in range(n):
        e_copy(i).wait()
        o_copy(i).wait()
    for member in range(members):
        for i in used[member][-RINGS[member] :]:
            c_copy(i).wait_send()
    for copy in sent_all:
        copy.wait_send()


def scatter_grads(kept, text, rest, own, rows, halves, ways, number, items):
    layers, members = len(kept), len(rows)
    sizes = (ways[0] // 2, 2, ways[1] // 2)
    n = len(items)
    sem = pltpu.SemaphoreType.DMA
    low = jnp.bfloat16
    chips = sizes[0] * sizes[1] * sizes[2]
    frames, tokens = kept[0]["n1"].shape[0], text.shape[0]
    most = [max(s for _, m, _, s, _ in items if m == member) for member in range(members)]
    vmem = pltpu.VMEM

    def part(item, phase):
        _, member, _, size, order = item
        order = order[::-1]
        left = tuple(sizes[axis] for axis in range(3) if axis not in order[: phase + 1])
        return vmem((sizes[order[phase]] - 1, *left, 2 * rows[member], size), low)

    full, devices = jnp.float32, 2 * chips
    tile = tuple(rest[1].shape[1:])
    sums = sem((len(ROUNDS), max(sizes)))
    scratch = [
        vmem((devices,) + MOD_TILE, full),
        vmem((devices,) + tile, full),
        vmem((len(ROUNDS) + 1, devices, D), full),
        vmem((sizes[0] + sizes[1] + sizes[2] - 2, devices, D), full),
        vmem((8, 128), full),
    ]
    scratch += split_shapes(sizes, tile) + [sums] * 8
    scratch += [vmem((len(ROUNDS) + 1, 8, 128), full), vmem((sizes[0] + sizes[1] + sizes[2] - 2, 8, 128), full)]
    scratch += [
        vmem((3, frames, D), low),
        vmem((8, frames, D), low),
        vmem(text.shape, low),
        vmem((2, tokens, D), low),
        vmem((frames, FF), low),
        vmem((2, frames, D), low),
        vmem((2, 3, frames, D // 2), low),
    ]
    scratch += [vmem((RINGS[m], chips * 2 * rows[m], most[m]), low) for m in range(members)]
    scratch += [vmem((chips * 2 * rows[m], s), low) for _, m, _, s, _ in items]
    scratch += [part(item, phase) for phase in range(3) for item in items]
    scratch += [vmem((2 * rows[m], s), jnp.float32) for _, m, _, s, _ in items]
    scratch += [sem((layers, members, 11))] + [sem((n,))] * 2 + [sem((n, max(sizes)))] * 6 + [sem((n,))] * 3
    flat = [text] + [k[name] for k in kept for name in ACTS]
    here, there = pl.BlockSpec(memory_space=vmem), pl.BlockSpec(memory_space=pl.ANY)
    return pl.pallas_call(
        functools.partial(scatter_kernel, ways, rows, halves, items, layers, own),
        out_shape=[
            jax.ShapeDtypeStruct((layers, rows[m], 2 * halves[m]), full) for m in range(members)
        ]
        + [
            jax.ShapeDtypeStruct((SHARE, MOD_ROWS * 128), full),
            jax.ShapeDtypeStruct((FREQS, SHARE), full),
            jax.ShapeDtypeStruct((SHARE, D), full),
            jax.ShapeDtypeStruct(tile, full),
            jax.ShapeDtypeStruct((8, 128), full),
        ],
        in_specs=[there] * len(flat) + [here] * len(rest),
        out_specs=[there] * members + [here] * 5,
        scratch_shapes=scratch,
        compiler_params=pltpu.CompilerParams(
            collective_id=number, has_side_effects=True, vmem_limit_bytes=VMEM_LIMIT
        ),
    )(*flat, *rest)


def to_low(values):
    return values.astype(jnp.bfloat16)


def dense(left, right):
    return jnp.dot(left, right, preferred_element_type=jnp.float32)


def dense_back(left, right):
    return lax.dot_general(left, right, (((1,), (1,)), ((), ())), preferred_element_type=jnp.float32)


def weight_grad(left, right):
    return lax.dot_general(left, right, (((0,), (0,)), ((), ())), preferred_element_type=jnp.float32)


def noise_level(steps):
    phase = (steps.astype(jnp.float32) / 1000.0 + 0.008) / 1.008 * (math.pi / 2)
    return jnp.cos(phase) ** 2


def time_features(steps):
    half_width = FREQS // 2
    frequency = jnp.exp(-math.log(10000.0) * jnp.arange(half_width, dtype=jnp.float32) / half_width)
    angles = steps.astype(jnp.float32)[:, None] * frequency[None, :]
    return jnp.concatenate([jnp.cos(angles), jnp.sin(angles)], -1)


ROOT = math.sqrt(2.0 / math.pi)
CUBE = 0.044715
CHUNK = 64
WIDE = 512


def dot_nn(left, right):
    return lax.dot_general(left, right, (((1,), (0,)), ((), ())), preferred_element_type=jnp.float32)


def dot_nt(left, right):
    return lax.dot_general(left, right, (((1,), (1,)), ((), ())), preferred_element_type=jnp.float32)


def dot_tn(left, right):
    return lax.dot_general(left, right, (((0,), (0,)), ((), ())), preferred_element_type=jnp.float32)


def over_rows(count, step):
    @pl.loop(0, count // CHUNK)
    def _(index):
        step(pl.ds(pl.multiple_of(index * CHUNK, CHUNK), CHUNK))


def over_columns(count, width, step):
    @pl.loop(0, count // width)
    def _(index):
        step(pl.multiple_of(index * width, width))


def scaled(values):
    centred = values - jnp.mean(values, -1, keepdims=True)
    factor = lax.rsqrt(jnp.mean(centred * centred, -1, keepdims=True) + EPSILON)
    return centred * factor, factor


def norm_pull(normed, factor, grad):
    middle = jnp.mean(grad, -1, keepdims=True)
    along = jnp.mean(grad * normed, -1, keepdims=True)
    return factor * (grad - middle - normed * along)


def row_sum(values):
    return jnp.sum(values, 0, keepdims=True)


def probabilities(query, key, keep):
    scores = dot_nt(query, key) * HEAD_DIM ** (-0.5)
    scores = jnp.where(keep, scores, NEGATIVE)
    shifted = jnp.exp(scores - jnp.max(scores, -1, keepdims=True))
    return shifted * (1.0 / jnp.sum(shifted, -1, keepdims=True))


def attend(q_at, k_at, v_at, keep, store):
    first = lax.broadcasted_iota(jnp.int32, (1, 2 * HEAD_DIM), 1) < HEAD_DIM

    def pair(index):
        query, key, value = q_at(index), k_at(index), v_at(index)
        zero = jnp.zeros_like(query)
        out_a = dot_nn(to_low(probabilities(jnp.where(first, query, zero), key, keep)), value)
        out_b = dot_nn(to_low(probabilities(jnp.where(first, zero, query), key, keep)), value)
        store(index, to_low(jnp.where(first, out_a, out_b)))

    for index in range(HEADS // 2):
        pair(index)


def attend_back(q_at, k_at, v_at, grad_at, keep, store):
    first = lax.broadcasted_iota(jnp.int32, (1, 2 * HEAD_DIM), 1) < HEAD_DIM

    def pair(index):
        query, key, value, grad = q_at(index), k_at(index), v_at(index), grad_at(index)
        zero = jnp.zeros_like(query)
        parts = []
        for mine in (first, jnp.logical_not(first)):
            probs = probabilities(jnp.where(mine, query, zero), key, keep)
            grad_value = dot_tn(to_low(probs), grad)
            grad_probs = dot_nt(jnp.where(mine, grad, zero), value)
            inner = jnp.sum(probs * grad_probs, -1, keepdims=True)
            grad_scores = to_low(probs * (grad_probs - inner))
            grad_query = dot_nn(grad_scores, key) * HEAD_DIM ** (-0.5)
            grad_key = dot_tn(grad_scores, query) * HEAD_DIM ** (-0.5)
            parts.append((grad_query, grad_key, grad_value))
        store(index, *(to_low(jnp.where(first, a, b)) for a, b in zip(*parts)))

    for index in range(HEADS // 2):
        pair(index)


def tile_of(ref, base):
    return lambda index: ref[:, base + index * 2 * HEAD_DIM : base + (index + 1) * 2 * HEAD_DIM]


SAVED = (
    ("stream", D, jnp.float32),
    ("n1", D, jnp.bfloat16),
    ("qkv", 3 * D, jnp.bfloat16),
    ("mixed1", D, jnp.bfloat16),
    ("branch1", D, jnp.float32),
    ("stream2", D, jnp.float32),
    ("n2", D, jnp.bfloat16),
    ("cq", D, jnp.bfloat16),
    ("ckv", 2 * D, jnp.bfloat16),
    ("mixed2", D, jnp.bfloat16),
    ("stream3", D, jnp.float32),
    ("n3", D, jnp.bfloat16),
    ("branch3", D, jnp.float32),
)
GRADS = (
    ("g_self", 3 * D),
    ("g_cq", D),
    ("g_pre", FF),
    ("g_ckv", 2 * D),
    ("g_one", D),
    ("g_cross", D),
    ("g_three", D),
)
PARTS = ("qkv", "cq", "up", "text", "ao", "co", "down")
KEPT = ("n1", "n2", "n3", "mixed1", "mixed2", "hidden") + tuple(name for name, _ in GRADS)


class Names:
    def __init__(self, **refs):
        self.__dict__.update(refs)


def block_forward(s, hidden, result, mods, text, frame_keep, text_keep, w, need, done, emit):
    frames = s.stream.shape[0]

    def norm_one(rows):
        normed, _ = scaled(s.stream[rows, :])
        s.n1[rows, :] = to_low(normed * (1.0 + mods[1:2, :]) + mods[0:1, :])

    over_rows(frames, norm_one)
    emit("n1", s.n1)
    need("qkv")

    def project(column):
        cols = pl.ds(column, 256)
        s.qkv[:, cols] = to_low(dot_nn(s.n1[...], w.win[:, cols]))

    over_columns(3 * D, 256, project)
    done("qkv")

    def mix_one(index, value):
        s.mixed1[:, index * 128 : (index + 1) * 128] = value

    attend(tile_of(s.qkv, 0), tile_of(s.qkv, D), tile_of(s.qkv, 2 * D), frame_keep, mix_one)
    emit("mixed1", s.mixed1)
    need("ao")

    def branch_one(column):
        cols = pl.ds(column, 256)
        branch = dot_nn(s.mixed1[...], w.wout[0:D, cols])
        s.branch1[:, cols] = branch
        s.stream2[:, cols] = s.stream[:, cols] + mods[2:3, cols] * branch

    over_columns(D, 256, branch_one)
    done("ao")

    def norm_two(rows):
        normed, _ = scaled(s.stream2[rows, :])
        s.n2[rows, :] = to_low(normed * mods[6:7, :])

    over_rows(frames, norm_two)
    emit("n2", s.n2)
    need("cq")

    def project_cross(column):
        cols = pl.ds(column, 256)
        s.cq[:, cols] = to_low(dot_nn(s.n2[...], w.win[:, pl.ds(3 * D + column, 256)]))

    over_columns(D, 256, project_cross)
    done("cq")
    need("text")

    def project_text(column):
        cols = pl.ds(column, 256)
        s.ckv[:, cols] = to_low(dot_nn(text[...], w.wtext[:, cols]))

    over_columns(2 * D, 256, project_text)
    done("text")

    def mix_two(index, value):
        s.mixed2[:, index * 128 : (index + 1) * 128] = value

    attend(tile_of(s.cq, 0), tile_of(s.ckv, 0), tile_of(s.ckv, D), text_keep, mix_two)
    emit("mixed2", s.mixed2)
    need("co")

    def branch_two(column):
        cols = pl.ds(column, 256)
        s.stream3[:, cols] = s.stream2[:, cols] + dot_nn(s.mixed2[...], w.wout[D : 2 * D, cols])

    over_columns(D, 256, branch_two)
    done("co")

    def norm_three(rows):
        normed, _ = scaled(s.stream3[rows, :])
        s.n3[rows, :] = to_low(normed * (1.0 + mods[4:5, :]) + mods[3:4, :])

    over_rows(frames, norm_three)
    emit("n3", s.n3)
    need("up")

    def expand(column):
        upper = dot_nn(s.n3[...], w.win[:, pl.ds(4 * D + column, WIDE)])
        tanh = jnp.tanh(ROOT * (upper + CUBE * (upper * upper * upper)))
        hidden[:, pl.ds(column, WIDE)] = to_low(0.5 * upper * (1.0 + tanh))

    over_columns(FF, WIDE, expand)
    done("up")
    emit("hidden", hidden)
    need("down")

    def branch_three(column):
        cols = pl.ds(column, 256)
        branch = dot_nn(hidden[...], w.wout[2 * D :, cols])
        s.branch3[:, cols] = branch
        result[:, cols] = s.stream3[:, cols] + mods[5:6, cols] * branch

    over_columns(D, 256, branch_three)
    done("down")


def block_backward(s, g, grad, mods, grad_mods, inner, mixed, frame_keep, text_keep, w, need, done, emit):
    frames = s.stream.shape[0]
    grad_mods[...] = jnp.zeros_like(grad_mods)

    def gate_three(rows):
        grad_out = grad[rows, :]
        g.g_three[rows, :] = to_low(grad_out * mods[5:6, :])
        grad_mods[5:6, :] += row_sum(grad_out * s.branch3[rows, :])

    over_rows(frames, gate_three)
    emit("g_three", g.g_three)
    need("down")
    need("up")

    def shrink(column):
        wide = pl.ds(column, WIDE)
        back = dot_nt(g.g_three[...], w.wout[pl.ds(2 * D + column, WIDE), :])
        upper = dot_nn(s.n3[...], w.win[:, pl.ds(4 * D + column, WIDE)])
        square = upper * upper
        tanh = jnp.tanh(ROOT * (upper + CUBE * (square * upper)))
        slope = 0.5 * (1.0 + tanh) + (0.5 * ROOT) * upper * (1.0 - tanh * tanh) * (1.0 + (3.0 * CUBE) * square)
        g.g_pre[:, wide] = to_low(back * slope)

    over_columns(FF, WIDE, shrink)
    done("down")
    emit("g_pre", g.g_pre)

    def inner_three(column):
        inner[:, pl.ds(column, 256)] = dot_nt(g.g_pre[...], w.win[pl.ds(column, 256), 4 * D :])

    over_columns(D, 256, inner_three)
    done("up")

    def pull_three(rows):
        normed, factor = scaled(s.stream3[rows, :])
        back = inner[rows, :]
        grad_mods[3:4, :] += row_sum(back)
        grad_mods[4:5, :] += row_sum(back * normed)
        total = grad[rows, :] + norm_pull(normed, factor, back * (1.0 + mods[4:5, :]))
        grad[rows, :] = total
        g.g_cross[rows, :] = to_low(total)

    over_rows(frames, pull_three)
    emit("g_cross", g.g_cross)
    need("co")

    def back_cross(column):
        mixed[:, pl.ds(column, 256)] = to_low(dot_nt(g.g_cross[...], w.wout[pl.ds(D + column, 256), :]))

    over_columns(D, 256, back_cross)
    done("co")

    def store_cross(index, grad_query, grad_key, grad_value):
        cols = slice(index * 128, (index + 1) * 128)
        g.g_cq[:, cols] = grad_query
        g.g_ckv[:, cols] = grad_key
        g.g_ckv[:, D + index * 128 : D + (index + 1) * 128] = grad_value

    attend_back(
        tile_of(s.cq, 0), tile_of(s.ckv, 0), tile_of(s.ckv, D), tile_of(mixed, 0), text_keep, store_cross
    )
    emit("g_cq", g.g_cq)
    emit("g_ckv", g.g_ckv)
    need("cq")

    def inner_two(column):
        inner[:, pl.ds(column, 256)] = dot_nt(g.g_cq[...], w.win[pl.ds(column, 256), 3 * D : 4 * D])

    over_columns(D, 256, inner_two)
    done("cq")

    def pull_two(rows):
        normed, factor = scaled(s.stream2[rows, :])
        back = inner[rows, :]
        grad_mods[6:7, :] += row_sum(back * normed)
        total = grad[rows, :] + norm_pull(normed, factor, back * mods[6:7, :])
        grad[rows, :] = total
        g.g_one[rows, :] = to_low(total * mods[2:3, :])
        grad_mods[2:3, :] += row_sum(total * s.branch1[rows, :])

    over_rows(frames, pull_two)
    emit("g_one", g.g_one)
    need("ao")

    def back_self(column):
        mixed[:, pl.ds(column, 256)] = to_low(dot_nt(g.g_one[...], w.wout[pl.ds(column, 256), :]))

    over_columns(D, 256, back_self)
    done("ao")

    def store_self(index, grad_query, grad_key, grad_value):
        cols = slice(index * 128, (index + 1) * 128)
        g.g_self[:, cols] = grad_query
        g.g_self[:, D + index * 128 : D + (index + 1) * 128] = grad_key
        g.g_self[:, 2 * D + index * 128 : 2 * D + (index + 1) * 128] = grad_value

    attend_back(
        tile_of(s.qkv, 0), tile_of(s.qkv, D), tile_of(s.qkv, 2 * D), tile_of(mixed, 0), frame_keep, store_self
    )
    emit("g_self", g.g_self)
    need("qkv")

    def inner_one(column):
        inner[:, pl.ds(column, 256)] = dot_nt(g.g_self[...], w.win[pl.ds(column, 256), : 3 * D])

    over_columns(D, 256, inner_one)
    done("qkv")

    def pull_one(rows):
        normed, factor = scaled(s.stream[rows, :])
        back = inner[rows, :]
        grad_mods[0:1, :] += row_sum(back)
        grad_mods[1:2, :] += row_sum(back * normed)
        grad[rows, :] = grad[rows, :] + norm_pull(normed, factor, back * (1.0 + mods[1:2, :]))

    over_rows(frames, pull_one)


def model_kernel(*refs):
    refs = list(refs)

    def take(count):
        taken = refs[:count]
        del refs[:count]
        return taken

    lengths, factor_ref, stream_ref, mods_ref, final_mods, text, noise, head = take(8)
    weights = [take(3) for _ in range(LAYERS)]
    loss_ref, grad_ref, grad_mods_ref, grad_final, grad_head = take(5)
    kept_out = [dict(zip(KEPT, take(len(KEPT)))) for _ in range(LAYERS)]
    win, wtext, wout = take(3)
    saved = [Names(**dict(zip((name for name, *_ in SAVED), take(len(SAVED))))) for _ in range(LAYERS)]
    g = Names(**dict(zip((name for name, _ in GRADS), take(len(GRADS)))))
    hidden, inner, mixed, final_low = take(4)
    load_sem, keep_sem = refs
    w = Names(win=win, wtext=wtext, wout=wout)
    frames, tokens = stream_ref.shape[0], text.shape[0]
    frame_keep = lax.broadcasted_iota(jnp.int32, (1, frames), 1) < lengths[0]
    text_keep = lax.broadcasted_iota(jnp.int32, (1, tokens), 1) < lengths[1]

    def load(layer, part):
        w_in, w_text, w_out = weights[layer]
        source, target = {
            "qkv": (w_in.at[:, : 3 * D], win.at[:, : 3 * D]),
            "cq": (w_in.at[:, 3 * D : 4 * D], win.at[:, 3 * D : 4 * D]),
            "up": (w_in.at[:, 4 * D :], win.at[:, 4 * D :]),
            "text": (w_text, wtext),
            "ao": (w_out.at[:D], wout.at[:D]),
            "co": (w_out.at[D : 2 * D], wout.at[D : 2 * D]),
            "down": (w_out.at[2 * D :], wout.at[2 * D :]),
        }[part]
        return pltpu.make_async_copy(source, target, load_sem.at[PARTS.index(part)])

    flying = {}

    def keep(layer):
        def emit(name, ref):
            copy = pltpu.make_async_copy(
                ref, kept_out[layer][name], keep_sem.at[layer, KEPT.index(name)]
            )
            copy.start()
            flying[name, layer] = copy

        return emit

    def settle(layer, names):
        for name in names:
            copy = flying.pop((name, layer), None)
            if copy is not None:
                copy.wait()

    nothing = lambda part: None
    for part in ("qkv", "ao", "cq", "text", "co", "up", "down"):
        load(0, part).start()
    over_rows(frames, lambda rows: saved[0].stream.__setitem__((rows, slice(None)), stream_ref[rows, :]))
    for layer in range(LAYERS):
        last = layer == LAYERS - 1
        if layer > 0:
            settle(layer - 1, ("hidden",))
        block_forward(
            saved[layer], hidden, grad_ref if last else saved[layer + 1].stream,
            mods_ref.at[layer], text, frame_keep, text_keep, w,
            lambda part: load(layer, part).wait(),
            nothing if last else (lambda part: load(layer + 1, part).start()),
            keep(layer),
        )

    def norm_final(rows):
        normed, _ = scaled(grad_ref[rows, :])
        final_low[rows, :] = to_low(normed * (1.0 + final_mods[1:2, :]) + final_mods[0:1, :])

    over_rows(frames, norm_final)
    error = dot_nn(final_low[...], head[...]) - noise[...]
    counted = lax.broadcasted_iota(jnp.int32, (frames, 1), 0) < lengths[0]
    error = jnp.where(counted, error, 0.0)
    loss_ref[...] = jnp.broadcast_to(row_sum(error * error), loss_ref.shape)
    grad_pred = to_low(error * factor_ref[0])
    grad_head[...] = dot_tn(final_low[...], grad_pred)
    inner[...] = dot_nt(grad_pred, head[...])
    grad_final[...] = jnp.zeros_like(grad_final)

    def pull_final(rows):
        normed, factor = scaled(grad_ref[rows, :])
        back = inner[rows, :]
        grad_final[0:1, :] += row_sum(back)
        grad_final[1:2, :] += row_sum(back * normed)
        grad_ref[rows, :] = norm_pull(normed, factor, back * (1.0 + final_mods[1:2, :]))

    over_rows(frames, pull_final)
    for layer in reversed(range(LAYERS)):
        last = layer == LAYERS - 1
        if not last:
            settle(layer + 1, [name for name, _ in GRADS])
        block_backward(
            saved[layer], g, grad_ref, mods_ref.at[layer], grad_mods_ref.at[layer], inner, mixed,
            frame_keep, text_keep, w,
            nothing if last else (lambda part: load(layer, part).wait()),
            nothing if layer == 0 else (lambda part: load(layer - 1, part).start()),
            keep(layer),
        )
    for layer in range(LAYERS):
        settle(layer, KEPT)


def run_model(stream, mods, final_mods, text, noise, head, lengths, factor, weights):
    frames, tokens = stream.shape[0], text.shape[0]
    low, full = jnp.bfloat16, jnp.float32
    widths = {**{name: width for name, width, _ in SAVED}, **dict(GRADS), "hidden": FF}

    def height(name):
        return tokens if name in ("ckv", "g_ckv") else frames

    kept = [jax.ShapeDtypeStruct((height(name), widths[name]), low) for name in KEPT]
    shape = jax.ShapeDtypeStruct
    here, there = pl.BlockSpec(memory_space=pltpu.VMEM), pl.BlockSpec(memory_space=pl.ANY)
    scalar = pl.BlockSpec(memory_space=pltpu.SMEM)
    out = pl.pallas_call(
        model_kernel,
        out_shape=[
            shape((8, noise.shape[1]), full),
            shape((frames, D), full),
            shape((LAYERS, 8, D), full),
            shape((8, D), full),
            shape((D, noise.shape[1]), full),
        ]
        + kept * LAYERS,
        in_specs=[scalar, scalar] + [here] * 6 + [there] * (3 * LAYERS),
        out_specs=[here] * 5 + [there] * (len(KEPT) * LAYERS),
        scratch_shapes=[pltpu.VMEM((D, JOINT), low), pltpu.VMEM((text.shape[1], 2 * D), low), pltpu.VMEM((2 * D + FF, D), low)]
        + [pltpu.VMEM((height(name), width), kind) for name, width, kind in SAVED] * LAYERS
        + [pltpu.VMEM((height(name), width), low) for name, width in GRADS]
        + [
            pltpu.VMEM((frames, FF), low),
            pltpu.VMEM((frames, D), full),
            pltpu.VMEM((frames, D), low),
            pltpu.VMEM((frames, D), low),
            pltpu.SemaphoreType.DMA((len(PARTS),)),
            pltpu.SemaphoreType.DMA((LAYERS, len(KEPT))),
        ],
        compiler_params=pltpu.CompilerParams(vmem_limit_bytes=VMEM_LIMIT),
    )(lengths, factor, stream, mods, final_mods, text, noise, head, *[w for layer in weights for w in layer])
    head_part, rest = out[:5], out[5:]
    count = len(KEPT)
    return head_part, [dict(zip(KEPT, rest[l * count : (l + 1) * count])) for l in range(LAYERS)]


def adam_update(weight, grad, first, second, rate):
    first_new = BETA_ONE * first + (1.0 - BETA_ONE) * grad
    second_new = BETA_TWO * second + (1.0 - BETA_TWO) * grad * grad
    first_hat = first_new / (1.0 - BETA_ONE**STEP)
    second_hat = second_new / (1.0 - BETA_TWO**STEP)
    weight_new = weight - rate * (
        first_hat / (jnp.sqrt(second_hat) + ADAM_EPSILON) + WEIGHT_DECAY * weight
    )
    return (first_new, second_new, weight_new)


def tiles(values, lead=()):
    flat = values.reshape(lead + (-1,))
    short = -flat.shape[-1] % 1024
    flat = jnp.pad(flat, [(0, 0)] * len(lead) + [(0, short)])
    return flat.reshape(lead + (-1, 128))


def body(
    ways,
    clean_latent,
    noise,
    text_feats,
    text_lengths,
    timesteps,
    valid_frames,
    w_in,
    w_text,
    w_out,
    gains,
    w_lead,
    w_head,
    first_in,
    second_in,
    first_text,
    second_text,
    first_out,
    second_out,
    first_gains,
    second_gains,
    first_lead,
    second_lead,
    first_head,
    second_head,
):
    count = ways[0] * ways[1]
    own = w_head.shape[0]
    channels = noise.shape[-1]
    clean_latent, noise, text_low = clean_latent[0], noise[0], text_feats[0]
    frames, caption = clean_latent.shape[0], text_low.shape[0]
    frame_keep = lax.iota(jnp.int32, frames) < valid_frames[0]
    text_keep = lax.iota(jnp.int32, caption) < text_lengths[0]
    rows = [w_in.shape[1], w_text.shape[1], w_out.shape[1]]
    halves = [JOINT // 2, D, D // 2]
    aligned = own <= SHARE and all(height % 8 == 0 for height in rows) and all(way % 2 == 0 for way in ways)

    sinus = time_features(timesteps)
    lead_low, head_low = to_low(w_lead), to_low(w_head)
    small = jnp.concatenate(
        [
            lead_low[FREQS:].astype(jnp.float32).reshape(-1),
            head_low[:, 3 * D :].astype(jnp.float32).reshape(-1),
            to_low(gains).astype(jnp.float32).reshape(-1),
        ]
    )
    facts = jnp.concatenate([to_low(sinus).astype(jnp.float32)[0], valid_frames.astype(jnp.float32)])
    facts = jnp.concatenate([tiles(facts), tiles(small)], 0)
    mod_low = jnp.concatenate(
        [to_low(w_in[layer, :, JOINT:]) for layer in range(LAYERS)] + [head_low[:, D : 3 * D]], 1
    )
    if aligned:
        lead_own = jnp.pad(lead_low[:FREQS], [(0, 0), (0, 128 - own)])
        head_own = jnp.pad(head_low[:, :D], [(0, SHARE - own), (0, 0)])
        mod_own = jnp.pad(mod_low, [(0, SHARE - own), (0, 0)])
        items = plan(halves, range(LAYERS), GATHER_PATTERN)
        weights, packed, pre_time, temb, mods = gather_weights(
            [w_in, w_text, w_out], facts, lead_own, head_own, mod_own, own, halves, ways, 1, items
        )
        mods = mods.reshape(-1)
    else:
        weights = [
            [
                lax.all_gather(to_low(shard[layer]), ALL, axis=0, tiled=True)
                for shard in (w_in[:, :, :JOINT], w_text, w_out)
            ]
            for layer in range(LAYERS)
        ]
        packed = lax.all_gather(facts, ALL, axis=0, tiled=False)
        sinus_all = to_low(packed.reshape(count, -1)[:, :FREQS])
        pre_time = dense(sinus_all, lead_low[:FREQS])
        act_low = to_low(jax.nn.silu(pre_time))
        temb = dense(act_low, head_low[:, :D]).reshape(count, count, own).transpose(1, 0, 2)
        temb = jnp.sum(lax.all_to_all(temb, ALL, 0, 0, tiled=True), 0)
        cond_low = to_low(jax.nn.silu(temb))
        mods = jnp.sum(lax.all_to_all(dense(cond_low, mod_low)[:, None], ALL, 0, 0, tiled=True), 0)[0]
    packed = packed.reshape(count, -1)
    frame_count = jnp.sum(packed[:, FREQS])
    small_all = packed[:, 1024:]
    at = channels * own
    lead_in = to_low(small_all[:, :at].reshape(count, channels, own).transpose(1, 0, 2).reshape(channels, D))
    head_pred = to_low(small_all[:, at : 2 * at].reshape(D, channels))
    gains_all = small_all[:, 2 * at : 2 * at + LAYERS * own].reshape(count, LAYERS, own)
    gains_all = gains_all.transpose(1, 0, 2).reshape(LAYERS, D)

    level = noise_level(timesteps)
    noisy_low = to_low(jnp.sqrt(level) * clean_latent + jnp.sqrt(1.0 - level) * noise)
    stream = dense(noisy_low, lead_in)
    block_mods = jnp.concatenate(
        [mods[: LAYERS * MOD].reshape(LAYERS, 6, D), gains_all[:, None], jnp.zeros((LAYERS, 1, D))], 1
    )
    final_mods = jnp.pad(mods[LAYERS * MOD : LAYERS * MOD + 2 * D].reshape(2, D), [(0, 6), (0, 0)])
    short = [(0, 0), (0, 128 - channels)]
    (loss_lanes, grad_stream, grad_blocks, grad_final, grad_pred_w), kept = run_model(
        stream,
        block_mods,
        final_mods,
        text_low,
        jnp.pad(noise, short),
        jnp.pad(head_pred, short),
        jnp.concatenate([valid_frames, text_lengths]),
        (2.0 / frame_count).reshape(1),
        weights,
    )
    grad_pred_w = grad_pred_w[:, :channels]
    grad_mods = jnp.concatenate([grad_blocks[:, :6].reshape(-1), grad_final[:2].reshape(-1)])
    grad_in_w = weight_grad(noisy_low, to_low(grad_stream))
    small_grads = jnp.concatenate(
        [
            grad_in_w.reshape(channels, count, own).transpose(1, 0, 2).reshape(count, -1),
            grad_pred_w.reshape(count, -1),
            grad_blocks[:, 6].reshape(LAYERS, count, own).transpose(1, 0, 2).reshape(count, -1),
        ],
        1,
    )
    if aligned:
        items = plan(halves, list(reversed(range(LAYERS))), SCATTER_PATTERN)
        rest = [
            tiles(to_low(grad_mods).astype(jnp.float32)),
            tiles(small_grads, (count,)),
            loss_lanes,
            packed.reshape(count, -1, 128),
            pre_time,
            temb,
            head_own,
            mod_own,
        ]
        *sums, grad_mod_w, grad_time_one, grad_time_two, small_sum, final = scatter_grads(
            kept, text_low, rest, own, rows, halves, ways, 2, items
        )
        grad_mod_w, grad_time_two = grad_mod_w[:own], grad_time_two[:own]
        grad_time_one = grad_time_one[:, :own]
        small_sum = small_sum.reshape(-1)
        loss_sum, squares = jnp.sum(final[1]), final[0, 0]
    else:
        sums = [[], [], []]
        for k in kept:
            joint = [weight_grad(k[a], k[b]) for a, b in (("n1", "g_self"), ("n2", "g_cq"), ("n3", "g_pre"))]
            back = [weight_grad(k[a], k[b]) for a, b in (("mixed1", "g_one"), ("mixed2", "g_cross"), ("hidden", "g_three"))]
            grads = (jnp.concatenate(joint, 1), weight_grad(text_low, k["g_ckv"]), jnp.concatenate(back, 0))
            for member, grad in enumerate(grads):
                sums[member].append(lax.psum_scatter(grad, ALL, scatter_dimension=0, tiled=True))
        sums = [jnp.stack(part) for part in sums]
        mods_all = lax.all_gather(to_low(grad_mods), ALL, axis=0, tiled=False)
        grad_mod_w = weight_grad(cond_low, mods_all)
        _, pull_cond = jax.vjp(jax.nn.silu, temb)
        (grad_temb,) = pull_cond(dense_back(mods_all, mod_low))
        grad_temb = lax.all_gather(to_low(grad_temb), ALL, axis=0, tiled=False)
        grad_temb = grad_temb.transpose(1, 0, 2).reshape(count, D)
        grad_time_two = weight_grad(act_low, grad_temb)
        _, pull_time = jax.vjp(jax.nn.silu, pre_time)
        (grad_pre_time,) = pull_time(dense_back(grad_temb, head_low[:, :D]))
        grad_time_one = weight_grad(sinus_all, to_low(grad_pre_time))
        small_sum = jnp.sum(lax.all_to_all(small_grads, ALL, 0, 0, tiled=True), 0)
    mod_grads = grad_mod_w[:, : LAYERS * MOD].reshape(own, LAYERS, MOD).transpose(1, 0, 2)
    grad_list = [
        jnp.concatenate([sums[0], mod_grads], 2),
        sums[1],
        sums[2],
        small_sum[2 * at : 2 * at + LAYERS * own].reshape(LAYERS, own),
        jnp.concatenate([grad_time_one, small_sum[:at].reshape(channels, own)], 0),
        jnp.concatenate(
            [grad_time_two, grad_mod_w[:, LAYERS * MOD :], small_sum[at : 2 * at].reshape(own, channels)], 1
        ),
    ]
    if not aligned:
        local = jnp.stack([jnp.sum(loss_lanes[0]), sum((jnp.sum(item * item) for item in grad_list))])
        loss_sum, squares = jnp.sum(lax.all_gather(local, ALL, axis=0, tiled=False), 0)
    grad_norm = jnp.sqrt(squares)
    factor = CLIP_NORM / jnp.maximum(grad_norm, CLIP_NORM)
    params = (w_in, w_text, w_out, gains, w_lead, w_head)
    firsts = (first_in, first_text, first_out, first_gains, first_lead, first_head)
    seconds = (second_in, second_text, second_out, second_gains, second_lead, second_head)
    rates = (LEARN_RATE, LEARN_RATE, LEARN_RATE, GAIN_RATE, LEARN_RATE, LEARN_RATE)
    results = []
    for weight, grad, first, second, rate in zip(params, grad_list, firsts, seconds, rates):
        results.extend(adam_update(weight, grad * factor, first, second, rate))
    return (loss_sum, frame_count, grad_norm, *results)


def solution(mesh):
    ways = (mesh.shape["dp"], mesh.shape["fsdp"])
    clips = [P(ALL, None, None)] * 3 + [P(ALL)] * 3
    weights = [P(None, ALL, None)] * 3 + [P(None, ALL)] * 2 + [P(ALL, None)]
    moments = [spec for spec in weights for _ in range(2)]
    results = [spec for spec in weights for _ in range(3)]
    return jax.shard_map(
        functools.partial(body, ways),
        mesh=mesh,
        in_specs=tuple(clips + weights + moments),
        out_specs=tuple([P()] * 3 + results),
        check_vma=False,
    )
```

```python
import functools
import math

import jax
import jax.numpy as jnp
from jax import lax
from jax.experimental import pallas as pl
from jax.experimental.pallas import tpu as pltpu
from jax.sharding import PartitionSpec as P

D = 768
HEADS = 12
HEAD_DIM = 64
FF = 3072
FREQS = 256
LAYERS = 2
STEP = 10
MOD = 6 * D
JOINT = 4 * D + FF

EPSILON = 1e-06
NEGATIVE = -1e30
BETA_ONE = 0.5
BETA_TWO = 0.5
LEARN_RATE = 0.02
GAIN_RATE = 0.3
WEIGHT_DECAY = 0.01
ADAM_EPSILON = 1e-08
CLIP_NORM = 1.0

ALL = ("dp", "fsdp")
MESH = pl.DeviceIdType.MESH
VMEM_LIMIT = 60 * 1024 * 1024


def place(ways):
    dp_ways, fsdp_ways = ways
    row, col = lax.axis_index("dp"), lax.axis_index("fsdp")
    sizes = (dp_ways // 2, 2, fsdp_ways // 2)
    spot = (row // 2, lax.rem(row, 2), col // 2)
    return sizes, spot, lax.rem(col, 2)


def device_at(spot, core):
    z, y, x = spot
    return (z * 2 + y, x * 2 + core)


def moved(spot, axis, size, steps):
    spot = list(spot)
    spot[axis] = lax.rem(spot[axis] + steps, size)
    return tuple(spot)


def greet_peers(sizes, spot, core):
    barrier = pltpu.get_barrier_semaphore()
    count = 1
    pl.semaphore_signal(barrier, inc=1, device_id=device_at(spot, 1 - core), device_id_type=MESH)
    for axis in range(3):
        for steps in range(1, sizes[axis]):
            count += 1
            pl.semaphore_signal(
                barrier,
                inc=1,
                device_id=device_at(moved(spot, axis, sizes[axis], steps), core),
                device_id_type=MESH,
            )
    pl.semaphore_wait(barrier, count)


def remote(source, target, send, recv, device):
    return pltpu.make_async_remote_copy(
        src_ref=source, dst_ref=target, send_sem=send, recv_sem=recv, device_id=device, device_id_type=MESH
    )


def greet_all(ways, me):
    count = ways[0] * ways[1]
    barrier = pltpu.get_barrier_semaphore()
    for step in range(1, count):
        pl.semaphore_signal(
            barrier, inc=1, device_id=numbered(ways, lax.rem(me + step, count)), device_id_type=MESH
        )
    pl.semaphore_wait(barrier, count - 1)


def numbered(ways, index):
    return (index // ways[1], lax.rem(index, ways[1]))


ROUNDS = ("core", 2, 1, 0)


class Hops:
    def __init__(self, sizes, spot, core):
        self.sizes, self.spot, self.core = sizes, spot, core

    def count(self, axis):
        return 2 if axis == "core" else self.sizes[axis]

    def place(self, axis):
        return self.core if axis == "core" else self.spot[axis]

    def other(self, axis, steps):
        if axis == "core":
            return 1 - self.core, device_at(self.spot, 1 - self.core)
        spot = moved(self.spot, axis, self.sizes[axis], steps)
        return spot[axis], device_at(spot, self.core)


def sum_steps(hops, totals, landed, send_sem, recv_sem, sent):
    first = [sum(hops.count(axis) - 1 for axis in ROUNDS[:turn]) for turn in range(len(ROUNDS))]

    def copies(turn):
        axis = ROUNDS[turn]
        return [
            remote(
                totals.at[turn], landed.at[first[turn] + steps - 1],
                send_sem.at[turn, steps - 1], recv_sem.at[turn, steps - 1], hops.other(axis, steps)[1],
            )
            for steps in range(1, hops.count(axis))
        ]

    def begin(turn):
        for copy in copies(turn):
            copy.start()
            sent.append(copy)

    def go_on(turn):
        for copy in copies(turn):
            copy.wait_recv()
        total = totals[turn]
        for steps in range(1, hops.count(ROUNDS[turn])):
            total = total + landed[first[turn] + steps - 1]
        totals[turn + 1] = total
        if turn + 1 < len(ROUNDS):
            begin(turn + 1)

    return [lambda: begin(0)] + [functools.partial(go_on, turn) for turn in range(len(ROUNDS))]


def split_steps(hops, rows, landed, out, send_sem, recv_sem, sent):
    places = {"core": 3, 2: 2, 1: 1, 0: 0}

    def index(turn, place_on):
        at = [slice(None)] * 4
        for early in ROUNDS[:turn]:
            at[places[early]] = hops.place(early)
        at[places[ROUNDS[turn]]] = place_on
        return tuple(at)

    def copies(turn):
        axis = ROUNDS[turn]
        made = []
        for steps in range(1, hops.count(axis)):
            place_on, device = hops.other(axis, steps)
            made.append(
                remote(
                    rows.at[index(turn, place_on)], landed[turn].at[steps - 1],
                    send_sem.at[turn, steps - 1], recv_sem.at[turn, steps - 1], device,
                )
            )
        return made

    def begin(turn):
        for copy in copies(turn):
            copy.start()
            sent.append(copy)

    def go_on(turn):
        for copy in copies(turn):
            copy.wait_recv()
        axis = ROUNDS[turn]
        mine = rows.at[index(turn, hops.place(axis))]
        others = range(hops.count(axis) - 1)
        if turn == 3:
            out[...] = sum((landed[turn][k] for k in others), mine[...])
        else:

            @pl.loop(0, hops.sizes[0])
            def _(z):
                mine[z] = sum((landed[turn][k, z] for k in others), mine[z])

            begin(turn + 1)

    return [lambda: begin(0)] + [functools.partial(go_on, turn) for turn in range(len(ROUNDS))]


def split_shapes(sizes, tile):
    z, y, x = sizes
    return [
        pltpu.VMEM((1, z, y, x) + tile, jnp.float32),
        pltpu.VMEM((x - 1, z, y) + tile, jnp.float32),
        pltpu.VMEM((y - 1, z) + tile, jnp.float32),
        pltpu.VMEM((z - 1,) + tile, jnp.float32),
    ]


def spread_steps(hops, rows, send_sem, recv_sem, sent):
    turns = (0, 2, 1, "core")
    places = {"core": 3, 2: 2, 1: 1, 0: 0}

    def index(turn, place_on):
        at = [hops.spot[0], hops.spot[1], hops.spot[2], hops.core]
        for early in turns[:turn]:
            at[places[early]] = slice(None)
        at[places[turns[turn]]] = place_on
        return tuple(at)

    def copies(turn, origin):
        axis = turns[turn]
        made = []
        for steps in range(1, hops.count(axis)):
            device = hops.other(axis, steps)[1]
            place_on = hops.other(axis, hops.count(axis) - steps)[0] if origin else hops.place(axis)
            part = rows.at[index(turn, place_on)]
            made.append(remote(part, part, send_sem.at[turn, steps - 1], recv_sem.at[turn, steps - 1], device))
        return made

    def begin(turn):
        for copy in copies(turn, False):
            copy.start()
            sent.append(copy)

    def go_on(turn):
        for copy in copies(turn, True):
            copy.wait_recv()
        if turn + 1 < len(turns):
            begin(turn + 1)

    return [lambda: begin(0)] + [functools.partial(go_on, turn) for turn in range(len(turns))]


def sigmoid(values):
    return 1.0 / (1.0 + jnp.exp(-values))


def chosen(me, own, width):
    shape = (D, width)
    row, column = (lax.broadcasted_iota(jnp.int32, shape, axis) for axis in range(2))
    return jnp.logical_and(row == me * own + column, column < own).astype(jnp.float32)


SHARE = 32
MOD_ROWS = (LAYERS * MOD + 2 * D) // 128
MOD_TILE = (-(-MOD_ROWS // 8) * 8, 128)


def gather_kernel(ways, rows, halves, items, layers, own, *refs):
    members = len(rows)
    refs = list(refs)

    def take(count):
        taken = refs[:count]
        del refs[:count]
        return taken

    shards = take(members)
    facts_in, lead_own, head_own, mod_own, lengths, text, noisy = take(7)
    fulls = take(members * layers)
    facts, pre_time, temb_own, block_mods, final_mods, small, result = take(7)
    early = dict(zip(EARLY, take(len(EARLY))))
    totals, landed, mod_parts = take(3)
    mod_landed = take(4)
    facts_send, facts_recv, sum_send, sum_recv, split_send, split_recv = take(6)
    mods, win, wtext, wout = take(4)
    saved = Names(**dict(zip((name for name, *_ in SAVED), take(len(SAVED)))))
    (hidden,) = take(1)
    load_sem, keep_sem = take(2)
    rest = refs
    stages = rest[:members]
    blocks = rest[members : 2 * members]
    pre_send, pre_recv, own_sem, put_sem, *sends, c_send, c_recv = rest[2 * members :]
    sends, recvs = sends[0::2], sends[1::2]
    sizes, spot, core = place(ways)
    z, y, x = spot
    partner = device_at(spot, 1 - core)
    count = ways[0] * ways[1]
    me = lax.axis_index("dp") * ways[1] + lax.axis_index("fsdp")
    greet_all(ways, me)

    def facts_copy(step):
        return remote(
            facts_in, facts.at[me], facts_send.at[step], facts_recv.at[step],
            numbered(ways, lax.rem(me + step, count)),
        )

    for step in range(1, count):
        facts_copy(step).start()
    facts[me] = facts_in[...]

    def full(layer, member):
        return fulls[layer * members + member]

    pre = []
    for layer in range(layers):
        for member in range(members):
            height, half = rows[member], halves[member]
            place_in = stages[member].at[layer, pl.ds(pl.multiple_of(core * height, 8), height)]
            mine = shards[member].at[layer, :, pl.ds(pl.multiple_of(core * half, 128), half)]
            other = shards[member].at[layer, :, pl.ds(pl.multiple_of((1 - core) * half, 128), half)]
            index = layer * members + member
            sent = remote(other, place_in, pre_send.at[index], pre_recv.at[index], partner)
            sent.start()
            kept = pltpu.make_async_copy(mine, place_in, own_sem.at[index])
            kept.start()
            pre.append((sent, kept))
    arrived = set()
    put_done = set()
    sent_all = []

    def columns(i, side):
        _, member, start, size, _ = items[i]
        return pl.ds(pl.multiple_of(side * halves[member] + start, 128), size)

    def put(layer, member):
        half = halves[member]
        return pltpu.make_async_copy(
            blocks[member].at[layer],
            full(layer, member).at[z, y, x, :, pl.ds(pl.multiple_of(core * half, 128), half)],
            put_sem.at[layer * members + member],
        )

    def ready(layer, member):
        if (layer, member) in arrived:
            return
        arrived.add((layer, member))
        index = layer * members + member
        height = rows[member]
        sent, kept = pre[index]
        kept.wait()
        theirs = stages[member].at[layer, pl.ds(pl.multiple_of((1 - core) * height, 8), height)]
        remote(theirs, theirs, pre_send.at[index], pre_recv.at[index], partner).wait_recv()
        blocks[member][layer] = stages[member][layer].astype(jnp.bfloat16)
        put(layer, member).start()

    def own_put(layer, member):
        if (layer, member) not in put_done:
            put_done.add((layer, member))
            put(layer, member).wait()

    def region(i, phase, origin, side):
        layer, member, start, size, order = items[i]
        index = [slice(None) if order.index(axis) < phase else spot[axis] for axis in range(3)]
        if phase < 3 and origin is not None:
            index[order[phase]] = origin
        return full(layer, member).at[(*index, slice(None), columns(i, side))]

    def send(copy):
        copy.start()
        sent_all.append(copy)

    def start(i, phase):
        layer, member, first, size, order = items[i]
        axis = order[phase]
        if phase == 0:
            ready(layer, member)
            source = blocks[member].at[layer, :, pl.ds(first, size)]
        else:
            own_put(layer, member)
            source = region(i, phase, None, core)
        for steps in range(1, sizes[axis]):
            send(
                remote(
                    source, region(i, phase, spot[axis], core),
                    sends[phase].at[i, steps - 1], recvs[phase].at[i, steps - 1],
                    device_at(moved(spot, axis, sizes[axis], steps), core),
                )
            )
        if phase == 2:
            send(remote(source, source, c_send.at[i, 0], c_recv.at[i, 0], partner))

    def finish(i, phase):
        axis = items[i][4][phase]
        for steps in range(1, sizes[axis]):
            land = region(i, phase, lax.rem(spot[axis] + sizes[axis] - steps, sizes[axis]), core)
            remote(land, land, sends[phase].at[i, steps - 1], recvs[phase].at[i, steps - 1], partner).wait_recv()
            if phase == 2:
                send(remote(land, land, c_send.at[i, steps], c_recv.at[i, steps], partner))

    def c_wait(i):
        axis = items[i][4][2]
        for steps in range(sizes[axis]):
            land = region(i, 2, lax.rem(spot[axis] + sizes[axis] - steps, sizes[axis]), 1 - core)
            remote(land, land, c_send.at[i, steps], c_recv.at[i, steps], partner).wait_recv()

    hops = Hops(sizes, spot, core)

    def time_layers():
        for step in range(1, count):
            origin = lax.rem(me + count - step, count)
            remote(
                facts_in, facts.at[origin], facts_send.at[step], facts_recv.at[step], numbered(ways, origin)
            ).wait_recv()
        value = dot_nn(to_low(facts[:, 0, :]), lead_own[:128, :]) + dot_nn(to_low(facts[:, 1, :]), lead_own[128:, :])
        pre_time[...] = value
        totals[0] = dot_nn(to_low(value * sigmoid(value))[:, :SHARE], head_own[...])
        sums[0]()

    def modulation():
        temb = lax.dot_general(
            totals[4], chosen(me, own, 128), (((1,), (0,)), ((), ())),
            precision=lax.Precision.HIGHEST, preferred_element_type=jnp.float32,
        )
        temb_own[...] = temb
        cond = to_low(temb * sigmoid(temb))[:, :SHARE]
        mod_parts[:, MOD_ROWS:, :] = jnp.zeros((count, MOD_TILE[0] - MOD_ROWS, 128), jnp.float32)
        for j in range(0, MOD_ROWS, 4):
            part = dot_nn(cond, mod_own[:, j * 128 : (j + 4) * 128])
            for k in range(4):
                mod_parts[:, j + k, :] = part[:, k * 128 : (k + 1) * 128]
        splits[0]()

    sums = sum_steps(hops, totals, landed, sum_send, sum_recv, sent_all)
    splits = split_steps(
        hops, mod_parts.reshape(sizes + (2,) + MOD_TILE), mod_landed, mods, split_send, split_recv, sent_all
    )
    side = [time_layers] + sums[1:] + [modulation] + splits[1:]

    def prepare():
        small[...] = to_low(facts[:, 8 : 8 + own, :].reshape(D, 128))
        gains = dot_nt(to_low(gain_pick().astype(jnp.float32)), small[...])

        def row(piece):
            tiles_of = [mods[piece * (D // 128) + k : piece * (D // 128) + k + 1, :] for k in range(D // 128)]
            return jnp.concatenate(tiles_of, 1)

        for layer in range(layers):
            for j in range(6):
                block_mods[layer, j : j + 1, :] = row(layer * 6 + j)
            block_mods[layer, 6:7, :] = gains[layer : layer + 1, :]
            block_mods[layer, 7:8, :] = jnp.zeros((1, D), jnp.float32)
        final_mods[...] = jnp.zeros_like(final_mods)
        for j in range(2):
            final_mods[j : j + 1, :] = row(layers * 6 + j)
        for column in range(0, D, 256):
            saved.stream[:, column : column + 256] = dot_nt(noisy[...], small[column : column + 256, :])

    def load(part):
        return pltpu.make_async_copy(
            *weight_parts(whole_weights, (win, wtext, wout))[part], load_sem.at[PARTS.index(part)]
        )

    def emit(name, ref):
        pltpu.make_async_copy(ref, early[name], keep_sem.at[EARLY.index(name)]).start()

    def first_block():
        frame_keep, text_keep = keeps(lengths, noisy.shape[0], text.shape[0])
        for part in ("qkv", "ao", "cq", "text", "co", "up", "down"):
            load(part).start()
        yield from block_forward(
            saved, hidden, result, block_mods.at[0], text, frame_keep, text_keep,
            Names(win=win, wtext=wtext, wout=wout), lambda part: load(part).wait(), lambda part: None, emit,
        )
        for name in NEEDED:
            if name not in KEPT:
                emit(name, getattr(saved, name))

    whole_weights = [
        full(0, member).reshape(sizes[0] * sizes[1] * sizes[2] * 2 * rows[member], 2 * halves[member]) for member in range(members)
    ]
    order = schedule(items, GATHER_LAGS)
    turn = max(k for k, (i, _) in enumerate(order) if items[i][0] == 0) + 1
    waited = set()

    def advance(i, phase):
        if phase > 0:
            finish(i, phase - 1)
        if phase < 3:
            start(i, phase)

    for i, phase in order[:turn]:
        if phase in (1, 2) and side:
            side.pop(0)()
        advance(i, phase)
    for step in side:
        step()
    side = []
    prepare()
    for i in range(len(items)):
        if items[i][0] == 0:
            c_wait(i)
            waited.add(i)
            own_put(*items[i][:2])
    later = list(order[turn:])
    pace = BLOCK_PARTS / max(len(later), 1)
    for part, _ in enumerate(first_block()):
        if later and part >= pace * (len(order) - turn - len(later)):
            advance(*later.pop(0))
    for i, phase in later:
        advance(i, phase)
    for i in range(len(items)):
        if i not in waited:
            c_wait(i)
    for name in EARLY:
        ref = hidden if name == "hidden" else getattr(saved, name)
        pltpu.make_async_copy(ref, early[name], keep_sem.at[EARLY.index(name)]).wait()
    for layer in range(layers):
        for member in range(members):
            own_put(layer, member)
    for step in range(1, count):
        facts_copy(step).wait_send()
    for sent, _ in pre:
        sent.wait_send()
    for copy in sent_all:
        copy.wait_send()


BLOCK_PARTS = 48
EARLY = ("n1", "n2", "n3", "mixed1", "mixed2", "hidden", "stream", "qkv", "branch1", "stream2", "cq", "ckv", "stream3", "branch3", "stats1", "stats2")


def gather_weights(shards, facts, lead_own, head_own, mod_own, lengths, text, noisy, own, halves, ways, number, items):
    layers = shards[0].shape[0]
    rows = [s.shape[1] for s in shards]
    members = len(shards)
    sizes = (ways[0] // 2, 2, ways[1] // 2)
    devices = ways[0] * ways[1]
    count = layers * members
    n = len(items)
    frames, tokens = noisy.shape[0], text.shape[0]
    sem, vmem, full, shape = pltpu.SemaphoreType.DMA, pltpu.VMEM, jnp.float32, jax.ShapeDtypeStruct
    here, there = pl.BlockSpec(memory_space=pltpu.VMEM), pl.BlockSpec(memory_space=pl.ANY)
    scalar = pl.BlockSpec(memory_space=pltpu.SMEM)
    out = pl.pallas_call(
        functools.partial(gather_kernel, ways, rows, halves, items, layers, own),
        out_shape=[
            shape(sizes + (2 * rows[m], 2 * halves[m]), jnp.bfloat16) for _ in range(layers) for m in range(members)
        ]
        + [
            shape((devices,) + facts.shape, full),
            shape((devices, 128), full),
            shape((devices, 128), full),
            shape((layers, 8, D), full),
            shape((8, D), full),
            shape((D, 128), jnp.bfloat16),
            shape((frames, D), full),
        ]
        + [shape(shape_of(name, frames, tokens), KINDS[name]) for name in EARLY],
        in_specs=[there] * members + [here] * 4 + [scalar] + [here] * 2,
        out_specs=[there] * count + [here] * 7 + [there] * len(EARLY),
        scratch_shapes=[
            vmem((len(ROUNDS) + 1, devices, D), full),
            vmem((sizes[0] + sizes[1] + sizes[2] - 2, devices, D), full),
            vmem((devices,) + MOD_TILE, full),
        ]
        + split_shapes(sizes, MOD_TILE)
        + [sem((devices,))] * 2
        + [sem((len(ROUNDS), max(sizes)))] * 4
        + [vmem(MOD_TILE, full), vmem((D, JOINT), jnp.bfloat16)]
        + [vmem((text.shape[1], 2 * D), jnp.bfloat16), vmem((2 * D + FF, D), jnp.bfloat16)]
        + [vmem(shape_of(name, frames, tokens), kind) for name, _, kind in SAVED]
        + [vmem((frames, FF), jnp.bfloat16), sem((len(PARTS),)), sem((len(EARLY),))]
        + [vmem((layers, 2 * rows[m], halves[m]), full) for m in range(members)]
        + [vmem((layers, 2 * rows[m], halves[m]), jnp.bfloat16) for m in range(members)]
        + [sem((count,))] * 4
        + [sem((n, max(sizes)))] * 8,
        compiler_params=pltpu.CompilerParams(
            collective_id=number, has_side_effects=True, vmem_limit_bytes=VMEM_LIMIT
        ),
    )(*shards, facts, lead_own, head_own, mod_own, lengths, text, noisy)
    weights = [
        [out[l * members + m].reshape(-1, 2 * halves[m]) for m in range(members)] for l in range(layers)
    ]
    return weights, out[count : count + 7], dict(zip(EARLY, out[count + 7 :]))


ORDERS = ((0, 2, 1), (0, 1, 2), (2, 0, 1), (1, 0, 2))
GATHER_LAGS = ((-1.5, 0.0, 3.0, 7.5), (-3.0, 0.0, 2.0, 6.5))
SCATTER_LAGS = ((-2.0, 0.0, 4.5, 7.5, 9.0), (-2.0, 0.0, 4.5, 6.5, 9.5))
GATHER_PATTERN = (1, 0, 1, 2, 1, 1, 0, 1, 0, 1, 2, 1, 2, 1, 3, 1, 2, 1)
SCATTER_PATTERN = GATHER_PATTERN[::-1]


def schedule(items, lags):
    steps = []
    for i, item in enumerate(items):
        own = lags[0 if item[4][0] == 0 else 1]
        steps.extend((i + lag, -phase, i) for phase, lag in enumerate(own))
    return [(i, -phase) for _, phase, i in sorted(steps)]


def plan(halves, layers, pattern):
    items = []
    for layer in layers:
        for member, width in enumerate(halves):
            size = width // 4 if width % 512 == 0 else (width // 2 if width % 256 == 0 else 128)
            for start in range(0, width, size):
                items.append((layer, member, start, size, ORDERS[pattern[len(items) % len(pattern)]]))
    return items


RINGS = (2, 1, 1)
ACTS = ("n1", "n2", "n3", "mixed1", "mixed2", "hidden", "g_self", "g_cq", "g_pre", "g_ckv", "g_one", "g_cross", "g_three")


def scatter_kernel(ways, rows, halves, items, layers, own, *refs):
    members = len(rows)
    n = len(items)
    rest = list(refs)

    def take(count):
        taken = rest[:count]
        del rest[:count]
        return taken

    (text_in,) = take(1)
    acts = [dict(zip(ACTS, take(len(ACTS)))) for _ in range(layers)]
    mods_in, small_in, loss_in, facts_in, pre_time, temb_own, head_own, mod_own = take(8)
    outs = take(members)
    grad_mod, grad_time_one, grad_time_two, small_out, final = take(5)
    all_mods, small_rows, totals, landed, squares = take(5)
    small_landed = take(4)
    spread_send, spread_recv, sum_send, sum_recv, split_send, split_recv, end_send, end_recv = take(8)
    ends, end_landed, backs, facts, bring_sem = take(5)
    lefts, rights, text, right_text, hidden, mixes, right_out = take(7)
    ring = take(members)
    whole = take(n)
    parts = [take(n) for _ in range(3)]
    partial = take(n)
    load_sem, c_send, c_recv, *sems, e_send, e_recv, o_sem = rest
    sends, recvs = sems[0::2], sems[1::2]
    sizes, spot, core = place(ways)
    partner = device_at(spot, 1 - core)
    greet_peers(sizes, spot, core)
    frames = hidden.shape[0]
    sent_all = []
    me = lax.axis_index("dp") * ways[1] + lax.axis_index("fsdp")
    hops = Hops(sizes, spot, core)
    squares[...] = jnp.zeros_like(squares)

    def count_squares(value):
        squares[...] += jnp.broadcast_to(jnp.sum(value * value, (0, 1), keepdims=True), squares.shape)

    temb = temb_own[...]
    share = sigmoid(temb)
    cond = to_low(temb * share)[:, :SHARE]
    gate = sigmoid(pre_time[...])
    act = to_low(pre_time[...] * gate)[:, :SHARE]
    slope_temb = (share * (1.0 + temb * (1.0 - share)))[:, :SHARE]
    slope_time = (gate * (1.0 + pre_time[...] * (1.0 - gate)))[:, :SHARE]
    all_mods[me] = mods_in[...]
    sums = sum_steps(hops, totals, landed, sum_send, sum_recv, sent_all)
    spreads = spread_steps(
        hops, all_mods.reshape(sizes + (2,) + MOD_TILE), spread_send, spread_recv, sent_all
    )
    tile = tuple(small_in.shape[1:])
    splits = split_steps(
        hops, small_rows.reshape(sizes + (2,) + tile), small_landed, small_out, split_send, split_recv, sent_all
    )

    bring = [
        pltpu.make_async_copy(small_in, small_rows, bring_sem.at[0]),
        pltpu.make_async_copy(facts_in.at[:, 0:8], facts, bring_sem.at[1]),
    ]
    for copy in bring:
        copy.start()

    def begin_small():
        for copy in bring:
            copy.wait()
        splits[0]()

    def modulation_part(begin, end):
        back = jnp.zeros_like(backs) if begin == 0 else backs[...]
        for j in range(begin, end):
            cols = slice(j * 128, (j + 1) * 128)
            grad = to_low(all_mods[:, j, :])
            back = back + dot_nt(grad, mod_own[:, cols])
            grad_mod[:, cols] = dot_tn(cond, grad)
        backs[...] = back
        count_squares(grad_mod[:, begin * 128 : end * 128])

    def modulation_back():
        grad_temb = to_low(backs[...] * slope_temb)
        pick = to_low(chosen(me, own, SHARE))
        totals[0] = dot_nt(grad_temb, pick)
        sums[0]()

    def time_back():
        grad_temb = to_low(totals[4])
        grad_time_two[...] = dot_tn(act, grad_temb)
        grad_time = to_low(dot_nt(grad_temb, head_own[...]) * slope_time)
        for j in range(2):
            grad_time_one[j * 128 : (j + 1) * 128, :] = dot_tn(to_low(facts[:, j, :]), grad_time)
        count_squares(grad_time_two[...])
        count_squares(grad_time_one[...])
        count_squares(small_out[...])

    def together(*steps):
        return lambda: [step() for step in steps]

    def rest():
        pass

    side = [together(spreads[0], begin_small)]
    for pair in zip(spreads[1:], splits[1:]):
        side += [rest, together(*pair)]
    parts_of = [functools.partial(modulation_part, j, j + 12) for j in range(0, MOD_ROWS, 12)]
    side += [together(*parts_of[k : k + 2]) for k in range(0, len(parts_of), 2)]
    side += [modulation_back] + sums[1:] + [time_back]

    def send(copy):
        copy.start()
        sent_all.append(copy)

    def loads(layer, member):
        a = acts[layer]
        if member == 0:
            pairs = [(a["n1"], lefts.at[0]), (a["n2"], lefts.at[1]), (a["n3"], lefts.at[2])]
            pairs += [(a["g_self"].at[:, j * D : (j + 1) * D], rights.at[j]) for j in range(3)]
            pairs += [(a["g_cq"], rights.at[3])]
            pairs += [(a["g_pre"].at[:, j * D : (j + 1) * D], rights.at[4 + j]) for j in range(4)]
        elif member == 1:
            pairs = [(a["g_ckv"].at[:, j * D : (j + 1) * D], right_text.at[j]) for j in range(2)]
            if layer == items[0][0]:
                pairs.append((text_in, text))
        else:
            pairs = [(a["mixed1"], mixes.at[0]), (a["mixed2"], mixes.at[1]), (a["hidden"], hidden)]
            for j, name in enumerate(("g_one", "g_cross", "g_three")):
                pairs += [(a[name].at[:, side * (D // 2) : (side + 1) * (D // 2)], right_out.at[side, j]) for side in range(2)]
        return [
            pltpu.make_async_copy(source, target, load_sem.at[layer, member, j])
            for j, (source, target) in enumerate(pairs)
        ]

    def load(layer, member):
        for copy in loads(layer, member):
            copy.start()

    loaded = set()

    def need(layer, member):
        if (layer, member) not in loaded:
            loaded.add((layer, member))
            for copy in loads(layer, member):
                copy.wait()

    def product(i, side, store):
        layer, member, start, size, _ = items[i]
        need(layer, member)
        if member == 0:
            j = start // D
            at = pl.ds(start % D, size)
            left = jnp.where(side == 1, 2, 0 if j < 3 else 1)
            right = rights[side * 4 + j, :, at]
            for row in range(0, D, 384):
                store(pl.ds(row, 384), dot_tn(lefts[left, :, row : row + 384], right))
        elif member == 1:
            right = right_text[side, :, pl.ds(start, size)]
            for row in range(0, text.shape[1], 512):
                store(pl.ds(row, 512), dot_tn(text[:, row : row + 512], right))
        else:
            cols = pl.ds(start, size)
            for j in range(2):
                store(pl.ds(j * D, D), dot_tn(mixes[j], right_out[side, j, :, cols]))

            @pl.loop(0, 4)
            def _(j):
                at = pl.multiple_of(j * D, D)
                store(pl.ds(pl.multiple_of(2 * D + j * D, D), D), dot_tn(hidden[:, pl.ds(at, D)], right_out[side, 2, :, cols]))

    def columns(i, side):
        _, member, start, size, _ = items[i]
        return pl.ds(pl.multiple_of(side * halves[member] + start, 128), size)

    def blocks(ref, i):
        return ref.reshape(sizes + (2 * rows[items[i][1]], items[i][3]))

    ring_at, used = [], {}
    for i, (_, member, *_) in enumerate(items):
        ring_at.append(used.setdefault(member, []))
        ring_at[-1] = len(used[member])
        used[member].append(i)

    def c_copy(i):
        member, size = items[i][1], items[i][3]
        slot = ring_at[i] % RINGS[member]
        return remote(ring[member].at[slot, :, pl.ds(0, size)], whole[i], c_send.at[i], c_recv.at[i], partner)

    def give(i):
        member, size = items[i][1], items[i][3]
        slot = ring_at[i] % RINGS[member]
        if ring_at[i] >= RINGS[member]:
            c_copy(used[member][ring_at[i] - RINGS[member]]).wait_send()
        target = ring[member].at[slot]

        def store(at, value):
            target[at, pl.ds(0, size)] = value.astype(jnp.bfloat16)

        product(i, 1 - core, store)
        c_copy(i).start()

    def combine(i):
        c_copy(i).wait_recv()
        target = whole[i]

        def store(at, value):
            target[at, :] = (target[at, :].astype(jnp.float32) + value).astype(jnp.bfloat16)

        product(i, core, store)
        layer, member = items[i][:2]
        if i == used_last[layer, member] and (layer, member) in after:
            load(*after[layer, member])

    used_last, after, seen_layers = {}, {}, []
    for i, item in enumerate(items):
        used_last[item[:2]] = i
        if item[0] not in seen_layers:
            seen_layers.append(item[0])
    for early, late in zip(seen_layers, seen_layers[1:]):
        for member in range(members):
            after[early, member] = (late, member)

    def way(i):
        return items[i][4][::-1]

    def region(i, phase, place_on):
        order = way(i)
        index = [spot[axis] if axis in order[:phase] else slice(None) for axis in range(3)]
        index[order[phase]] = place_on
        return blocks(whole[i], i).at[tuple(index)]

    def start(i, phase):
        axis = way(i)[phase]
        for steps in range(1, sizes[axis]):
            target = moved(spot, axis, sizes[axis], steps)
            send(
                remote(
                    region(i, phase, target[axis]), parts[phase][i].at[steps - 1],
                    sends[phase].at[i, steps - 1], recvs[phase].at[i, steps - 1], device_at(target, core),
                )
            )

    def owned(i, side):
        height = rows[items[i][1]]
        return partial[i].at[pl.ds(pl.multiple_of(side * height, 8), height)]

    def e_copy(i):
        layer, member = items[i][:2]
        return remote(
            owned(i, 1 - core), outs[member].at[layer, :, columns(i, core)], e_send.at[i], e_recv.at[i], partner
        )

    def o_copy(i):
        layer, member = items[i][:2]
        return pltpu.make_async_copy(owned(i, core), outs[member].at[layer, :, columns(i, core)], o_sem.at[i])

    def finish(i, phase):
        axis = way(i)[phase]
        for steps in range(1, sizes[axis]):
            land = parts[phase][i].at[steps - 1]
            remote(land, land, sends[phase].at[i, steps - 1], recvs[phase].at[i, steps - 1], partner).wait_recv()
        mine = region(i, phase, spot[axis])
        landed = parts[phase][i]

        def total(index):
            value = mine[index].astype(jnp.float32)
            for steps in range(1, sizes[axis]):
                value = value + landed[(steps - 1, *index)].astype(jnp.float32)
            return value

        if phase == 2:
            pieces_sum = total((Ellipsis,))
            partial[i][...] = pieces_sum
            count_squares(pieces_sum)
            e_copy(i).start()
            o_copy(i).start()
        else:
            left = [sizes[other] for other in range(3) if other not in way(i)[: phase + 1]]

            @pl.loop(0, left[0])
            def _(index):
                mine[index] = total((index,)).astype(jnp.bfloat16)

    for member in range(members):
        load(items[0][0], member)
    for i, step in schedule(items, SCATTER_LAGS):
        if step == 0:
            give(i)
            continue
        if step in (1, 4) and side:
            side.pop(0)()
        if step == 1:
            combine(i)
        else:
            finish(i, step - 2)
        if step < 4:
            start(i, step - 1)
    for step in side:
        step()
    lane = lax.broadcasted_iota(jnp.int32, squares.shape, 0)
    ends[0] = jnp.where(lane == 0, squares[...], loss_in[...])
    for step in sum_steps(hops, ends, end_landed, end_send, end_recv, sent_all):
        step()
    final[...] = ends[len(ROUNDS)]
    for i in range(n):
        e_copy(i).wait()
        o_copy(i).wait()
    for member in range(members):
        for i in used[member][-RINGS[member] :]:
            c_copy(i).wait_send()
    for copy in sent_all:
        copy.wait_send()


def scatter_grads(kept, text, rest, own, rows, halves, ways, number, items):
    layers, members = len(kept), len(rows)
    sizes = (ways[0] // 2, 2, ways[1] // 2)
    n = len(items)
    sem = pltpu.SemaphoreType.DMA
    low = jnp.bfloat16
    chips = sizes[0] * sizes[1] * sizes[2]
    frames, tokens = kept[0]["n1"].shape[0], text.shape[0]
    most = [max(s for _, m, _, s, _ in items if m == member) for member in range(members)]
    vmem = pltpu.VMEM

    def part(item, phase):
        _, member, _, size, order = item
        order = order[::-1]
        left = tuple(sizes[axis] for axis in range(3) if axis not in order[: phase + 1])
        return vmem((sizes[order[phase]] - 1, *left, 2 * rows[member], size), low)

    full, devices = jnp.float32, 2 * chips
    tile = tuple(rest[1].shape[1:])
    sums = sem((len(ROUNDS), max(sizes)))
    scratch = [
        vmem((devices,) + MOD_TILE, full),
        vmem((devices,) + tile, full),
        vmem((len(ROUNDS) + 1, devices, D), full),
        vmem((sizes[0] + sizes[1] + sizes[2] - 2, devices, D), full),
        vmem((8, 128), full),
    ]
    scratch += split_shapes(sizes, tile) + [sums] * 8
    scratch += [vmem((len(ROUNDS) + 1, 8, 128), full), vmem((sizes[0] + sizes[1] + sizes[2] - 2, 8, 128), full)]
    scratch += [vmem((devices, SHARE), full), vmem((devices, 8, 128), full), sem((2,))]
    scratch += [
        vmem((3, frames, D), low),
        vmem((8, frames, D), low),
        vmem(text.shape, low),
        vmem((2, tokens, D), low),
        vmem((frames, FF), low),
        vmem((2, frames, D), low),
        vmem((2, 3, frames, D // 2), low),
    ]
    scratch += [vmem((RINGS[m], chips * 2 * rows[m], most[m]), low) for m in range(members)]
    scratch += [vmem((chips * 2 * rows[m], s), low) for _, m, _, s, _ in items]
    scratch += [part(item, phase) for phase in range(3) for item in items]
    scratch += [vmem((2 * rows[m], s), jnp.float32) for _, m, _, s, _ in items]
    scratch += [sem((layers, members, 11))] + [sem((n,))] * 2 + [sem((n, max(sizes)))] * 6 + [sem((n,))] * 3
    flat = [text] + [k[name] for k in kept for name in ACTS]
    here, there = pl.BlockSpec(memory_space=vmem), pl.BlockSpec(memory_space=pl.ANY)
    return pl.pallas_call(
        functools.partial(scatter_kernel, ways, rows, halves, items, layers, own),
        out_shape=[
            jax.ShapeDtypeStruct((layers, rows[m], 2 * halves[m]), full) for m in range(members)
        ]
        + [
            jax.ShapeDtypeStruct((SHARE, MOD_ROWS * 128), full),
            jax.ShapeDtypeStruct((FREQS, SHARE), full),
            jax.ShapeDtypeStruct((SHARE, D), full),
            jax.ShapeDtypeStruct(tile, full),
            jax.ShapeDtypeStruct((8, 128), full),
        ],
        in_specs=[there] * len(flat) + [here, there, here, there] + [here] * (len(rest) - 4),
        out_specs=[there] * members + [here] * 5,
        scratch_shapes=scratch,
        compiler_params=pltpu.CompilerParams(
            collective_id=number, has_side_effects=True, vmem_limit_bytes=VMEM_LIMIT
        ),
    )(*flat, *rest)


def to_low(values):
    return values.astype(jnp.bfloat16)


def norm_rows(values):
    centred = values - jnp.mean(values, -1, keepdims=True)
    return centred * lax.rsqrt(jnp.mean(centred * centred, -1, keepdims=True) + EPSILON)


def modulate(stream, shift, scale_part):
    return norm_rows(stream) * (1.0 + scale_part) + shift


def gained_norm(stream, gain):
    return norm_rows(stream) * gain


def dense(left, right):
    return jnp.dot(left, right, preferred_element_type=jnp.float32)


def dense_back(left, right):
    return lax.dot_general(left, right, (((1,), (1,)), ((), ())), preferred_element_type=jnp.float32)


def weight_grad(left, right):
    return lax.dot_general(left, right, (((0,), (0,)), ((), ())), preferred_element_type=jnp.float32)


def split_heads(values):
    return values.reshape(values.shape[0], HEADS, HEAD_DIM)


def attention(queries, keys, values, keep):
    scores = jnp.einsum(
        "qhd,khd->hqk", split_heads(queries), split_heads(keys), preferred_element_type=jnp.float32
    ) * HEAD_DIM ** (-0.5)
    scores = jnp.where(keep[None, None, :], scores, NEGATIVE)
    shifted = jnp.exp(scores - jnp.max(scores, -1, keepdims=True))
    probs = shifted / jnp.sum(shifted, -1, keepdims=True)
    mixed = jnp.einsum(
        "hqk,khd->qhd", to_low(probs), split_heads(values), preferred_element_type=jnp.float32
    )
    return (to_low(mixed.reshape(queries.shape)), probs)


def attention_back(queries, keys, values, probs, grad_mixed):
    grad_heads = split_heads(to_low(grad_mixed))
    grad_values = jnp.einsum(
        "hqk,qhd->khd", to_low(probs), grad_heads, preferred_element_type=jnp.float32
    )
    grad_probs = jnp.einsum(
        "qhd,khd->hqk", grad_heads, split_heads(values), preferred_element_type=jnp.float32
    )
    grad_scores = to_low(probs * (grad_probs - jnp.sum(probs * grad_probs, -1, keepdims=True)))
    grad_queries = jnp.einsum(
        "hqk,khd->qhd", grad_scores, split_heads(keys), preferred_element_type=jnp.float32
    ) * HEAD_DIM ** (-0.5)
    grad_keys = jnp.einsum(
        "hqk,qhd->khd", grad_scores, split_heads(queries), preferred_element_type=jnp.float32
    ) * HEAD_DIM ** (-0.5)
    return (
        grad_queries.reshape(queries.shape),
        grad_keys.reshape(keys.shape),
        grad_values.reshape(values.shape),
    )


def noise_level(steps):
    phase = (steps.astype(jnp.float32) / 1000.0 + 0.008) / 1.008 * (math.pi / 2)
    return jnp.cos(phase) ** 2


def time_features(steps):
    half_width = FREQS // 2
    frequency = jnp.exp(-math.log(10000.0) * jnp.arange(half_width, dtype=jnp.float32) / half_width)
    angles = steps.astype(jnp.float32)[:, None] * frequency[None, :]
    return jnp.concatenate([jnp.cos(angles), jnp.sin(angles)], -1)


def layer_forward(stream, modulation, text_low, frame_keep, text_keep, weights):
    w_joint, w_textkv, w_back, gain = weights
    normed_one, pull_one = jax.vjp(modulate, stream, modulation[:D], modulation[D : 2 * D])
    input_one = to_low(normed_one)
    self_proj = to_low(dense(input_one, w_joint[:, : 3 * D]))
    mixed_one, probs_one = attention(
        self_proj[:, :D], self_proj[:, D : 2 * D], self_proj[:, 2 * D :], frame_keep
    )
    branch_one = dense(mixed_one, w_back[:D])
    stream_two = stream + modulation[2 * D : 3 * D] * branch_one
    normed_two, pull_two = jax.vjp(gained_norm, stream_two, gain)
    input_two = to_low(normed_two)
    cross_query = to_low(dense(input_two, w_joint[:, 3 * D : 4 * D]))
    cross_kv = to_low(dense(text_low, w_textkv))
    mixed_two, probs_two = attention(cross_query, cross_kv[:, :D], cross_kv[:, D:], text_keep)
    stream_three = stream_two + dense(mixed_two, w_back[D : 2 * D])
    normed_three, pull_three = jax.vjp(
        modulate, stream_three, modulation[3 * D : 4 * D], modulation[4 * D : 5 * D]
    )
    input_three = to_low(normed_three)
    hidden_act, pull_act = jax.vjp(jax.nn.gelu, dense(input_three, w_joint[:, 4 * D :]))
    hidden_low = to_low(hidden_act)
    branch_three = dense(hidden_low, w_back[2 * D :])
    result = stream_three + modulation[5 * D :] * branch_three
    saved = (
        pull_one,
        input_one,
        self_proj,
        mixed_one,
        probs_one,
        branch_one,
        pull_two,
        input_two,
        cross_query,
        cross_kv,
        mixed_two,
        probs_two,
        pull_three,
        input_three,
        pull_act,
        hidden_low,
        branch_three,
    )
    return (result, saved)


def layer_backward(saved, grad_out, modulation, text_low, weights):
    w_joint, w_textkv, w_back, gain = weights
    (
        pull_one,
        input_one,
        self_proj,
        mixed_one,
        probs_one,
        branch_one,
        pull_two,
        input_two,
        cross_query,
        cross_kv,
        mixed_two,
        probs_two,
        pull_three,
        input_three,
        pull_act,
        hidden_low,
        branch_three,
    ) = saved
    grad_three = to_low(grad_out * modulation[5 * D :])
    grad_gate_two = jnp.sum(grad_out * branch_three, 0)
    grad_down = weight_grad(hidden_low, grad_three)
    (grad_pre,) = pull_act(dense_back(grad_three, w_back[2 * D :]))
    grad_pre = to_low(grad_pre)
    grad_up = weight_grad(input_three, grad_pre)
    grad_inner, grad_shift_two, grad_scale_two = pull_three(dense_back(grad_pre, w_joint[:, 4 * D :]))
    grad_stream = grad_out + grad_inner
    grad_cross_out = to_low(grad_stream)
    grad_co = weight_grad(mixed_two, grad_cross_out)
    grad_cq, grad_ck, grad_cv = attention_back(
        cross_query,
        cross_kv[:, :D],
        cross_kv[:, D:],
        probs_two,
        dense_back(grad_cross_out, w_back[D : 2 * D]),
    )
    grad_cq = to_low(grad_cq)
    grad_text_w = weight_grad(text_low, to_low(jnp.concatenate([grad_ck, grad_cv], -1)))
    grad_query_w = weight_grad(input_two, grad_cq)
    grad_inner, grad_gain = pull_two(dense_back(grad_cq, w_joint[:, 3 * D : 4 * D]))
    grad_stream = grad_stream + grad_inner
    grad_one = to_low(grad_stream * modulation[2 * D : 3 * D])
    grad_gate_one = jnp.sum(grad_stream * branch_one, 0)
    grad_ao = weight_grad(mixed_one, grad_one)
    grad_q, grad_k, grad_v = attention_back(
        self_proj[:, :D],
        self_proj[:, D : 2 * D],
        self_proj[:, 2 * D :],
        probs_one,
        dense_back(grad_one, w_back[:D]),
    )
    grad_self = to_low(jnp.concatenate([grad_q, grad_k, grad_v], -1))
    grad_self_w = weight_grad(input_one, grad_self)
    grad_inner, grad_shift_one, grad_scale_one = pull_one(dense_back(grad_self, w_joint[:, : 3 * D]))
    grad_stream = grad_stream + grad_inner
    grad_mod = jnp.concatenate(
        [grad_shift_one, grad_scale_one, grad_gate_one, grad_shift_two, grad_scale_two, grad_gate_two]
    )
    grads = (
        jnp.concatenate([grad_self_w, grad_query_w, grad_up], 1),
        grad_text_w,
        jnp.concatenate([grad_ao, grad_co, grad_down], 0),
    )
    return (grad_stream, grad_mod, grads, grad_gain)


ROOT = math.sqrt(2.0 / math.pi)
CUBE = 0.044715
CHUNK = 160
WIDE = 512


def dot_nn(left, right):
    return lax.dot_general(left, right, (((1,), (0,)), ((), ())), preferred_element_type=jnp.float32)


def dot_nt(left, right):
    return lax.dot_general(left, right, (((1,), (1,)), ((), ())), preferred_element_type=jnp.float32)


def dot_tn(left, right):
    return lax.dot_general(left, right, (((0,), (0,)), ((), ())), preferred_element_type=jnp.float32)


def over_rows(count, step):
    @pl.loop(0, count // CHUNK)
    def _(index):
        step(pl.ds(pl.multiple_of(index * CHUNK, CHUNK), CHUNK))


def over_columns(count, width, step):
    for index in range(count // width):
        step(index * width)
        yield


def scaled(values):
    centred = values - jnp.mean(values, -1, keepdims=True)
    factor = lax.rsqrt(jnp.mean(centred * centred, -1, keepdims=True) + EPSILON)
    return centred * factor, factor


def norm_pull(normed, factor, grad):
    middle = jnp.mean(grad, -1, keepdims=True)
    along = jnp.mean(grad * normed, -1, keepdims=True)
    return factor * (grad - middle - normed * along)


def row_sum(values):
    return jnp.sum(values, 0, keepdims=True)


def attend(q_at, k_at, v_at, keep, stats, store):
    first = lax.broadcasted_iota(jnp.int32, (1, 2 * HEAD_DIM), 1) < HEAD_DIM

    for index in range(HEADS // 2):
        query, key = q_at(index) * HEAD_DIM ** (-0.5), k_at(index)
        zero = jnp.zeros_like(query)
        value = jnp.transpose(v_at(index))
        outs = []
        for head in range(2):
            mine = jnp.where(first, query, zero) if head == 0 else jnp.where(first, zero, query)
            scores = jnp.where(keep, dot_nt(key, mine), NEGATIVE)
            top = jnp.max(scores, 0, keepdims=True)
            shifted = jnp.exp(scores - top)
            total = jnp.sum(shifted, 0, keepdims=True)
            stats[2 * index + head : 2 * index + head + 1, :] = top + jnp.log(total)
            probs = to_low(shifted * (1.0 / total))
            outs.append(dot_nn(value[head * HEAD_DIM : (head + 1) * HEAD_DIM], probs))
        store(index, jnp.transpose(to_low(jnp.concatenate(outs, 0))))
        yield


def attend_back(q_at, k_at, v_at, grad_at, keep, stats, store):
    first = lax.broadcasted_iota(jnp.int32, (1, 2 * HEAD_DIM), 1) < HEAD_DIM

    for index in range(HEADS // 2):
        query, key = q_at(index) * HEAD_DIM ** (-0.5), k_at(index)
        value, grad = v_at(index), grad_at(index)
        key_turned = jnp.transpose(key * HEAD_DIM ** (-0.5))
        zero, zero_value = jnp.zeros_like(query), jnp.zeros_like(value)
        queries, keys, values = [], [], []
        for head in range(2):
            mine = jnp.where(first, query, zero) if head == 0 else jnp.where(first, zero, query)
            mine_value = jnp.where(first, value, zero_value) if head == 0 else jnp.where(first, zero_value, value)
            scores = jnp.where(keep, dot_nt(key, mine), NEGATIVE)
            probs = jnp.exp(scores - stats[2 * index + head : 2 * index + head + 1, :])
            values.append(dot_nn(to_low(probs), grad))
            grad_probs = dot_nt(mine_value, grad)
            inner = jnp.sum(probs * grad_probs, 0, keepdims=True)
            grad_scores = to_low(probs * (grad_probs - inner))
            keys.append(dot_nn(grad_scores, query))
            queries.append(dot_nn(key_turned[head * HEAD_DIM : (head + 1) * HEAD_DIM], grad_scores))
        store(
            index,
            jnp.transpose(to_low(jnp.concatenate(queries, 0))),
            to_low(jnp.where(first, *keys)),
            to_low(jnp.where(first, *values)),
        )
        yield


def tile_of(ref, base):
    return lambda index: ref[:, base + index * 2 * HEAD_DIM : base + (index + 1) * 2 * HEAD_DIM]


def run(steps):
    for _ in steps:
        pass


SAVED = (
    ("stream", D, jnp.float32),
    ("n1", D, jnp.bfloat16),
    ("qkv", 3 * D, jnp.bfloat16),
    ("mixed1", D, jnp.bfloat16),
    ("branch1", D, jnp.float32),
    ("stream2", D, jnp.float32),
    ("n2", D, jnp.bfloat16),
    ("cq", D, jnp.bfloat16),
    ("ckv", 2 * D, jnp.bfloat16),
    ("mixed2", D, jnp.bfloat16),
    ("stream3", D, jnp.float32),
    ("n3", D, jnp.bfloat16),
    ("branch3", D, jnp.float32),
    ("stats1", None, jnp.float32),
    ("stats2", None, jnp.float32),
)
GRADS = (
    ("g_self", 3 * D),
    ("g_cq", D),
    ("g_pre", FF),
    ("g_ckv", 2 * D),
    ("g_one", D),
    ("g_cross", D),
    ("g_three", D),
)
PARTS = ("qkv", "cq", "up", "text", "ao", "co", "down")
KEPT = ("n1", "n2", "n3", "mixed1", "mixed2", "hidden") + tuple(name for name, _ in GRADS)


NEEDED = ("stream", "qkv", "branch1", "stream2", "cq", "ckv", "stream3", "n3", "branch3", "stats1", "stats2")


class Names:
    def __init__(self, **refs):
        self.__dict__.update(refs)


def block_forward(s, hidden, result, mods, text, frame_keep, text_keep, w, need, done, emit):
    frames = s.stream.shape[0]

    def norm_one(rows):
        normed, _ = scaled(s.stream[rows, :])
        s.n1[rows, :] = to_low(normed * (1.0 + mods[1:2, :]) + mods[0:1, :])

    over_rows(frames, norm_one)
    yield
    emit("n1", s.n1)
    need("qkv")

    def project(column):
        cols = pl.ds(column, 256)
        s.qkv[:, cols] = to_low(dot_nn(s.n1[...], w.win[:, cols]))

    yield from over_columns(3 * D, 256, project)
    done("qkv")

    def mix_one(index, value):
        s.mixed1[:, index * 128 : (index + 1) * 128] = value

    yield from attend(tile_of(s.qkv, 0), tile_of(s.qkv, D), tile_of(s.qkv, 2 * D), frame_keep, s.stats1, mix_one)
    emit("mixed1", s.mixed1)
    need("ao")

    def branch_one(column):
        cols = pl.ds(column, 256)
        branch = dot_nn(s.mixed1[...], w.wout[0:D, cols])
        s.branch1[:, cols] = branch
        s.stream2[:, cols] = s.stream[:, cols] + mods[2:3, cols] * branch

    yield from over_columns(D, 256, branch_one)
    done("ao")

    def norm_two(rows):
        normed, _ = scaled(s.stream2[rows, :])
        s.n2[rows, :] = to_low(normed * mods[6:7, :])

    over_rows(frames, norm_two)
    yield
    emit("n2", s.n2)
    need("cq")

    def project_cross(column):
        cols = pl.ds(column, 256)
        s.cq[:, cols] = to_low(dot_nn(s.n2[...], w.win[:, pl.ds(3 * D + column, 256)]))

    yield from over_columns(D, 256, project_cross)
    done("cq")
    need("text")

    def project_text(column):
        cols = pl.ds(column, 256)
        s.ckv[:, cols] = to_low(dot_nn(text[...], w.wtext[:, cols]))

    yield from over_columns(2 * D, 256, project_text)
    done("text")

    def mix_two(index, value):
        s.mixed2[:, index * 128 : (index + 1) * 128] = value

    yield from attend(tile_of(s.cq, 0), tile_of(s.ckv, 0), tile_of(s.ckv, D), text_keep, s.stats2, mix_two)
    emit("mixed2", s.mixed2)
    need("co")

    def branch_two(column):
        cols = pl.ds(column, 256)
        s.stream3[:, cols] = s.stream2[:, cols] + dot_nn(s.mixed2[...], w.wout[D : 2 * D, cols])

    yield from over_columns(D, 256, branch_two)
    done("co")

    def norm_three(rows):
        normed, _ = scaled(s.stream3[rows, :])
        s.n3[rows, :] = to_low(normed * (1.0 + mods[4:5, :]) + mods[3:4, :])

    over_rows(frames, norm_three)
    yield
    emit("n3", s.n3)
    need("up")

    def expand(column):
        upper = dot_nn(s.n3[...], w.win[:, pl.ds(4 * D + column, WIDE)])
        tanh = jnp.tanh(ROOT * (upper + CUBE * (upper * upper * upper)))
        hidden[:, pl.ds(column, WIDE)] = to_low(0.5 * upper * (1.0 + tanh))

    yield from over_columns(FF, WIDE, expand)
    done("up")
    emit("hidden", hidden)
    need("down")

    def branch_three(column):
        cols = pl.ds(column, 256)
        branch = dot_nn(hidden[...], w.wout[2 * D :, cols])
        s.branch3[:, cols] = branch
        result[:, cols] = s.stream3[:, cols] + mods[5:6, cols] * branch

    yield from over_columns(D, 256, branch_three)
    done("down")


def block_backward(s, g, grad, mods, grad_mods, inner, mixed, frame_keep, text_keep, w, need, done, emit):
    frames = s.stream.shape[0]
    grad_mods[...] = jnp.zeros_like(grad_mods)

    def gate_three(rows):
        grad_out = grad[rows, :]
        g.g_three[rows, :] = to_low(grad_out * mods[5:6, :])
        grad_mods[5:6, :] += row_sum(grad_out * s.branch3[rows, :])

    over_rows(frames, gate_three)
    yield
    emit("g_three", g.g_three)
    need("down")
    need("up")

    def shrink(column):
        wide = pl.ds(column, WIDE)
        back = dot_nt(g.g_three[...], w.wout[pl.ds(2 * D + column, WIDE), :])
        upper = dot_nn(s.n3[...], w.win[:, pl.ds(4 * D + column, WIDE)])
        square = upper * upper
        tanh = jnp.tanh(ROOT * (upper + CUBE * (square * upper)))
        slope = 0.5 * (1.0 + tanh) + (0.5 * ROOT) * upper * (1.0 - tanh * tanh) * (1.0 + (3.0 * CUBE) * square)
        g.g_pre[:, wide] = to_low(back * slope)

    yield from over_columns(FF, WIDE, shrink)
    done("down")
    emit("g_pre", g.g_pre)

    def inner_three(column):
        inner[:, pl.ds(column, 256)] = dot_nt(g.g_pre[...], w.win[pl.ds(column, 256), 4 * D :])

    yield from over_columns(D, 256, inner_three)
    done("up")

    def pull_three(rows):
        normed, factor = scaled(s.stream3[rows, :])
        back = inner[rows, :]
        grad_mods[3:4, :] += row_sum(back)
        grad_mods[4:5, :] += row_sum(back * normed)
        total = grad[rows, :] + norm_pull(normed, factor, back * (1.0 + mods[4:5, :]))
        grad[rows, :] = total
        g.g_cross[rows, :] = to_low(total)

    over_rows(frames, pull_three)
    yield
    emit("g_cross", g.g_cross)
    need("co")

    def back_cross(column):
        mixed[:, pl.ds(column, 256)] = to_low(dot_nt(g.g_cross[...], w.wout[pl.ds(D + column, 256), :]))

    yield from over_columns(D, 256, back_cross)
    done("co")

    def store_cross(index, grad_query, grad_key, grad_value):
        cols = slice(index * 128, (index + 1) * 128)
        g.g_cq[:, cols] = grad_query
        g.g_ckv[:, cols] = grad_key
        g.g_ckv[:, D + index * 128 : D + (index + 1) * 128] = grad_value

    yield from attend_back(
        tile_of(s.cq, 0), tile_of(s.ckv, 0), tile_of(s.ckv, D), tile_of(mixed, 0), text_keep, s.stats2, store_cross
    )
    emit("g_cq", g.g_cq)
    emit("g_ckv", g.g_ckv)
    need("cq")

    def inner_two(column):
        inner[:, pl.ds(column, 256)] = dot_nt(g.g_cq[...], w.win[pl.ds(column, 256), 3 * D : 4 * D])

    yield from over_columns(D, 256, inner_two)
    done("cq")

    def pull_two(rows):
        normed, factor = scaled(s.stream2[rows, :])
        back = inner[rows, :]
        grad_mods[6:7, :] += row_sum(back * normed)
        total = grad[rows, :] + norm_pull(normed, factor, back * mods[6:7, :])
        grad[rows, :] = total
        g.g_one[rows, :] = to_low(total * mods[2:3, :])
        grad_mods[2:3, :] += row_sum(total * s.branch1[rows, :])

    over_rows(frames, pull_two)
    yield
    emit("g_one", g.g_one)
    need("ao")

    def back_self(column):
        mixed[:, pl.ds(column, 256)] = to_low(dot_nt(g.g_one[...], w.wout[pl.ds(column, 256), :]))

    yield from over_columns(D, 256, back_self)
    done("ao")

    def store_self(index, grad_query, grad_key, grad_value):
        cols = slice(index * 128, (index + 1) * 128)
        g.g_self[:, cols] = grad_query
        g.g_self[:, D + index * 128 : D + (index + 1) * 128] = grad_key
        g.g_self[:, 2 * D + index * 128 : 2 * D + (index + 1) * 128] = grad_value

    yield from attend_back(
        tile_of(s.qkv, 0), tile_of(s.qkv, D), tile_of(s.qkv, 2 * D), tile_of(mixed, 0), frame_keep, s.stats1, store_self
    )
    emit("g_self", g.g_self)
    need("qkv")

    def inner_one(column):
        inner[:, pl.ds(column, 256)] = dot_nt(g.g_self[...], w.win[pl.ds(column, 256), : 3 * D])

    yield from over_columns(D, 256, inner_one)
    done("qkv")

    def pull_one(rows):
        normed, factor = scaled(s.stream[rows, :])
        back = inner[rows, :]
        grad_mods[0:1, :] += row_sum(back)
        grad_mods[1:2, :] += row_sum(back * normed)
        grad[rows, :] = grad[rows, :] + norm_pull(normed, factor, back * (1.0 + mods[1:2, :]))

    over_rows(frames, pull_one)
    yield


def heights(frames, tokens):
    return {name: tokens if name in ("ckv", "g_ckv") else 16 if name in ("stats1", "stats2") else frames for name in WIDTHS}


WIDTHS = {**{name: width for name, width, _ in SAVED}, **dict(GRADS), "hidden": FF}
KINDS = {**{name: kind for name, _, kind in SAVED}, **{name: jnp.bfloat16 for name, _ in GRADS}, "hidden": jnp.bfloat16}


def shape_of(name, frames, tokens):
    return (heights(frames, tokens)[name], WIDTHS[name] or frames)


def weight_parts(source, target):
    (w_in, w_text, w_out), (win, wtext, wout) = source, target
    return {
        "qkv": (w_in.at[:, : 3 * D], win.at[:, : 3 * D]),
        "cq": (w_in.at[:, 3 * D : 4 * D], win.at[:, 3 * D : 4 * D]),
        "up": (w_in.at[:, 4 * D :], win.at[:, 4 * D :]),
        "text": (w_text, wtext),
        "ao": (w_out.at[:D], wout.at[:D]),
        "co": (w_out.at[D : 2 * D], wout.at[D : 2 * D]),
        "down": (w_out.at[2 * D :], wout.at[2 * D :]),
    }


def keeps(lengths, frames, tokens):
    return (
        lax.broadcasted_iota(jnp.int32, (frames, 1), 0) < lengths[0],
        lax.broadcasted_iota(jnp.int32, (tokens, 1), 0) < lengths[1],
    )


def lanes(first, count):
    lane = lax.broadcasted_iota(jnp.int32, (1, 128), 1)
    return jnp.logical_and(lane >= first, lane < first + count)


def gain_pick():
    row, lane = (lax.broadcasted_iota(jnp.int32, (8, 128), axis) for axis in range(2))
    return jnp.logical_and(row < LAYERS, lane == GAIN_LANE + row)


LEAD_LANE = 32
GAIN_LANE = 64


def model_kernel(channels, *refs):
    refs = list(refs)

    def take(count):
        taken = refs[:count]
        del refs[:count]
        return taken

    lengths, facts, stream_ref, mods_ref, final_mods, text, noise, noisy, small = take(9)
    weights = [take(3) for _ in range(LAYERS)]
    early = [dict(zip(NEEDED, take(len(NEEDED)))) for _ in range(LAYERS - 1)]
    end_ref, grad_small, grad_tile = take(3)
    kept_out = [dict(zip(KEPT if layer == LAYERS - 1 else GRAD_NAMES, take(len(KEPT) if layer == LAYERS - 1 else len(GRADS)))) for layer in range(LAYERS)]
    win, wtext, wout = take(3)
    saved = [Names(**dict(zip((name for name, *_ in SAVED), take(len(SAVED)))))]
    for _ in range(LAYERS - 1):
        saved.insert(0, Names(**dict(zip(NEEDED, take(len(NEEDED))))))
    g = Names(**dict(zip((name for name, _ in GRADS), take(len(GRADS)))))
    hidden, inner, mixed, final_low, grad_ref, grad_mods_ref, grad_final = take(7)
    load_sem, keep_sem, early_sem = refs
    w = Names(win=win, wtext=wtext, wout=wout)
    frames, tokens = noisy.shape[0], text.shape[0]
    frame_keep, text_keep = keeps(lengths, frames, tokens)
    last = LAYERS - 1

    def load(layer, part):
        return pltpu.make_async_copy(
            *weight_parts(weights[layer], (win, wtext, wout))[part], load_sem.at[PARTS.index(part)]
        )

    def early_copies(layer):
        return [
            pltpu.make_async_copy(early[layer][name], getattr(saved[layer], name), early_sem.at[layer, j])
            for j, name in enumerate(NEEDED)
        ]

    flying = {}

    def keep(layer):
        def emit(name, ref):
            copy = pltpu.make_async_copy(
                ref, kept_out[layer][name], keep_sem.at[layer, KEPT.index(name)]
            )
            copy.start()
            flying[name, layer] = copy

        return emit

    def settle(layer, names):
        for name in names:
            copy = flying.pop((name, layer), None)
            if copy is not None:
                copy.wait()

    def nothing(part):
        pass

    for part in ("qkv", "ao", "cq", "text", "co", "up", "down"):
        load(last, part).start()
    for layer in range(last):
        for copy in early_copies(layer):
            copy.start()
    over_rows(frames, lambda rows: saved[last].stream.__setitem__((rows, slice(None)), stream_ref[rows, :]))
    run(
        block_forward(
            saved[last], hidden, grad_ref, mods_ref.at[last], text, frame_keep, text_keep, w,
            lambda part: load(last, part).wait(), nothing, keep(last),
        )
    )

    def norm_final(rows):
        normed, _ = scaled(grad_ref[rows, :])
        final_low[rows, :] = to_low(normed * (1.0 + final_mods[1:2, :]) + final_mods[0:1, :])

    over_rows(frames, norm_final)
    counted = lax.broadcasted_iota(jnp.int32, (frames, 1), 0) < lengths[0]
    error = dot_nn(final_low[...], small[...]) - noise[...]
    error = jnp.where(jnp.logical_and(counted, lanes(0, channels)), error, 0.0)
    row, lane = (lax.broadcasted_iota(jnp.int32, end_ref.shape, axis) for axis in range(2))
    own = jnp.where(jnp.logical_and(row == 2, lane == 0), jnp.full(end_ref.shape, lengths[0].astype(jnp.float32)), 0.0)
    end_ref[...] = jnp.where(row == 1, jnp.broadcast_to(row_sum(error * error), end_ref.shape), own)
    factor = 2.0 / jnp.sum(facts[:, 2, :], (0, 1), keepdims=True)
    grad_pred = to_low(error * factor)
    grad_small[...] = dot_tn(final_low[...], grad_pred)
    inner[...] = dot_nt(grad_pred, small[...])
    grad_final[...] = jnp.zeros_like(grad_final)

    def pull_final(rows):
        normed, factor = scaled(grad_ref[rows, :])
        back = inner[rows, :]
        grad_final[0:1, :] += row_sum(back)
        grad_final[1:2, :] += row_sum(back * normed)
        grad_ref[rows, :] = norm_pull(normed, factor, back * (1.0 + final_mods[1:2, :]))

    over_rows(frames, pull_final)
    for layer in reversed(range(LAYERS)):
        if layer < last:
            settle(layer + 1, [name for name, _ in GRADS])
            for copy in early_copies(layer):
                copy.wait()
        run(
            block_backward(
                saved[layer], g, grad_ref, mods_ref.at[layer], grad_mods_ref.at[layer], inner, mixed,
                frame_keep, text_keep, w,
                nothing if layer == last else (lambda part: load(layer, part).wait()),
                nothing if layer == 0 else (lambda part: load(layer - 1, part).start()),
                keep(layer),
            )
        )
    over_rows(frames, lambda rows: final_low.__setitem__((rows, slice(None)), to_low(grad_ref[rows, :])))
    gains = jnp.concatenate(
        [grad_mods_ref[layer, 6:7, :] for layer in range(LAYERS)] + [jnp.zeros((8 - LAYERS, D), jnp.float32)], 0
    )
    grad_small[...] += dot_tn(final_low[...], noisy[...]) + lax.dot_general(
        gains, gain_pick().astype(jnp.float32), (((0,), (0,)), ((), ())),
        precision=lax.Precision.HIGHEST, preferred_element_type=jnp.float32,
    )
    grad_tile[...] = jnp.zeros_like(grad_tile)
    pieces = [(grad_mods_ref.at[layer], j) for layer in range(LAYERS) for j in range(6)]
    pieces += [(grad_final, j) for j in range(2)]
    for p, (ref, j) in enumerate(pieces):
        for k in range(D // 128):
            part = ref[j : j + 1, k * 128 : (k + 1) * 128]
            at = p * (D // 128) + k
            grad_tile[at : at + 1, :] = to_low(part).astype(jnp.float32)
    for layer in range(LAYERS):
        settle(layer, KEPT)


GRAD_NAMES = tuple(name for name, _ in GRADS)


def run_model(lengths, facts, stream, mods, final_mods, text, noise, noisy, small, weights, early, channels):
    frames, tokens = noisy.shape[0], text.shape[0]
    low, full = jnp.bfloat16, jnp.float32
    shape = jax.ShapeDtypeStruct
    here, there = pl.BlockSpec(memory_space=pltpu.VMEM), pl.BlockSpec(memory_space=pl.ANY)
    scalar = pl.BlockSpec(memory_space=pltpu.SMEM)

    def names(layer):
        return KEPT if layer == LAYERS - 1 else GRAD_NAMES

    def vmem(name):
        return pltpu.VMEM(shape_of(name, frames, tokens), KINDS[name])

    kept = [shape(shape_of(name, frames, tokens), low) for layer in range(LAYERS) for name in names(layer)]
    early_flat = [layer[name] for layer in early for name in NEEDED]
    out = pl.pallas_call(
        functools.partial(model_kernel, channels),
        out_shape=[shape((8, 128), full), shape((D, 128), full), shape(MOD_TILE, full)] + kept,
        in_specs=[scalar] + [here] * 8 + [there] * (3 * LAYERS + len(early_flat)),
        out_specs=[here] * 3 + [there] * len(kept),
        scratch_shapes=[pltpu.VMEM((D, JOINT), low), pltpu.VMEM((text.shape[1], 2 * D), low), pltpu.VMEM((2 * D + FF, D), low)]
        + [vmem(name) for name, *_ in SAVED]
        + [vmem(name) for name in NEEDED] * (LAYERS - 1)
        + [vmem(name) for name, _ in GRADS]
        + [
            pltpu.VMEM((frames, FF), low),
            pltpu.VMEM((frames, D), full),
            pltpu.VMEM((frames, D), low),
            pltpu.VMEM((frames, D), low),
            pltpu.VMEM((frames, D), full),
            pltpu.VMEM((LAYERS, 8, D), full),
            pltpu.VMEM((8, D), full),
            pltpu.SemaphoreType.DMA((len(PARTS),)),
            pltpu.SemaphoreType.DMA((LAYERS, len(KEPT))),
            pltpu.SemaphoreType.DMA((LAYERS, len(NEEDED))),
        ],
        compiler_params=pltpu.CompilerParams(vmem_limit_bytes=VMEM_LIMIT),
    )(
        lengths, facts, stream, mods, final_mods, text, noise, noisy, small,
        *[w for layer in weights for w in layer], *early_flat,
    )
    rest = list(out[3:])
    made = []
    for layer in range(LAYERS):
        count = len(names(layer))
        made.append(dict(zip(names(layer), rest[:count])))
        rest = rest[count:]
    return out[:3], made


def adam_update(weight, grad, first, second, rate):
    first_new = BETA_ONE * first + (1.0 - BETA_ONE) * grad
    second_new = BETA_TWO * second + (1.0 - BETA_TWO) * grad * grad
    first_hat = first_new / (1.0 - BETA_ONE**STEP)
    second_hat = second_new / (1.0 - BETA_TWO**STEP)
    weight_new = weight - rate * (
        first_hat / (jnp.sqrt(second_hat) + ADAM_EPSILON) + WEIGHT_DECAY * weight
    )
    return (first_new, second_new, weight_new)


def adam_kernel(layers, *refs):
    refs = list(refs)

    def take(count):
        taken = refs[:count]
        del refs[:count]
        return taken

    final, grad_mod, time_two, small = take(4)
    sums = take(3)
    given = [take(3) for _ in range(4)]
    results = [take(3) for _ in range(4)]
    held = [take(3) for _ in range(4)]
    grads = take(3)
    load_sem, grad_sem, store_sem = refs
    own = held[3][0].shape[0]
    groups = [(member, layer) for layer in range(layers) for member in (0, 2)] + [(1, None), (3, None)]

    def at(ref, layer):
        return ref if layer is None else ref.at[layer]

    def loads(number):
        member, layer = groups[number]
        copies = [
            pltpu.make_async_copy(at(given[member][j], layer), at(held[member][j], layer), load_sem.at[number, j])
            for j in range(3)
        ]
        if member < 3:
            copies.append(
                pltpu.make_async_copy(at(sums[member], layer), at(grads[member], layer), grad_sem.at[number])
            )
        return copies

    def stores(number):
        member, layer = groups[number]
        return [
            pltpu.make_async_copy(
                at(held[member][(j + 1) % 3], layer), at(results[member][j], layer), store_sem.at[number, j]
            )
            for j in range(3)
        ]

    for number in range(len(groups)):
        for copy in loads(number):
            copy.start()
    factor = CLIP_NORM / jnp.maximum(jnp.sqrt(final[0:1, 0:1]), CLIP_NORM)

    def update(member, index, grad):
        weight, first, second = held[member]
        first_new, second_new, weight_new = adam_update(
            weight[index], grad * factor, first[index], second[index], LEARN_RATE
        )
        first[index], second[index], weight[index] = first_new, second_new, weight_new

    for number, (member, layer) in enumerate(groups):
        for copy in loads(number):
            copy.wait()
        if member == 0:
            for column in range(0, JOINT, 1536):
                cols = slice(column, column + 1536)
                update(0, (layer, slice(None), cols), grads[0][layer, :, cols])
            for column in range(0, MOD, 1536):
                start = layer * MOD + column
                update(
                    0, (layer, slice(None), slice(JOINT + column, JOINT + column + 1536)),
                    grad_mod[:own, start : start + 1536],
                )
        elif member == 2:
            for row in range(0, held[2][0].shape[1], 48):
                rows = slice(row, row + 48)
                update(2, (layer, rows), grads[2][layer, rows])
        elif member == 1:
            for other in range(layers):
                for column in range(0, 2 * D, D):
                    index = (other, slice(None), slice(column, column + D))
                    update(1, index, grads[1][index])
        else:
            update(3, (slice(None), slice(0, D)), time_two[:own, :])
            update(3, (slice(None), slice(D, 3 * D)), grad_mod[:own, layers * MOD : layers * MOD + 2 * D])
            tail = held[3][0].shape[1] - 3 * D
            update(3, (slice(None), slice(3 * D, 3 * D + tail)), small[:, :tail])
        for copy in stores(number):
            copy.start()
    for number in range(len(groups)):
        for copy in stores(number):
            copy.wait()


def run_adam(final, grad_mod, time_two, small, sums, given):
    here, there = pl.BlockSpec(memory_space=pltpu.VMEM), pl.BlockSpec(memory_space=pl.ANY)
    layers = given[0][0].shape[0]
    full = jnp.float32
    shapes = [group[0].shape for group in given]
    count = 2 * layers + 2
    sem = pltpu.SemaphoreType.DMA
    out = pl.pallas_call(
        functools.partial(adam_kernel, layers),
        out_shape=[jax.ShapeDtypeStruct(shape, full) for shape in shapes for _ in range(3)],
        in_specs=[here] * 4 + [there] * 15,
        out_specs=[there] * 12,
        scratch_shapes=[pltpu.VMEM(shape, full) for shape in shapes for _ in range(3)]
        + [pltpu.VMEM(item.shape, full) for item in sums]
        + [sem((count, 3)), sem((count,)), sem((count, 3))],
        compiler_params=pltpu.CompilerParams(vmem_limit_bytes=VMEM_LIMIT),
    )(final, grad_mod, time_two, small, *sums, *[item for group in given for item in group])
    return [out[3 * k : 3 * k + 3] for k in range(4)]


def tiles(values, lead=()):
    flat = values.reshape(lead + (-1,))
    short = -flat.shape[-1] % 1024
    flat = jnp.pad(flat, [(0, 0)] * len(lead) + [(0, short)])
    return flat.reshape(lead + (-1, 128))


def fast_grads(ways, clean_latent, noise, text_low, text_lengths, timesteps, valid_frames, w_in, w_text, w_out, gains, w_lead, w_head):
    count = ways[0] * ways[1]
    own, channels = w_head.shape[0], noise.shape[-1]
    rows = [w_in.shape[1], w_text.shape[1], w_out.shape[1]]
    halves = [JOINT // 2, D, D // 2]
    lead_low, head_low = to_low(w_lead), to_low(w_head)
    mod_low = jnp.concatenate(
        [to_low(w_in[layer, :, JOINT:]) for layer in range(LAYERS)] + [head_low[:, D : 3 * D]], 1
    )
    sinus = time_features(timesteps)
    facts = jnp.concatenate([to_low(sinus).astype(jnp.float32)[0], valid_frames.astype(jnp.float32)])
    wide = [(0, 0), (0, LEAD_LANE - channels)]
    small = jnp.concatenate(
        [
            jnp.pad(head_low[:, 3 * D :].astype(jnp.float32), wide),
            jnp.pad(lead_low[FREQS:].astype(jnp.float32).T, wide),
            jnp.pad(to_low(gains).astype(jnp.float32).T, [(0, 0), (0, 128 - GAIN_LANE - LAYERS)]),
        ],
        1,
    )
    lead_own = jnp.pad(lead_low[:FREQS], [(0, 0), (0, 128 - own)])
    head_own = jnp.pad(head_low[:, :D], [(0, SHARE - own), (0, 0)])
    mod_own = jnp.pad(mod_low, [(0, SHARE - own), (0, 0)])
    level = noise_level(timesteps)
    noisy = jnp.sqrt(level) * clean_latent + jnp.sqrt(1.0 - level) * noise
    noisy = jnp.pad(to_low(noisy), [(0, 0), (LEAD_LANE, 128 - LEAD_LANE - channels)])
    lengths = jnp.concatenate([valid_frames, text_lengths])
    items = plan(halves, range(LAYERS), GATHER_PATTERN)
    weights, given, early = gather_weights(
        [w_in, w_text, w_out], jnp.concatenate([tiles(facts), small], 0), lead_own, head_own, mod_own,
        lengths, text_low, noisy, own, halves, ways, 1, items,
    )
    packed, pre_time, temb, block_mods, final_mods, small, stream = given
    (ends, grad_small, grad_tile), kept = run_model(
        lengths, packed, stream, block_mods, final_mods, text_low,
        jnp.pad(noise, [(0, 0), (0, 128 - channels)]), noisy, small, weights, [early], channels,
    )
    kept[0] = {**early, **kept[0]}
    items = plan(halves, list(reversed(range(LAYERS))), SCATTER_PATTERN)
    rest = [grad_tile, grad_small.reshape(count, own, 128), ends, packed, pre_time, temb, head_own, mod_own]
    *sums, grad_mod_w, grad_time_one, grad_time_two, small_sum, final = scatter_grads(
        kept, text_low, rest, own, rows, halves, ways, 2, items
    )
    lead_grad = jnp.concatenate([grad_time_one[:, :own], small_sum[:, LEAD_LANE : LEAD_LANE + channels].T], 0)
    gain_grad = small_sum[:, GAIN_LANE : GAIN_LANE + LAYERS].T
    grads = (gain_grad, lead_grad), (final, grad_mod_w, grad_time_two, small_sum, sums)
    return jnp.sum(final[1]), final[2, 0], jnp.sqrt(final[0, 0]), grads


def plain_grads(ways, clean_latent, noise, text_low, text_lengths, timesteps, valid_frames, w_in, w_text, w_out, gains, w_lead, w_head):
    count = ways[0] * ways[1]
    own, channels = w_head.shape[0], noise.shape[-1]
    frame_keep = lax.iota(jnp.int32, clean_latent.shape[0]) < valid_frames[0]
    text_keep = lax.iota(jnp.int32, text_low.shape[0]) < text_lengths[0]

    def to_all(values):
        return lax.all_gather(values, ALL, axis=0, tiled=True)

    def by_columns(values):
        return values.transpose(1, 0, 2).reshape(values.shape[1], -1)

    lead_low, head_low = to_low(w_lead), to_low(w_head)
    frame_count = jnp.sum(to_all(valid_frames)).astype(jnp.float32)
    sinus_all = to_low(time_features(to_all(timesteps)))
    lead_in = by_columns(to_all(lead_low[None, FREQS:]))
    head_pred = to_all(head_low[:, 3 * D :])
    gains_all = by_columns(to_all(to_low(gains)[None])).astype(jnp.float32)
    act_time, pull_time = jax.vjp(jax.nn.silu, dense(sinus_all, lead_low[:FREQS]))
    act_low = to_low(act_time)
    temb = dense(act_low, head_low[:, :D]).reshape(count, count, own).transpose(1, 0, 2)
    temb = jnp.sum(lax.all_to_all(temb, ALL, 0, 0, tiled=True), 0)
    cond, pull_cond = jax.vjp(jax.nn.silu, temb)
    cond_low = to_low(cond)
    mod_low = jnp.concatenate(
        [to_low(w_in[layer, :, JOINT:]) for layer in range(LAYERS)] + [head_low[:, D : 3 * D]], 1
    )
    mods = jnp.sum(lax.all_to_all(dense(cond_low, mod_low)[:, None], ALL, 0, 0, tiled=True), 0)[0]
    weights = [
        [to_all(to_low(shard[layer])) for shard in (w_in[:, :, :JOINT], w_text, w_out)] for layer in range(LAYERS)
    ]
    level = noise_level(timesteps)
    noisy_low = to_low(jnp.sqrt(level) * clean_latent + jnp.sqrt(1.0 - level) * noise)
    stream = dense(noisy_low, lead_in)
    saved = []
    for layer in range(LAYERS):
        stream, kept = layer_forward(
            stream, mods[layer * MOD : (layer + 1) * MOD], text_low, frame_keep, text_keep,
            (*weights[layer], gains_all[layer]),
        )
        saved.append(kept)
    final_mod = mods[LAYERS * MOD :]
    normed_final, pull_final = jax.vjp(modulate, stream, final_mod[:D], final_mod[D:])
    final_low = to_low(normed_final)
    error = dense(final_low, head_pred) - noise
    loss_part = jnp.sum(jnp.where(frame_keep[:, None], error * error, 0.0))
    grad_pred = to_low(jnp.where(frame_keep[:, None], error * (2.0 / frame_count), 0.0))
    grad_pred_w = weight_grad(final_low, grad_pred)
    grad_stream, grad_shift_f, grad_scale_f = pull_final(dense_back(grad_pred, head_pred))
    grad_mods = [None] * LAYERS + [jnp.concatenate([grad_shift_f, grad_scale_f])]
    big, grad_gains = [None] * LAYERS, [None] * LAYERS
    for layer in reversed(range(LAYERS)):
        grad_stream, grad_mods[layer], big[layer], grad_gains[layer] = layer_backward(
            saved[layer], grad_stream, mods[layer * MOD : (layer + 1) * MOD], text_low,
            (*weights[layer], gains_all[layer]),
        )
    grad_in_w = weight_grad(noisy_low, to_low(grad_stream))
    sums = [
        jnp.stack(
            [lax.psum_scatter(big[layer][member], ALL, scatter_dimension=0, tiled=True) for layer in range(LAYERS)]
        )
        for member in range(3)
    ]
    mods_all = lax.all_gather(to_low(jnp.concatenate(grad_mods)), ALL, axis=0, tiled=False)
    grad_mod_w = weight_grad(cond_low, mods_all)
    (grad_temb,) = pull_cond(dense_back(mods_all, mod_low))
    grad_temb = by_columns(lax.all_gather(to_low(grad_temb), ALL, axis=0, tiled=False))
    grad_time_two = weight_grad(act_low, grad_temb)
    (grad_pre_time,) = pull_time(dense_back(grad_temb, head_low[:, :D]))
    grad_time_one = weight_grad(sinus_all, to_low(grad_pre_time))

    def to_owner(values):
        return lax.psum_scatter(values, ALL, scatter_dimension=0, tiled=True)

    mod_grads = grad_mod_w[:, : LAYERS * MOD].reshape(own, LAYERS, MOD).transpose(1, 0, 2)
    grad_list = [
        jnp.concatenate([sums[0], mod_grads], 2),
        sums[1],
        sums[2],
        to_owner(jnp.stack(grad_gains).T).T,
        jnp.concatenate([grad_time_one, to_owner(grad_in_w.T).T], 0),
        jnp.concatenate([grad_time_two, grad_mod_w[:, LAYERS * MOD :], to_owner(grad_pred_w)], 1),
    ]
    squares = sum((jnp.sum(item * item) for item in grad_list))
    loss_sum, squares = lax.psum((loss_part, squares), ALL)
    return loss_sum, frame_count, jnp.sqrt(squares), grad_list


def body(
    ways,
    clean_latent,
    noise,
    text_feats,
    text_lengths,
    timesteps,
    valid_frames,
    w_in,
    w_text,
    w_out,
    gains,
    w_lead,
    w_head,
    first_in,
    second_in,
    first_text,
    second_text,
    first_out,
    second_out,
    first_gains,
    second_gains,
    first_lead,
    second_lead,
    first_head,
    second_head,
):
    aligned = all(shard.shape[1] % 8 == 0 for shard in (w_in, w_text, w_out)) and all(way % 2 == 0 for way in ways)
    aligned = aligned and w_head.shape[0] <= SHARE and noise.shape[-1] <= LEAD_LANE
    grads_of = fast_grads if aligned else plain_grads
    loss_sum, frame_count, grad_norm, grads = grads_of(
        ways, clean_latent[0], noise[0], text_feats[0], text_lengths, timesteps, valid_frames,
        w_in, w_text, w_out, gains, w_lead, w_head,
    )
    factor = CLIP_NORM / jnp.maximum(grad_norm, CLIP_NORM)
    params = (w_in, w_text, w_out, gains, w_lead, w_head)
    firsts = (first_in, first_text, first_out, first_gains, first_lead, first_head)
    seconds = (second_in, second_text, second_out, second_gains, second_lead, second_head)
    rates = (LEARN_RATE, LEARN_RATE, LEARN_RATE, GAIN_RATE, LEARN_RATE, LEARN_RATE)
    results = [None] * 6
    if aligned:
        given = list(zip(params, firsts, seconds))
        wide = (0, 1, 2, 5)
        for k, made in zip(wide, run_adam(*grads[1], [given[k] for k in wide])):
            results[k] = made
        grads = dict(zip((3, 4), grads[0]))
    else:
        grads = dict(enumerate(grads))
    for k, grad in grads.items():
        results[k] = adam_update(params[k], grad * factor, firsts[k], seconds[k], rates[k])
    return (loss_sum, frame_count, grad_norm, *(item for made in results for item in made))


def solution(mesh):
    ways = (mesh.shape["dp"], mesh.shape["fsdp"])
    clips = [P(ALL, None, None)] * 3 + [P(ALL)] * 3
    weights = [P(None, ALL, None)] * 3 + [P(None, ALL)] * 2 + [P(ALL, None)]
    moments = [spec for spec in weights for _ in range(2)]
    results = [spec for spec in weights for _ in range(3)]
    return jax.shard_map(
        functools.partial(body, ways),
        mesh=mesh,
        in_specs=tuple(clips + weights + moments),
        out_specs=tuple([P()] * 3 + results),
        check_vma=False,
    )
```

```python
import functools
import math

import jax
import jax.numpy as jnp
from jax import lax
from jax.experimental import pallas as pl
from jax.experimental.pallas import tpu as pltpu
from jax.sharding import PartitionSpec as P

D = 768
HEADS = 12
HEAD_DIM = 64
FF = 3072
FREQS = 256
LAYERS = 2
STEP = 10
MOD = 6 * D
JOINT = 4 * D + FF

EPSILON = 1e-06
NEGATIVE = -1e30
BETA_ONE = 0.5
BETA_TWO = 0.5
LEARN_RATE = 0.02
GAIN_RATE = 0.3
WEIGHT_DECAY = 0.01
ADAM_EPSILON = 1e-08
CLIP_NORM = 1.0

ALL = ("dp", "fsdp")
MESH = pl.DeviceIdType.MESH
VMEM_LIMIT = 60 * 1024 * 1024


def place(ways):
    dp_ways, fsdp_ways = ways
    row, col = lax.axis_index("dp"), lax.axis_index("fsdp")
    sizes = (dp_ways // 2, 2, fsdp_ways // 2)
    spot = (row // 2, lax.rem(row, 2), col // 2)
    return sizes, spot, lax.rem(col, 2)


def device_at(spot, core):
    z, y, x = spot
    return (z * 2 + y, x * 2 + core)


def moved(spot, axis, size, steps):
    spot = list(spot)
    spot[axis] = lax.rem(spot[axis] + steps, size)
    return tuple(spot)


def remote(source, target, send, recv, device):
    return pltpu.make_async_remote_copy(
        src_ref=source, dst_ref=target, send_sem=send, recv_sem=recv, device_id=device, device_id_type=MESH
    )


def greet_all(ways, me):
    count = ways[0] * ways[1]
    barrier = pltpu.get_barrier_semaphore()
    for step in range(1, count):
        pl.semaphore_signal(
            barrier, inc=1, device_id=numbered(ways, lax.rem(me + step, count)), device_id_type=MESH
        )
    pl.semaphore_wait(barrier, count - 1)


def numbered(ways, index):
    return (index // ways[1], lax.rem(index, ways[1]))


ROUNDS = ("core", 2, 1, 0)


class Hops:
    def __init__(self, sizes, spot, core):
        self.sizes, self.spot, self.core = sizes, spot, core

    def count(self, axis):
        return 2 if axis == "core" else self.sizes[axis]

    def place(self, axis):
        return self.core if axis == "core" else self.spot[axis]

    def other(self, axis, steps):
        if axis == "core":
            return 1 - self.core, device_at(self.spot, 1 - self.core)
        spot = moved(self.spot, axis, self.sizes[axis], steps)
        return spot[axis], device_at(spot, self.core)


def sum_steps(hops, totals, landed, send_sem, recv_sem, sent):
    first = [sum(hops.count(axis) - 1 for axis in ROUNDS[:turn]) for turn in range(len(ROUNDS))]

    def copies(turn):
        axis = ROUNDS[turn]
        return [
            remote(
                totals.at[turn], landed.at[first[turn] + steps - 1],
                send_sem.at[turn, steps - 1], recv_sem.at[turn, steps - 1], hops.other(axis, steps)[1],
            )
            for steps in range(1, hops.count(axis))
        ]

    def begin(turn):
        for copy in copies(turn):
            copy.start()
            sent.append(copy)

    def go_on(turn):
        for copy in copies(turn):
            copy.wait_recv()
        total = totals[turn]
        for steps in range(1, hops.count(ROUNDS[turn])):
            total = total + landed[first[turn] + steps - 1]
        totals[turn + 1] = total
        if turn + 1 < len(ROUNDS):
            begin(turn + 1)

    return [lambda: begin(0)] + [functools.partial(go_on, turn) for turn in range(len(ROUNDS))]


def split_steps(hops, rows, landed, out, send_sem, recv_sem, sent):
    places = {"core": 3, 2: 2, 1: 1, 0: 0}

    def index(turn, place_on):
        at = [slice(None)] * 4
        for early in ROUNDS[:turn]:
            at[places[early]] = hops.place(early)
        at[places[ROUNDS[turn]]] = place_on
        return tuple(at)

    def copies(turn):
        axis = ROUNDS[turn]
        made = []
        for steps in range(1, hops.count(axis)):
            place_on, device = hops.other(axis, steps)
            made.append(
                remote(
                    rows.at[index(turn, place_on)], landed[turn].at[steps - 1],
                    send_sem.at[turn, steps - 1], recv_sem.at[turn, steps - 1], device,
                )
            )
        return made

    def begin(turn):
        for copy in copies(turn):
            copy.start()
            sent.append(copy)

    def go_on(turn):
        for copy in copies(turn):
            copy.wait_recv()
        axis = ROUNDS[turn]
        mine = rows.at[index(turn, hops.place(axis))]
        others = range(hops.count(axis) - 1)
        if turn == 3:
            out[...] = sum((landed[turn][k] for k in others), mine[...])
        else:

            @pl.loop(0, hops.sizes[0])
            def _(z):
                mine[z] = sum((landed[turn][k, z] for k in others), mine[z])

            begin(turn + 1)

    return [lambda: begin(0)] + [functools.partial(go_on, turn) for turn in range(len(ROUNDS))]


def split_shapes(sizes, tile):
    z, y, x = sizes
    return [
        pltpu.VMEM((1, z, y, x) + tile, jnp.float32),
        pltpu.VMEM((x - 1, z, y) + tile, jnp.float32),
        pltpu.VMEM((y - 1, z) + tile, jnp.float32),
        pltpu.VMEM((z - 1,) + tile, jnp.float32),
    ]


def spread_steps(hops, rows, send_sem, recv_sem, sent):
    turns = (0, 2, 1, "core")
    places = {"core": 3, 2: 2, 1: 1, 0: 0}

    def index(turn, place_on):
        at = [hops.spot[0], hops.spot[1], hops.spot[2], hops.core]
        for early in turns[:turn]:
            at[places[early]] = slice(None)
        at[places[turns[turn]]] = place_on
        return tuple(at)

    def copies(turn, origin):
        axis = turns[turn]
        made = []
        for steps in range(1, hops.count(axis)):
            device = hops.other(axis, steps)[1]
            place_on = hops.other(axis, hops.count(axis) - steps)[0] if origin else hops.place(axis)
            part = rows.at[index(turn, place_on)]
            made.append(remote(part, part, send_sem.at[turn, steps - 1], recv_sem.at[turn, steps - 1], device))
        return made

    def begin(turn):
        for copy in copies(turn, False):
            copy.start()
            sent.append(copy)

    def go_on(turn):
        for copy in copies(turn, True):
            copy.wait_recv()
        if turn + 1 < len(turns):
            begin(turn + 1)

    return [lambda: begin(0)] + [functools.partial(go_on, turn) for turn in range(len(turns))]


def sigmoid(values):
    return 1.0 / (1.0 + jnp.exp(-values))


def chosen(me, own, width):
    shape = (D, width)
    row, column = (lax.broadcasted_iota(jnp.int32, shape, axis) for axis in range(2))
    return jnp.logical_and(row == me * own + column, column < own).astype(jnp.float32)


SHARE = 32
MOD_ROWS = (LAYERS * MOD + 2 * D) // 128
MOD_TILE = (-(-MOD_ROWS // 8) * 8, 128)


def gather_kernel(ways, rows, halves, items, layers, own, *refs):
    members = len(rows)
    refs = list(refs)

    def take(count):
        taken = refs[:count]
        del refs[:count]
        return taken

    shards = take(members)
    w_head, facts_in, lead_turned, lengths, text, noisy = take(6)
    fulls = take(members * layers)
    facts, pre_time, temb_own, block_mods, final_mods, small, result, head_own, mod_own = take(9)
    early = dict(zip(EARLY, take(len(EARLY))))
    totals, landed, mod_parts = take(3)
    mod_landed = take(4)
    facts_send, facts_recv, sum_send, sum_recv, split_send, split_recv = take(6)
    mods, win, wtext, wout = take(4)
    saved = Names(**dict(zip((name for name, *_ in SAVED), take(len(SAVED)))))
    (hidden,) = take(1)
    load_sem, keep_sem, mod_stage, head_stage, side_sem = take(5)
    rest = refs
    stages = rest[:members]
    blocks = rest[members : 2 * members]
    pre_send, pre_recv, own_sem, put_sem, *sends, c_send, c_recv = rest[2 * members :]
    sends, recvs = sends[0::2], sends[1::2]
    sizes, spot, core = place(ways)
    z, y, x = spot
    partner = device_at(spot, 1 - core)
    count = ways[0] * ways[1]
    me = lax.axis_index("dp") * ways[1] + lax.axis_index("fsdp")
    greet_all(ways, me)

    def facts_copy(step):
        return remote(
            facts_in, facts.at[me], facts_send.at[step], facts_recv.at[step],
            numbered(ways, lax.rem(me + step, count)),
        )

    for step in range(1, count):
        facts_copy(step).start()
    facts[me] = facts_in[...]

    def full(layer, member):
        return fulls[layer * members + member]

    pre = []
    for layer in range(layers):
        for member in range(members):
            height, half = rows[member], halves[member]
            place_in = stages[member].at[layer, pl.ds(pl.multiple_of(core * height, 8), height)]
            mine = shards[member].at[layer, :, pl.ds(pl.multiple_of(core * half, 128), half)]
            other = shards[member].at[layer, :, pl.ds(pl.multiple_of((1 - core) * half, 128), half)]
            index = layer * members + member
            sent = remote(other, place_in, pre_send.at[index], pre_recv.at[index], partner)
            sent.start()
            kept = pltpu.make_async_copy(mine, place_in, own_sem.at[index])
            kept.start()
            pre.append((sent, kept))
    arrived = set()
    put_done = set()
    sent_all = []

    def columns(i, side):
        _, member, start, size, _ = items[i]
        return pl.ds(pl.multiple_of(side * halves[member] + start, 128), size)

    def put(layer, member):
        half = halves[member]
        return pltpu.make_async_copy(
            blocks[member].at[layer],
            full(layer, member).at[z, y, x, :, pl.ds(pl.multiple_of(core * half, 128), half)],
            put_sem.at[layer * members + member],
        )

    def ready(layer, member):
        if (layer, member) in arrived:
            return
        arrived.add((layer, member))
        index = layer * members + member
        height = rows[member]
        sent, kept = pre[index]
        kept.wait()
        theirs = stages[member].at[layer, pl.ds(pl.multiple_of((1 - core) * height, 8), height)]
        remote(theirs, theirs, pre_send.at[index], pre_recv.at[index], partner).wait_recv()
        blocks[member][layer] = stages[member][layer].astype(jnp.bfloat16)
        put(layer, member).start()

    def own_put(layer, member):
        if (layer, member) not in put_done:
            put_done.add((layer, member))
            put(layer, member).wait()

    def region(i, phase, origin, side):
        layer, member, start, size, order = items[i]
        index = [slice(None) if order.index(axis) < phase else spot[axis] for axis in range(3)]
        if phase < 3 and origin is not None:
            index[order[phase]] = origin
        return full(layer, member).at[(*index, slice(None), columns(i, side))]

    def send(copy):
        copy.start()
        sent_all.append(copy)

    def start(i, phase):
        layer, member, first, size, order = items[i]
        axis = order[phase]
        if phase == 0:
            ready(layer, member)
            source = blocks[member].at[layer, :, pl.ds(first, size)]
        else:
            own_put(layer, member)
            source = region(i, phase, None, core)
        for steps in range(1, sizes[axis]):
            send(
                remote(
                    source, region(i, phase, spot[axis], core),
                    sends[phase].at[i, steps - 1], recvs[phase].at[i, steps - 1],
                    device_at(moved(spot, axis, sizes[axis], steps), core),
                )
            )
        if phase == 2:
            send(remote(source, source, c_send.at[i, 0], c_recv.at[i, 0], partner))

    def finish(i, phase):
        axis = items[i][4][phase]
        for steps in range(1, sizes[axis]):
            land = region(i, phase, lax.rem(spot[axis] + sizes[axis] - steps, sizes[axis]), core)
            remote(land, land, sends[phase].at[i, steps - 1], recvs[phase].at[i, steps - 1], partner).wait_recv()
            if phase == 2:
                send(remote(land, land, c_send.at[i, steps], c_recv.at[i, steps], partner))

    def c_wait(i):
        axis = items[i][4][2]
        for steps in range(sizes[axis]):
            land = region(i, 2, lax.rem(spot[axis] + sizes[axis] - steps, sizes[axis]), 1 - core)
            remote(land, land, c_send.at[i, steps], c_recv.at[i, steps], partner).wait_recv()

    hops = Hops(sizes, spot, core)

    bring = [
        pltpu.make_async_copy(shards[0].at[layer, :, pl.ds(JOINT, MOD)], mod_stage.at[layer], side_sem.at[layer])
        for layer in range(layers)
    ]
    bring.append(pltpu.make_async_copy(w_head.at[:, pl.ds(0, 3 * D)], head_stage, side_sem.at[layers]))
    for copy in bring:
        copy.start()

    def low_rows(value):
        return to_low(jnp.concatenate([value, jnp.zeros((SHARE - own, value.shape[1]), jnp.float32)], 0))

    def time_layers():
        for copy in bring:
            copy.wait()
        head_own[...] = low_rows(head_stage[:, :D])
        for layer in range(layers):
            for column in range(0, MOD, D):
                start_at = layer * MOD + column
                mod_own[:, start_at : start_at + D] = low_rows(mod_stage[layer, :, column : column + D])
        for column in range(0, 2 * D, D):
            start_at = layers * MOD + column
            mod_own[:, start_at : start_at + D] = low_rows(head_stage[:, D + column : 2 * D + column])
        lead = lead_turned[:, :FREQS]
        lead = to_low(jnp.concatenate([lead, jnp.zeros((128 - own, FREQS), jnp.float32)], 0))
        for step in range(1, count):
            origin = lax.rem(me + count - step, count)
            remote(
                facts_in, facts.at[origin], facts_send.at[step], facts_recv.at[step], numbered(ways, origin)
            ).wait_recv()
        value = dot_nt(to_low(facts[:, 0, :]), lead[:, :128]) + dot_nt(to_low(facts[:, 1, :]), lead[:, 128:])
        pre_time[...] = value
        totals[0] = dot_nn(to_low(value * sigmoid(value))[:, :SHARE], head_own[...])
        sums[0]()

    def modulation():
        temb = lax.dot_general(
            totals[4], chosen(me, own, 128), (((1,), (0,)), ((), ())),
            precision=lax.Precision.HIGHEST, preferred_element_type=jnp.float32,
        )
        temb_own[...] = temb
        cond = to_low(temb * sigmoid(temb))[:, :SHARE]
        mod_parts[:, MOD_ROWS:, :] = jnp.zeros((count, MOD_TILE[0] - MOD_ROWS, 128), jnp.float32)
        for j in range(0, MOD_ROWS, 4):
            part = dot_nn(cond, mod_own[:, j * 128 : (j + 4) * 128])
            for k in range(4):
                mod_parts[:, j + k, :] = part[:, k * 128 : (k + 1) * 128]
        splits[0]()

    sums = sum_steps(hops, totals, landed, sum_send, sum_recv, sent_all)
    splits = split_steps(
        hops, mod_parts.reshape(sizes + (2,) + MOD_TILE), mod_landed, mods, split_send, split_recv, sent_all
    )
    side = [time_layers] + sums[1:] + [modulation] + splits[1:]

    def prepare():
        small[...] = to_low(facts[:, 8 : 8 + own, :].reshape(D, 128))
        gains = dot_nt(to_low(gain_pick().astype(jnp.float32)), small[...])

        def row(piece):
            tiles_of = [mods[piece * (D // 128) + k : piece * (D // 128) + k + 1, :] for k in range(D // 128)]
            return jnp.concatenate(tiles_of, 1)

        for layer in range(layers):
            for j in range(6):
                block_mods[layer, j : j + 1, :] = row(layer * 6 + j)
            block_mods[layer, 6:7, :] = gains[layer : layer + 1, :]
            block_mods[layer, 7:8, :] = jnp.zeros((1, D), jnp.float32)
        final_mods[...] = jnp.zeros_like(final_mods)
        for j in range(2):
            final_mods[j : j + 1, :] = row(layers * 6 + j)
        for column in range(0, D, 256):
            saved.stream[:, column : column + 256] = dot_nt(noisy[...], small[column : column + 256, :])

    def load(part):
        return pltpu.make_async_copy(
            *weight_parts(whole_weights, (win, wtext, wout))[part], load_sem.at[PARTS.index(part)]
        )

    def emit(name, ref):
        pltpu.make_async_copy(ref, early[name], keep_sem.at[EARLY.index(name)]).start()

    def first_block():
        frame_keep, text_keep = keeps(lengths, noisy.shape[0], text.shape[0])
        for part in ("qkv", "ao", "cq", "text", "co", "up", "down"):
            load(part).start()
        yield from block_forward(
            saved, hidden, result, block_mods.at[0], text, frame_keep, text_keep,
            Names(win=win, wtext=wtext, wout=wout), lambda part: load(part).wait(), lambda part: None, emit,
        )
        for name in NEEDED:
            if name not in KEPT:
                emit(name, getattr(saved, name))

    whole_weights = [
        full(0, member).reshape(sizes[0] * sizes[1] * sizes[2] * 2 * rows[member], 2 * halves[member]) for member in range(members)
    ]
    order = schedule(items, GATHER_LAGS)
    turn = max(k for k, (i, _) in enumerate(order) if items[i][0] == 0) + 1
    waited = set()

    def advance(i, phase):
        if phase > 0:
            finish(i, phase - 1)
        if phase < 3:
            start(i, phase)

    for i, phase in order[:turn]:
        if phase in (1, 2) and side:
            side.pop(0)()
        advance(i, phase)
    for step in side:
        step()
    side = []
    prepare()
    for i in range(len(items)):
        if items[i][0] == 0:
            c_wait(i)
            waited.add(i)
            own_put(*items[i][:2])
    later = list(order[turn:])
    pace = BLOCK_PARTS / max(len(later), 1)
    for part, _ in enumerate(first_block()):
        if later and part >= pace * (len(order) - turn - len(later)):
            advance(*later.pop(0))
    for i, phase in later:
        advance(i, phase)
    for i in range(len(items)):
        if i not in waited:
            c_wait(i)
    for name in EARLY:
        ref = hidden if name == "hidden" else getattr(saved, name)
        pltpu.make_async_copy(ref, early[name], keep_sem.at[EARLY.index(name)]).wait()
    for layer in range(layers):
        for member in range(members):
            own_put(layer, member)
    for step in range(1, count):
        facts_copy(step).wait_send()
    for sent, _ in pre:
        sent.wait_send()
    for copy in sent_all:
        copy.wait_send()


BLOCK_PARTS = 48
EARLY = ("n1", "n2", "n3", "mixed1", "mixed2", "hidden", "stream", "qkv", "branch1", "stream2", "cq", "ckv", "stream3", "branch3", "stats1", "stats2")


def gather_weights(shards, w_head, facts, lead_turned, lengths, text, noisy, own, halves, ways, number, items):
    layers = shards[0].shape[0]
    rows = [s.shape[1] for s in shards]
    members = len(shards)
    sizes = (ways[0] // 2, 2, ways[1] // 2)
    devices = ways[0] * ways[1]
    count = layers * members
    n = len(items)
    frames, tokens = noisy.shape[0], text.shape[0]
    sem, vmem, full, shape = pltpu.SemaphoreType.DMA, pltpu.VMEM, jnp.float32, jax.ShapeDtypeStruct
    here, there = pl.BlockSpec(memory_space=pltpu.VMEM), pl.BlockSpec(memory_space=pl.ANY)
    scalar = pl.BlockSpec(memory_space=pltpu.SMEM)
    out = pl.pallas_call(
        functools.partial(gather_kernel, ways, rows, halves, items, layers, own),
        out_shape=[
            shape(sizes + (2 * rows[m], 2 * halves[m]), jnp.bfloat16) for _ in range(layers) for m in range(members)
        ]
        + [
            shape((devices,) + facts.shape, full),
            shape((devices, 128), full),
            shape((devices, 128), full),
            shape((layers, 8, D), full),
            shape((8, D), full),
            shape((D, 128), jnp.bfloat16),
            shape((frames, D), full),
            shape((SHARE, D), jnp.bfloat16),
            shape((SHARE, MOD_ROWS * 128), jnp.bfloat16),
        ]
        + [shape(shape_of(name, frames, tokens), KINDS[name]) for name in EARLY],
        in_specs=[there] * (members + 1) + [here] * 2 + [scalar] + [here] * 2,
        out_specs=[there] * count + [here] * 9 + [there] * len(EARLY),
        scratch_shapes=[
            vmem((len(ROUNDS) + 1, devices, D), full),
            vmem((sizes[0] + sizes[1] + sizes[2] - 2, devices, D), full),
            vmem((devices,) + MOD_TILE, full),
        ]
        + split_shapes(sizes, MOD_TILE)
        + [sem((devices,))] * 2
        + [sem((len(ROUNDS), max(sizes)))] * 4
        + [vmem(MOD_TILE, full), vmem((D, JOINT), jnp.bfloat16)]
        + [vmem((text.shape[1], 2 * D), jnp.bfloat16), vmem((2 * D + FF, D), jnp.bfloat16)]
        + [vmem(shape_of(name, frames, tokens), kind) for name, _, kind in SAVED]
        + [vmem((frames, FF), jnp.bfloat16), sem((len(PARTS),)), sem((len(EARLY),))]
        + [vmem((layers, own, MOD), full), vmem((own, 3 * D), full), sem((layers + 1,))]
        + [vmem((layers, 2 * rows[m], halves[m]), full) for m in range(members)]
        + [vmem((layers, 2 * rows[m], halves[m]), jnp.bfloat16) for m in range(members)]
        + [sem((count,))] * 4
        + [sem((n, max(sizes)))] * 8,
        compiler_params=pltpu.CompilerParams(
            collective_id=number, has_side_effects=True, vmem_limit_bytes=VMEM_LIMIT
        ),
    )(*shards, w_head, facts, lead_turned, lengths, text, noisy)
    weights = [
        [out[l * members + m].reshape(-1, 2 * halves[m]) for m in range(members)] for l in range(layers)
    ]
    return weights, out[count : count + 9], dict(zip(EARLY, out[count + 9 :]))


ORDERS = ((0, 2, 1), (0, 1, 2), (2, 0, 1), (1, 0, 2))
GATHER_LAGS = ((-1.5, 0.0, 3.0, 7.5), (-3.0, 0.0, 2.0, 6.5))
SCATTER_LAGS = ((-2.0, 0.0, 3.0, 5.0, 7.0), (-2.0, 0.0, 3.0, 5.0, 7.0))
GATHER_PATTERN = (1, 0, 1, 2, 1, 1, 0, 1, 0, 1, 2, 1, 2, 1, 3, 1, 2, 1)
SCATTER_PATTERN = GATHER_PATTERN[::-1]


def schedule(items, lags):
    steps = []
    for i, item in enumerate(items):
        own = lags[0 if item[4][0] == 0 else 1]
        steps.extend((i + lag, -phase, i) for phase, lag in enumerate(own))
    return [(i, -phase) for _, phase, i in sorted(steps)]


def plan(halves, layers, pattern):
    items = []
    for layer in layers:
        for member, width in enumerate(halves):
            size = width // 4 if width % 512 == 0 else (width // 2 if width % 256 == 0 else 128)
            for start in range(0, width, size):
                items.append((layer, member, start, size, ORDERS[pattern[len(items) % len(pattern)]]))
    return items


RINGS = (2, 1, 1)
ACTS = ("n1", "n2", "n3", "mixed1", "mixed2", "hidden", "g_self", "g_cq", "g_pre", "g_ckv", "g_one", "g_cross", "g_three")


def scatter_kernel(ways, rows, halves, items, layers, own, *refs):
    members = len(rows)
    n = len(items)
    rest = list(refs)

    def take(count):
        taken = rest[:count]
        del rest[:count]
        return taken

    (text_in,) = take(1)
    acts = [dict(zip(ACTS, take(len(ACTS)))) for _ in range(layers)]
    mods_in, small_in, loss_in, facts_in, pre_time, temb_own, head_own, mod_own = take(8)
    outs = take(members)
    grad_mod, grad_time_one, grad_time_two, small_out, final = take(5)
    all_mods, small_rows, totals, landed, squares = take(5)
    small_landed = take(4)
    spread_send, spread_recv, sum_send, sum_recv, split_send, split_recv, end_send, end_recv = take(8)
    ends, end_landed, backs, facts, bring_sem = take(5)
    lefts, rights, text, right_text, hidden, mixes, right_out = take(7)
    ring = take(members)
    whole = take(n)
    parts = [take(n) for _ in range(3)]
    partial = take(n)
    load_sem, c_send, c_recv, *sems, e_send, e_recv, o_sem = rest
    sends, recvs = sems[0::2], sems[1::2]
    sizes, spot, core = place(ways)
    partner = device_at(spot, 1 - core)
    frames = hidden.shape[0]
    sent_all = []
    count = ways[0] * ways[1]
    me = lax.axis_index("dp") * ways[1] + lax.axis_index("fsdp")
    greet_all(ways, me)
    hops = Hops(sizes, spot, core)
    squares[...] = jnp.zeros_like(squares)

    def count_squares(value):
        squares[...] += jnp.broadcast_to(jnp.sum(value * value, (0, 1), keepdims=True), squares.shape)

    temb = temb_own[...]
    share = sigmoid(temb)
    cond = to_low(temb * share)[:, :SHARE]
    gate = sigmoid(pre_time[...])
    act = to_low(pre_time[...] * gate)[:, :SHARE]
    slope_temb = (share * (1.0 + temb * (1.0 - share)))[:, :SHARE]
    slope_time = (gate * (1.0 + pre_time[...] * (1.0 - gate)))[:, :SHARE]
    all_mods[me] = mods_in[...]
    sums = sum_steps(hops, totals, landed, sum_send, sum_recv, sent_all)
    spreads = spread_steps(
        hops, all_mods.reshape(sizes + (2,) + MOD_TILE), spread_send, spread_recv, sent_all
    )
    tile = tuple(small_in.shape[1:])
    splits = split_steps(
        hops, small_rows.reshape(sizes + (2,) + tile), small_landed, small_out, split_send, split_recv, sent_all
    )

    bring = [
        pltpu.make_async_copy(small_in, small_rows, bring_sem.at[0]),
        pltpu.make_async_copy(facts_in.at[:, 0:8], facts, bring_sem.at[1]),
    ]
    for copy in bring:
        copy.start()

    def begin_small():
        for copy in bring:
            copy.wait()
        splits[0]()

    def modulation_part(begin, end):
        back = jnp.zeros_like(backs) if begin == 0 else backs[...]
        for j in range(begin, end):
            cols = slice(j * 128, (j + 1) * 128)
            grad = to_low(all_mods[:, j, :])
            back = back + dot_nt(grad, mod_own[:, cols])
            grad_mod[:, cols] = dot_tn(cond, grad)
        backs[...] = back
        count_squares(grad_mod[:, begin * 128 : end * 128])

    def modulation_back():
        grad_temb = to_low(backs[...] * slope_temb)
        pick = to_low(chosen(me, own, SHARE))
        totals[0] = dot_nt(grad_temb, pick)
        sums[0]()

    def time_back():
        grad_temb = to_low(totals[4])
        grad_time_two[...] = dot_tn(act, grad_temb)
        grad_time = to_low(dot_nt(grad_temb, head_own[...]) * slope_time)
        for j in range(2):
            grad_time_one[:, j * 128 : (j + 1) * 128] = dot_tn(grad_time, to_low(facts[:, j, :]))
        count_squares(grad_time_two[...])
        count_squares(grad_time_one[...])
        count_squares(small_out[...])

    def together(*steps):
        return lambda: [step() for step in steps]

    def rest():
        pass

    side = [together(spreads[0], begin_small)]
    for pair in zip(spreads[1:], splits[1:]):
        side += [rest, together(*pair)]
    parts_of = [functools.partial(modulation_part, j, j + 12) for j in range(0, MOD_ROWS, 12)]
    side += [together(*parts_of[k : k + 2]) for k in range(0, len(parts_of), 2)]
    side += [modulation_back] + sums[1:] + [time_back]

    def send(copy):
        copy.start()
        sent_all.append(copy)

    def loads(layer, member):
        a = acts[layer]
        if member == 0:
            pairs = [(a["n1"], lefts.at[0]), (a["n2"], lefts.at[1]), (a["n3"], lefts.at[2])]
            pairs += [(a["g_self"].at[:, j * D : (j + 1) * D], rights.at[j]) for j in range(3)]
            pairs += [(a["g_cq"], rights.at[3])]
            pairs += [(a["g_pre"].at[:, j * D : (j + 1) * D], rights.at[4 + j]) for j in range(4)]
        elif member == 1:
            pairs = [(a["g_ckv"].at[:, j * D : (j + 1) * D], right_text.at[j]) for j in range(2)]
            if layer == items[0][0]:
                pairs.append((text_in, text))
        else:
            pairs = [(a["mixed1"], mixes.at[0]), (a["mixed2"], mixes.at[1]), (a["hidden"], hidden)]
            for j, name in enumerate(("g_one", "g_cross", "g_three")):
                pairs += [(a[name].at[:, side * (D // 2) : (side + 1) * (D // 2)], right_out.at[side, j]) for side in range(2)]
        return [
            pltpu.make_async_copy(source, target, load_sem.at[layer, member, j])
            for j, (source, target) in enumerate(pairs)
        ]

    def load(layer, member):
        for copy in loads(layer, member):
            copy.start()

    loaded = set()

    def need(layer, member):
        if (layer, member) not in loaded:
            loaded.add((layer, member))
            for copy in loads(layer, member):
                copy.wait()

    def product(i, side, store):
        layer, member, start, size, _ = items[i]
        need(layer, member)
        if member == 0:
            j = start // D
            at = pl.ds(start % D, size)
            left = jnp.where(side == 1, 2, 0 if j < 3 else 1)
            right = rights[side * 4 + j, :, at]
            for row in range(0, D, 384):
                store(pl.ds(row, 384), dot_tn(lefts[left, :, row : row + 384], right))
        elif member == 1:
            right = right_text[side, :, pl.ds(start, size)]
            for row in range(0, text.shape[1], 512):
                store(pl.ds(row, 512), dot_tn(text[:, row : row + 512], right))
        else:
            cols = pl.ds(start, size)
            for j in range(2):
                store(pl.ds(j * D, D), dot_tn(mixes[j], right_out[side, j, :, cols]))

            @pl.loop(0, 4)
            def _(j):
                at = pl.multiple_of(j * D, D)
                store(pl.ds(pl.multiple_of(2 * D + j * D, D), D), dot_tn(hidden[:, pl.ds(at, D)], right_out[side, 2, :, cols]))

    def columns(i, side):
        _, member, start, size, _ = items[i]
        return pl.ds(pl.multiple_of(side * halves[member] + start, 128), size)

    def blocks(ref, i):
        return ref.reshape(sizes + (2 * rows[items[i][1]], items[i][3]))

    ring_at, used = [], {}
    for i, (_, member, *_) in enumerate(items):
        ring_at.append(used.setdefault(member, []))
        ring_at[-1] = len(used[member])
        used[member].append(i)

    def c_copy(i):
        member, size = items[i][1], items[i][3]
        slot = ring_at[i] % RINGS[member]
        return remote(ring[member].at[slot, :, pl.ds(0, size)], whole[i], c_send.at[i], c_recv.at[i], partner)

    def give(i):
        member, size = items[i][1], items[i][3]
        slot = ring_at[i] % RINGS[member]
        if ring_at[i] >= RINGS[member]:
            c_copy(used[member][ring_at[i] - RINGS[member]]).wait_send()
        target = ring[member].at[slot]

        def store(at, value):
            target[at, pl.ds(0, size)] = value.astype(jnp.bfloat16)

        product(i, 1 - core, store)
        c_copy(i).start()

    def combine(i):
        c_copy(i).wait_recv()
        target = whole[i]

        def store(at, value):
            target[at, :] = (target[at, :].astype(jnp.float32) + value).astype(jnp.bfloat16)

        product(i, core, store)
        layer, member = items[i][:2]
        if i == used_last[layer, member] and (layer, member) in after:
            load(*after[layer, member])

    used_last, after, seen_layers = {}, {}, []
    for i, item in enumerate(items):
        used_last[item[:2]] = i
        if item[0] not in seen_layers:
            seen_layers.append(item[0])
    for early, late in zip(seen_layers, seen_layers[1:]):
        for member in range(members):
            after[early, member] = (late, member)

    def way(i):
        return items[i][4][::-1]

    def region(i, phase, place_on):
        order = way(i)
        index = [spot[axis] if axis in order[:phase] else slice(None) for axis in range(3)]
        index[order[phase]] = place_on
        return blocks(whole[i], i).at[tuple(index)]

    def start(i, phase):
        axis = way(i)[phase]
        for steps in range(1, sizes[axis]):
            target = moved(spot, axis, sizes[axis], steps)
            send(
                remote(
                    region(i, phase, target[axis]), parts[phase][i].at[steps - 1],
                    sends[phase].at[i, steps - 1], recvs[phase].at[i, steps - 1], device_at(target, core),
                )
            )

    def owned(i, side):
        height = rows[items[i][1]]
        return partial[i].at[pl.ds(pl.multiple_of(side * height, 8), height)]

    def e_copy(i):
        layer, member = items[i][:2]
        return remote(
            owned(i, 1 - core), outs[member].at[layer, :, columns(i, core)], e_send.at[i], e_recv.at[i], partner
        )

    def o_copy(i):
        layer, member = items[i][:2]
        return pltpu.make_async_copy(owned(i, core), outs[member].at[layer, :, columns(i, core)], o_sem.at[i])

    def finish(i, phase):
        axis = way(i)[phase]
        for steps in range(1, sizes[axis]):
            land = parts[phase][i].at[steps - 1]
            remote(land, land, sends[phase].at[i, steps - 1], recvs[phase].at[i, steps - 1], partner).wait_recv()
        mine = region(i, phase, spot[axis])
        landed = parts[phase][i]

        def total(index):
            value = mine[index].astype(jnp.float32)
            for steps in range(1, sizes[axis]):
                value = value + landed[(steps - 1, *index)].astype(jnp.float32)
            return value

        if phase == 2:
            pieces_sum = total((Ellipsis,))
            partial[i][...] = pieces_sum
            count_squares(pieces_sum)
            e_copy(i).start()
            o_copy(i).start()
        else:
            left = [sizes[other] for other in range(3) if other not in way(i)[: phase + 1]]

            @pl.loop(0, left[0])
            def _(index):
                mine[index] = total((index,)).astype(jnp.bfloat16)

    for member in range(members):
        load(items[0][0], member)
    for i, step in schedule(items, SCATTER_LAGS):
        if step == 0:
            give(i)
            continue
        if step in (1, 4) and side:
            side.pop(0)()
        if step == 1:
            combine(i)
        else:
            finish(i, step - 2)
        if step < 4:
            start(i, step - 1)
    for step in side:
        step()
    lane = lax.broadcasted_iota(jnp.int32, squares.shape, 0)
    ends[...] = jnp.where(lane == 0, squares[...], loss_in[...])
    for step in range(1, count):
        send(
            remote(
                ends, end_landed.at[me], end_send.at[step], end_recv.at[step],
                numbered(ways, lax.rem(me + step, count)),
            )
        )
    end_landed[me] = ends[...]
    for step in range(1, count):
        origin = lax.rem(me + count - step, count)
        remote(
            ends, end_landed.at[origin], end_send.at[step], end_recv.at[step], numbered(ways, origin)
        ).wait_recv()
    final[...] = jnp.sum(end_landed[...], 0)
    for i in range(n):
        e_copy(i).wait()
        o_copy(i).wait()
    for member in range(members):
        for i in used[member][-RINGS[member] :]:
            c_copy(i).wait_send()
    for copy in sent_all:
        copy.wait_send()


def scatter_grads(kept, text, rest, own, rows, halves, ways, number, items):
    layers, members = len(kept), len(rows)
    sizes = (ways[0] // 2, 2, ways[1] // 2)
    n = len(items)
    sem = pltpu.SemaphoreType.DMA
    low = jnp.bfloat16
    chips = sizes[0] * sizes[1] * sizes[2]
    frames, tokens = kept[0]["n1"].shape[0], text.shape[0]
    most = [max(s for _, m, _, s, _ in items if m == member) for member in range(members)]
    vmem = pltpu.VMEM

    def part(item, phase):
        _, member, _, size, order = item
        order = order[::-1]
        left = tuple(sizes[axis] for axis in range(3) if axis not in order[: phase + 1])
        return vmem((sizes[order[phase]] - 1, *left, 2 * rows[member], size), low)

    full, devices = jnp.float32, 2 * chips
    tile = tuple(rest[1].shape[1:])
    sums = sem((len(ROUNDS), max(sizes)))
    scratch = [
        vmem((devices,) + MOD_TILE, full),
        vmem((devices,) + tile, full),
        vmem((len(ROUNDS) + 1, devices, D), full),
        vmem((sizes[0] + sizes[1] + sizes[2] - 2, devices, D), full),
        vmem((8, 128), full),
    ]
    scratch += split_shapes(sizes, tile) + [sums] * 6 + [sem((devices,))] * 2
    scratch += [vmem((8, 128), full), vmem((devices, 8, 128), full)]
    scratch += [vmem((devices, SHARE), full), vmem((devices, 8, 128), full), sem((2,))]
    scratch += [
        vmem((3, frames, D), low),
        vmem((8, frames, D), low),
        vmem(text.shape, low),
        vmem((2, tokens, D), low),
        vmem((frames, FF), low),
        vmem((2, frames, D), low),
        vmem((2, 3, frames, D // 2), low),
    ]
    scratch += [vmem((RINGS[m], chips * 2 * rows[m], most[m]), low) for m in range(members)]
    scratch += [vmem((chips * 2 * rows[m], s), low) for _, m, _, s, _ in items]
    scratch += [part(item, phase) for phase in range(3) for item in items]
    scratch += [vmem((2 * rows[m], s), jnp.float32) for _, m, _, s, _ in items]
    scratch += [sem((layers, members, 11))] + [sem((n,))] * 2 + [sem((n, max(sizes)))] * 6 + [sem((n,))] * 3
    flat = [text] + [k[name] for k in kept for name in ACTS]
    here, there = pl.BlockSpec(memory_space=vmem), pl.BlockSpec(memory_space=pl.ANY)
    return pl.pallas_call(
        functools.partial(scatter_kernel, ways, rows, halves, items, layers, own),
        out_shape=[
            jax.ShapeDtypeStruct((layers, rows[m], 2 * halves[m]), full) for m in range(members)
        ]
        + [
            jax.ShapeDtypeStruct((SHARE, MOD_ROWS * 128), full),
            jax.ShapeDtypeStruct((SHARE, FREQS), full),
            jax.ShapeDtypeStruct((SHARE, D), full),
            jax.ShapeDtypeStruct(tile, full),
            jax.ShapeDtypeStruct((8, 128), full),
        ],
        in_specs=[there] * len(flat) + [here, there, here, there] + [here] * (len(rest) - 4),
        out_specs=[there] * members + [here] * 5,
        scratch_shapes=scratch,
        compiler_params=pltpu.CompilerParams(
            collective_id=number, has_side_effects=True, vmem_limit_bytes=VMEM_LIMIT
        ),
    )(*flat, *rest)


def to_low(values):
    return values.astype(jnp.bfloat16)


def norm_rows(values):
    centred = values - jnp.mean(values, -1, keepdims=True)
    return centred * lax.rsqrt(jnp.mean(centred * centred, -1, keepdims=True) + EPSILON)


def modulate(stream, shift, scale_part):
    return norm_rows(stream) * (1.0 + scale_part) + shift


def gained_norm(stream, gain):
    return norm_rows(stream) * gain


def dense(left, right):
    return jnp.dot(left, right, preferred_element_type=jnp.float32)


def dense_back(left, right):
    return lax.dot_general(left, right, (((1,), (1,)), ((), ())), preferred_element_type=jnp.float32)


def weight_grad(left, right):
    return lax.dot_general(left, right, (((0,), (0,)), ((), ())), preferred_element_type=jnp.float32)


def split_heads(values):
    return values.reshape(values.shape[0], HEADS, HEAD_DIM)


def attention(queries, keys, values, keep):
    scores = jnp.einsum(
        "qhd,khd->hqk", split_heads(queries), split_heads(keys), preferred_element_type=jnp.float32
    ) * HEAD_DIM ** (-0.5)
    scores = jnp.where(keep[None, None, :], scores, NEGATIVE)
    shifted = jnp.exp(scores - jnp.max(scores, -1, keepdims=True))
    probs = shifted / jnp.sum(shifted, -1, keepdims=True)
    mixed = jnp.einsum(
        "hqk,khd->qhd", to_low(probs), split_heads(values), preferred_element_type=jnp.float32
    )
    return (to_low(mixed.reshape(queries.shape)), probs)


def attention_back(queries, keys, values, probs, grad_mixed):
    grad_heads = split_heads(to_low(grad_mixed))
    grad_values = jnp.einsum(
        "hqk,qhd->khd", to_low(probs), grad_heads, preferred_element_type=jnp.float32
    )
    grad_probs = jnp.einsum(
        "qhd,khd->hqk", grad_heads, split_heads(values), preferred_element_type=jnp.float32
    )
    grad_scores = to_low(probs * (grad_probs - jnp.sum(probs * grad_probs, -1, keepdims=True)))
    grad_queries = jnp.einsum(
        "hqk,khd->qhd", grad_scores, split_heads(keys), preferred_element_type=jnp.float32
    ) * HEAD_DIM ** (-0.5)
    grad_keys = jnp.einsum(
        "hqk,qhd->khd", grad_scores, split_heads(queries), preferred_element_type=jnp.float32
    ) * HEAD_DIM ** (-0.5)
    return (
        grad_queries.reshape(queries.shape),
        grad_keys.reshape(keys.shape),
        grad_values.reshape(values.shape),
    )


def noise_level(steps):
    phase = (steps.astype(jnp.float32) / 1000.0 + 0.008) / 1.008 * (math.pi / 2)
    return jnp.cos(phase) ** 2


def time_features(steps):
    half_width = FREQS // 2
    frequency = jnp.exp(-math.log(10000.0) * jnp.arange(half_width, dtype=jnp.float32) / half_width)
    angles = steps.astype(jnp.float32)[:, None] * frequency[None, :]
    return jnp.concatenate([jnp.cos(angles), jnp.sin(angles)], -1)


def layer_forward(stream, modulation, text_low, frame_keep, text_keep, weights):
    w_joint, w_textkv, w_back, gain = weights
    normed_one, pull_one = jax.vjp(modulate, stream, modulation[:D], modulation[D : 2 * D])
    input_one = to_low(normed_one)
    self_proj = to_low(dense(input_one, w_joint[:, : 3 * D]))
    mixed_one, probs_one = attention(
        self_proj[:, :D], self_proj[:, D : 2 * D], self_proj[:, 2 * D :], frame_keep
    )
    branch_one = dense(mixed_one, w_back[:D])
    stream_two = stream + modulation[2 * D : 3 * D] * branch_one
    normed_two, pull_two = jax.vjp(gained_norm, stream_two, gain)
    input_two = to_low(normed_two)
    cross_query = to_low(dense(input_two, w_joint[:, 3 * D : 4 * D]))
    cross_kv = to_low(dense(text_low, w_textkv))
    mixed_two, probs_two = attention(cross_query, cross_kv[:, :D], cross_kv[:, D:], text_keep)
    stream_three = stream_two + dense(mixed_two, w_back[D : 2 * D])
    normed_three, pull_three = jax.vjp(
        modulate, stream_three, modulation[3 * D : 4 * D], modulation[4 * D : 5 * D]
    )
    input_three = to_low(normed_three)
    hidden_act, pull_act = jax.vjp(jax.nn.gelu, dense(input_three, w_joint[:, 4 * D :]))
    hidden_low = to_low(hidden_act)
    branch_three = dense(hidden_low, w_back[2 * D :])
    result = stream_three + modulation[5 * D :] * branch_three
    saved = (
        pull_one,
        input_one,
        self_proj,
        mixed_one,
        probs_one,
        branch_one,
        pull_two,
        input_two,
        cross_query,
        cross_kv,
        mixed_two,
        probs_two,
        pull_three,
        input_three,
        pull_act,
        hidden_low,
        branch_three,
    )
    return (result, saved)


def layer_backward(saved, grad_out, modulation, text_low, weights):
    w_joint, w_textkv, w_back, gain = weights
    (
        pull_one,
        input_one,
        self_proj,
        mixed_one,
        probs_one,
        branch_one,
        pull_two,
        input_two,
        cross_query,
        cross_kv,
        mixed_two,
        probs_two,
        pull_three,
        input_three,
        pull_act,
        hidden_low,
        branch_three,
    ) = saved
    grad_three = to_low(grad_out * modulation[5 * D :])
    grad_gate_two = jnp.sum(grad_out * branch_three, 0)
    grad_down = weight_grad(hidden_low, grad_three)
    (grad_pre,) = pull_act(dense_back(grad_three, w_back[2 * D :]))
    grad_pre = to_low(grad_pre)
    grad_up = weight_grad(input_three, grad_pre)
    grad_inner, grad_shift_two, grad_scale_two = pull_three(dense_back(grad_pre, w_joint[:, 4 * D :]))
    grad_stream = grad_out + grad_inner
    grad_cross_out = to_low(grad_stream)
    grad_co = weight_grad(mixed_two, grad_cross_out)
    grad_cq, grad_ck, grad_cv = attention_back(
        cross_query,
        cross_kv[:, :D],
        cross_kv[:, D:],
        probs_two,
        dense_back(grad_cross_out, w_back[D : 2 * D]),
    )
    grad_cq = to_low(grad_cq)
    grad_text_w = weight_grad(text_low, to_low(jnp.concatenate([grad_ck, grad_cv], -1)))
    grad_query_w = weight_grad(input_two, grad_cq)
    grad_inner, grad_gain = pull_two(dense_back(grad_cq, w_joint[:, 3 * D : 4 * D]))
    grad_stream = grad_stream + grad_inner
    grad_one = to_low(grad_stream * modulation[2 * D : 3 * D])
    grad_gate_one = jnp.sum(grad_stream * branch_one, 0)
    grad_ao = weight_grad(mixed_one, grad_one)
    grad_q, grad_k, grad_v = attention_back(
        self_proj[:, :D],
        self_proj[:, D : 2 * D],
        self_proj[:, 2 * D :],
        probs_one,
        dense_back(grad_one, w_back[:D]),
    )
    grad_self = to_low(jnp.concatenate([grad_q, grad_k, grad_v], -1))
    grad_self_w = weight_grad(input_one, grad_self)
    grad_inner, grad_shift_one, grad_scale_one = pull_one(dense_back(grad_self, w_joint[:, : 3 * D]))
    grad_stream = grad_stream + grad_inner
    grad_mod = jnp.concatenate(
        [grad_shift_one, grad_scale_one, grad_gate_one, grad_shift_two, grad_scale_two, grad_gate_two]
    )
    grads = (
        jnp.concatenate([grad_self_w, grad_query_w, grad_up], 1),
        grad_text_w,
        jnp.concatenate([grad_ao, grad_co, grad_down], 0),
    )
    return (grad_stream, grad_mod, grads, grad_gain)


ROOT = math.sqrt(2.0 / math.pi)
CUBE = 0.044715
CHUNK = 160
WIDE = 512


def dot_nn(left, right):
    return lax.dot_general(left, right, (((1,), (0,)), ((), ())), preferred_element_type=jnp.float32)


def dot_nt(left, right):
    return lax.dot_general(left, right, (((1,), (1,)), ((), ())), preferred_element_type=jnp.float32)


def dot_tn(left, right):
    return lax.dot_general(left, right, (((0,), (0,)), ((), ())), preferred_element_type=jnp.float32)


def over_rows(count, step):
    @pl.loop(0, count // CHUNK)
    def _(index):
        step(pl.ds(pl.multiple_of(index * CHUNK, CHUNK), CHUNK))


def over_columns(count, width, step):
    for index in range(count // width):
        step(index * width)
        yield


def scaled(values):
    centred = values - jnp.mean(values, -1, keepdims=True)
    factor = lax.rsqrt(jnp.mean(centred * centred, -1, keepdims=True) + EPSILON)
    return centred * factor, factor


def norm_pull(normed, factor, grad):
    middle = jnp.mean(grad, -1, keepdims=True)
    along = jnp.mean(grad * normed, -1, keepdims=True)
    return factor * (grad - middle - normed * along)


def row_sum(values):
    return jnp.sum(values, 0, keepdims=True)


def attend(q_at, k_at, v_at, keep, stats, store):
    first = lax.broadcasted_iota(jnp.int32, (1, 2 * HEAD_DIM), 1) < HEAD_DIM

    for index in range(HEADS // 2):
        query, key = q_at(index) * HEAD_DIM ** (-0.5), k_at(index)
        zero = jnp.zeros_like(query)
        value = jnp.transpose(v_at(index))
        outs = []
        for head in range(2):
            mine = jnp.where(first, query, zero) if head == 0 else jnp.where(first, zero, query)
            scores = jnp.where(keep, dot_nt(key, mine), NEGATIVE)
            top = jnp.max(scores, 0, keepdims=True)
            shifted = jnp.exp(scores - top)
            total = jnp.sum(shifted, 0, keepdims=True)
            stats[2 * index + head : 2 * index + head + 1, :] = top + jnp.log(total)
            probs = to_low(shifted * (1.0 / total))
            outs.append(dot_nn(value[head * HEAD_DIM : (head + 1) * HEAD_DIM], probs))
        store(index, jnp.transpose(to_low(jnp.concatenate(outs, 0))))
        yield


def attend_back(q_at, k_at, v_at, grad_at, keep, stats, store):
    first = lax.broadcasted_iota(jnp.int32, (1, 2 * HEAD_DIM), 1) < HEAD_DIM

    for index in range(HEADS // 2):
        query, key = q_at(index) * HEAD_DIM ** (-0.5), k_at(index)
        value, grad = v_at(index), grad_at(index)
        key_turned = jnp.transpose(key * HEAD_DIM ** (-0.5))
        zero, zero_value = jnp.zeros_like(query), jnp.zeros_like(value)
        queries, keys, values = [], [], []
        for head in range(2):
            mine = jnp.where(first, query, zero) if head == 0 else jnp.where(first, zero, query)
            mine_value = jnp.where(first, value, zero_value) if head == 0 else jnp.where(first, zero_value, value)
            scores = jnp.where(keep, dot_nt(key, mine), NEGATIVE)
            probs = jnp.exp(scores - stats[2 * index + head : 2 * index + head + 1, :])
            values.append(dot_nn(to_low(probs), grad))
            grad_probs = dot_nt(mine_value, grad)
            inner = jnp.sum(probs * grad_probs, 0, keepdims=True)
            grad_scores = to_low(probs * (grad_probs - inner))
            keys.append(dot_nn(grad_scores, query))
            queries.append(dot_nn(key_turned[head * HEAD_DIM : (head + 1) * HEAD_DIM], grad_scores))
        store(
            index,
            jnp.transpose(to_low(jnp.concatenate(queries, 0))),
            to_low(jnp.where(first, *keys)),
            to_low(jnp.where(first, *values)),
        )
        yield


def tile_of(ref, base):
    return lambda index: ref[:, base + index * 2 * HEAD_DIM : base + (index + 1) * 2 * HEAD_DIM]


def run(steps):
    for _ in steps:
        pass


SAVED = (
    ("stream", D, jnp.float32),
    ("n1", D, jnp.bfloat16),
    ("qkv", 3 * D, jnp.bfloat16),
    ("mixed1", D, jnp.bfloat16),
    ("branch1", D, jnp.float32),
    ("stream2", D, jnp.float32),
    ("n2", D, jnp.bfloat16),
    ("cq", D, jnp.bfloat16),
    ("ckv", 2 * D, jnp.bfloat16),
    ("mixed2", D, jnp.bfloat16),
    ("stream3", D, jnp.float32),
    ("n3", D, jnp.bfloat16),
    ("branch3", D, jnp.float32),
    ("stats1", None, jnp.float32),
    ("stats2", None, jnp.float32),
)
GRADS = (
    ("g_self", 3 * D),
    ("g_cq", D),
    ("g_pre", FF),
    ("g_ckv", 2 * D),
    ("g_one", D),
    ("g_cross", D),
    ("g_three", D),
)
PARTS = ("qkv", "cq", "up", "text", "ao", "co", "down")
KEPT = ("n1", "n2", "n3", "mixed1", "mixed2", "hidden") + tuple(name for name, _ in GRADS)


NEEDED = ("stream", "qkv", "branch1", "stream2", "cq", "ckv", "stream3", "n3", "branch3", "stats1", "stats2")


class Names:
    def __init__(self, **refs):
        self.__dict__.update(refs)


def block_forward(s, hidden, result, mods, text, frame_keep, text_keep, w, need, done, emit):
    frames = s.stream.shape[0]

    def norm_one(rows):
        normed, _ = scaled(s.stream[rows, :])
        s.n1[rows, :] = to_low(normed * (1.0 + mods[1:2, :]) + mods[0:1, :])

    over_rows(frames, norm_one)
    yield
    emit("n1", s.n1)
    need("qkv")

    def project(column):
        cols = pl.ds(column, 256)
        s.qkv[:, cols] = to_low(dot_nn(s.n1[...], w.win[:, cols]))

    yield from over_columns(3 * D, 256, project)
    done("qkv")

    def mix_one(index, value):
        s.mixed1[:, index * 128 : (index + 1) * 128] = value

    yield from attend(tile_of(s.qkv, 0), tile_of(s.qkv, D), tile_of(s.qkv, 2 * D), frame_keep, s.stats1, mix_one)
    emit("mixed1", s.mixed1)
    need("ao")

    def branch_one(column):
        cols = pl.ds(column, 256)
        branch = dot_nn(s.mixed1[...], w.wout[0:D, cols])
        s.branch1[:, cols] = branch
        s.stream2[:, cols] = s.stream[:, cols] + mods[2:3, cols] * branch

    yield from over_columns(D, 256, branch_one)
    done("ao")

    def norm_two(rows):
        normed, _ = scaled(s.stream2[rows, :])
        s.n2[rows, :] = to_low(normed * mods[6:7, :])

    over_rows(frames, norm_two)
    yield
    emit("n2", s.n2)
    need("cq")

    def project_cross(column):
        cols = pl.ds(column, 256)
        s.cq[:, cols] = to_low(dot_nn(s.n2[...], w.win[:, pl.ds(3 * D + column, 256)]))

    yield from over_columns(D, 256, project_cross)
    done("cq")
    need("text")

    def project_text(column):
        cols = pl.ds(column, 256)
        s.ckv[:, cols] = to_low(dot_nn(text[...], w.wtext[:, cols]))

    yield from over_columns(2 * D, 256, project_text)
    done("text")

    def mix_two(index, value):
        s.mixed2[:, index * 128 : (index + 1) * 128] = value

    yield from attend(tile_of(s.cq, 0), tile_of(s.ckv, 0), tile_of(s.ckv, D), text_keep, s.stats2, mix_two)
    emit("mixed2", s.mixed2)
    need("co")

    def branch_two(column):
        cols = pl.ds(column, 256)
        s.stream3[:, cols] = s.stream2[:, cols] + dot_nn(s.mixed2[...], w.wout[D : 2 * D, cols])

    yield from over_columns(D, 256, branch_two)
    done("co")

    def norm_three(rows):
        normed, _ = scaled(s.stream3[rows, :])
        s.n3[rows, :] = to_low(normed * (1.0 + mods[4:5, :]) + mods[3:4, :])

    over_rows(frames, norm_three)
    yield
    emit("n3", s.n3)
    need("up")

    def expand(column):
        upper = dot_nn(s.n3[...], w.win[:, pl.ds(4 * D + column, WIDE)])
        tanh = jnp.tanh(ROOT * (upper + CUBE * (upper * upper * upper)))
        hidden[:, pl.ds(column, WIDE)] = to_low(0.5 * upper * (1.0 + tanh))

    yield from over_columns(FF, WIDE, expand)
    done("up")
    emit("hidden", hidden)
    need("down")

    def branch_three(column):
        cols = pl.ds(column, 256)
        branch = dot_nn(hidden[...], w.wout[2 * D :, cols])
        s.branch3[:, cols] = branch
        result[:, cols] = s.stream3[:, cols] + mods[5:6, cols] * branch

    yield from over_columns(D, 256, branch_three)
    done("down")


def block_backward(s, g, grad, mods, grad_mods, inner, mixed, frame_keep, text_keep, w, need, done, emit):
    frames = s.stream.shape[0]
    grad_mods[...] = jnp.zeros_like(grad_mods)

    def gate_three(rows):
        grad_out = grad[rows, :]
        g.g_three[rows, :] = to_low(grad_out * mods[5:6, :])
        grad_mods[5:6, :] += row_sum(grad_out * s.branch3[rows, :])

    over_rows(frames, gate_three)
    yield
    emit("g_three", g.g_three)
    need("down")
    need("up")

    def shrink(column):
        wide = pl.ds(column, WIDE)
        back = dot_nt(g.g_three[...], w.wout[pl.ds(2 * D + column, WIDE), :])
        upper = dot_nn(s.n3[...], w.win[:, pl.ds(4 * D + column, WIDE)])
        square = upper * upper
        tanh = jnp.tanh(ROOT * (upper + CUBE * (square * upper)))
        slope = 0.5 * (1.0 + tanh) + (0.5 * ROOT) * upper * (1.0 - tanh * tanh) * (1.0 + (3.0 * CUBE) * square)
        g.g_pre[:, wide] = to_low(back * slope)

    yield from over_columns(FF, WIDE, shrink)
    done("down")
    emit("g_pre", g.g_pre)

    def inner_three(column):
        inner[:, pl.ds(column, 256)] = dot_nt(g.g_pre[...], w.win[pl.ds(column, 256), 4 * D :])

    yield from over_columns(D, 256, inner_three)
    done("up")

    def pull_three(rows):
        normed, factor = scaled(s.stream3[rows, :])
        back = inner[rows, :]
        grad_mods[3:4, :] += row_sum(back)
        grad_mods[4:5, :] += row_sum(back * normed)
        total = grad[rows, :] + norm_pull(normed, factor, back * (1.0 + mods[4:5, :]))
        grad[rows, :] = total
        g.g_cross[rows, :] = to_low(total)

    over_rows(frames, pull_three)
    yield
    emit("g_cross", g.g_cross)
    need("co")

    def back_cross(column):
        mixed[:, pl.ds(column, 256)] = to_low(dot_nt(g.g_cross[...], w.wout[pl.ds(D + column, 256), :]))

    yield from over_columns(D, 256, back_cross)
    done("co")

    def store_cross(index, grad_query, grad_key, grad_value):
        cols = slice(index * 128, (index + 1) * 128)
        g.g_cq[:, cols] = grad_query
        g.g_ckv[:, cols] = grad_key
        g.g_ckv[:, D + index * 128 : D + (index + 1) * 128] = grad_value

    yield from attend_back(
        tile_of(s.cq, 0), tile_of(s.ckv, 0), tile_of(s.ckv, D), tile_of(mixed, 0), text_keep, s.stats2, store_cross
    )
    emit("g_cq", g.g_cq)
    emit("g_ckv", g.g_ckv)
    need("cq")

    def inner_two(column):
        inner[:, pl.ds(column, 256)] = dot_nt(g.g_cq[...], w.win[pl.ds(column, 256), 3 * D : 4 * D])

    yield from over_columns(D, 256, inner_two)
    done("cq")

    def pull_two(rows):
        normed, factor = scaled(s.stream2[rows, :])
        back = inner[rows, :]
        grad_mods[6:7, :] += row_sum(back * normed)
        total = grad[rows, :] + norm_pull(normed, factor, back * mods[6:7, :])
        grad[rows, :] = total
        g.g_one[rows, :] = to_low(total * mods[2:3, :])
        grad_mods[2:3, :] += row_sum(total * s.branch1[rows, :])

    over_rows(frames, pull_two)
    yield
    emit("g_one", g.g_one)
    need("ao")

    def back_self(column):
        mixed[:, pl.ds(column, 256)] = to_low(dot_nt(g.g_one[...], w.wout[pl.ds(column, 256), :]))

    yield from over_columns(D, 256, back_self)
    done("ao")

    def store_self(index, grad_query, grad_key, grad_value):
        cols = slice(index * 128, (index + 1) * 128)
        g.g_self[:, cols] = grad_query
        g.g_self[:, D + index * 128 : D + (index + 1) * 128] = grad_key
        g.g_self[:, 2 * D + index * 128 : 2 * D + (index + 1) * 128] = grad_value

    yield from attend_back(
        tile_of(s.qkv, 0), tile_of(s.qkv, D), tile_of(s.qkv, 2 * D), tile_of(mixed, 0), frame_keep, s.stats1, store_self
    )
    emit("g_self", g.g_self)
    need("qkv")

    def inner_one(column):
        inner[:, pl.ds(column, 256)] = dot_nt(g.g_self[...], w.win[pl.ds(column, 256), : 3 * D])

    yield from over_columns(D, 256, inner_one)
    done("qkv")

    def pull_one(rows):
        normed, factor = scaled(s.stream[rows, :])
        back = inner[rows, :]
        grad_mods[0:1, :] += row_sum(back)
        grad_mods[1:2, :] += row_sum(back * normed)
        grad[rows, :] = grad[rows, :] + norm_pull(normed, factor, back * (1.0 + mods[1:2, :]))

    over_rows(frames, pull_one)
    yield


def heights(frames, tokens):
    return {name: tokens if name in ("ckv", "g_ckv") else 16 if name in ("stats1", "stats2") else frames for name in WIDTHS}


WIDTHS = {**{name: width for name, width, _ in SAVED}, **dict(GRADS), "hidden": FF}
KINDS = {**{name: kind for name, _, kind in SAVED}, **{name: jnp.bfloat16 for name, _ in GRADS}, "hidden": jnp.bfloat16}


def shape_of(name, frames, tokens):
    return (heights(frames, tokens)[name], WIDTHS[name] or frames)


def weight_parts(source, target):
    (w_in, w_text, w_out), (win, wtext, wout) = source, target
    return {
        "qkv": (w_in.at[:, : 3 * D], win.at[:, : 3 * D]),
        "cq": (w_in.at[:, 3 * D : 4 * D], win.at[:, 3 * D : 4 * D]),
        "up": (w_in.at[:, 4 * D :], win.at[:, 4 * D :]),
        "text": (w_text, wtext),
        "ao": (w_out.at[:D], wout.at[:D]),
        "co": (w_out.at[D : 2 * D], wout.at[D : 2 * D]),
        "down": (w_out.at[2 * D :], wout.at[2 * D :]),
    }


def keeps(lengths, frames, tokens):
    return (
        lax.broadcasted_iota(jnp.int32, (frames, 1), 0) < lengths[0],
        lax.broadcasted_iota(jnp.int32, (tokens, 1), 0) < lengths[1],
    )


def lanes(first, count):
    lane = lax.broadcasted_iota(jnp.int32, (1, 128), 1)
    return jnp.logical_and(lane >= first, lane < first + count)


def gain_pick():
    row, lane = (lax.broadcasted_iota(jnp.int32, (8, 128), axis) for axis in range(2))
    return jnp.logical_and(row < LAYERS, lane == GAIN_LANE + row)


LEAD_LANE = 32
GAIN_LANE = 64


def model_kernel(channels, *refs):
    refs = list(refs)

    def take(count):
        taken = refs[:count]
        del refs[:count]
        return taken

    lengths, facts, stream_ref, mods_ref, final_mods, text, noise, noisy, small = take(9)
    weights = [take(3) for _ in range(LAYERS)]
    early = [dict(zip(NEEDED, take(len(NEEDED)))) for _ in range(LAYERS - 1)]
    end_ref, grad_small, grad_tile = take(3)
    kept_out = [dict(zip(KEPT if layer == LAYERS - 1 else GRAD_NAMES, take(len(KEPT) if layer == LAYERS - 1 else len(GRADS)))) for layer in range(LAYERS)]
    win, wtext, wout = take(3)
    saved = [Names(**dict(zip((name for name, *_ in SAVED), take(len(SAVED)))))]
    for _ in range(LAYERS - 1):
        saved.insert(0, Names(**dict(zip(NEEDED, take(len(NEEDED))))))
    g = Names(**dict(zip((name for name, _ in GRADS), take(len(GRADS)))))
    hidden, inner, mixed, final_low, grad_ref, grad_mods_ref, grad_final = take(7)
    load_sem, keep_sem, early_sem = refs
    w = Names(win=win, wtext=wtext, wout=wout)
    frames, tokens = noisy.shape[0], text.shape[0]
    frame_keep, text_keep = keeps(lengths, frames, tokens)
    last = LAYERS - 1

    def load(layer, part):
        return pltpu.make_async_copy(
            *weight_parts(weights[layer], (win, wtext, wout))[part], load_sem.at[PARTS.index(part)]
        )

    def early_copies(layer):
        return [
            pltpu.make_async_copy(early[layer][name], getattr(saved[layer], name), early_sem.at[layer, j])
            for j, name in enumerate(NEEDED)
        ]

    flying = {}

    def keep(layer):
        def emit(name, ref):
            copy = pltpu.make_async_copy(
                ref, kept_out[layer][name], keep_sem.at[layer, KEPT.index(name)]
            )
            copy.start()
            flying[name, layer] = copy

        return emit

    def settle(layer, names):
        for name in names:
            copy = flying.pop((name, layer), None)
            if copy is not None:
                copy.wait()

    def nothing(part):
        pass

    for part in ("qkv", "ao", "cq", "text", "co", "up", "down"):
        load(last, part).start()
    for layer in range(last):
        for copy in early_copies(layer):
            copy.start()
    over_rows(frames, lambda rows: saved[last].stream.__setitem__((rows, slice(None)), stream_ref[rows, :]))
    run(
        block_forward(
            saved[last], hidden, grad_ref, mods_ref.at[last], text, frame_keep, text_keep, w,
            lambda part: load(last, part).wait(), nothing, keep(last),
        )
    )

    def norm_final(rows):
        normed, _ = scaled(grad_ref[rows, :])
        final_low[rows, :] = to_low(normed * (1.0 + final_mods[1:2, :]) + final_mods[0:1, :])

    over_rows(frames, norm_final)
    counted = lax.broadcasted_iota(jnp.int32, (frames, 1), 0) < lengths[0]
    error = dot_nn(final_low[...], small[...]) - noise[...]
    error = jnp.where(jnp.logical_and(counted, lanes(0, channels)), error, 0.0)
    row, lane = (lax.broadcasted_iota(jnp.int32, end_ref.shape, axis) for axis in range(2))
    own = jnp.where(jnp.logical_and(row == 2, lane == 0), jnp.full(end_ref.shape, lengths[0].astype(jnp.float32)), 0.0)
    end_ref[...] = jnp.where(row == 1, jnp.broadcast_to(row_sum(error * error), end_ref.shape), own)
    factor = 2.0 / jnp.sum(facts[:, 2, :], (0, 1), keepdims=True)
    grad_pred = to_low(error * factor)
    grad_small[...] = dot_tn(final_low[...], grad_pred)
    inner[...] = dot_nt(grad_pred, small[...])
    grad_final[...] = jnp.zeros_like(grad_final)

    def pull_final(rows):
        normed, factor = scaled(grad_ref[rows, :])
        back = inner[rows, :]
        grad_final[0:1, :] += row_sum(back)
        grad_final[1:2, :] += row_sum(back * normed)
        grad_ref[rows, :] = norm_pull(normed, factor, back * (1.0 + final_mods[1:2, :]))

    over_rows(frames, pull_final)
    for layer in reversed(range(LAYERS)):
        if layer < last:
            settle(layer + 1, [name for name, _ in GRADS])
            for copy in early_copies(layer):
                copy.wait()
        run(
            block_backward(
                saved[layer], g, grad_ref, mods_ref.at[layer], grad_mods_ref.at[layer], inner, mixed,
                frame_keep, text_keep, w,
                nothing if layer == last else (lambda part: load(layer, part).wait()),
                nothing if layer == 0 else (lambda part: load(layer - 1, part).start()),
                keep(layer),
            )
        )
    over_rows(frames, lambda rows: final_low.__setitem__((rows, slice(None)), to_low(grad_ref[rows, :])))
    gains = jnp.concatenate(
        [grad_mods_ref[layer, 6:7, :] for layer in range(LAYERS)] + [jnp.zeros((8 - LAYERS, D), jnp.float32)], 0
    )
    grad_small[...] += dot_tn(final_low[...], noisy[...]) + lax.dot_general(
        gains, gain_pick().astype(jnp.float32), (((0,), (0,)), ((), ())),
        precision=lax.Precision.HIGHEST, preferred_element_type=jnp.float32,
    )
    grad_tile[...] = jnp.zeros_like(grad_tile)
    pieces = [(grad_mods_ref.at[layer], j) for layer in range(LAYERS) for j in range(6)]
    pieces += [(grad_final, j) for j in range(2)]
    for p, (ref, j) in enumerate(pieces):
        for k in range(D // 128):
            part = ref[j : j + 1, k * 128 : (k + 1) * 128]
            at = p * (D // 128) + k
            grad_tile[at : at + 1, :] = to_low(part).astype(jnp.float32)
    for layer in range(LAYERS):
        settle(layer, KEPT)


GRAD_NAMES = tuple(name for name, _ in GRADS)


def run_model(lengths, facts, stream, mods, final_mods, text, noise, noisy, small, weights, early, channels):
    frames, tokens = noisy.shape[0], text.shape[0]
    low, full = jnp.bfloat16, jnp.float32
    shape = jax.ShapeDtypeStruct
    here, there = pl.BlockSpec(memory_space=pltpu.VMEM), pl.BlockSpec(memory_space=pl.ANY)
    scalar = pl.BlockSpec(memory_space=pltpu.SMEM)

    def names(layer):
        return KEPT if layer == LAYERS - 1 else GRAD_NAMES

    def vmem(name):
        return pltpu.VMEM(shape_of(name, frames, tokens), KINDS[name])

    kept = [shape(shape_of(name, frames, tokens), low) for layer in range(LAYERS) for name in names(layer)]
    early_flat = [layer[name] for layer in early for name in NEEDED]
    out = pl.pallas_call(
        functools.partial(model_kernel, channels),
        out_shape=[shape((8, 128), full), shape((D, 128), full), shape(MOD_TILE, full)] + kept,
        in_specs=[scalar] + [here] * 8 + [there] * (3 * LAYERS + len(early_flat)),
        out_specs=[here] * 3 + [there] * len(kept),
        scratch_shapes=[pltpu.VMEM((D, JOINT), low), pltpu.VMEM((text.shape[1], 2 * D), low), pltpu.VMEM((2 * D + FF, D), low)]
        + [vmem(name) for name, *_ in SAVED]
        + [vmem(name) for name in NEEDED] * (LAYERS - 1)
        + [vmem(name) for name, _ in GRADS]
        + [
            pltpu.VMEM((frames, FF), low),
            pltpu.VMEM((frames, D), full),
            pltpu.VMEM((frames, D), low),
            pltpu.VMEM((frames, D), low),
            pltpu.VMEM((frames, D), full),
            pltpu.VMEM((LAYERS, 8, D), full),
            pltpu.VMEM((8, D), full),
            pltpu.SemaphoreType.DMA((len(PARTS),)),
            pltpu.SemaphoreType.DMA((LAYERS, len(KEPT))),
            pltpu.SemaphoreType.DMA((LAYERS, len(NEEDED))),
        ],
        compiler_params=pltpu.CompilerParams(vmem_limit_bytes=VMEM_LIMIT),
    )(
        lengths, facts, stream, mods, final_mods, text, noise, noisy, small,
        *[w for layer in weights for w in layer], *early_flat,
    )
    rest = list(out[3:])
    made = []
    for layer in range(LAYERS):
        count = len(names(layer))
        made.append(dict(zip(names(layer), rest[:count])))
        rest = rest[count:]
    return out[:3], made


def adam_update(weight, grad, first, second, rate):
    first_new = BETA_ONE * first + (1.0 - BETA_ONE) * grad
    second_new = BETA_TWO * second + (1.0 - BETA_TWO) * grad * grad
    first_hat = first_new / (1.0 - BETA_ONE**STEP)
    second_hat = second_new / (1.0 - BETA_TWO**STEP)
    weight_new = weight - rate * (
        first_hat / (jnp.sqrt(second_hat) + ADAM_EPSILON) + WEIGHT_DECAY * weight
    )
    return (first_new, second_new, weight_new)


def adam_kernel(layers, *refs):
    refs = list(refs)

    def take(count):
        taken = refs[:count]
        del refs[:count]
        return taken

    final, grad_mod, time_one, time_two, small = take(5)
    sums = take(3)
    given = [take(3) for _ in range(6)]
    results = [take(3) for _ in range(6)]
    held = [take(3) for _ in range(6)]
    grads = take(3)
    load_sem, grad_sem, store_sem = refs
    own = held[3][0].shape[0]
    groups = [(member, layer) for layer in range(layers) for member in (0, 2)] + [(1, None), (3, None), (4, None), (5, None)]

    def at(ref, layer):
        return ref if layer is None else ref.at[layer]

    def loads(number):
        member, layer = groups[number]
        copies = [
            pltpu.make_async_copy(at(given[member][j], layer), at(held[member][j], layer), load_sem.at[number, j])
            for j in range(3)
        ]
        if member < 3:
            copies.append(
                pltpu.make_async_copy(at(sums[member], layer), at(grads[member], layer), grad_sem.at[number])
            )
        return copies

    def stores(number):
        member, layer = groups[number]
        return [
            pltpu.make_async_copy(
                at(held[member][(j + 1) % 3], layer), at(results[member][j], layer), store_sem.at[number, j]
            )
            for j in range(3)
        ]

    for number in range(len(groups)):
        for copy in loads(number):
            copy.start()
    factor = CLIP_NORM / jnp.maximum(jnp.sqrt(final[0:1, 0:1]), CLIP_NORM)

    def update(member, index, grad, rate=LEARN_RATE):
        weight, first, second = held[member]
        first_new, second_new, weight_new = adam_update(
            weight[index], grad * factor, first[index], second[index], rate
        )
        first[index], second[index], weight[index] = first_new, second_new, weight_new

    for number, (member, layer) in enumerate(groups):
        for copy in loads(number):
            copy.wait()
        if member == 0:
            for column in range(0, JOINT, 1536):
                cols = slice(column, column + 1536)
                update(0, (layer, slice(None), cols), grads[0][layer, :, cols])
            for column in range(0, MOD, 1536):
                start = layer * MOD + column
                update(
                    0, (layer, slice(None), slice(JOINT + column, JOINT + column + 1536)),
                    grad_mod[:own, start : start + 1536],
                )
        elif member == 2:
            for row in range(0, held[2][0].shape[1], 48):
                rows = slice(row, row + 48)
                update(2, (layer, rows), grads[2][layer, rows])
        elif member == 1:
            for other in range(layers):
                for column in range(0, 2 * D, D):
                    index = (other, slice(None), slice(column, column + D))
                    update(1, index, grads[1][index])
        elif member == 4:
            update(4, (slice(None), slice(0, FREQS)), time_one[:own, :])
            tail = held[4][0].shape[1] - FREQS
            update(4, (slice(None), slice(FREQS, FREQS + tail)), small[:, LEAD_LANE : LEAD_LANE + tail])
        elif member == 5:
            turned = jnp.transpose(small[...])
            update(5, (slice(None), slice(None)), turned[GAIN_LANE : GAIN_LANE + layers, :], GAIN_RATE)
        else:
            update(3, (slice(None), slice(0, D)), time_two[:own, :])
            update(3, (slice(None), slice(D, 3 * D)), grad_mod[:own, layers * MOD : layers * MOD + 2 * D])
            tail = held[3][0].shape[1] - 3 * D
            update(3, (slice(None), slice(3 * D, 3 * D + tail)), small[:, :tail])
        for copy in stores(number):
            copy.start()
    for number in range(len(groups)):
        for copy in stores(number):
            copy.wait()


def run_adam(final, grad_mod, time_one, time_two, small, sums, given):
    here, there = pl.BlockSpec(memory_space=pltpu.VMEM), pl.BlockSpec(memory_space=pl.ANY)
    layers = given[0][0].shape[0]
    full = jnp.float32
    shapes = [group[0].shape for group in given]
    count = 2 * layers + 4
    sem = pltpu.SemaphoreType.DMA
    out = pl.pallas_call(
        functools.partial(adam_kernel, layers),
        out_shape=[jax.ShapeDtypeStruct(shape, full) for shape in shapes for _ in range(3)],
        in_specs=[here] * 5 + [there] * 21,
        out_specs=[there] * 18,
        scratch_shapes=[pltpu.VMEM(shape, full) for shape in shapes for _ in range(3)]
        + [pltpu.VMEM(item.shape, full) for item in sums]
        + [sem((count, 3)), sem((count,)), sem((count, 3))],
        compiler_params=pltpu.CompilerParams(vmem_limit_bytes=VMEM_LIMIT),
    )(final, grad_mod, time_one, time_two, small, *sums, *[item for group in given for item in group])
    return [out[3 * k : 3 * k + 3] for k in range(6)]


def tiles(values, lead=()):
    flat = values.reshape(lead + (-1,))
    short = -flat.shape[-1] % 1024
    flat = jnp.pad(flat, [(0, 0)] * len(lead) + [(0, short)])
    return flat.reshape(lead + (-1, 128))


def fast_grads(ways, clean_latent, noise, text_low, text_lengths, timesteps, valid_frames, w_in, w_text, w_out, gains, w_lead, w_head):
    count = ways[0] * ways[1]
    own, channels = w_head.shape[0], noise.shape[-1]
    rows = [w_in.shape[1], w_text.shape[1], w_out.shape[1]]
    halves = [JOINT // 2, D, D // 2]
    sinus = time_features(timesteps)
    facts = jnp.concatenate([to_low(sinus).astype(jnp.float32)[0], valid_frames.astype(jnp.float32)])
    wide = [(0, 0), (0, LEAD_LANE - channels)]
    small = jnp.concatenate(
        [
            jnp.pad(to_low(w_head[:, 3 * D :]).astype(jnp.float32), wide),
            jnp.pad(to_low(w_lead[FREQS:]).astype(jnp.float32).T, wide),
            jnp.pad(to_low(gains).astype(jnp.float32).T, [(0, 0), (0, 128 - GAIN_LANE - LAYERS)]),
        ],
        1,
    )
    level = noise_level(timesteps)
    noisy = jnp.sqrt(level) * clean_latent + jnp.sqrt(1.0 - level) * noise
    noisy = jnp.pad(to_low(noisy), [(0, 0), (LEAD_LANE, 128 - LEAD_LANE - channels)])
    lengths = jnp.concatenate([valid_frames, text_lengths])
    items = plan(halves, range(LAYERS), GATHER_PATTERN)
    weights, given, early = gather_weights(
        [w_in, w_text, w_out], w_head, jnp.concatenate([tiles(facts), small], 0), w_lead.T, lengths, text_low, noisy, own, halves, ways, 1, items,
    )
    packed, pre_time, temb, block_mods, final_mods, small, stream, head_own, mod_own = given
    (ends, grad_small, grad_tile), kept = run_model(
        lengths, packed, stream, block_mods, final_mods, text_low,
        jnp.pad(noise, [(0, 0), (0, 128 - channels)]), noisy, small, weights, [early], channels,
    )
    kept[0] = {**early, **kept[0]}
    items = plan(halves, list(reversed(range(LAYERS))), SCATTER_PATTERN)
    rest = [grad_tile, grad_small.reshape(count, own, 128), ends, packed, pre_time, temb, head_own, mod_own]
    *sums, grad_mod_w, grad_time_one, grad_time_two, small_sum, final = scatter_grads(
        kept, text_low, rest, own, rows, halves, ways, 2, items
    )
    grads = final, grad_mod_w, grad_time_one, grad_time_two, small_sum, sums
    return jnp.sum(final[1]), final[2, 0], jnp.sqrt(final[0, 0]), grads


def plain_grads(ways, clean_latent, noise, text_low, text_lengths, timesteps, valid_frames, w_in, w_text, w_out, gains, w_lead, w_head):
    count = ways[0] * ways[1]
    own, channels = w_head.shape[0], noise.shape[-1]
    frame_keep = lax.iota(jnp.int32, clean_latent.shape[0]) < valid_frames[0]
    text_keep = lax.iota(jnp.int32, text_low.shape[0]) < text_lengths[0]

    def to_all(values):
        return lax.all_gather(values, ALL, axis=0, tiled=True)

    def by_columns(values):
        return values.transpose(1, 0, 2).reshape(values.shape[1], -1)

    lead_low, head_low = to_low(w_lead), to_low(w_head)
    frame_count = jnp.sum(to_all(valid_frames)).astype(jnp.float32)
    sinus_all = to_low(time_features(to_all(timesteps)))
    lead_in = by_columns(to_all(lead_low[None, FREQS:]))
    head_pred = to_all(head_low[:, 3 * D :])
    gains_all = by_columns(to_all(to_low(gains)[None])).astype(jnp.float32)
    act_time, pull_time = jax.vjp(jax.nn.silu, dense(sinus_all, lead_low[:FREQS]))
    act_low = to_low(act_time)
    temb = dense(act_low, head_low[:, :D]).reshape(count, count, own).transpose(1, 0, 2)
    temb = jnp.sum(lax.all_to_all(temb, ALL, 0, 0, tiled=True), 0)
    cond, pull_cond = jax.vjp(jax.nn.silu, temb)
    cond_low = to_low(cond)
    mod_low = jnp.concatenate(
        [to_low(w_in[layer, :, JOINT:]) for layer in range(LAYERS)] + [head_low[:, D : 3 * D]], 1
    )
    mods = jnp.sum(lax.all_to_all(dense(cond_low, mod_low)[:, None], ALL, 0, 0, tiled=True), 0)[0]
    weights = [
        [to_all(to_low(shard[layer])) for shard in (w_in[:, :, :JOINT], w_text, w_out)] for layer in range(LAYERS)
    ]
    level = noise_level(timesteps)
    noisy_low = to_low(jnp.sqrt(level) * clean_latent + jnp.sqrt(1.0 - level) * noise)
    stream = dense(noisy_low, lead_in)
    saved = []
    for layer in range(LAYERS):
        stream, kept = layer_forward(
            stream, mods[layer * MOD : (layer + 1) * MOD], text_low, frame_keep, text_keep,
            (*weights[layer], gains_all[layer]),
        )
        saved.append(kept)
    final_mod = mods[LAYERS * MOD :]
    normed_final, pull_final = jax.vjp(modulate, stream, final_mod[:D], final_mod[D:])
    final_low = to_low(normed_final)
    error = dense(final_low, head_pred) - noise
    loss_part = jnp.sum(jnp.where(frame_keep[:, None], error * error, 0.0))
    grad_pred = to_low(jnp.where(frame_keep[:, None], error * (2.0 / frame_count), 0.0))
    grad_pred_w = weight_grad(final_low, grad_pred)
    grad_stream, grad_shift_f, grad_scale_f = pull_final(dense_back(grad_pred, head_pred))
    grad_mods = [None] * LAYERS + [jnp.concatenate([grad_shift_f, grad_scale_f])]
    big, grad_gains = [None] * LAYERS, [None] * LAYERS
    for layer in reversed(range(LAYERS)):
        grad_stream, grad_mods[layer], big[layer], grad_gains[layer] = layer_backward(
            saved[layer], grad_stream, mods[layer * MOD : (layer + 1) * MOD], text_low,
            (*weights[layer], gains_all[layer]),
        )
    grad_in_w = weight_grad(noisy_low, to_low(grad_stream))
    sums = [
        jnp.stack(
            [lax.psum_scatter(big[layer][member], ALL, scatter_dimension=0, tiled=True) for layer in range(LAYERS)]
        )
        for member in range(3)
    ]
    mods_all = lax.all_gather(to_low(jnp.concatenate(grad_mods)), ALL, axis=0, tiled=False)
    grad_mod_w = weight_grad(cond_low, mods_all)
    (grad_temb,) = pull_cond(dense_back(mods_all, mod_low))
    grad_temb = by_columns(lax.all_gather(to_low(grad_temb), ALL, axis=0, tiled=False))
    grad_time_two = weight_grad(act_low, grad_temb)
    (grad_pre_time,) = pull_time(dense_back(grad_temb, head_low[:, :D]))
    grad_time_one = weight_grad(sinus_all, to_low(grad_pre_time))

    def to_owner(values):
        return lax.psum_scatter(values, ALL, scatter_dimension=0, tiled=True)

    mod_grads = grad_mod_w[:, : LAYERS * MOD].reshape(own, LAYERS, MOD).transpose(1, 0, 2)
    grad_list = [
        jnp.concatenate([sums[0], mod_grads], 2),
        sums[1],
        sums[2],
        to_owner(jnp.stack(grad_gains).T).T,
        jnp.concatenate([grad_time_one, to_owner(grad_in_w.T).T], 0),
        jnp.concatenate([grad_time_two, grad_mod_w[:, LAYERS * MOD :], to_owner(grad_pred_w)], 1),
    ]
    squares = sum((jnp.sum(item * item) for item in grad_list))
    loss_sum, squares = lax.psum((loss_part, squares), ALL)
    return loss_sum, frame_count, jnp.sqrt(squares), grad_list


def body(
    ways,
    clean_latent,
    noise,
    text_feats,
    text_lengths,
    timesteps,
    valid_frames,
    w_in,
    w_text,
    w_out,
    gains,
    w_lead,
    w_head,
    first_in,
    second_in,
    first_text,
    second_text,
    first_out,
    second_out,
    first_gains,
    second_gains,
    first_lead,
    second_lead,
    first_head,
    second_head,
):
    aligned = all(shard.shape[1] % 8 == 0 for shard in (w_in, w_text, w_out)) and all(way % 2 == 0 for way in ways)
    aligned = aligned and w_head.shape[0] <= SHARE and noise.shape[-1] <= LEAD_LANE
    grads_of = fast_grads if aligned else plain_grads
    loss_sum, frame_count, grad_norm, grads = grads_of(
        ways, clean_latent[0], noise[0], text_feats[0], text_lengths, timesteps, valid_frames,
        w_in, w_text, w_out, gains, w_lead, w_head,
    )
    factor = CLIP_NORM / jnp.maximum(grad_norm, CLIP_NORM)
    params = (w_in, w_text, w_out, gains, w_lead, w_head)
    firsts = (first_in, first_text, first_out, first_gains, first_lead, first_head)
    seconds = (second_in, second_text, second_out, second_gains, second_lead, second_head)
    rates = (LEARN_RATE, LEARN_RATE, LEARN_RATE, GAIN_RATE, LEARN_RATE, LEARN_RATE)
    results = [None] * 6
    if aligned:
        given = list(zip(params, firsts, seconds))
        order = (0, 1, 2, 5, 4, 3)
        given[4] = tuple(item.T for item in given[4])
        for k, made in zip(order, run_adam(*grads, [given[k] for k in order])):
            results[k] = [item.T for item in made] if k == 4 else made
    else:
        for k, grad in enumerate(grads):
            results[k] = adam_update(params[k], grad * factor, firsts[k], seconds[k], rates[k])
    return (loss_sum, frame_count, grad_norm, *(item for made in results for item in made))


def solution(mesh):
    ways = (mesh.shape["dp"], mesh.shape["fsdp"])
    clips = [P(ALL, None, None)] * 3 + [P(ALL)] * 3
    weights = [P(None, ALL, None)] * 3 + [P(None, ALL)] * 2 + [P(ALL, None)]
    moments = [spec for spec in weights for _ in range(2)]
    results = [spec for spec in weights for _ in range(3)]
    return jax.shard_map(
        functools.partial(body, ways),
        mesh=mesh,
        in_specs=tuple(clips + weights + moments),
        out_specs=tuple([P()] * 3 + results),
        check_vma=False,
    )
```

```python
import functools
import math

import jax
import jax.numpy as jnp
from jax import lax
from jax.experimental import pallas as pl
from jax.experimental.pallas import tpu as pltpu
from jax.sharding import PartitionSpec as P

D = 768
HEADS = 12
HEAD_DIM = 64
FF = 3072
FREQS = 256
LAYERS = 2
STEP = 10
MOD = 6 * D
JOINT = 4 * D + FF

EPSILON = 1e-06
NEGATIVE = -1e30
BETA_ONE = 0.5
BETA_TWO = 0.5
LEARN_RATE = 0.02
GAIN_RATE = 0.3
WEIGHT_DECAY = 0.01
ADAM_EPSILON = 1e-08
CLIP_NORM = 1.0

ALL = ("dp", "fsdp")
MESH = pl.DeviceIdType.MESH
VMEM_LIMIT = 60 * 1024 * 1024


def place(ways):
    dp_ways, fsdp_ways = ways
    row, col = lax.axis_index("dp"), lax.axis_index("fsdp")
    sizes = (dp_ways // 2, 2, fsdp_ways // 2)
    spot = (row // 2, lax.rem(row, 2), col // 2)
    return sizes, spot, lax.rem(col, 2)


def device_at(spot, core):
    z, y, x = spot
    return (z * 2 + y, x * 2 + core)


def moved(spot, axis, size, steps):
    spot = list(spot)
    spot[axis] = lax.rem(spot[axis] + steps, size)
    return tuple(spot)


def remote(source, target, send, recv, device):
    return pltpu.make_async_remote_copy(
        src_ref=source, dst_ref=target, send_sem=send, recv_sem=recv, device_id=device, device_id_type=MESH
    )


def greet_all(ways, me):
    count = ways[0] * ways[1]
    barrier = pltpu.get_barrier_semaphore()
    for step in range(1, count):
        pl.semaphore_signal(
            barrier, inc=1, device_id=numbered(ways, lax.rem(me + step, count)), device_id_type=MESH
        )
    pl.semaphore_wait(barrier, count - 1)


def numbered(ways, index):
    return (index // ways[1], lax.rem(index, ways[1]))


ROUNDS = ("core", 2, 1, 0)


class Hops:
    def __init__(self, sizes, spot, core):
        self.sizes, self.spot, self.core = sizes, spot, core

    def count(self, axis):
        return 2 if axis == "core" else self.sizes[axis]

    def place(self, axis):
        return self.core if axis == "core" else self.spot[axis]

    def other(self, axis, steps):
        if axis == "core":
            return 1 - self.core, device_at(self.spot, 1 - self.core)
        spot = moved(self.spot, axis, self.sizes[axis], steps)
        return spot[axis], device_at(spot, self.core)


def sum_steps(hops, totals, landed, send_sem, recv_sem, sent):
    first = [sum(hops.count(axis) - 1 for axis in ROUNDS[:turn]) for turn in range(len(ROUNDS))]

    def copies(turn):
        axis = ROUNDS[turn]
        return [
            remote(
                totals.at[turn], landed.at[first[turn] + steps - 1],
                send_sem.at[turn, steps - 1], recv_sem.at[turn, steps - 1], hops.other(axis, steps)[1],
            )
            for steps in range(1, hops.count(axis))
        ]

    def begin(turn):
        for copy in copies(turn):
            copy.start()
            sent.append(copy)

    def go_on(turn):
        for copy in copies(turn):
            copy.wait_recv()
        total = totals[turn]
        for steps in range(1, hops.count(ROUNDS[turn])):
            total = total + landed[first[turn] + steps - 1]
        totals[turn + 1] = total
        if turn + 1 < len(ROUNDS):
            begin(turn + 1)

    return [lambda: begin(0)] + [functools.partial(go_on, turn) for turn in range(len(ROUNDS))]


def split_steps(hops, rows, landed, out, send_sem, recv_sem, sent):
    places = {"core": 3, 2: 2, 1: 1, 0: 0}

    def index(turn, place_on):
        at = [slice(None)] * 4
        for early in ROUNDS[:turn]:
            at[places[early]] = hops.place(early)
        at[places[ROUNDS[turn]]] = place_on
        return tuple(at)

    def copies(turn):
        axis = ROUNDS[turn]
        made = []
        for steps in range(1, hops.count(axis)):
            place_on, device = hops.other(axis, steps)
            made.append(
                remote(
                    rows.at[index(turn, place_on)], landed[turn].at[steps - 1],
                    send_sem.at[turn, steps - 1], recv_sem.at[turn, steps - 1], device,
                )
            )
        return made

    def begin(turn):
        for copy in copies(turn):
            copy.start()
            sent.append(copy)

    def go_on(turn):
        for copy in copies(turn):
            copy.wait_recv()
        axis = ROUNDS[turn]
        mine = rows.at[index(turn, hops.place(axis))]
        others = range(hops.count(axis) - 1)
        if turn == 3:
            out[...] = sum((landed[turn][k] for k in others), mine[...])
        else:

            @pl.loop(0, hops.sizes[0])
            def _(z):
                mine[z] = sum((landed[turn][k, z] for k in others), mine[z])

            begin(turn + 1)

    return [lambda: begin(0)] + [functools.partial(go_on, turn) for turn in range(len(ROUNDS))]


def split_shapes(sizes, tile):
    z, y, x = sizes
    return [
        pltpu.VMEM((1, z, y, x) + tile, jnp.float32),
        pltpu.VMEM((x - 1, z, y) + tile, jnp.float32),
        pltpu.VMEM((y - 1, z) + tile, jnp.float32),
        pltpu.VMEM((z - 1,) + tile, jnp.float32),
    ]


def spread_steps(hops, rows, send_sem, recv_sem, sent):
    turns = (0, 2, 1, "core")
    places = {"core": 3, 2: 2, 1: 1, 0: 0}

    def index(turn, place_on):
        at = [hops.spot[0], hops.spot[1], hops.spot[2], hops.core]
        for early in turns[:turn]:
            at[places[early]] = slice(None)
        at[places[turns[turn]]] = place_on
        return tuple(at)

    def copies(turn, origin):
        axis = turns[turn]
        made = []
        for steps in range(1, hops.count(axis)):
            device = hops.other(axis, steps)[1]
            place_on = hops.other(axis, hops.count(axis) - steps)[0] if origin else hops.place(axis)
            part = rows.at[index(turn, place_on)]
            made.append(remote(part, part, send_sem.at[turn, steps - 1], recv_sem.at[turn, steps - 1], device))
        return made

    def begin(turn):
        for copy in copies(turn, False):
            copy.start()
            sent.append(copy)

    def go_on(turn):
        for copy in copies(turn, True):
            copy.wait_recv()
        if turn + 1 < len(turns):
            begin(turn + 1)

    return [lambda: begin(0)] + [functools.partial(go_on, turn) for turn in range(len(turns))]


def sigmoid(values):
    return 1.0 / (1.0 + jnp.exp(-values))


def chosen(me, own, width):
    shape = (D, width)
    row, column = (lax.broadcasted_iota(jnp.int32, shape, axis) for axis in range(2))
    return jnp.logical_and(row == me * own + column, column < own).astype(jnp.float32)


SHARE = 32
MOD_ROWS = (LAYERS * MOD + 2 * D) // 128
MOD_TILE = (-(-MOD_ROWS // 8) * 8, 128)


def gather_kernel(ways, rows, halves, items, layers, own, *refs):
    members = len(rows)
    refs = list(refs)

    def take(count):
        taken = refs[:count]
        del refs[:count]
        return taken

    shards = take(members)
    w_head, facts_in, lead_turned, lengths, text, noisy = take(6)
    fulls = take(members * layers)
    facts, pre_time, temb_own, block_mods, final_mods, small, result, head_own, mod_own = take(9)
    early = dict(zip(EARLY, take(len(EARLY))))
    totals, landed, mod_parts = take(3)
    mod_landed = take(4)
    facts_send, facts_recv, sum_send, sum_recv, split_send, split_recv = take(6)
    mods, win, wtext, wout = take(4)
    saved = Names(**dict(zip((name for name, *_ in SAVED), take(len(SAVED)))))
    (hidden,) = take(1)
    load_sem, keep_sem, mod_stage, head_stage, side_sem = take(5)
    rest = refs
    stages = rest[:members]
    blocks = rest[members : 2 * members]
    pre_send, pre_recv, own_sem, put_sem, *sends, c_send, c_recv = rest[2 * members :]
    sends, recvs = sends[0::2], sends[1::2]
    sizes, spot, core = place(ways)
    z, y, x = spot
    partner = device_at(spot, 1 - core)
    count = ways[0] * ways[1]
    me = lax.axis_index("dp") * ways[1] + lax.axis_index("fsdp")
    greet_all(ways, me)

    def facts_copy(step):
        return remote(
            facts_in, facts.at[me], facts_send.at[step], facts_recv.at[step],
            numbered(ways, lax.rem(me + step, count)),
        )

    for step in range(1, count):
        facts_copy(step).start()
    facts[me] = facts_in[...]

    def full(layer, member):
        return fulls[layer * members + member]

    pre = []
    for layer in range(layers):
        for member in range(members):
            height, half = rows[member], halves[member]
            place_in = stages[member].at[layer, pl.ds(pl.multiple_of(core * height, 8), height)]
            mine = shards[member].at[layer, :, pl.ds(pl.multiple_of(core * half, 128), half)]
            other = shards[member].at[layer, :, pl.ds(pl.multiple_of((1 - core) * half, 128), half)]
            index = layer * members + member
            sent = remote(other, place_in, pre_send.at[index], pre_recv.at[index], partner)
            sent.start()
            kept = pltpu.make_async_copy(mine, place_in, own_sem.at[index])
            kept.start()
            pre.append((sent, kept))
    arrived = set()
    put_done = set()
    sent_all = []

    def columns(i, side):
        _, member, start, size, _ = items[i]
        return pl.ds(pl.multiple_of(side * halves[member] + start, 128), size)

    def put(layer, member):
        half = halves[member]
        return pltpu.make_async_copy(
            blocks[member].at[layer],
            full(layer, member).at[z, y, x, :, pl.ds(pl.multiple_of(core * half, 128), half)],
            put_sem.at[layer * members + member],
        )

    def ready(layer, member):
        if (layer, member) in arrived:
            return
        arrived.add((layer, member))
        index = layer * members + member
        height = rows[member]
        sent, kept = pre[index]
        kept.wait()
        theirs = stages[member].at[layer, pl.ds(pl.multiple_of((1 - core) * height, 8), height)]
        remote(theirs, theirs, pre_send.at[index], pre_recv.at[index], partner).wait_recv()
        blocks[member][layer] = stages[member][layer].astype(jnp.bfloat16)
        put(layer, member).start()

    def own_put(layer, member):
        if (layer, member) not in put_done:
            put_done.add((layer, member))
            put(layer, member).wait()

    def region(i, phase, origin, side):
        layer, member, start, size, order = items[i]
        index = [slice(None) if order.index(axis) < phase else spot[axis] for axis in range(3)]
        if phase < 3 and origin is not None:
            index[order[phase]] = origin
        return full(layer, member).at[(*index, slice(None), columns(i, side))]

    def send(copy):
        copy.start()
        sent_all.append(copy)

    def start(i, phase):
        layer, member, first, size, order = items[i]
        axis = order[phase]
        if phase == 0:
            ready(layer, member)
            source = blocks[member].at[layer, :, pl.ds(first, size)]
        else:
            own_put(layer, member)
            source = region(i, phase, None, core)
        for steps in range(1, sizes[axis]):
            send(
                remote(
                    source, region(i, phase, spot[axis], core),
                    sends[phase].at[i, steps - 1], recvs[phase].at[i, steps - 1],
                    device_at(moved(spot, axis, sizes[axis], steps), core),
                )
            )
        if phase == 2:
            send(remote(source, source, c_send.at[i, 0], c_recv.at[i, 0], partner))

    def finish(i, phase):
        axis = items[i][4][phase]
        for steps in range(1, sizes[axis]):
            land = region(i, phase, lax.rem(spot[axis] + sizes[axis] - steps, sizes[axis]), core)
            remote(land, land, sends[phase].at[i, steps - 1], recvs[phase].at[i, steps - 1], partner).wait_recv()
            if phase == 2:
                send(remote(land, land, c_send.at[i, steps], c_recv.at[i, steps], partner))

    def c_wait(i):
        axis = items[i][4][2]
        for steps in range(sizes[axis]):
            land = region(i, 2, lax.rem(spot[axis] + sizes[axis] - steps, sizes[axis]), 1 - core)
            remote(land, land, c_send.at[i, steps], c_recv.at[i, steps], partner).wait_recv()

    hops = Hops(sizes, spot, core)

    bring = [
        pltpu.make_async_copy(shards[0].at[layer, :, pl.ds(JOINT, MOD)], mod_stage.at[layer], side_sem.at[layer])
        for layer in range(layers)
    ]
    bring.append(pltpu.make_async_copy(w_head.at[:, pl.ds(0, 3 * D)], head_stage, side_sem.at[layers]))
    for copy in bring:
        copy.start()

    def low_rows(value):
        return to_low(jnp.concatenate([value, jnp.zeros((SHARE - own, value.shape[1]), jnp.float32)], 0))

    def time_layers():
        for copy in bring:
            copy.wait()
        head_own[...] = low_rows(head_stage[:, :D])
        for layer in range(layers):
            for column in range(0, MOD, D):
                start_at = layer * MOD + column
                mod_own[:, start_at : start_at + D] = low_rows(mod_stage[layer, :, column : column + D])
        for column in range(0, 2 * D, D):
            start_at = layers * MOD + column
            mod_own[:, start_at : start_at + D] = low_rows(head_stage[:, D + column : 2 * D + column])
        lead = lead_turned[:, :FREQS]
        lead = to_low(jnp.concatenate([lead, jnp.zeros((128 - own, FREQS), jnp.float32)], 0))
        for step in range(1, count):
            origin = lax.rem(me + count - step, count)
            remote(
                facts_in, facts.at[origin], facts_send.at[step], facts_recv.at[step], numbered(ways, origin)
            ).wait_recv()
        value = dot_nt(to_low(facts[:, 0, :]), lead[:, :128]) + dot_nt(to_low(facts[:, 1, :]), lead[:, 128:])
        pre_time[...] = value
        totals[0] = dot_nn(to_low(value * sigmoid(value))[:, :SHARE], head_own[...])
        sums[0]()

    def modulation():
        temb = lax.dot_general(
            totals[4], chosen(me, own, 128), (((1,), (0,)), ((), ())),
            precision=lax.Precision.HIGHEST, preferred_element_type=jnp.float32,
        )
        temb_own[...] = temb
        cond = to_low(temb * sigmoid(temb))[:, :SHARE]
        mod_parts[:, MOD_ROWS:, :] = jnp.zeros((count, MOD_TILE[0] - MOD_ROWS, 128), jnp.float32)
        for j in range(0, MOD_ROWS, 4):
            part = dot_nn(cond, mod_own[:, j * 128 : (j + 4) * 128])
            for k in range(4):
                mod_parts[:, j + k, :] = part[:, k * 128 : (k + 1) * 128]
        splits[0]()

    sums = sum_steps(hops, totals, landed, sum_send, sum_recv, sent_all)
    splits = split_steps(
        hops, mod_parts.reshape(sizes + (2,) + MOD_TILE), mod_landed, mods, split_send, split_recv, sent_all
    )
    side = [time_layers] + sums[1:] + [modulation] + splits[1:]

    def prepare():
        small[...] = to_low(facts[:, 8 : 8 + own, :].reshape(D, 128))
        gains = dot_nt(to_low(gain_pick().astype(jnp.float32)), small[...])

        def row(piece):
            tiles_of = [mods[piece * (D // 128) + k : piece * (D // 128) + k + 1, :] for k in range(D // 128)]
            return jnp.concatenate(tiles_of, 1)

        for layer in range(layers):
            for j in range(6):
                block_mods[layer, j : j + 1, :] = row(layer * 6 + j)
            block_mods[layer, 6:7, :] = gains[layer : layer + 1, :]
            block_mods[layer, 7:8, :] = jnp.zeros((1, D), jnp.float32)
        final_mods[...] = jnp.zeros_like(final_mods)
        for j in range(2):
            final_mods[j : j + 1, :] = row(layers * 6 + j)
        for column in range(0, D, 256):
            saved.stream[:, column : column + 256] = dot_nt(noisy[...], small[column : column + 256, :])

    def load(part):
        return pltpu.make_async_copy(
            *weight_parts(whole_weights, (win, wtext, wout))[part], load_sem.at[PARTS.index(part)]
        )

    def emit(name, ref):
        pltpu.make_async_copy(ref, early[name], keep_sem.at[EARLY.index(name)]).start()

    def first_block():
        frame_keep, text_keep = keeps(lengths, noisy.shape[0], text.shape[0])
        yield from block_forward(
            saved, hidden, result, block_mods.at[0], text, frame_keep, text_keep,
            Names(win=win, wtext=wtext, wout=wout), need, lambda part: None, emit,
        )
        for name in NEEDED:
            if name not in KEPT:
                emit(name, getattr(saved, name))

    whole_weights = [
        full(0, member).reshape(sizes[0] * sizes[1] * sizes[2] * 2 * rows[member], 2 * halves[member]) for member in range(members)
    ]
    order = schedule(items, GATHER_LAGS)
    members_of = {"text": 1, "ao": 2, "co": 2, "down": 2}

    def pieces_of(part):
        found = []
        for i, (layer, member, begin, _, _) in enumerate(items):
            if layer == 0 and member == members_of.get(part, 0):
                if part not in ("qkv", "cq") or (begin < 3 * D) == (part == "qkv"):
                    found.append(i)
        return found

    turn = max(order.index((i, 3)) for i in pieces_of("qkv")) + 1
    later = list(order[turn:])
    finished, waited = set(), set()

    def advance(i, phase):
        if phase > 0:
            finish(i, phase - 1)
        if phase < 3:
            start(i, phase)
        else:
            finished.add(i)

    def need(part):
        for i in pieces_of(part):
            while i not in finished:
                advance(*later.pop(0))
            if i not in waited:
                waited.add(i)
                c_wait(i)
                own_put(*items[i][:2])
        load(part).start()
        load(part).wait()

    for i, phase in order[:turn]:
        if phase in (1, 2) and side:
            side.pop(0)()
        advance(i, phase)
    for step in side:
        step()
    side = []
    prepare()
    pace = BLOCK_PARTS / max(len(later), 1)
    for part, _ in enumerate(first_block()):
        if later and part >= pace * (len(order) - turn - len(later)):
            advance(*later.pop(0))
    for i, phase in later:
        advance(i, phase)
    for i in range(len(items)):
        if i not in waited:
            c_wait(i)
    for name in EARLY:
        ref = hidden if name == "hidden" else getattr(saved, name)
        pltpu.make_async_copy(ref, early[name], keep_sem.at[EARLY.index(name)]).wait()
    for layer in range(layers):
        for member in range(members):
            own_put(layer, member)
    for step in range(1, count):
        facts_copy(step).wait_send()
    for sent, _ in pre:
        sent.wait_send()
    for copy in sent_all:
        copy.wait_send()


BLOCK_PARTS = 48
EARLY = ("n1", "n2", "n3", "mixed1", "mixed2", "hidden", "stream", "qkv", "branch1", "stream2", "cq", "ckv", "stream3", "branch3", "stats1", "stats2")


def gather_weights(shards, w_head, facts, lead_turned, lengths, text, noisy, own, halves, ways, number, items):
    layers = shards[0].shape[0]
    rows = [s.shape[1] for s in shards]
    members = len(shards)
    sizes = (ways[0] // 2, 2, ways[1] // 2)
    devices = ways[0] * ways[1]
    count = layers * members
    n = len(items)
    frames, tokens = noisy.shape[0], text.shape[0]
    sem, vmem, full, shape = pltpu.SemaphoreType.DMA, pltpu.VMEM, jnp.float32, jax.ShapeDtypeStruct
    here, there = pl.BlockSpec(memory_space=pltpu.VMEM), pl.BlockSpec(memory_space=pl.ANY)
    scalar = pl.BlockSpec(memory_space=pltpu.SMEM)
    out = pl.pallas_call(
        functools.partial(gather_kernel, ways, rows, halves, items, layers, own),
        out_shape=[
            shape(sizes + (2 * rows[m], 2 * halves[m]), jnp.bfloat16) for _ in range(layers) for m in range(members)
        ]
        + [
            shape((devices,) + facts.shape, full),
            shape((devices, 128), full),
            shape((devices, 128), full),
            shape((layers, 8, D), full),
            shape((8, D), full),
            shape((D, 128), jnp.bfloat16),
            shape((frames, D), full),
            shape((SHARE, D), jnp.bfloat16),
            shape((SHARE, MOD_ROWS * 128), jnp.bfloat16),
        ]
        + [shape(shape_of(name, frames, tokens), KINDS[name]) for name in EARLY],
        in_specs=[there] * (members + 1) + [here] * 2 + [scalar] + [here] * 2,
        out_specs=[there] * count + [here] * 9 + [there] * len(EARLY),
        scratch_shapes=[
            vmem((len(ROUNDS) + 1, devices, D), full),
            vmem((sizes[0] + sizes[1] + sizes[2] - 2, devices, D), full),
            vmem((devices,) + MOD_TILE, full),
        ]
        + split_shapes(sizes, MOD_TILE)
        + [sem((devices,))] * 2
        + [sem((len(ROUNDS), max(sizes)))] * 4
        + [vmem(MOD_TILE, full), vmem((D, JOINT), jnp.bfloat16)]
        + [vmem((text.shape[1], 2 * D), jnp.bfloat16), vmem((2 * D + FF, D), jnp.bfloat16)]
        + [vmem(shape_of(name, frames, tokens), kind) for name, _, kind in SAVED]
        + [vmem((frames, FF), jnp.bfloat16), sem((len(PARTS),)), sem((len(EARLY),))]
        + [vmem((layers, own, MOD), full), vmem((own, 3 * D), full), sem((layers + 1,))]
        + [vmem((layers, 2 * rows[m], halves[m]), full) for m in range(members)]
        + [vmem((layers, 2 * rows[m], halves[m]), jnp.bfloat16) for m in range(members)]
        + [sem((count,))] * 4
        + [sem((n, max(sizes)))] * 8,
        compiler_params=pltpu.CompilerParams(
            collective_id=number, has_side_effects=True, vmem_limit_bytes=VMEM_LIMIT
        ),
    )(*shards, w_head, facts, lead_turned, lengths, text, noisy)
    weights = [
        [out[l * members + m].reshape(-1, 2 * halves[m]) for m in range(members)] for l in range(layers)
    ]
    return weights, out[count : count + 9], dict(zip(EARLY, out[count + 9 :]))


ORDERS = ((0, 2, 1), (0, 1, 2), (2, 0, 1), (1, 0, 2))
GATHER_LAGS = ((-1.5, 0.0, 3.0, 7.5), (-3.0, 0.0, 2.0, 6.5))
SCATTER_LAGS = ((-2.0, 0.0, 3.0, 5.0, 7.0), (-2.0, 0.0, 3.0, 5.0, 7.0))
GATHER_PATTERN = (1, 0, 1, 2, 1, 1, 0, 1, 0, 1, 2, 1, 2, 1, 3, 1, 2, 1)
SCATTER_PATTERN = GATHER_PATTERN[::-1]


def schedule(items, lags):
    steps = []
    for i, item in enumerate(items):
        own = lags[0 if item[4][0] == 0 else 1]
        steps.extend((i + lag, -phase, i) for phase, lag in enumerate(own))
    return [(i, -phase) for _, phase, i in sorted(steps)]


def plan(halves, layers, pattern):
    items = []
    for layer in layers:
        for member, width in enumerate(halves):
            size = width // 4 if width % 512 == 0 else (width // 2 if width % 256 == 0 else 128)
            for start in range(0, width, size):
                items.append((layer, member, start, size, ORDERS[pattern[len(items) % len(pattern)]]))
    return items


RINGS = (2, 1, 1)
ACTS = ("n1", "n2", "n3", "mixed1", "mixed2", "hidden", "g_self", "g_cq", "g_pre", "g_ckv", "g_one", "g_cross", "g_three")


def scatter_kernel(ways, rows, halves, items, layers, own, *refs):
    members = len(rows)
    n = len(items)
    rest = list(refs)

    def take(count):
        taken = rest[:count]
        del rest[:count]
        return taken

    (text_in,) = take(1)
    acts = [dict(zip(ACTS, take(len(ACTS)))) for _ in range(layers)]
    mods_in, small_in, loss_in, facts_in, pre_time, temb_own, head_own, mod_own = take(8)
    outs = take(members)
    grad_mod, grad_time_one, grad_time_two, small_out, final = take(5)
    all_mods, small_rows, totals, landed, squares = take(5)
    small_landed = take(4)
    spread_send, spread_recv, sum_send, sum_recv, split_send, split_recv, end_send, end_recv = take(8)
    ends, end_landed, backs, facts, bring_sem = take(5)
    lefts, rights, text, right_text, hidden, mixes, right_out = take(7)
    ring = take(members)
    whole = take(n)
    parts = [take(n) for _ in range(3)]
    partial = take(n)
    load_sem, c_send, c_recv, *sems, e_send, e_recv, o_sem = rest
    sends, recvs = sems[0::2], sems[1::2]
    sizes, spot, core = place(ways)
    partner = device_at(spot, 1 - core)
    frames = hidden.shape[0]
    sent_all = []
    count = ways[0] * ways[1]
    me = lax.axis_index("dp") * ways[1] + lax.axis_index("fsdp")
    greet_all(ways, me)
    hops = Hops(sizes, spot, core)
    squares[...] = jnp.zeros_like(squares)

    def count_squares(value):
        squares[...] += jnp.broadcast_to(jnp.sum(value * value, (0, 1), keepdims=True), squares.shape)

    temb = temb_own[...]
    share = sigmoid(temb)
    cond = to_low(temb * share)[:, :SHARE]
    gate = sigmoid(pre_time[...])
    act = to_low(pre_time[...] * gate)[:, :SHARE]
    slope_temb = (share * (1.0 + temb * (1.0 - share)))[:, :SHARE]
    slope_time = (gate * (1.0 + pre_time[...] * (1.0 - gate)))[:, :SHARE]
    all_mods[me] = mods_in[...]
    sums = sum_steps(hops, totals, landed, sum_send, sum_recv, sent_all)
    spreads = spread_steps(
        hops, all_mods.reshape(sizes + (2,) + MOD_TILE), spread_send, spread_recv, sent_all
    )
    tile = tuple(small_in.shape[1:])
    splits = split_steps(
        hops, small_rows.reshape(sizes + (2,) + tile), small_landed, small_out, split_send, split_recv, sent_all
    )

    bring = [
        pltpu.make_async_copy(small_in, small_rows, bring_sem.at[0]),
        pltpu.make_async_copy(facts_in.at[:, 0:8], facts, bring_sem.at[1]),
    ]
    for copy in bring:
        copy.start()

    def begin_small():
        for copy in bring:
            copy.wait()
        splits[0]()

    def modulation_part(begin, end):
        back = jnp.zeros_like(backs) if begin == 0 else backs[...]
        for j in range(begin, end):
            cols = slice(j * 128, (j + 1) * 128)
            grad = to_low(all_mods[:, j, :])
            back = back + dot_nt(grad, mod_own[:, cols])
            grad_mod[:, cols] = dot_tn(cond, grad)
        backs[...] = back
        count_squares(grad_mod[:, begin * 128 : end * 128])

    def modulation_back():
        grad_temb = to_low(backs[...] * slope_temb)
        pick = to_low(chosen(me, own, SHARE))
        totals[0] = dot_nt(grad_temb, pick)
        sums[0]()

    def time_back():
        grad_temb = to_low(totals[4])
        grad_time_two[...] = dot_tn(act, grad_temb)
        grad_time = to_low(dot_nt(grad_temb, head_own[...]) * slope_time)
        for j in range(2):
            grad_time_one[:, j * 128 : (j + 1) * 128] = dot_tn(grad_time, to_low(facts[:, j, :]))
        count_squares(grad_time_two[...])
        count_squares(grad_time_one[...])
        count_squares(small_out[...])

    def together(*steps):
        return lambda: [step() for step in steps]

    def rest():
        pass

    side = [together(spreads[0], begin_small)]
    for pair in zip(spreads[1:], splits[1:]):
        side += [rest, together(*pair)]
    parts_of = [functools.partial(modulation_part, j, j + 12) for j in range(0, MOD_ROWS, 12)]
    side += [together(*parts_of[k : k + 2]) for k in range(0, len(parts_of), 2)]
    side += [modulation_back] + sums[1:] + [time_back]

    def send(copy):
        copy.start()
        sent_all.append(copy)

    def loads(layer, member):
        a = acts[layer]
        if member == 0:
            pairs = [(a["n1"], lefts.at[0]), (a["n2"], lefts.at[1]), (a["n3"], lefts.at[2])]
            pairs += [(a["g_self"].at[:, j * D : (j + 1) * D], rights.at[j]) for j in range(3)]
            pairs += [(a["g_cq"], rights.at[3])]
            pairs += [(a["g_pre"].at[:, j * D : (j + 1) * D], rights.at[4 + j]) for j in range(4)]
        elif member == 1:
            pairs = [(a["g_ckv"].at[:, j * D : (j + 1) * D], right_text.at[j]) for j in range(2)]
            if layer == items[0][0]:
                pairs.append((text_in, text))
        else:
            pairs = [(a["mixed1"], mixes.at[0]), (a["mixed2"], mixes.at[1]), (a["hidden"], hidden)]
            for j, name in enumerate(("g_one", "g_cross", "g_three")):
                pairs += [(a[name].at[:, side * (D // 2) : (side + 1) * (D // 2)], right_out.at[side, j]) for side in range(2)]
        return [
            pltpu.make_async_copy(source, target, load_sem.at[layer, member, j])
            for j, (source, target) in enumerate(pairs)
        ]

    def load(layer, member):
        for copy in loads(layer, member):
            copy.start()

    loaded = set()

    def need(layer, member):
        if (layer, member) not in loaded:
            loaded.add((layer, member))
            for copy in loads(layer, member):
                copy.wait()

    def product(i, side, store):
        layer, member, start, size, _ = items[i]
        need(layer, member)
        if member == 0:
            j = start // D
            at = pl.ds(start % D, size)
            left = jnp.where(side == 1, 2, 0 if j < 3 else 1)
            right = rights[side * 4 + j, :, at]
            for row in range(0, D, 384):
                store(pl.ds(row, 384), dot_tn(lefts[left, :, row : row + 384], right))
        elif member == 1:
            right = right_text[side, :, pl.ds(start, size)]
            for row in range(0, text.shape[1], 512):
                store(pl.ds(row, 512), dot_tn(text[:, row : row + 512], right))
        else:
            cols = pl.ds(start, size)
            for j in range(2):
                store(pl.ds(j * D, D), dot_tn(mixes[j], right_out[side, j, :, cols]))

            @pl.loop(0, 4)
            def _(j):
                at = pl.multiple_of(j * D, D)
                store(pl.ds(pl.multiple_of(2 * D + j * D, D), D), dot_tn(hidden[:, pl.ds(at, D)], right_out[side, 2, :, cols]))

    def columns(i, side):
        _, member, start, size, _ = items[i]
        return pl.ds(pl.multiple_of(side * halves[member] + start, 128), size)

    def blocks(ref, i):
        return ref.reshape(sizes + (2 * rows[items[i][1]], items[i][3]))

    ring_at, used = [], {}
    for i, (_, member, *_) in enumerate(items):
        ring_at.append(used.setdefault(member, []))
        ring_at[-1] = len(used[member])
        used[member].append(i)

    def c_copy(i):
        member, size = items[i][1], items[i][3]
        slot = ring_at[i] % RINGS[member]
        return remote(ring[member].at[slot, :, pl.ds(0, size)], whole[i], c_send.at[i], c_recv.at[i], partner)

    def give(i):
        member, size = items[i][1], items[i][3]
        slot = ring_at[i] % RINGS[member]
        if ring_at[i] >= RINGS[member]:
            c_copy(used[member][ring_at[i] - RINGS[member]]).wait_send()
        target = ring[member].at[slot]

        def store(at, value):
            target[at, pl.ds(0, size)] = value.astype(jnp.bfloat16)

        product(i, 1 - core, store)
        c_copy(i).start()

    def combine(i):
        c_copy(i).wait_recv()
        target = whole[i]

        def store(at, value):
            target[at, :] = (target[at, :].astype(jnp.float32) + value).astype(jnp.bfloat16)

        product(i, core, store)
        layer, member = items[i][:2]
        if i == used_last[layer, member] and (layer, member) in after:
            load(*after[layer, member])

    used_last, after, seen_layers = {}, {}, []
    for i, item in enumerate(items):
        used_last[item[:2]] = i
        if item[0] not in seen_layers:
            seen_layers.append(item[0])
    for early, late in zip(seen_layers, seen_layers[1:]):
        for member in range(members):
            after[early, member] = (late, member)

    def way(i):
        return items[i][4][::-1]

    def region(i, phase, place_on):
        order = way(i)
        index = [spot[axis] if axis in order[:phase] else slice(None) for axis in range(3)]
        index[order[phase]] = place_on
        return blocks(whole[i], i).at[tuple(index)]

    def start(i, phase):
        axis = way(i)[phase]
        for steps in range(1, sizes[axis]):
            target = moved(spot, axis, sizes[axis], steps)
            send(
                remote(
                    region(i, phase, target[axis]), parts[phase][i].at[steps - 1],
                    sends[phase].at[i, steps - 1], recvs[phase].at[i, steps - 1], device_at(target, core),
                )
            )

    def owned(i, side):
        height = rows[items[i][1]]
        return partial[i].at[pl.ds(pl.multiple_of(side * height, 8), height)]

    def e_copy(i):
        layer, member = items[i][:2]
        return remote(
            owned(i, 1 - core), outs[member].at[layer, :, columns(i, core)], e_send.at[i], e_recv.at[i], partner
        )

    def o_copy(i):
        layer, member = items[i][:2]
        return pltpu.make_async_copy(owned(i, core), outs[member].at[layer, :, columns(i, core)], o_sem.at[i])

    def finish(i, phase):
        axis = way(i)[phase]
        for steps in range(1, sizes[axis]):
            land = parts[phase][i].at[steps - 1]
            remote(land, land, sends[phase].at[i, steps - 1], recvs[phase].at[i, steps - 1], partner).wait_recv()
        mine = region(i, phase, spot[axis])
        landed = parts[phase][i]

        def total(index):
            value = mine[index].astype(jnp.float32)
            for steps in range(1, sizes[axis]):
                value = value + landed[(steps - 1, *index)].astype(jnp.float32)
            return value

        if phase == 2:
            pieces_sum = total((Ellipsis,))
            partial[i][...] = pieces_sum
            count_squares(pieces_sum)
            e_copy(i).start()
            o_copy(i).start()
        else:
            left = [sizes[other] for other in range(3) if other not in way(i)[: phase + 1]]

            @pl.loop(0, left[0])
            def _(index):
                mine[index] = total((index,)).astype(jnp.bfloat16)

    for member in range(members):
        load(items[0][0], member)
    for i, step in schedule(items, SCATTER_LAGS):
        if step == 0:
            give(i)
            continue
        if step in (1, 4) and side:
            side.pop(0)()
        if step == 1:
            combine(i)
        else:
            finish(i, step - 2)
        if step < 4:
            start(i, step - 1)
    for step in side:
        step()
    lane = lax.broadcasted_iota(jnp.int32, squares.shape, 0)
    ends[...] = jnp.where(lane == 0, squares[...], loss_in[...])
    for step in range(1, count):
        send(
            remote(
                ends, end_landed.at[me], end_send.at[step], end_recv.at[step],
                numbered(ways, lax.rem(me + step, count)),
            )
        )
    end_landed[me] = ends[...]
    for step in range(1, count):
        origin = lax.rem(me + count - step, count)
        remote(
            ends, end_landed.at[origin], end_send.at[step], end_recv.at[step], numbered(ways, origin)
        ).wait_recv()
    final[...] = jnp.sum(end_landed[...], 0)
    for i in range(n):
        e_copy(i).wait()
        o_copy(i).wait()
    for member in range(members):
        for i in used[member][-RINGS[member] :]:
            c_copy(i).wait_send()
    for copy in sent_all:
        copy.wait_send()


def scatter_grads(kept, text, rest, own, rows, halves, ways, number, items):
    layers, members = len(kept), len(rows)
    sizes = (ways[0] // 2, 2, ways[1] // 2)
    n = len(items)
    sem = pltpu.SemaphoreType.DMA
    low = jnp.bfloat16
    chips = sizes[0] * sizes[1] * sizes[2]
    frames, tokens = kept[0]["n1"].shape[0], text.shape[0]
    most = [max(s for _, m, _, s, _ in items if m == member) for member in range(members)]
    vmem = pltpu.VMEM

    def part(item, phase):
        _, member, _, size, order = item
        order = order[::-1]
        left = tuple(sizes[axis] for axis in range(3) if axis not in order[: phase + 1])
        return vmem((sizes[order[phase]] - 1, *left, 2 * rows[member], size), low)

    full, devices = jnp.float32, 2 * chips
    tile = tuple(rest[1].shape[1:])
    sums = sem((len(ROUNDS), max(sizes)))
    scratch = [
        vmem((devices,) + MOD_TILE, full),
        vmem((devices,) + tile, full),
        vmem((len(ROUNDS) + 1, devices, D), full),
        vmem((sizes[0] + sizes[1] + sizes[2] - 2, devices, D), full),
        vmem((8, 128), full),
    ]
    scratch += split_shapes(sizes, tile) + [sums] * 6 + [sem((devices,))] * 2
    scratch += [vmem((8, 128), full), vmem((devices, 8, 128), full)]
    scratch += [vmem((devices, SHARE), full), vmem((devices, 8, 128), full), sem((2,))]
    scratch += [
        vmem((3, frames, D), low),
        vmem((8, frames, D), low),
        vmem(text.shape, low),
        vmem((2, tokens, D), low),
        vmem((frames, FF), low),
        vmem((2, frames, D), low),
        vmem((2, 3, frames, D // 2), low),
    ]
    scratch += [vmem((RINGS[m], chips * 2 * rows[m], most[m]), low) for m in range(members)]
    scratch += [vmem((chips * 2 * rows[m], s), low) for _, m, _, s, _ in items]
    scratch += [part(item, phase) for phase in range(3) for item in items]
    scratch += [vmem((2 * rows[m], s), jnp.float32) for _, m, _, s, _ in items]
    scratch += [sem((layers, members, 11))] + [sem((n,))] * 2 + [sem((n, max(sizes)))] * 6 + [sem((n,))] * 3
    flat = [text] + [k[name] for k in kept for name in ACTS]
    here, there = pl.BlockSpec(memory_space=vmem), pl.BlockSpec(memory_space=pl.ANY)
    return pl.pallas_call(
        functools.partial(scatter_kernel, ways, rows, halves, items, layers, own),
        out_shape=[
            jax.ShapeDtypeStruct((layers, rows[m], 2 * halves[m]), full) for m in range(members)
        ]
        + [
            jax.ShapeDtypeStruct((SHARE, MOD_ROWS * 128), full),
            jax.ShapeDtypeStruct((SHARE, FREQS), full),
            jax.ShapeDtypeStruct((SHARE, D), full),
            jax.ShapeDtypeStruct(tile, full),
            jax.ShapeDtypeStruct((8, 128), full),
        ],
        in_specs=[there] * len(flat) + [here, there, here, there] + [here] * (len(rest) - 4),
        out_specs=[there] * members + [here] * 5,
        scratch_shapes=scratch,
        compiler_params=pltpu.CompilerParams(
            collective_id=number, has_side_effects=True, vmem_limit_bytes=VMEM_LIMIT
        ),
    )(*flat, *rest)


def to_low(values):
    return values.astype(jnp.bfloat16)


def norm_rows(values):
    centred = values - jnp.mean(values, -1, keepdims=True)
    return centred * lax.rsqrt(jnp.mean(centred * centred, -1, keepdims=True) + EPSILON)


def modulate(stream, shift, scale_part):
    return norm_rows(stream) * (1.0 + scale_part) + shift


def gained_norm(stream, gain):
    return norm_rows(stream) * gain


def dense(left, right):
    return jnp.dot(left, right, preferred_element_type=jnp.float32)


def dense_back(left, right):
    return lax.dot_general(left, right, (((1,), (1,)), ((), ())), preferred_element_type=jnp.float32)


def weight_grad(left, right):
    return lax.dot_general(left, right, (((0,), (0,)), ((), ())), preferred_element_type=jnp.float32)


def split_heads(values):
    return values.reshape(values.shape[0], HEADS, HEAD_DIM)


def attention(queries, keys, values, keep):
    scores = jnp.einsum(
        "qhd,khd->hqk", split_heads(queries), split_heads(keys), preferred_element_type=jnp.float32
    ) * HEAD_DIM ** (-0.5)
    scores = jnp.where(keep[None, None, :], scores, NEGATIVE)
    shifted = jnp.exp(scores - jnp.max(scores, -1, keepdims=True))
    probs = shifted / jnp.sum(shifted, -1, keepdims=True)
    mixed = jnp.einsum(
        "hqk,khd->qhd", to_low(probs), split_heads(values), preferred_element_type=jnp.float32
    )
    return (to_low(mixed.reshape(queries.shape)), probs)


def attention_back(queries, keys, values, probs, grad_mixed):
    grad_heads = split_heads(to_low(grad_mixed))
    grad_values = jnp.einsum(
        "hqk,qhd->khd", to_low(probs), grad_heads, preferred_element_type=jnp.float32
    )
    grad_probs = jnp.einsum(
        "qhd,khd->hqk", grad_heads, split_heads(values), preferred_element_type=jnp.float32
    )
    grad_scores = to_low(probs * (grad_probs - jnp.sum(probs * grad_probs, -1, keepdims=True)))
    grad_queries = jnp.einsum(
        "hqk,khd->qhd", grad_scores, split_heads(keys), preferred_element_type=jnp.float32
    ) * HEAD_DIM ** (-0.5)
    grad_keys = jnp.einsum(
        "hqk,qhd->khd", grad_scores, split_heads(queries), preferred_element_type=jnp.float32
    ) * HEAD_DIM ** (-0.5)
    return (
        grad_queries.reshape(queries.shape),
        grad_keys.reshape(keys.shape),
        grad_values.reshape(values.shape),
    )


def noise_level(steps):
    phase = (steps.astype(jnp.float32) / 1000.0 + 0.008) / 1.008 * (math.pi / 2)
    return jnp.cos(phase) ** 2


def time_features(steps):
    half_width = FREQS // 2
    frequency = jnp.exp(-math.log(10000.0) * jnp.arange(half_width, dtype=jnp.float32) / half_width)
    angles = steps.astype(jnp.float32)[:, None] * frequency[None, :]
    return jnp.concatenate([jnp.cos(angles), jnp.sin(angles)], -1)


def layer_forward(stream, modulation, text_low, frame_keep, text_keep, weights):
    w_joint, w_textkv, w_back, gain = weights
    normed_one, pull_one = jax.vjp(modulate, stream, modulation[:D], modulation[D : 2 * D])
    input_one = to_low(normed_one)
    self_proj = to_low(dense(input_one, w_joint[:, : 3 * D]))
    mixed_one, probs_one = attention(
        self_proj[:, :D], self_proj[:, D : 2 * D], self_proj[:, 2 * D :], frame_keep
    )
    branch_one = dense(mixed_one, w_back[:D])
    stream_two = stream + modulation[2 * D : 3 * D] * branch_one
    normed_two, pull_two = jax.vjp(gained_norm, stream_two, gain)
    input_two = to_low(normed_two)
    cross_query = to_low(dense(input_two, w_joint[:, 3 * D : 4 * D]))
    cross_kv = to_low(dense(text_low, w_textkv))
    mixed_two, probs_two = attention(cross_query, cross_kv[:, :D], cross_kv[:, D:], text_keep)
    stream_three = stream_two + dense(mixed_two, w_back[D : 2 * D])
    normed_three, pull_three = jax.vjp(
        modulate, stream_three, modulation[3 * D : 4 * D], modulation[4 * D : 5 * D]
    )
    input_three = to_low(normed_three)
    hidden_act, pull_act = jax.vjp(jax.nn.gelu, dense(input_three, w_joint[:, 4 * D :]))
    hidden_low = to_low(hidden_act)
    branch_three = dense(hidden_low, w_back[2 * D :])
    result = stream_three + modulation[5 * D :] * branch_three
    saved = (
        pull_one,
        input_one,
        self_proj,
        mixed_one,
        probs_one,
        branch_one,
        pull_two,
        input_two,
        cross_query,
        cross_kv,
        mixed_two,
        probs_two,
        pull_three,
        input_three,
        pull_act,
        hidden_low,
        branch_three,
    )
    return (result, saved)


def layer_backward(saved, grad_out, modulation, text_low, weights):
    w_joint, w_textkv, w_back, gain = weights
    (
        pull_one,
        input_one,
        self_proj,
        mixed_one,
        probs_one,
        branch_one,
        pull_two,
        input_two,
        cross_query,
        cross_kv,
        mixed_two,
        probs_two,
        pull_three,
        input_three,
        pull_act,
        hidden_low,
        branch_three,
    ) = saved
    grad_three = to_low(grad_out * modulation[5 * D :])
    grad_gate_two = jnp.sum(grad_out * branch_three, 0)
    grad_down = weight_grad(hidden_low, grad_three)
    (grad_pre,) = pull_act(dense_back(grad_three, w_back[2 * D :]))
    grad_pre = to_low(grad_pre)
    grad_up = weight_grad(input_three, grad_pre)
    grad_inner, grad_shift_two, grad_scale_two = pull_three(dense_back(grad_pre, w_joint[:, 4 * D :]))
    grad_stream = grad_out + grad_inner
    grad_cross_out = to_low(grad_stream)
    grad_co = weight_grad(mixed_two, grad_cross_out)
    grad_cq, grad_ck, grad_cv = attention_back(
        cross_query,
        cross_kv[:, :D],
        cross_kv[:, D:],
        probs_two,
        dense_back(grad_cross_out, w_back[D : 2 * D]),
    )
    grad_cq = to_low(grad_cq)
    grad_text_w = weight_grad(text_low, to_low(jnp.concatenate([grad_ck, grad_cv], -1)))
    grad_query_w = weight_grad(input_two, grad_cq)
    grad_inner, grad_gain = pull_two(dense_back(grad_cq, w_joint[:, 3 * D : 4 * D]))
    grad_stream = grad_stream + grad_inner
    grad_one = to_low(grad_stream * modulation[2 * D : 3 * D])
    grad_gate_one = jnp.sum(grad_stream * branch_one, 0)
    grad_ao = weight_grad(mixed_one, grad_one)
    grad_q, grad_k, grad_v = attention_back(
        self_proj[:, :D],
        self_proj[:, D : 2 * D],
        self_proj[:, 2 * D :],
        probs_one,
        dense_back(grad_one, w_back[:D]),
    )
    grad_self = to_low(jnp.concatenate([grad_q, grad_k, grad_v], -1))
    grad_self_w = weight_grad(input_one, grad_self)
    grad_inner, grad_shift_one, grad_scale_one = pull_one(dense_back(grad_self, w_joint[:, : 3 * D]))
    grad_stream = grad_stream + grad_inner
    grad_mod = jnp.concatenate(
        [grad_shift_one, grad_scale_one, grad_gate_one, grad_shift_two, grad_scale_two, grad_gate_two]
    )
    grads = (
        jnp.concatenate([grad_self_w, grad_query_w, grad_up], 1),
        grad_text_w,
        jnp.concatenate([grad_ao, grad_co, grad_down], 0),
    )
    return (grad_stream, grad_mod, grads, grad_gain)


ROOT = math.sqrt(2.0 / math.pi)
CUBE = 0.044715
CHUNK = 160
WIDE = 512


def dot_nn(left, right):
    return lax.dot_general(left, right, (((1,), (0,)), ((), ())), preferred_element_type=jnp.float32)


def dot_nt(left, right):
    return lax.dot_general(left, right, (((1,), (1,)), ((), ())), preferred_element_type=jnp.float32)


def dot_tn(left, right):
    return lax.dot_general(left, right, (((0,), (0,)), ((), ())), preferred_element_type=jnp.float32)


def over_rows(count, step):
    @pl.loop(0, count // CHUNK)
    def _(index):
        step(pl.ds(pl.multiple_of(index * CHUNK, CHUNK), CHUNK))


def over_columns(count, width, step):
    for index in range(count // width):
        step(index * width)
        yield


def scaled(values):
    centred = values - jnp.mean(values, -1, keepdims=True)
    factor = lax.rsqrt(jnp.mean(centred * centred, -1, keepdims=True) + EPSILON)
    return centred * factor, factor


def norm_pull(normed, factor, grad):
    middle = jnp.mean(grad, -1, keepdims=True)
    along = jnp.mean(grad * normed, -1, keepdims=True)
    return factor * (grad - middle - normed * along)


def row_sum(values):
    return jnp.sum(values, 0, keepdims=True)


def attend(q_at, k_at, v_at, keep, stats, store):
    first = lax.broadcasted_iota(jnp.int32, (1, 2 * HEAD_DIM), 1) < HEAD_DIM

    for index in range(HEADS // 2):
        query, key = q_at(index) * HEAD_DIM ** (-0.5), k_at(index)
        zero = jnp.zeros_like(query)
        value = jnp.transpose(v_at(index))
        outs = []
        for head in range(2):
            mine = jnp.where(first, query, zero) if head == 0 else jnp.where(first, zero, query)
            scores = jnp.where(keep, dot_nt(key, mine), NEGATIVE)
            top = jnp.max(scores, 0, keepdims=True)
            shifted = jnp.exp(scores - top)
            total = jnp.sum(shifted, 0, keepdims=True)
            stats[2 * index + head : 2 * index + head + 1, :] = top + jnp.log(total)
            probs = to_low(shifted * (1.0 / total))
            outs.append(dot_nn(value[head * HEAD_DIM : (head + 1) * HEAD_DIM], probs))
        store(index, jnp.transpose(to_low(jnp.concatenate(outs, 0))))
        yield


def attend_back(q_at, k_at, v_at, grad_at, keep, stats, store):
    first = lax.broadcasted_iota(jnp.int32, (1, 2 * HEAD_DIM), 1) < HEAD_DIM

    for index in range(HEADS // 2):
        query, key = q_at(index) * HEAD_DIM ** (-0.5), k_at(index)
        value, grad = v_at(index), grad_at(index)
        key_turned = jnp.transpose(key * HEAD_DIM ** (-0.5))
        zero, zero_value = jnp.zeros_like(query), jnp.zeros_like(value)
        queries, keys, values = [], [], []
        for head in range(2):
            mine = jnp.where(first, query, zero) if head == 0 else jnp.where(first, zero, query)
            mine_value = jnp.where(first, value, zero_value) if head == 0 else jnp.where(first, zero_value, value)
            scores = jnp.where(keep, dot_nt(key, mine), NEGATIVE)
            probs = jnp.exp(scores - stats[2 * index + head : 2 * index + head + 1, :])
            values.append(dot_nn(to_low(probs), grad))
            grad_probs = dot_nt(mine_value, grad)
            inner = jnp.sum(probs * grad_probs, 0, keepdims=True)
            grad_scores = to_low(probs * (grad_probs - inner))
            keys.append(dot_nn(grad_scores, query))
            queries.append(dot_nn(key_turned[head * HEAD_DIM : (head + 1) * HEAD_DIM], grad_scores))
        store(
            index,
            jnp.transpose(to_low(jnp.concatenate(queries, 0))),
            to_low(jnp.where(first, *keys)),
            to_low(jnp.where(first, *values)),
        )
        yield


def tile_of(ref, base):
    return lambda index: ref[:, base + index * 2 * HEAD_DIM : base + (index + 1) * 2 * HEAD_DIM]


def run(steps):
    for _ in steps:
        pass


SAVED = (
    ("stream", D, jnp.float32),
    ("n1", D, jnp.bfloat16),
    ("qkv", 3 * D, jnp.bfloat16),
    ("mixed1", D, jnp.bfloat16),
    ("branch1", D, jnp.float32),
    ("stream2", D, jnp.float32),
    ("n2", D, jnp.bfloat16),
    ("cq", D, jnp.bfloat16),
    ("ckv", 2 * D, jnp.bfloat16),
    ("mixed2", D, jnp.bfloat16),
    ("stream3", D, jnp.float32),
    ("n3", D, jnp.bfloat16),
    ("branch3", D, jnp.float32),
    ("stats1", None, jnp.float32),
    ("stats2", None, jnp.float32),
)
GRADS = (
    ("g_self", 3 * D),
    ("g_cq", D),
    ("g_pre", FF),
    ("g_ckv", 2 * D),
    ("g_one", D),
    ("g_cross", D),
    ("g_three", D),
)
PARTS = ("qkv", "cq", "up", "text", "ao", "co", "down")
KEPT = ("n1", "n2", "n3", "mixed1", "mixed2", "hidden") + tuple(name for name, _ in GRADS)


NEEDED = ("stream", "qkv", "branch1", "stream2", "cq", "ckv", "stream3", "n3", "branch3", "stats1", "stats2")


class Names:
    def __init__(self, **refs):
        self.__dict__.update(refs)


def block_forward(s, hidden, result, mods, text, frame_keep, text_keep, w, need, done, emit):
    frames = s.stream.shape[0]

    def norm_one(rows):
        normed, _ = scaled(s.stream[rows, :])
        s.n1[rows, :] = to_low(normed * (1.0 + mods[1:2, :]) + mods[0:1, :])

    over_rows(frames, norm_one)
    yield
    emit("n1", s.n1)
    need("qkv")

    def project(column):
        cols = pl.ds(column, 256)
        s.qkv[:, cols] = to_low(dot_nn(s.n1[...], w.win[:, cols]))

    yield from over_columns(3 * D, 256, project)
    done("qkv")

    def mix_one(index, value):
        s.mixed1[:, index * 128 : (index + 1) * 128] = value

    yield from attend(tile_of(s.qkv, 0), tile_of(s.qkv, D), tile_of(s.qkv, 2 * D), frame_keep, s.stats1, mix_one)
    emit("mixed1", s.mixed1)
    need("ao")

    def branch_one(column):
        cols = pl.ds(column, 256)
        branch = dot_nn(s.mixed1[...], w.wout[0:D, cols])
        s.branch1[:, cols] = branch
        s.stream2[:, cols] = s.stream[:, cols] + mods[2:3, cols] * branch

    yield from over_columns(D, 256, branch_one)
    done("ao")

    def norm_two(rows):
        normed, _ = scaled(s.stream2[rows, :])
        s.n2[rows, :] = to_low(normed * mods[6:7, :])

    over_rows(frames, norm_two)
    yield
    emit("n2", s.n2)
    need("cq")

    def project_cross(column):
        cols = pl.ds(column, 256)
        s.cq[:, cols] = to_low(dot_nn(s.n2[...], w.win[:, pl.ds(3 * D + column, 256)]))

    yield from over_columns(D, 256, project_cross)
    done("cq")
    need("text")

    def project_text(column):
        cols = pl.ds(column, 256)
        s.ckv[:, cols] = to_low(dot_nn(text[...], w.wtext[:, cols]))

    yield from over_columns(2 * D, 256, project_text)
    done("text")

    def mix_two(index, value):
        s.mixed2[:, index * 128 : (index + 1) * 128] = value

    yield from attend(tile_of(s.cq, 0), tile_of(s.ckv, 0), tile_of(s.ckv, D), text_keep, s.stats2, mix_two)
    emit("mixed2", s.mixed2)
    need("co")

    def branch_two(column):
        cols = pl.ds(column, 256)
        s.stream3[:, cols] = s.stream2[:, cols] + dot_nn(s.mixed2[...], w.wout[D : 2 * D, cols])

    yield from over_columns(D, 256, branch_two)
    done("co")

    def norm_three(rows):
        normed, _ = scaled(s.stream3[rows, :])
        s.n3[rows, :] = to_low(normed * (1.0 + mods[4:5, :]) + mods[3:4, :])

    over_rows(frames, norm_three)
    yield
    emit("n3", s.n3)
    need("up")

    def expand(column):
        upper = dot_nn(s.n3[...], w.win[:, pl.ds(4 * D + column, WIDE)])
        tanh = jnp.tanh(ROOT * (upper + CUBE * (upper * upper * upper)))
        hidden[:, pl.ds(column, WIDE)] = to_low(0.5 * upper * (1.0 + tanh))

    yield from over_columns(FF, WIDE, expand)
    done("up")
    emit("hidden", hidden)
    need("down")

    def branch_three(column):
        cols = pl.ds(column, 256)
        branch = dot_nn(hidden[...], w.wout[2 * D :, cols])
        s.branch3[:, cols] = branch
        result[:, cols] = s.stream3[:, cols] + mods[5:6, cols] * branch

    yield from over_columns(D, 256, branch_three)
    done("down")


def block_backward(s, g, grad, mods, grad_mods, inner, mixed, frame_keep, text_keep, w, need, done, emit):
    frames = s.stream.shape[0]
    grad_mods[...] = jnp.zeros_like(grad_mods)

    def gate_three(rows):
        grad_out = grad[rows, :]
        g.g_three[rows, :] = to_low(grad_out * mods[5:6, :])
        grad_mods[5:6, :] += row_sum(grad_out * s.branch3[rows, :])

    over_rows(frames, gate_three)
    yield
    emit("g_three", g.g_three)
    need("down")
    need("up")

    def shrink(column):
        wide = pl.ds(column, WIDE)
        back = dot_nt(g.g_three[...], w.wout[pl.ds(2 * D + column, WIDE), :])
        upper = dot_nn(s.n3[...], w.win[:, pl.ds(4 * D + column, WIDE)])
        square = upper * upper
        tanh = jnp.tanh(ROOT * (upper + CUBE * (square * upper)))
        slope = 0.5 * (1.0 + tanh) + (0.5 * ROOT) * upper * (1.0 - tanh * tanh) * (1.0 + (3.0 * CUBE) * square)
        g.g_pre[:, wide] = to_low(back * slope)

    yield from over_columns(FF, WIDE, shrink)
    done("down")
    emit("g_pre", g.g_pre)

    def inner_three(column):
        inner[:, pl.ds(column, 256)] = dot_nt(g.g_pre[...], w.win[pl.ds(column, 256), 4 * D :])

    yield from over_columns(D, 256, inner_three)
    done("up")

    def pull_three(rows):
        normed, factor = scaled(s.stream3[rows, :])
        back = inner[rows, :]
        grad_mods[3:4, :] += row_sum(back)
        grad_mods[4:5, :] += row_sum(back * normed)
        total = grad[rows, :] + norm_pull(normed, factor, back * (1.0 + mods[4:5, :]))
        grad[rows, :] = total
        g.g_cross[rows, :] = to_low(total)

    over_rows(frames, pull_three)
    yield
    emit("g_cross", g.g_cross)
    need("co")

    def back_cross(column):
        mixed[:, pl.ds(column, 256)] = to_low(dot_nt(g.g_cross[...], w.wout[pl.ds(D + column, 256), :]))

    yield from over_columns(D, 256, back_cross)
    done("co")

    def store_cross(index, grad_query, grad_key, grad_value):
        cols = slice(index * 128, (index + 1) * 128)
        g.g_cq[:, cols] = grad_query
        g.g_ckv[:, cols] = grad_key
        g.g_ckv[:, D + index * 128 : D + (index + 1) * 128] = grad_value

    yield from attend_back(
        tile_of(s.cq, 0), tile_of(s.ckv, 0), tile_of(s.ckv, D), tile_of(mixed, 0), text_keep, s.stats2, store_cross
    )
    emit("g_cq", g.g_cq)
    emit("g_ckv", g.g_ckv)
    need("cq")

    def inner_two(column):
        inner[:, pl.ds(column, 256)] = dot_nt(g.g_cq[...], w.win[pl.ds(column, 256), 3 * D : 4 * D])

    yield from over_columns(D, 256, inner_two)
    done("cq")

    def pull_two(rows):
        normed, factor = scaled(s.stream2[rows, :])
        back = inner[rows, :]
        grad_mods[6:7, :] += row_sum(back * normed)
        total = grad[rows, :] + norm_pull(normed, factor, back * mods[6:7, :])
        grad[rows, :] = total
        g.g_one[rows, :] = to_low(total * mods[2:3, :])
        grad_mods[2:3, :] += row_sum(total * s.branch1[rows, :])

    over_rows(frames, pull_two)
    yield
    emit("g_one", g.g_one)
    need("ao")

    def back_self(column):
        mixed[:, pl.ds(column, 256)] = to_low(dot_nt(g.g_one[...], w.wout[pl.ds(column, 256), :]))

    yield from over_columns(D, 256, back_self)
    done("ao")

    def store_self(index, grad_query, grad_key, grad_value):
        cols = slice(index * 128, (index + 1) * 128)
        g.g_self[:, cols] = grad_query
        g.g_self[:, D + index * 128 : D + (index + 1) * 128] = grad_key
        g.g_self[:, 2 * D + index * 128 : 2 * D + (index + 1) * 128] = grad_value

    yield from attend_back(
        tile_of(s.qkv, 0), tile_of(s.qkv, D), tile_of(s.qkv, 2 * D), tile_of(mixed, 0), frame_keep, s.stats1, store_self
    )
    emit("g_self", g.g_self)
    need("qkv")

    def inner_one(column):
        inner[:, pl.ds(column, 256)] = dot_nt(g.g_self[...], w.win[pl.ds(column, 256), : 3 * D])

    yield from over_columns(D, 256, inner_one)
    done("qkv")

    def pull_one(rows):
        normed, factor = scaled(s.stream[rows, :])
        back = inner[rows, :]
        grad_mods[0:1, :] += row_sum(back)
        grad_mods[1:2, :] += row_sum(back * normed)
        grad[rows, :] = grad[rows, :] + norm_pull(normed, factor, back * (1.0 + mods[1:2, :]))

    over_rows(frames, pull_one)
    yield


def heights(frames, tokens):
    return {name: tokens if name in ("ckv", "g_ckv") else 16 if name in ("stats1", "stats2") else frames for name in WIDTHS}


WIDTHS = {**{name: width for name, width, _ in SAVED}, **dict(GRADS), "hidden": FF}
KINDS = {**{name: kind for name, _, kind in SAVED}, **{name: jnp.bfloat16 for name, _ in GRADS}, "hidden": jnp.bfloat16}


def shape_of(name, frames, tokens):
    return (heights(frames, tokens)[name], WIDTHS[name] or frames)


def weight_parts(source, target):
    (w_in, w_text, w_out), (win, wtext, wout) = source, target
    return {
        "qkv": (w_in.at[:, : 3 * D], win.at[:, : 3 * D]),
        "cq": (w_in.at[:, 3 * D : 4 * D], win.at[:, 3 * D : 4 * D]),
        "up": (w_in.at[:, 4 * D :], win.at[:, 4 * D :]),
        "text": (w_text, wtext),
        "ao": (w_out.at[:D], wout.at[:D]),
        "co": (w_out.at[D : 2 * D], wout.at[D : 2 * D]),
        "down": (w_out.at[2 * D :], wout.at[2 * D :]),
    }


def keeps(lengths, frames, tokens):
    return (
        lax.broadcasted_iota(jnp.int32, (frames, 1), 0) < lengths[0],
        lax.broadcasted_iota(jnp.int32, (tokens, 1), 0) < lengths[1],
    )


def lanes(first, count):
    lane = lax.broadcasted_iota(jnp.int32, (1, 128), 1)
    return jnp.logical_and(lane >= first, lane < first + count)


def gain_pick():
    row, lane = (lax.broadcasted_iota(jnp.int32, (8, 128), axis) for axis in range(2))
    return jnp.logical_and(row < LAYERS, lane == GAIN_LANE + row)


LEAD_LANE = 32
GAIN_LANE = 64


def model_kernel(channels, *refs):
    refs = list(refs)

    def take(count):
        taken = refs[:count]
        del refs[:count]
        return taken

    lengths, facts, stream_ref, mods_ref, final_mods, text, noise, noisy, small = take(9)
    weights = [take(3) for _ in range(LAYERS)]
    early = [dict(zip(NEEDED, take(len(NEEDED)))) for _ in range(LAYERS - 1)]
    end_ref, grad_small, grad_tile = take(3)
    kept_out = [dict(zip(KEPT if layer == LAYERS - 1 else GRAD_NAMES, take(len(KEPT) if layer == LAYERS - 1 else len(GRADS)))) for layer in range(LAYERS)]
    win, wtext, wout = take(3)
    saved = [Names(**dict(zip((name for name, *_ in SAVED), take(len(SAVED)))))]
    for _ in range(LAYERS - 1):
        saved.insert(0, Names(**dict(zip(NEEDED, take(len(NEEDED))))))
    g = Names(**dict(zip((name for name, _ in GRADS), take(len(GRADS)))))
    hidden, inner, mixed, final_low, grad_ref, grad_mods_ref, grad_final = take(7)
    load_sem, keep_sem, early_sem = refs
    w = Names(win=win, wtext=wtext, wout=wout)
    frames, tokens = noisy.shape[0], text.shape[0]
    frame_keep, text_keep = keeps(lengths, frames, tokens)
    last = LAYERS - 1

    def load(layer, part):
        return pltpu.make_async_copy(
            *weight_parts(weights[layer], (win, wtext, wout))[part], load_sem.at[PARTS.index(part)]
        )

    def early_copies(layer):
        return [
            pltpu.make_async_copy(early[layer][name], getattr(saved[layer], name), early_sem.at[layer, j])
            for j, name in enumerate(NEEDED)
        ]

    flying = {}

    def keep(layer):
        def emit(name, ref):
            copy = pltpu.make_async_copy(
                ref, kept_out[layer][name], keep_sem.at[layer, KEPT.index(name)]
            )
            copy.start()
            flying[name, layer] = copy

        return emit

    def settle(layer, names):
        for name in names:
            copy = flying.pop((name, layer), None)
            if copy is not None:
                copy.wait()

    def nothing(part):
        pass

    for part in ("qkv", "ao", "cq", "text", "co", "up", "down"):
        load(last, part).start()
    for layer in range(last):
        for copy in early_copies(layer):
            copy.start()
    over_rows(frames, lambda rows: saved[last].stream.__setitem__((rows, slice(None)), stream_ref[rows, :]))
    run(
        block_forward(
            saved[last], hidden, grad_ref, mods_ref.at[last], text, frame_keep, text_keep, w,
            lambda part: load(last, part).wait(), nothing, keep(last),
        )
    )

    def norm_final(rows):
        normed, _ = scaled(grad_ref[rows, :])
        final_low[rows, :] = to_low(normed * (1.0 + final_mods[1:2, :]) + final_mods[0:1, :])

    over_rows(frames, norm_final)
    counted = lax.broadcasted_iota(jnp.int32, (frames, 1), 0) < lengths[0]
    error = dot_nn(final_low[...], small[...]) - noise[...]
    error = jnp.where(jnp.logical_and(counted, lanes(0, channels)), error, 0.0)
    row, lane = (lax.broadcasted_iota(jnp.int32, end_ref.shape, axis) for axis in range(2))
    own = jnp.where(jnp.logical_and(row == 2, lane == 0), jnp.full(end_ref.shape, lengths[0].astype(jnp.float32)), 0.0)
    end_ref[...] = jnp.where(row == 1, jnp.broadcast_to(row_sum(error * error), end_ref.shape), own)
    factor = 2.0 / jnp.sum(facts[:, 2, :], (0, 1), keepdims=True)
    grad_pred = to_low(error * factor)
    grad_small[...] = dot_tn(final_low[...], grad_pred)
    inner[...] = dot_nt(grad_pred, small[...])
    grad_final[...] = jnp.zeros_like(grad_final)

    def pull_final(rows):
        normed, factor = scaled(grad_ref[rows, :])
        back = inner[rows, :]
        grad_final[0:1, :] += row_sum(back)
        grad_final[1:2, :] += row_sum(back * normed)
        grad_ref[rows, :] = norm_pull(normed, factor, back * (1.0 + final_mods[1:2, :]))

    over_rows(frames, pull_final)
    for layer in reversed(range(LAYERS)):
        if layer < last:
            settle(layer + 1, [name for name, _ in GRADS])
            for copy in early_copies(layer):
                copy.wait()
        run(
            block_backward(
                saved[layer], g, grad_ref, mods_ref.at[layer], grad_mods_ref.at[layer], inner, mixed,
                frame_keep, text_keep, w,
                nothing if layer == last else (lambda part: load(layer, part).wait()),
                nothing if layer == 0 else (lambda part: load(layer - 1, part).start()),
                keep(layer),
            )
        )
    over_rows(frames, lambda rows: final_low.__setitem__((rows, slice(None)), to_low(grad_ref[rows, :])))
    gains = jnp.concatenate(
        [grad_mods_ref[layer, 6:7, :] for layer in range(LAYERS)] + [jnp.zeros((8 - LAYERS, D), jnp.float32)], 0
    )
    grad_small[...] += dot_tn(final_low[...], noisy[...]) + lax.dot_general(
        gains, gain_pick().astype(jnp.float32), (((0,), (0,)), ((), ())),
        precision=lax.Precision.HIGHEST, preferred_element_type=jnp.float32,
    )
    grad_tile[...] = jnp.zeros_like(grad_tile)
    pieces = [(grad_mods_ref.at[layer], j) for layer in range(LAYERS) for j in range(6)]
    pieces += [(grad_final, j) for j in range(2)]
    for p, (ref, j) in enumerate(pieces):
        for k in range(D // 128):
            part = ref[j : j + 1, k * 128 : (k + 1) * 128]
            at = p * (D // 128) + k
            grad_tile[at : at + 1, :] = to_low(part).astype(jnp.float32)
    for layer in range(LAYERS):
        settle(layer, KEPT)


GRAD_NAMES = tuple(name for name, _ in GRADS)


def run_model(lengths, facts, stream, mods, final_mods, text, noise, noisy, small, weights, early, channels):
    frames, tokens = noisy.shape[0], text.shape[0]
    low, full = jnp.bfloat16, jnp.float32
    shape = jax.ShapeDtypeStruct
    here, there = pl.BlockSpec(memory_space=pltpu.VMEM), pl.BlockSpec(memory_space=pl.ANY)
    scalar = pl.BlockSpec(memory_space=pltpu.SMEM)

    def names(layer):
        return KEPT if layer == LAYERS - 1 else GRAD_NAMES

    def vmem(name):
        return pltpu.VMEM(shape_of(name, frames, tokens), KINDS[name])

    kept = [shape(shape_of(name, frames, tokens), low) for layer in range(LAYERS) for name in names(layer)]
    early_flat = [layer[name] for layer in early for name in NEEDED]
    out = pl.pallas_call(
        functools.partial(model_kernel, channels),
        out_shape=[shape((8, 128), full), shape((D, 128), full), shape(MOD_TILE, full)] + kept,
        in_specs=[scalar] + [here] * 8 + [there] * (3 * LAYERS + len(early_flat)),
        out_specs=[here] * 3 + [there] * len(kept),
        scratch_shapes=[pltpu.VMEM((D, JOINT), low), pltpu.VMEM((text.shape[1], 2 * D), low), pltpu.VMEM((2 * D + FF, D), low)]
        + [vmem(name) for name, *_ in SAVED]
        + [vmem(name) for name in NEEDED] * (LAYERS - 1)
        + [vmem(name) for name, _ in GRADS]
        + [
            pltpu.VMEM((frames, FF), low),
            pltpu.VMEM((frames, D), full),
            pltpu.VMEM((frames, D), low),
            pltpu.VMEM((frames, D), low),
            pltpu.VMEM((frames, D), full),
            pltpu.VMEM((LAYERS, 8, D), full),
            pltpu.VMEM((8, D), full),
            pltpu.SemaphoreType.DMA((len(PARTS),)),
            pltpu.SemaphoreType.DMA((LAYERS, len(KEPT))),
            pltpu.SemaphoreType.DMA((LAYERS, len(NEEDED))),
        ],
        compiler_params=pltpu.CompilerParams(vmem_limit_bytes=VMEM_LIMIT),
    )(
        lengths, facts, stream, mods, final_mods, text, noise, noisy, small,
        *[w for layer in weights for w in layer], *early_flat,
    )
    rest = list(out[3:])
    made = []
    for layer in range(LAYERS):
        count = len(names(layer))
        made.append(dict(zip(names(layer), rest[:count])))
        rest = rest[count:]
    return out[:3], made


def adam_update(weight, grad, first, second, rate):
    first_new = BETA_ONE * first + (1.0 - BETA_ONE) * grad
    second_new = BETA_TWO * second + (1.0 - BETA_TWO) * grad * grad
    first_hat = first_new / (1.0 - BETA_ONE**STEP)
    second_hat = second_new / (1.0 - BETA_TWO**STEP)
    weight_new = weight - rate * (
        first_hat / (jnp.sqrt(second_hat) + ADAM_EPSILON) + WEIGHT_DECAY * weight
    )
    return (first_new, second_new, weight_new)


def adam_kernel(layers, *refs):
    refs = list(refs)

    def take(count):
        taken = refs[:count]
        del refs[:count]
        return taken

    final, grad_mod, time_one, time_two, small = take(5)
    sums = take(3)
    given = [take(3) for _ in range(6)]
    results = [take(3) for _ in range(6)]
    held = [take(3) for _ in range(6)]
    grads = take(3)
    load_sem, grad_sem, store_sem = refs
    own = held[3][0].shape[0]
    groups = [(member, layer) for layer in range(layers) for member in (0, 2)] + [(1, None), (3, None), (4, None), (5, None)]

    def at(ref, layer):
        return ref if layer is None else ref.at[layer]

    def loads(number):
        member, layer = groups[number]
        copies = [
            pltpu.make_async_copy(at(given[member][j], layer), at(held[member][j], layer), load_sem.at[number, j])
            for j in range(3)
        ]
        if member < 3:
            copies.append(
                pltpu.make_async_copy(at(sums[member], layer), at(grads[member], layer), grad_sem.at[number])
            )
        return copies

    def stores(number):
        member, layer = groups[number]
        return [
            pltpu.make_async_copy(
                at(held[member][(j + 1) % 3], layer), at(results[member][j], layer), store_sem.at[number, j]
            )
            for j in range(3)
        ]

    for number in range(len(groups)):
        for copy in loads(number):
            copy.start()
    factor = CLIP_NORM / jnp.maximum(jnp.sqrt(final[0:1, 0:1]), CLIP_NORM)

    def update(member, index, grad, rate=LEARN_RATE):
        weight, first, second = held[member]
        first_new, second_new, weight_new = adam_update(
            weight[index], grad * factor, first[index], second[index], rate
        )
        first[index], second[index], weight[index] = first_new, second_new, weight_new

    for number, (member, layer) in enumerate(groups):
        for copy in loads(number):
            copy.wait()
        if member == 0:
            for column in range(0, JOINT, 1536):
                cols = slice(column, column + 1536)
                update(0, (layer, slice(None), cols), grads[0][layer, :, cols])
            for column in range(0, MOD, 1536):
                start = layer * MOD + column
                update(
                    0, (layer, slice(None), slice(JOINT + column, JOINT + column + 1536)),
                    grad_mod[:own, start : start + 1536],
                )
        elif member == 2:
            for row in range(0, held[2][0].shape[1], 48):
                rows = slice(row, row + 48)
                update(2, (layer, rows), grads[2][layer, rows])
        elif member == 1:
            for other in range(layers):
                for column in range(0, 2 * D, D):
                    index = (other, slice(None), slice(column, column + D))
                    update(1, index, grads[1][index])
        elif member == 4:
            update(4, (slice(None), slice(0, FREQS)), time_one[:own, :])
            tail = held[4][0].shape[1] - FREQS
            update(4, (slice(None), slice(FREQS, FREQS + tail)), small[:, LEAD_LANE : LEAD_LANE + tail])
        elif member == 5:
            turned = jnp.transpose(small[...])
            update(5, (slice(None), slice(None)), turned[GAIN_LANE : GAIN_LANE + layers, :], GAIN_RATE)
        else:
            update(3, (slice(None), slice(0, D)), time_two[:own, :])
            update(3, (slice(None), slice(D, 3 * D)), grad_mod[:own, layers * MOD : layers * MOD + 2 * D])
            tail = held[3][0].shape[1] - 3 * D
            update(3, (slice(None), slice(3 * D, 3 * D + tail)), small[:, :tail])
        for copy in stores(number):
            copy.start()
    for number in range(len(groups)):
        for copy in stores(number):
            copy.wait()


def run_adam(final, grad_mod, time_one, time_two, small, sums, given):
    here, there = pl.BlockSpec(memory_space=pltpu.VMEM), pl.BlockSpec(memory_space=pl.ANY)
    layers = given[0][0].shape[0]
    full = jnp.float32
    shapes = [group[0].shape for group in given]
    count = 2 * layers + 4
    sem = pltpu.SemaphoreType.DMA
    out = pl.pallas_call(
        functools.partial(adam_kernel, layers),
        out_shape=[jax.ShapeDtypeStruct(shape, full) for shape in shapes for _ in range(3)],
        in_specs=[here] * 5 + [there] * 21,
        out_specs=[there] * 18,
        scratch_shapes=[pltpu.VMEM(shape, full) for shape in shapes for _ in range(3)]
        + [pltpu.VMEM(item.shape, full) for item in sums]
        + [sem((count, 3)), sem((count,)), sem((count, 3))],
        compiler_params=pltpu.CompilerParams(vmem_limit_bytes=VMEM_LIMIT),
    )(final, grad_mod, time_one, time_two, small, *sums, *[item for group in given for item in group])
    return [out[3 * k : 3 * k + 3] for k in range(6)]


def tiles(values, lead=()):
    flat = values.reshape(lead + (-1,))
    short = -flat.shape[-1] % 1024
    flat = jnp.pad(flat, [(0, 0)] * len(lead) + [(0, short)])
    return flat.reshape(lead + (-1, 128))


def fast_grads(ways, clean_latent, noise, text_low, text_lengths, timesteps, valid_frames, w_in, w_text, w_out, gains, w_lead, w_head):
    count = ways[0] * ways[1]
    own, channels = w_head.shape[0], noise.shape[-1]
    rows = [w_in.shape[1], w_text.shape[1], w_out.shape[1]]
    halves = [JOINT // 2, D, D // 2]
    sinus = time_features(timesteps)
    facts = jnp.concatenate([to_low(sinus).astype(jnp.float32)[0], valid_frames.astype(jnp.float32)])
    wide = [(0, 0), (0, LEAD_LANE - channels)]
    small = jnp.concatenate(
        [
            jnp.pad(to_low(w_head[:, 3 * D :]).astype(jnp.float32), wide),
            jnp.pad(to_low(w_lead[FREQS:]).astype(jnp.float32).T, wide),
            jnp.pad(to_low(gains).astype(jnp.float32).T, [(0, 0), (0, 128 - GAIN_LANE - LAYERS)]),
        ],
        1,
    )
    level = noise_level(timesteps)
    noisy = jnp.sqrt(level) * clean_latent + jnp.sqrt(1.0 - level) * noise
    noisy = jnp.pad(to_low(noisy), [(0, 0), (LEAD_LANE, 128 - LEAD_LANE - channels)])
    lengths = jnp.concatenate([valid_frames, text_lengths])
    items = plan(halves, range(LAYERS), GATHER_PATTERN)
    weights, given, early = gather_weights(
        [w_in, w_text, w_out], w_head, jnp.concatenate([tiles(facts), small], 0), w_lead.T, lengths, text_low, noisy, own, halves, ways, 1, items,
    )
    packed, pre_time, temb, block_mods, final_mods, small, stream, head_own, mod_own = given
    (ends, grad_small, grad_tile), kept = run_model(
        lengths, packed, stream, block_mods, final_mods, text_low,
        jnp.pad(noise, [(0, 0), (0, 128 - channels)]), noisy, small, weights, [early], channels,
    )
    kept[0] = {**early, **kept[0]}
    items = plan(halves, list(reversed(range(LAYERS))), SCATTER_PATTERN)
    rest = [grad_tile, grad_small.reshape(count, own, 128), ends, packed, pre_time, temb, head_own, mod_own]
    *sums, grad_mod_w, grad_time_one, grad_time_two, small_sum, final = scatter_grads(
        kept, text_low, rest, own, rows, halves, ways, 2, items
    )
    grads = final, grad_mod_w, grad_time_one, grad_time_two, small_sum, sums
    return jnp.sum(final[1]), final[2, 0], jnp.sqrt(final[0, 0]), grads


def plain_grads(ways, clean_latent, noise, text_low, text_lengths, timesteps, valid_frames, w_in, w_text, w_out, gains, w_lead, w_head):
    count = ways[0] * ways[1]
    own, channels = w_head.shape[0], noise.shape[-1]
    frame_keep = lax.iota(jnp.int32, clean_latent.shape[0]) < valid_frames[0]
    text_keep = lax.iota(jnp.int32, text_low.shape[0]) < text_lengths[0]

    def to_all(values):
        return lax.all_gather(values, ALL, axis=0, tiled=True)

    def by_columns(values):
        return values.transpose(1, 0, 2).reshape(values.shape[1], -1)

    lead_low, head_low = to_low(w_lead), to_low(w_head)
    frame_count = jnp.sum(to_all(valid_frames)).astype(jnp.float32)
    sinus_all = to_low(time_features(to_all(timesteps)))
    lead_in = by_columns(to_all(lead_low[None, FREQS:]))
    head_pred = to_all(head_low[:, 3 * D :])
    gains_all = by_columns(to_all(to_low(gains)[None])).astype(jnp.float32)
    act_time, pull_time = jax.vjp(jax.nn.silu, dense(sinus_all, lead_low[:FREQS]))
    act_low = to_low(act_time)
    temb = dense(act_low, head_low[:, :D]).reshape(count, count, own).transpose(1, 0, 2)
    temb = jnp.sum(lax.all_to_all(temb, ALL, 0, 0, tiled=True), 0)
    cond, pull_cond = jax.vjp(jax.nn.silu, temb)
    cond_low = to_low(cond)
    mod_low = jnp.concatenate(
        [to_low(w_in[layer, :, JOINT:]) for layer in range(LAYERS)] + [head_low[:, D : 3 * D]], 1
    )
    mods = jnp.sum(lax.all_to_all(dense(cond_low, mod_low)[:, None], ALL, 0, 0, tiled=True), 0)[0]
    weights = [
        [to_all(to_low(shard[layer])) for shard in (w_in[:, :, :JOINT], w_text, w_out)] for layer in range(LAYERS)
    ]
    level = noise_level(timesteps)
    noisy_low = to_low(jnp.sqrt(level) * clean_latent + jnp.sqrt(1.0 - level) * noise)
    stream = dense(noisy_low, lead_in)
    saved = []
    for layer in range(LAYERS):
        stream, kept = layer_forward(
            stream, mods[layer * MOD : (layer + 1) * MOD], text_low, frame_keep, text_keep,
            (*weights[layer], gains_all[layer]),
        )
        saved.append(kept)
    final_mod = mods[LAYERS * MOD :]
    normed_final, pull_final = jax.vjp(modulate, stream, final_mod[:D], final_mod[D:])
    final_low = to_low(normed_final)
    error = dense(final_low, head_pred) - noise
    loss_part = jnp.sum(jnp.where(frame_keep[:, None], error * error, 0.0))
    grad_pred = to_low(jnp.where(frame_keep[:, None], error * (2.0 / frame_count), 0.0))
    grad_pred_w = weight_grad(final_low, grad_pred)
    grad_stream, grad_shift_f, grad_scale_f = pull_final(dense_back(grad_pred, head_pred))
    grad_mods = [None] * LAYERS + [jnp.concatenate([grad_shift_f, grad_scale_f])]
    big, grad_gains = [None] * LAYERS, [None] * LAYERS
    for layer in reversed(range(LAYERS)):
        grad_stream, grad_mods[layer], big[layer], grad_gains[layer] = layer_backward(
            saved[layer], grad_stream, mods[layer * MOD : (layer + 1) * MOD], text_low,
            (*weights[layer], gains_all[layer]),
        )
    grad_in_w = weight_grad(noisy_low, to_low(grad_stream))
    sums = [
        jnp.stack(
            [lax.psum_scatter(big[layer][member], ALL, scatter_dimension=0, tiled=True) for layer in range(LAYERS)]
        )
        for member in range(3)
    ]
    mods_all = lax.all_gather(to_low(jnp.concatenate(grad_mods)), ALL, axis=0, tiled=False)
    grad_mod_w = weight_grad(cond_low, mods_all)
    (grad_temb,) = pull_cond(dense_back(mods_all, mod_low))
    grad_temb = by_columns(lax.all_gather(to_low(grad_temb), ALL, axis=0, tiled=False))
    grad_time_two = weight_grad(act_low, grad_temb)
    (grad_pre_time,) = pull_time(dense_back(grad_temb, head_low[:, :D]))
    grad_time_one = weight_grad(sinus_all, to_low(grad_pre_time))

    def to_owner(values):
        return lax.psum_scatter(values, ALL, scatter_dimension=0, tiled=True)

    mod_grads = grad_mod_w[:, : LAYERS * MOD].reshape(own, LAYERS, MOD).transpose(1, 0, 2)
    grad_list = [
        jnp.concatenate([sums[0], mod_grads], 2),
        sums[1],
        sums[2],
        to_owner(jnp.stack(grad_gains).T).T,
        jnp.concatenate([grad_time_one, to_owner(grad_in_w.T).T], 0),
        jnp.concatenate([grad_time_two, grad_mod_w[:, LAYERS * MOD :], to_owner(grad_pred_w)], 1),
    ]
    squares = sum((jnp.sum(item * item) for item in grad_list))
    loss_sum, squares = lax.psum((loss_part, squares), ALL)
    return loss_sum, frame_count, jnp.sqrt(squares), grad_list


def body(
    ways,
    clean_latent,
    noise,
    text_feats,
    text_lengths,
    timesteps,
    valid_frames,
    w_in,
    w_text,
    w_out,
    gains,
    w_lead,
    w_head,
    first_in,
    second_in,
    first_text,
    second_text,
    first_out,
    second_out,
    first_gains,
    second_gains,
    first_lead,
    second_lead,
    first_head,
    second_head,
):
    aligned = all(shard.shape[1] % 8 == 0 for shard in (w_in, w_text, w_out)) and all(way % 2 == 0 for way in ways)
    aligned = aligned and w_head.shape[0] <= SHARE and noise.shape[-1] <= LEAD_LANE
    grads_of = fast_grads if aligned else plain_grads
    loss_sum, frame_count, grad_norm, grads = grads_of(
        ways, clean_latent[0], noise[0], text_feats[0], text_lengths, timesteps, valid_frames,
        w_in, w_text, w_out, gains, w_lead, w_head,
    )
    factor = CLIP_NORM / jnp.maximum(grad_norm, CLIP_NORM)
    params = (w_in, w_text, w_out, gains, w_lead, w_head)
    firsts = (first_in, first_text, first_out, first_gains, first_lead, first_head)
    seconds = (second_in, second_text, second_out, second_gains, second_lead, second_head)
    rates = (LEARN_RATE, LEARN_RATE, LEARN_RATE, GAIN_RATE, LEARN_RATE, LEARN_RATE)
    results = [None] * 6
    if aligned:
        given = list(zip(params, firsts, seconds))
        order = (0, 1, 2, 5, 4, 3)
        given[4] = tuple(item.T for item in given[4])
        for k, made in zip(order, run_adam(*grads, [given[k] for k in order])):
            results[k] = [item.T for item in made] if k == 4 else made
    else:
        for k, grad in enumerate(grads):
            results[k] = adam_update(params[k], grad * factor, firsts[k], seconds[k], rates[k])
    return (loss_sum, frame_count, grad_norm, *(item for made in results for item in made))


def solution(mesh):
    ways = (mesh.shape["dp"], mesh.shape["fsdp"])
    clips = [P(ALL, None, None)] * 3 + [P(ALL)] * 3
    weights = [P(None, ALL, None)] * 3 + [P(None, ALL)] * 2 + [P(ALL, None)]
    moments = [spec for spec in weights for _ in range(2)]
    results = [spec for spec in weights for _ in range(3)]
    return jax.shard_map(
        functools.partial(body, ways),
        mesh=mesh,
        in_specs=tuple(clips + weights + moments),
        out_specs=tuple([P()] * 3 + results),
        check_vma=False,
    )
```
